32 devices in a mesh: fsdp: 8 (over z, y), dp: 4 (over x, core).
Axes of the slice: x: 2, y: 2, z: 4, core: 2. Of those that a mesh axis runs over, the one named last changes fastest.
Arguments:
- tokens: bfloat16 [16, 1024, 768], P('fsdp', 'dp'), may hold values from -6 to 6
- condition: bfloat16 [16, 128], P('fsdp'), may hold values from -6 to 6
- segments: int32 [16, 1024], P('fsdp'), may hold values from 0 to 7, as said below
- w_ada: bfloat16 [128, 4608], P(None, 'fsdp'), may hold values from -0.5 to 0.5
- b_ada: bfloat16 [4608], P('fsdp'), may hold values from -1.5 to 1.5
- gain_attn: bfloat16 [768], P('fsdp'), may hold values from 0.5 to 1.5
- w_qkv: bfloat16 [768, 2304], P(None, 'fsdp'), may hold values from -0.21875 to 0.21875
- w_out: bfloat16 [768, 768], P(None, 'fsdp'), may hold values from -0.875 to 0.875
- gain_mlp: bfloat16 [768], P('fsdp'), may hold values from 0.5 to 1.5
- w_up: bfloat16 [768, 3072], P(None, 'fsdp'), may hold values from -0.21875 to 0.21875
- b_up: bfloat16 [3072], P('fsdp'), may hold values from -3 to 3
- w_down: bfloat16 [3072, 768], P(None, 'fsdp'), may hold values from -0.109375 to 0.109375
- b_down: bfloat16 [768], P('fsdp'), may hold values from -3 to 3
- cotangent: bfloat16 [16, 1024, 768], P('fsdp', 'dp'), may hold values from -8 to 8
Outputs:
- outputs: bfloat16 [16, 1024, 768], P('fsdp', 'dp')
- d_tokens: bfloat16 [16, 1024, 768], P('fsdp', 'dp')
- d_condition: bfloat16 [16, 128], P('fsdp')
- d_w_ada: float32 [128, 4608], P(None, 'fsdp')
- d_b_ada: float32 [4608], P('fsdp')
- d_gain_attn: float32 [768], P('fsdp')
- d_w_qkv: float32 [768, 2304], P(None, 'fsdp')
- d_w_out: float32 [768, 768], P(None, 'fsdp')
- d_gain_mlp: float32 [768], P('fsdp')
- d_w_up: float32 [768, 3072], P(None, 'fsdp')
- d_b_up: float32 [3072], P('fsdp')
- d_w_down: float32 [3072, 768], P(None, 'fsdp')
- d_b_down: float32 [768], P('fsdp')
The draws below stay inside these ranges and needn't reach their ends.
Inputs may be any that keep to these rules, and one draw needn't show every extreme that they name: `segments`: within each slot the ids never fall, are 0 at the first position and 7 at the last; of each aligned run of 2 slots, one holds a document that covers positions 128 to 895.
All inputs are finite; a program needn't handle non-finite values.
Results may differ from the reference program's by a relative error of at most 0.018.
Values may be sent and summed in bfloat16 or wider, within the bound.
A program may use at most 192 MiB of HBM per device.

```python
import math
import jax
import jax.numpy as jnp
from jax import lax

D = 768
HEAD = 64
FF = 3072
COND = 128
SEQ = 1024
NDOC = 8
SLOT_DEV = 2
SLOTS = 16
QUART = 256


def drawn_values(key, shape, spread, bound):
    return jax.random.truncated_normal(key, -bound, bound, shape, jnp.float32) * spread


def draw_tokens(key, part):
    key = jax.random.fold_in(key, 21)
    return drawn_values(key, (SLOTS, SEQ, D), 1.0, 6.0).astype(jnp.bfloat16)


def draw_condition(key, part):
    key = jax.random.fold_in(key, 22)
    return drawn_values(key, (SLOTS, COND), 1.0, 6.0).astype(jnp.bfloat16)


def draw_b_ada(key, part):
    key = jax.random.fold_in(key, 23)
    return drawn_values(key, (6 * D,), 0.5, 3.0).astype(jnp.bfloat16)


def draw_segments(key, part):
    key = jax.random.fold_in(key, 11)
    key_free, key_low, key_high, key_pick = jax.random.split(key, 4)
    free_bounds = jax.random.randint(key_free, (SLOTS, NDOC - 1), 1, SEQ)
    low_bounds = jax.random.randint(key_low, (SLOTS, NDOC - 1), 1, QUART // 2 + 1)
    high_bounds = jax.random.randint(key_high, (SLOTS, NDOC - 1), SEQ - QUART // 2, SEQ)
    chosen = jax.random.randint(key_pick, (SLOTS // SLOT_DEV,), 0, SLOT_DEV)
    slot_ids = jnp.arange(SLOTS, dtype=jnp.int32)
    spanning = slot_ids % SLOT_DEV == jnp.repeat(chosen, SLOT_DEV)
    bound_ids = jnp.arange(NDOC - 1, dtype=jnp.int32)
    forced = jnp.where(bound_ids[None, :] % 2 == 0, low_bounds, high_bounds)
    bounds = jnp.where(spanning[:, None], forced, free_bounds)
    places = jnp.arange(SEQ, dtype=jnp.int32)
    crossed = (places[None, :, None] >= bounds[:, None, :]).astype(jnp.int32)
    return jnp.sum(crossed, axis=2).astype(jnp.int32)


def with_spikes(drawn, stream_key, source, target, blocks, factor):
    def block_of(dim):
        return (jnp.arange(drawn.shape[dim]) // (drawn.shape[dim] // blocks)).reshape((-1,) + (1,) * (drawn.ndim - 1 - dim))

    one_side = jax.random.permutation(stream_key, blocks)[block_of(target)]
    other_side = (block_of(target) + blocks // 2) % blocks
    return jnp.where((block_of(source) == one_side) | (block_of(source) == other_side), factor * drawn, drawn)


def level_of(rng, extent, cuts, least, largest):
    loudness = 1.0
    for position, parts in cuts:
        steps = jax.random.uniform(jax.random.fold_in(jax.random.fold_in(rng, 6), position), (parts,), jnp.float32, least / len(cuts), largest / len(cuts))
        loudness = loudness * jnp.repeat(jnp.exp(steps), extent[position] // parts).reshape((-1,) + (1,) * (len(extent) - 1 - position))
    return loudness


def bell_draw(own_key, extent, deviation, reach, cuts=(), kind=jnp.bfloat16):
    array = jax.random.normal(own_key, extent, jnp.float32) * deviation
    if len(cuts) > 0:
        array = level_of(own_key, extent, cuts, -0.22, 0.18) * array
    return jnp.clip(array, min=-reach, max=reach).astype(kind)


def bell_draw_with(own_key, dims, deviation, reach, shards, heavy, kind=jnp.bfloat16):
    array = deviation * jax.random.normal(own_key, dims, jnp.float32)
    if shards:
        array = array * level_of(own_key, dims, shards, -0.22, 0.18)
    return jnp.clip(with_spikes(array, jax.random.fold_in(own_key, 3), *heavy), -reach, reach).astype(kind)


def setup_inputs(seed: int = 0) -> dict:
    key_list = jax.random.split(jax.random.key(seed), 15)
    return {
        "tokens": draw_tokens(jax.random.fold_in(key_list[14], 71), 0),
        "condition": draw_condition(jax.random.fold_in(key_list[14], 71), 0),
        "segments": draw_segments(jax.random.fold_in(key_list[14], 71), 0),
        "w_ada": bell_draw(key_list[3], (COND, 6 * D), COND ** -0.5, 0.5, ((1, 8),)),
        "b_ada": draw_b_ada(jax.random.fold_in(key_list[14], 71), 0),
        "gain_attn": jnp.clip(1.0 + 0.1 * jax.random.normal(key_list[5], (D,), jnp.float32), 0.5, 1.5).astype(jnp.bfloat16),
        "w_qkv": bell_draw(key_list[6], (D, 3 * D), D ** -0.5, 0.21875, ((1, 8),)),
        "w_out": bell_draw(key_list[7], (D, D), (D // 16) ** -0.5, 0.875, ((1, 8),)),
        "gain_mlp": jnp.clip(1.0 + 0.1 * jax.random.normal(key_list[8], (D,), jnp.float32), 0.5, 1.5).astype(jnp.bfloat16),
        "w_up": bell_draw(key_list[9], (D, FF), D ** -0.5, 0.21875, ((1, 8),)),
        "b_up": bell_draw(key_list[10], (FF,), 0.5, 3.0, ((0, 8),)),
        "w_down": bell_draw(key_list[11], (FF, D), FF ** -0.5, 0.109375, ((1, 8),)),
        "b_down": bell_draw(key_list[12], (D,), 0.5, 3.0, ((0, 8),)),
        "cotangent": bell_draw_with(key_list[13], (SLOTS, SEQ, D), 1.0, 8.0, ((0, 8), (1, 4)), (0, 2, 8, 2.0)),
    }


epsilon = 1e-05
rope_base = 10000.0
masked_fill = -1e+30
highest = lax.Precision.HIGHEST

@jax.custom_vjp
def low(v):
    return lax.optimization_barrier(v.astype(jnp.bfloat16)).astype(jnp.float32)

@jax.custom_vjp
def low_back(v):
    return v

def low_keep(v):
    return (low(v), None)

def low_pass(kept, grad):
    return (grad,)

def back_keep(v):
    return (v, None)

def back_low(kept, grad):
    return (low(grad),)
low.defvjp(low_keep, low_pass)
low_back.defvjp(back_keep, back_low)

def norm_mod(stream, gain_row, shift_rows, scale_rows):
    average = lax.optimization_barrier(jnp.mean(stream, axis=-1, keepdims=True))
    centered = stream - average
    variance = lax.optimization_barrier(jnp.mean(centered * centered, axis=-1, keepdims=True))
    normal = centered * lax.rsqrt(variance + epsilon)
    return normal * gain_row * (1.0 + scale_rows[..., None, :]) + shift_rows[..., None, :]

def doc_positions(segments):
    length = segments.shape[-1]
    places = jnp.broadcast_to(jnp.arange(length, dtype=jnp.int32), segments.shape)
    starts_here = jnp.concatenate([jnp.ones(segments.shape[:-1] + (1,), jnp.bool_), segments[..., 1:] != segments[..., :-1]], axis=-1)
    openings = jnp.where(starts_here, places, jnp.zeros_like(places))
    return places - lax.cummax(openings, axis=segments.ndim - 1)

def rope_tables(positions, head_size):
    half_steps = jnp.arange(head_size // 2, dtype=jnp.float32)
    inverse = rope_base ** (-2.0 * half_steps / head_size)
    angles = positions.astype(jnp.float32)[..., None] * inverse
    return (jnp.cos(angles), jnp.sin(angles))

def rotate(vectors, cosine, sine_table):
    half_size = vectors.shape[-1] // 2
    former = vectors[..., :half_size]
    latter = vectors[..., half_size:]
    cosine_wide = cosine[..., None, :]
    sine_wide = sine_table[..., None, :]
    return jnp.concatenate([former * cosine_wide - latter * sine_wide, latter * cosine_wide + former * sine_wide], axis=-1)

def slot_attention(inputs):
    queries, keys, values, segments = inputs
    scores = low_back(jnp.einsum('qhd,khd->hqk', queries, keys, precision=highest) * (1.0 / math.sqrt(HEAD)))
    allowed = segments[:, None] == segments[None, :]
    weights = low(jax.nn.softmax(jnp.where(allowed[None], scores, masked_fill), axis=-1))
    attended = jnp.einsum('hqk,khd->qhd', weights, values, precision=highest)
    return low(low_back(attended)).reshape(segments.shape[0], -1)

def block_forward(stream, condition, segments, w_ada, b_ada, gain_attn, w_qkv, w_out, gain_mlp, w_up, b_up, w_down, b_down):
    modulation = low_back(jnp.dot(condition, w_ada, precision=highest) + b_ada)
    groups = jnp.split(modulation, 6, axis=-1)
    normed = low(norm_mod(stream, gain_attn, groups[0], groups[1]))
    projected = low_back(jnp.einsum('gsd,de->gse', normed, w_qkv, precision=highest))
    model_width = stream.shape[-1]
    positions = doc_positions(segments)
    cosine, sine_table = rope_tables(positions, HEAD)
    head_shape = segments.shape + (model_width // HEAD, HEAD)
    queries = low(rotate(projected[..., :model_width].reshape(head_shape), cosine, sine_table))
    keys = low(rotate(projected[..., model_width:2 * model_width].reshape(head_shape), cosine, sine_table))
    values = low(projected[..., 2 * model_width:].reshape(head_shape))
    attended = lax.map(jax.checkpoint(slot_attention), (queries, keys, values, segments))
    branch_attn = low_back(jnp.einsum('gsd,de->gse', attended, w_out, precision=highest))
    middle = stream + groups[2][:, None, :] * branch_attn
    normed_mlp = low(norm_mod(middle, gain_mlp, groups[3], groups[4]))
    hidden = low_back(jnp.einsum('gsd,df->gsf', normed_mlp, w_up, precision=highest) + b_up)
    activated = low(jax.nn.gelu(hidden, approximate=True))
    branch_mlp = low_back(jnp.einsum('gsf,fd->gsd', activated, w_down, precision=highest) + b_down)
    return middle + groups[5][:, None, :] * branch_mlp

def reference(tokens, condition, segments, w_ada, b_ada, gain_attn, w_qkv, w_out, gain_mlp, w_up, b_up, w_down, b_down, cotangent):
    weight_list = tuple((weight_arg.astype(jnp.float32) for weight_arg in (w_ada, b_ada, gain_attn, w_qkv, w_out, gain_mlp, w_up, b_up, w_down, b_down)))
    group = math.gcd(SLOTS, max(1, 4096 // SEQ))
    steps_count = SLOTS // group

    def batched(source):
        return source.reshape((steps_count, group) + source.shape[1:])
    inputs = (batched(tokens.astype(jnp.float32)), batched(condition.astype(jnp.float32)), batched(segments), batched(cotangent.astype(jnp.float32)))

    def scan_step(totals, batch_rows):
        stream, cond_rows, seg_rows, cot_rows = batch_rows

        def forward_rows(stream_in, cond_in, *weights_in):
            return block_forward(stream_in, cond_in, seg_rows, *weights_in)
        result, pullback = jax.vjp(forward_rows, stream, cond_rows, *weight_list)
        gradients = pullback(cot_rows)
        new_totals = tuple((summed + gradient for summed, gradient in zip(totals, gradients[2:])))
        return (new_totals, (result.astype(jnp.bfloat16), gradients[0].astype(jnp.bfloat16), gradients[1].astype(jnp.bfloat16)))
    initial = tuple((jnp.zeros_like(weight_arg) for weight_arg in weight_list))
    totals, stacked = lax.scan(scan_step, initial, inputs)
    outputs = stacked[0].reshape(tokens.shape)
    d_tokens = stacked[1].reshape(tokens.shape)
    d_condition = stacked[2].reshape(condition.shape)
    return (outputs, d_tokens, d_condition, totals[0], totals[1], totals[2], totals[3], totals[4], totals[5], totals[6], totals[7], totals[8], totals[9])
```

```python
import functools
import math

import jax
import jax.numpy as jnp
import numpy as np
from jax import lax
from jax.experimental import pallas as pl
from jax.experimental.pallas import tpu as pltpu
from jax.sharding import PartitionSpec as P

HEAD = 64
EPS = 1e-05
ROPE_BASE = 10000.0
MASKED = -1e30
F32 = jnp.float32
BF16 = jnp.bfloat16

NN = (((1,), (0,)), ((), ()))
NT = (((1,), (1,)), ((), ()))
TN = (((0,), (0,)), ((), ()))


def mm(a, b, dims):
    return lax.dot_general(a, b, dims, preferred_element_type=F32)


def rope_table(length):
    inverse = ROPE_BASE ** (-2.0 * np.arange(HEAD // 2) / HEAD)
    angles = np.arange(length)[:, None] * inverse[None, :]
    cosine = np.concatenate([np.cos(angles)] * 2, axis=1)
    sine = np.concatenate([-np.sin(angles), np.sin(angles)], axis=1)
    return cosine.astype(np.float32), sine.astype(np.float32)


def swap_halves(v):
    half = HEAD // 2
    return jnp.concatenate([v[..., half:], v[..., :half]], axis=-1)


def key_window(segments_row, own_row, tile):
    first = jnp.min(own_row)
    last = jnp.max(own_row)
    low = jnp.sum((segments_row < first).astype(jnp.int32))
    high = jnp.sum((segments_row <= last).astype(jnp.int32)) - 1
    start = low // tile
    return start, high // tile - start + 1


def as_column(row):
    size = row.shape[1]
    return jnp.transpose(jnp.broadcast_to(row, (128, size)))[:, :1]


def attend_kernel(tile, seg_ref, qkv_ref, out_ref, log_ref):
    length = seg_ref.shape[2]
    part = qkv_ref.shape[2] // 3
    heads = part // HEAD
    rows = pl.ds(pl.multiple_of(pl.program_id(1) * tile, tile), tile)
    own_row = seg_ref[0, :, rows]
    start, width = key_window(seg_ref[0], own_row, tile)
    own_col = as_column(own_row)
    keys = pl.multiple_of(start * tile, tile)
    for w in range(1, length // tile + 1):

        @pl.when(width == w)
        def _(w=w):
            cols = pl.ds(keys, w * tile)
            same = own_col == seg_ref[0, :, cols]
            for h in range(heads):
                at = h * HEAD
                q = qkv_ref[0, rows, at : at + HEAD]
                k = qkv_ref[0, cols, part + at : part + at + HEAD]
                v = qkv_ref[0, cols, 2 * part + at : 2 * part + at + HEAD]
                scores = jnp.where(same, mm(q, k, NT), MASKED)
                largest = jnp.max(scores, axis=1, keepdims=True)
                weights = jnp.exp(scores - largest)
                total = jnp.sum(weights, axis=1, keepdims=True)
                result = mm(weights.astype(BF16), v, NN) / total
                out_ref[0, :, at : at + HEAD] = result.astype(BF16)
                log_ref[0, :, h : h + 1] = largest + jnp.log(total)


def attend(segments, qkv, tile):
    slots, length, wide = qkv.shape
    part = wide // 3
    return pl.pallas_call(
        functools.partial(attend_kernel, tile),
        grid=(slots, length // tile),
        out_shape=(
            jax.ShapeDtypeStruct((slots, length, part), BF16),
            jax.ShapeDtypeStruct((slots, length, 128), F32),
        ),
        in_specs=[
            pl.BlockSpec((1, 1, length), lambda s, b: (s, 0, 0)),
            pl.BlockSpec((1, length, wide), lambda s, b: (s, 0, 0)),
        ],
        out_specs=(
            pl.BlockSpec((1, tile, part), lambda s, b: (s, b, 0)),
            pl.BlockSpec((1, tile, 128), lambda s, b: (s, b, 0)),
        ),
        compiler_params=pltpu.CompilerParams(vmem_limit_bytes=48 << 20),
        name="attend",
    )(segments[:, None, :], qkv)


def attend_back_kernel(
    tile, seg_ref, qkv_ref, grad_ref, out_ref, log_ref, cos_ref, sin_ref, back_ref, dk_ref, dv_ref
):
    length = seg_ref.shape[2]
    part = qkv_ref.shape[2] // 3
    heads = part // HEAD
    step = pl.program_id(1)
    rows = pl.ds(pl.multiple_of(step * tile, tile), tile)
    own_row = seg_ref[0, :, rows]
    start, width = key_window(seg_ref[0], own_row, tile)
    own_col = as_column(own_row)
    keys = pl.multiple_of(start * tile, tile)
    scale = 1.0 / math.sqrt(HEAD)

    @pl.when(step == 0)
    def _():
        dk_ref[...] = jnp.zeros_like(dk_ref)
        dv_ref[...] = jnp.zeros_like(dv_ref)

    for w in range(1, length // tile + 1):

        @pl.when(width == w)
        def _(w=w):
            cols = pl.ds(keys, w * tile)
            same = own_col == seg_ref[0, :, cols]
            cosine = cos_ref[rows, :]
            sine = sin_ref[rows, :]
            for h in range(heads):
                at = h * HEAD
                q = qkv_ref[0, rows, at : at + HEAD]
                k = qkv_ref[0, cols, part + at : part + at + HEAD]
                v = qkv_ref[0, cols, 2 * part + at : 2 * part + at + HEAD]
                g = grad_ref[0, :, at : at + HEAD]
                o = out_ref[0, :, at : at + HEAD]
                inner = jnp.sum(g.astype(F32) * o.astype(F32), axis=1, keepdims=True)
                scores = jnp.where(same, mm(q, k, NT), MASKED)
                weights = jnp.exp(scores - log_ref[0, :, h : h + 1])
                dots = mm(g, v, NT)
                dscores = (weights * (dots - inner)).astype(BF16)
                dq = mm(dscores, k, NN) * scale
                back_ref[0, rows, at : at + HEAD] = (dq * cosine - swap_halves(dq) * sine).astype(BF16)
                dk_ref[cols, at : at + HEAD] += mm(dscores, q, TN)
                dv_ref[cols, at : at + HEAD] += mm(weights.astype(BF16), g, TN)

    @pl.when(step == pl.num_programs(1) - 1)
    def _():
        cosine = cos_ref[...]
        sine = sin_ref[...]
        for h in range(heads):
            at = h * HEAD
            dk = dk_ref[:, at : at + HEAD]
            back_ref[0, :, part + at : part + at + HEAD] = (
                dk * cosine - swap_halves(dk) * sine
            ).astype(BF16)
        back_ref[0, :, 2 * part :] = dv_ref[...].astype(BF16)


def attend_back(segments, qkv, grad, out, log, cosine, sine, tile):
    slots, length, wide = qkv.shape
    part = wide // 3
    whole = lambda s, b: (s, 0, 0)
    step = lambda s, b: (s, b, 0)
    table = lambda s, b: (0, 0)
    return pl.pallas_call(
        functools.partial(attend_back_kernel, tile),
        grid=(slots, length // tile),
        out_shape=jax.ShapeDtypeStruct((slots, length, wide), BF16),
        in_specs=[
            pl.BlockSpec((1, 1, length), whole),
            pl.BlockSpec((1, length, wide), whole),
            pl.BlockSpec((1, tile, part), step),
            pl.BlockSpec((1, tile, part), step),
            pl.BlockSpec((1, tile, 128), step),
            pl.BlockSpec((length, HEAD), table),
            pl.BlockSpec((length, HEAD), table),
        ],
        out_specs=pl.BlockSpec((1, length, wide), whole),
        scratch_shapes=[pltpu.VMEM((length, part), F32)] * 2,
        compiler_params=pltpu.CompilerParams(vmem_limit_bytes=48 << 20),
        name="attend_back",
    )(segments[:, None, :], qkv, grad, out, log, cosine, sine)


def norm_parts(stream):
    average = jnp.mean(stream, axis=-1, keepdims=True)
    centered = stream - average
    variance = jnp.mean(centered * centered, axis=-1, keepdims=True)
    inverse = lax.rsqrt(variance + EPS)
    return centered * inverse, inverse


def norm_back(grad, normal, inverse, factor):
    e = grad * factor
    mean_e = jnp.mean(e, axis=-1, keepdims=True)
    mean_en = jnp.mean(e * normal, axis=-1, keepdims=True)
    return inverse * (e - mean_e - normal * mean_en)


def column_plan(shards_n, ranks, columns):
    per = columns // shards_n
    rank_of = (np.arange(columns) // HEAD) % ranks
    lists = [
        [[c for c in range(per) if rank_of[f * per + c] == r] for r in range(ranks)]
        for f in range(shards_n)
    ]
    most = max(len(l) for row in lists for l in row)
    most = -(-most // 16) * 16
    take = np.full((shards_n, ranks, most), -1, np.int32)
    place = np.full((ranks, shards_n * most), -1, np.int32)
    home = np.full((shards_n, ranks * most), -1, np.int32)
    for r in range(ranks):
        order = {c: i for i, c in enumerate(np.flatnonzero(rank_of == r))}
        for f in range(shards_n):
            for i, c in enumerate(lists[f][r]):
                take[f, r, i] = c
                place[r, f * most + i] = order[f * per + c]
                home[f, r * most + i] = c
    return most, take, place, home


def pick(indices, size):
    return (indices[:, None] == jnp.arange(size, dtype=jnp.int32)[None, :]).astype(BF16)


def shards(
    tokens,
    condition,
    segments,
    w_ada,
    b_ada,
    gain_attn,
    w_qkv,
    w_out,
    gain_mlp,
    w_up,
    b_up,
    w_down,
    b_down,
    cotangent,
):
    slots, quarter, width = tokens.shape
    length = segments.shape[1]
    n = lax.axis_size("fsdp")
    m = lax.axis_size("dp")
    f = lax.axis_index("fsdp")
    d = lax.axis_index("dp")
    heads = width // HEAD
    part = width // m
    hidden_part = w_up.shape[1] * n // m
    tile = 256
    cos_np, sin_np = rope_table(length)
    cosine, sine = jnp.asarray(cos_np), jnp.asarray(sin_np)

    cond_all = lax.all_gather(condition, "fsdp", axis=0, tiled=True)
    mod_cols = mm(cond_all, w_ada, NN) + b_ada.astype(F32)
    modulation = lax.all_to_all(mod_cols, "fsdp", 0, 1, tiled=True)
    shift_attn, scale_attn, gate_attn, shift_mlp, scale_mlp, gate_mlp = [
        g[:, None, :] for g in jnp.split(modulation, 6, axis=-1)
    ]
    own_vec = jnp.concatenate([b_up, gain_attn, gain_mlp, b_down])[None]
    vecs = lax.all_gather(own_vec, "fsdp", axis=0, tiled=True).astype(F32)
    ups = b_up.shape[0]
    small = gain_attn.shape[0]
    b_up_all = vecs[:, :ups].reshape(n, m, ups // m)
    b_up_rank = lax.dynamic_index_in_dim(b_up_all, d, 1, False).reshape(-1)
    gain_attn_all = vecs[:, ups : ups + small].reshape(-1)
    gain_mlp_all = vecs[:, ups + small : ups + 2 * small].reshape(-1)
    b_down_all = vecs[:, ups + 2 * small :].reshape(-1)

    most, take, place, home = column_plan(n, m, w_qkv.shape[1] * n)
    picked = pick(jnp.asarray(take)[f, d], w_qkv.shape[1])
    qkv_rows = mm(picked, w_qkv, NT).astype(BF16)
    up_rows = lax.dynamic_slice_in_dim(w_up, d * (ups // m), ups // m, 1).T
    down_rows = lax.dynamic_index_in_dim(
        w_down.reshape(n, m, ups // m, small), d, 1, False
    ).reshape(-1, small).T
    out_rows = w_out.reshape(heads // m, m, HEAD, small).transpose(1, 0, 2, 3).reshape(-1, small).T
    qkv_packed = lax.all_gather(qkv_rows, "fsdp", axis=0, tiled=True)
    placing = pick(jnp.asarray(place)[d], 3 * part)
    w_qkv_t = mm(placing, qkv_packed, TN).astype(BF16)
    w_out_t = lax.all_gather(out_rows, "fsdp", axis=0, tiled=True)
    w_up_t = lax.all_gather(up_rows, "fsdp", axis=0, tiled=True)
    w_down_t = lax.all_gather(down_rows, "fsdp", axis=0, tiled=True)

    group_tokens = lax.all_gather(tokens, "dp", axis=1, tiled=True)
    normal, _ = norm_parts(group_tokens.astype(F32))
    normed = (normal * (gain_attn_all * (1.0 + scale_attn)) + shift_attn).astype(BF16)
    projected = mm(normed.reshape(-1, width), w_qkv_t, NT).reshape(slots, length, 3 * heads // m, HEAD)
    rot = projected * cosine[:, None, :] + swap_halves(projected) * sine[:, None, :]
    hr = heads // m
    qkv = jnp.concatenate(
        [rot[:, :, :hr] * (1.0 / math.sqrt(HEAD)), rot[:, :, hr : 2 * hr], projected[:, :, 2 * hr :]],
        axis=2,
    ).astype(BF16).reshape(slots, length, 3 * part)

    attended, logs = attend(segments, qkv, tile)

    own = lax.all_to_all(attended, "dp", 1, 2, tiled=True)
    own_tokens = tokens.astype(F32)
    flat = lambda v: v.reshape(-1, v.shape[-1])
    back = lambda v: v.reshape(slots, -1, v.shape[-1])
    branch_attn = back(mm(flat(own), w_out_t, NT))
    middle = own_tokens + gate_attn * branch_attn
    normal_mlp, inverse_mlp = norm_parts(middle)
    normed_mlp = (normal_mlp * (gain_mlp_all * (1.0 + scale_mlp)) + shift_mlp).astype(BF16)
    normed_mlp_all = flat(lax.all_gather(normed_mlp, "dp", axis=1, tiled=True))
    cot_all = lax.all_gather(cotangent, "dp", axis=1, tiled=True)
    gbm = flat((cot_all.astype(F32) * gate_mlp).astype(BF16))
    hidden = mm(normed_mlp_all, w_up_t, NT) + b_up_rank
    activated, gelu_pull = jax.vjp(lambda h: jax.nn.gelu(h, approximate=True), hidden)
    activated = activated.astype(BF16)
    branch_part = back(mm(activated, w_down_t, NT).astype(BF16))
    branch_mlp = lax.psum_scatter(branch_part, "dp", scatter_dimension=1, tiled=True).astype(F32) + b_down_all
    outputs = (middle + gate_mlp * branch_mlp).astype(BF16)
    grad_act = mm(gbm, w_down_t, NN)
    grad_hidden = gelu_pull(grad_act)[0].astype(BF16)
    grad_normed_part = back(mm(grad_hidden, w_up_t, NN).astype(BF16))
    grad_normed_mlp = lax.psum_scatter(
        grad_normed_part, "dp", scatter_dimension=1, tiled=True
    ).astype(F32)
    cot = cotangent.astype(F32)
    own_gbm = (cot * gate_mlp).astype(BF16).astype(F32)
    grad_middle = cot + norm_back(
        grad_normed_mlp, normal_mlp, inverse_mlp, gain_mlp_all * (1.0 + scale_mlp)
    )
    grad_branch_attn = (grad_middle * gate_attn).astype(BF16)
    grad_att_own = back(mm(flat(grad_branch_attn), w_out_t, NN).astype(BF16))
    grad_attended = lax.all_to_all(grad_att_own, "dp", 2, 1, tiled=True)

    dw_down_t = mm(gbm, activated, TN).astype(BF16)
    dw_up_t = mm(grad_hidden, normed_mlp_all, TN).astype(BF16)
    dw_out_t = mm(flat(grad_branch_attn), flat(own), TN).astype(BF16)
    db_up = jnp.sum(grad_hidden.astype(F32), axis=0)

    gqkv = attend_back(segments, qkv, grad_attended, attended, logs, cosine, sine, tile)
    gqkv_flat = flat(gqkv)
    dw_qkv_t = mm(gqkv_flat, flat(normed), TN).astype(BF16)
    grad_normed = lax.psum_scatter(
        back(mm(gqkv_flat, w_qkv_t, NN).astype(BF16)), "dp", scatter_dimension=1, tiled=True
    ).astype(F32)
    normal_attn, inverse_attn = norm_parts(own_tokens)
    d_tokens = (
        grad_middle
        + norm_back(grad_normed, normal_attn, inverse_attn, gain_attn_all * (1.0 + scale_attn))
    ).astype(BF16)

    sum_attn = jnp.sum(grad_normed * normal_attn, axis=1)
    sum_mlp = jnp.sum(grad_normed_mlp * normal_mlp, axis=1)
    sums = jnp.concatenate(
        [
            jnp.sum(grad_normed, axis=1),
            sum_attn,
            jnp.sum(grad_middle * branch_attn, axis=1),
            jnp.sum(grad_normed_mlp, axis=1),
            sum_mlp,
            jnp.sum(cot * branch_mlp, axis=1),
            jnp.sum(own_gbm, axis=1),
        ],
        axis=-1,
    )
    sums = lax.psum(sums, "dp")
    sh_a, sc_a, ga_a, sh_m, sc_m, ga_m, gb = jnp.split(sums, 7, axis=-1)
    d_gain_attn = jnp.sum(sc_a * (1.0 + scale_attn[:, 0]), axis=0)
    d_gain_mlp = jnp.sum(sc_m * (1.0 + scale_mlp[:, 0]), axis=0)
    d_b_down = jnp.sum(gb, axis=0)
    gmod = jnp.concatenate(
        [sh_a, sc_a * gain_attn_all, ga_a, sh_m, sc_m * gain_mlp_all, ga_m], axis=-1
    ).astype(BF16)
    gmod_cols = lax.all_to_all(gmod, "fsdp", 1, 0, tiled=True)
    d_w_ada = mm(cond_all, gmod_cols, TN)
    d_b_ada = jnp.sum(gmod_cols.astype(F32), axis=0)
    d_condition = lax.psum_scatter(
        mm(gmod_cols, w_ada, NT), "fsdp", scatter_dimension=0, tiled=True
    ).astype(BF16)
    vec_sums = lax.psum_scatter(
        jnp.stack([d_gain_attn, d_gain_mlp, d_b_down]), "fsdp", scatter_dimension=1, tiled=True
    )

    def scatter(v):
        return lax.psum_scatter(v, "fsdp", scatter_dimension=0, tiled=True)

    def spread(v):
        return lax.all_gather(v, "dp", axis=0)

    up_all = spread(scatter(dw_up_t))
    d_w_up = up_all.reshape(-1, width).astype(F32).T
    down_all = spread(scatter(dw_down_t))
    d_w_down = (
        down_all.reshape(m, small, n, ups // m).transpose(2, 0, 3, 1).reshape(-1, small).astype(F32)
    )
    out_all = lax.psum(scatter(dw_out_t).astype(F32), "dp")
    d_w_out = (
        out_all.reshape(small, m, heads // m, HEAD).transpose(2, 1, 3, 0).reshape(-1, small)
    )
    d_b_up = spread(scatter(db_up)).reshape(-1)
    qkv_all = spread(scatter(mm(placing, dw_qkv_t, NN).astype(BF16)))
    homing = pick(jnp.asarray(home)[f], w_qkv.shape[1])
    d_w_qkv = mm(qkv_all.reshape(-1, width), homing, TN)
    return (
        outputs,
        d_tokens,
        d_condition,
        d_w_ada,
        d_b_ada,
        vec_sums[0],
        d_w_qkv,
        d_w_out,
        vec_sums[1],
        d_w_up,
        d_b_up,
        d_w_down,
        vec_sums[2],
    )


def solution(mesh):
    return jax.shard_map(
        shards,
        mesh=mesh,
        in_specs=(
            P("fsdp", "dp", None),
            P("fsdp", None),
            P("fsdp", None),
            P(None, "fsdp"),
            P("fsdp"),
            P("fsdp"),
            P(None, "fsdp"),
            P(None, "fsdp"),
            P("fsdp"),
            P(None, "fsdp"),
            P("fsdp"),
            P(None, "fsdp"),
            P("fsdp"),
            P("fsdp", "dp", None),
        ),
        out_specs=(
            P("fsdp", "dp", None),
            P("fsdp", "dp", None),
            P("fsdp", None),
            P(None, "fsdp"),
            P("fsdp"),
            P("fsdp"),
            P(None, "fsdp"),
            P(None, "fsdp"),
            P("fsdp"),
            P(None, "fsdp"),
            P("fsdp"),
            P(None, "fsdp"),
            P("fsdp"),
        ),
        check_vma=False,
    )
```

```python
import functools
import math

import jax
import jax.numpy as jnp
import numpy as np
from jax import lax
from jax.experimental import pallas as pl
from jax.experimental.pallas import tpu as pltpu
from jax.sharding import PartitionSpec as P

HEAD = 64
EPS = 1e-05
ROPE_BASE = 10000.0
MASKED = -1e30
F32 = jnp.float32
BF16 = jnp.bfloat16

NN = (((1,), (0,)), ((), ()))
NT = (((1,), (1,)), ((), ()))
TN = (((0,), (0,)), ((), ()))


def mm(a, b, dims):
    return lax.dot_general(a, b, dims, preferred_element_type=F32)


def rope_table(length):
    inverse = ROPE_BASE ** (-2.0 * np.arange(HEAD // 2) / HEAD)
    angles = np.arange(length)[:, None] * inverse[None, :]
    cosine = np.concatenate([np.cos(angles)] * 2, axis=1)
    sine = np.concatenate([-np.sin(angles), np.sin(angles)], axis=1)
    return cosine.astype(np.float32), sine.astype(np.float32)


def swap_halves(v):
    half = HEAD // 2
    return jnp.concatenate([v[..., half:], v[..., :half]], axis=-1)


def key_window(segments_row, own_row, tile):
    first = jnp.min(own_row)
    last = jnp.max(own_row)
    low = jnp.sum((segments_row < first).astype(jnp.int32))
    high = jnp.sum((segments_row <= last).astype(jnp.int32)) - 1
    start = low // tile
    return start, high // tile - start + 1


def as_column(row):
    size = row.shape[1]
    return jnp.transpose(jnp.broadcast_to(row, (128, size)))[:, :1]


def attend_kernel(tile, seg_ref, qkv_ref, out_ref, log_ref):
    length = seg_ref.shape[2]
    part = qkv_ref.shape[2] // 3
    heads = part // HEAD
    rows = pl.ds(pl.multiple_of(pl.program_id(1) * tile, tile), tile)
    own_row = seg_ref[0, :, rows]
    start, width = key_window(seg_ref[0], own_row, tile)
    own_col = as_column(own_row)
    keys = pl.multiple_of(start * tile, tile)
    for w in range(1, length // tile + 1):

        @pl.when(width == w)
        def _(w=w):
            cols = pl.ds(keys, w * tile)
            same = own_col == seg_ref[0, :, cols]
            for h in range(heads):
                at = h * HEAD
                q = qkv_ref[0, rows, at : at + HEAD]
                k = qkv_ref[0, cols, part + at : part + at + HEAD]
                v = qkv_ref[0, cols, 2 * part + at : 2 * part + at + HEAD]
                scores = jnp.where(same, mm(q, k, NT), MASKED)
                largest = jnp.max(scores, axis=1, keepdims=True)
                weights = jnp.exp(scores - largest)
                total = jnp.sum(weights, axis=1, keepdims=True)
                result = mm(weights.astype(BF16), v, NN) / total
                out_ref[0, :, at : at + HEAD] = result.astype(BF16)
                log_ref[0, :, h : h + 1] = largest + jnp.log(total)


def attend(segments, qkv, tile):
    slots, length, wide = qkv.shape
    part = wide // 3
    return pl.pallas_call(
        functools.partial(attend_kernel, tile),
        grid=(slots, length // tile),
        out_shape=(
            jax.ShapeDtypeStruct((slots, length, part), BF16),
            jax.ShapeDtypeStruct((slots, length, 128), F32),
        ),
        in_specs=[
            pl.BlockSpec((1, 1, length), lambda s, b: (s, 0, 0)),
            pl.BlockSpec((1, length, wide), lambda s, b: (s, 0, 0)),
        ],
        out_specs=(
            pl.BlockSpec((1, tile, part), lambda s, b: (s, b, 0)),
            pl.BlockSpec((1, tile, 128), lambda s, b: (s, b, 0)),
        ),
        compiler_params=pltpu.CompilerParams(vmem_limit_bytes=48 << 20),
        name="attend",
    )(segments[:, None, :], qkv)


def attend_back_kernel(
    tile, seg_ref, qkv_ref, grad_ref, out_ref, log_ref, cos_ref, sin_ref, back_ref, dk_ref, dv_ref
):
    length = seg_ref.shape[2]
    part = qkv_ref.shape[2] // 3
    heads = part // HEAD
    step = pl.program_id(1)
    rows = pl.ds(pl.multiple_of(step * tile, tile), tile)
    own_row = seg_ref[0, :, rows]
    start, width = key_window(seg_ref[0], own_row, tile)
    own_col = as_column(own_row)
    keys = pl.multiple_of(start * tile, tile)
    scale = 1.0 / math.sqrt(HEAD)

    @pl.when(step == 0)
    def _():
        dk_ref[...] = jnp.zeros_like(dk_ref)
        dv_ref[...] = jnp.zeros_like(dv_ref)

    for w in range(1, length // tile + 1):

        @pl.when(width == w)
        def _(w=w):
            cols = pl.ds(keys, w * tile)
            same = own_col == seg_ref[0, :, cols]
            cosine = cos_ref[rows, :]
            sine = sin_ref[rows, :]
            for h in range(heads):
                at = h * HEAD
                q = qkv_ref[0, rows, at : at + HEAD]
                k = qkv_ref[0, cols, part + at : part + at + HEAD]
                v = qkv_ref[0, cols, 2 * part + at : 2 * part + at + HEAD]
                g = grad_ref[0, :, at : at + HEAD]
                o = out_ref[0, :, at : at + HEAD]
                inner = jnp.sum(g.astype(F32) * o.astype(F32), axis=1, keepdims=True)
                scores = jnp.where(same, mm(q, k, NT), MASKED)
                weights = jnp.exp(scores - log_ref[0, :, h : h + 1])
                dots = mm(g, v, NT)
                dscores = (weights * (dots - inner)).astype(BF16)
                dq = mm(dscores, k, NN) * scale
                back_ref[0, rows, at : at + HEAD] = (dq * cosine - swap_halves(dq) * sine).astype(BF16)
                dk_ref[cols, at : at + HEAD] += mm(dscores, q, TN)
                dv_ref[cols, at : at + HEAD] += mm(weights.astype(BF16), g, TN)

    @pl.when(step == pl.num_programs(1) - 1)
    def _():
        cosine = cos_ref[...]
        sine = sin_ref[...]
        for h in range(heads):
            at = h * HEAD
            dk = dk_ref[:, at : at + HEAD]
            back_ref[0, :, part + at : part + at + HEAD] = (
                dk * cosine - swap_halves(dk) * sine
            ).astype(BF16)
        back_ref[0, :, 2 * part :] = dv_ref[...].astype(BF16)


def attend_back(segments, qkv, grad, out, log, cosine, sine, tile):
    slots, length, wide = qkv.shape
    part = wide // 3
    whole = lambda s, b: (s, 0, 0)
    step = lambda s, b: (s, b, 0)
    table = lambda s, b: (0, 0)
    return pl.pallas_call(
        functools.partial(attend_back_kernel, tile),
        grid=(slots, length // tile),
        out_shape=jax.ShapeDtypeStruct((slots, length, wide), BF16),
        in_specs=[
            pl.BlockSpec((1, 1, length), whole),
            pl.BlockSpec((1, length, wide), whole),
            pl.BlockSpec((1, tile, part), step),
            pl.BlockSpec((1, tile, part), step),
            pl.BlockSpec((1, tile, 128), step),
            pl.BlockSpec((length, HEAD), table),
            pl.BlockSpec((length, HEAD), table),
        ],
        out_specs=pl.BlockSpec((1, length, wide), whole),
        scratch_shapes=[pltpu.VMEM((length, part), F32)] * 2,
        compiler_params=pltpu.CompilerParams(vmem_limit_bytes=48 << 20),
        name="attend_back",
    )(segments[:, None, :], qkv, grad, out, log, cosine, sine)


def norm_parts(stream):
    average = jnp.mean(stream, axis=-1, keepdims=True)
    centered = stream - average
    variance = jnp.mean(centered * centered, axis=-1, keepdims=True)
    inverse = lax.rsqrt(variance + EPS)
    return centered * inverse, inverse


def norm_back(grad, normal, inverse, factor):
    e = grad * factor
    mean_e = jnp.mean(e, axis=-1, keepdims=True)
    mean_en = jnp.mean(e * normal, axis=-1, keepdims=True)
    return inverse * (e - mean_e - normal * mean_en)


MESH = pl.DeviceIdType.MESH
VM = pl.BlockSpec(memory_space=pltpu.VMEM)
ANY = pl.BlockSpec(memory_space=pl.ANY)


def round16(size):
    return -(-size // 16) * 16


def greet(peers):
    barrier = pltpu.get_barrier_semaphore()
    for peer in peers:
        pl.semaphore_signal(barrier, inc=1, device_id=peer, device_id_type=MESH)
    pl.semaphore_wait(barrier, len(peers))


def push(src, dst, send, recv, peer):
    return pltpu.make_async_remote_copy(
        src_ref=src,
        dst_ref=dst,
        send_sem=send,
        recv_sem=recv,
        device_id=peer,
        device_id_type=MESH,
    )


class Place:
    def __init__(self, n, m):
        self.n, self.m = n, m
        self.f = lax.axis_index("fsdp")
        self.d = lax.axis_index("dp")
        self.lines = n // 2
        self.a = self.f // 2
        self.b = self.f % 2
        self.x = self.d // 2
        self.c = self.d % 2
        self.sib_d = self.x * 2 + 1 - self.c
        self.far_d = (1 - self.x) * 2 + self.c
        self.diag_d = (1 - self.x) * 2 + 1 - self.c
        self.sib = (self.f, self.sib_d)
        self.far = (self.f, self.far_d)
        self.diag = (self.f, self.diag_d)
        self.side_f = self.a * 2 + 1 - self.b
        self.side = (self.side_f, self.d)

    def line_f(self, step):
        return (self.a + step + self.lines) % self.lines * 2 + self.b

    def ring_f(self, step):
        return (self.f + step + self.n) % self.n


def gather_start(p, src, buf, zs, zr, ys, yr):
    copies = []
    for i in range(1, p.lines):
        copies.append(push(src, buf.at[p.f], zs.at[i], zr.at[i], (p.line_f(i), p.d)))
    copies.append(push(src, buf.at[p.f], ys.at[0], yr.at[0], p.side))
    for copy in copies:
        copy.start()


def gather_forward(p, buf, zs, zr, ys, yr):
    for i in range(1, p.lines):
        block = buf.at[p.line_f(-i)]
        push(block, block, zs.at[i], zr.at[i], (p.line_f(i), p.d)).wait_recv()
        push(block, block, ys.at[i], yr.at[i], p.side).start()


def gather_finish(p, src, buf, zs, zr, ys, yr):
    for i in range(p.lines):
        theirs = buf.at[(p.a - i + p.lines) % p.lines * 2 + 1 - p.b]
        push(theirs, theirs, ys.at[i], yr.at[i], p.side).wait_recv()


def gather_drain(p, src, buf, zs, zr, ys, yr):
    for i in range(1, p.lines):
        push(src, buf.at[p.f], zs.at[i], zr.at[i], (p.line_f(i), p.d)).wait_send()
    for i in range(p.lines):
        push(src, buf.at[p.f], ys.at[i], yr.at[i], p.side).wait_send()


def norm_rows(stream):
    average = jnp.mean(stream, axis=-1, keepdims=True)
    centered = stream - average
    variance = jnp.mean(centered * centered, axis=-1, keepdims=True)
    inverse = lax.rsqrt(variance + EPS)
    return centered * inverse, inverse


def turned(v):
    lanes = lax.broadcasted_iota(jnp.int32, v.shape, 1)
    half = HEAD // 2
    return jnp.where(lanes % HEAD < half, pltpu.roll(v, 128 - half, 1), pltpu.roll(v, half, 1))


def front_kernel(
    n,
    m,
    per,
    tok_ref,
    cond_ref,
    wada_ref,
    bada_ref,
    vec_ref,
    qrow_ref,
    orow_ref,
    place_ref,
    cos_ref,
    sin_ref,
    qkv_out,
    normed_out,
    mod_ref,
    vecs_ref,
    wqkv_ref,
    wout_out,
    cond_out,
    cond_all_ref,
    qkv_ref,
    normed_ref,
    tall_ref,
    mod_send,
    mod_recv,
    vbuf,
    qbuf,
    obuf,
    cs,
    cr,
    ms,
    mr,
    gz,
    ts,
    tr,
    local,
):
    p = Place(n, m)
    slots, quarter, width = tok_ref.shape
    half = quarter // 2
    part = width // m
    greet([p.sib, p.far] + [(p.ring_f(i), p.d) for i in range(1, n)])

    cond_all_ref[p.f] = cond_ref[...]
    for i in range(1, n):
        push(cond_ref, cond_all_ref.at[p.f], cs.at[i], cr.at[i], (p.ring_f(i), p.d)).start()
    vec = (p, vec_ref, vbuf) + tuple(gz.at[0, k] for k in range(4))
    qry = (p, qrow_ref, qbuf) + tuple(gz.at[1, k] for k in range(4))
    out = (p, orow_ref, obuf) + tuple(gz.at[2, k] for k in range(4))
    gather_start(*vec)

    def token_copy(kind, k):
        s, rows = k // 2, pl.ds(k % 2 * half, half)
        if kind == 2:
            block = tall_ref.at[p.far_d, s, rows]
            return push(block, block, ts.at[kind, k], tr.at[kind, k], p.sib)
        return push(
            tok_ref.at[s, rows],
            tall_ref.at[p.d, s, rows],
            ts.at[kind, k],
            tr.at[kind, k],
            p.sib if kind == 0 else p.far,
        )

    for k in range(2 * slots):
        token_copy(1, k).start()
    gather_start(*qry)
    for k in range(2 * slots):
        token_copy(0, k).start()
    gather_start(*out)
    vbuf[p.f] = vec_ref[...]
    qbuf[p.f] = qrow_ref[...]
    obuf[p.f] = orow_ref[...]

    def pass_on(k):
        token_copy(1, k).wait_recv()
        token_copy(2, k).start()

    for i in range(1, n):
        push(cond_ref, cond_all_ref.at[p.f], cs.at[i], cr.at[i], (p.ring_f(i), p.d)).wait_recv()
    cond_out[...] = cond_all_ref[...]
    conds = cond_all_ref[...].reshape(n * 16, cond_ref.shape[1])
    mod_cols = mm(conds, wada_ref[...], NN) + bada_ref[...].astype(F32)
    mod_send[...] = mod_cols.reshape(n, 16, mod_cols.shape[1])[:, :8]
    mod_recv[p.f] = mod_send[p.f]
    for i in range(1, n):
        peer = p.ring_f(i)
        push(mod_send.at[peer], mod_recv.at[p.f], ms.at[i], mr.at[i], (peer, p.d)).start()
    gather_forward(*vec[:1], *vec[2:])
    pass_on(0)
    for i in range(1, n):
        peer = p.ring_f(i)
        push(mod_send.at[peer], mod_recv.at[p.f], ms.at[i], mr.at[i], (peer, p.d)).wait_recv()
    cols = mod_cols.shape[1]
    for g in range(n):
        mod_ref[:, g * cols : (g + 1) * cols] = mod_recv[g]
    gather_finish(*vec)
    for g in range(n):
        row = vbuf[g].astype(F32)
        for k in range(4):
            vecs_ref[k : k + 1, g * per[k] : (g + 1) * per[k]] = row[k : k + 1, : per[k]]
    vecs_ref[4:8, :] = jnp.zeros((4, vecs_ref.shape[1]), F32)
    pass_on(1)

    gain = vecs_ref[1:2, :width]

    def normed_of(q, s):
        stream = tall_ref[q, s].astype(F32)
        normal, _ = norm_rows(stream)
        shift = mod_ref[s : s + 1, :width]
        scale = mod_ref[s : s + 1, width : 2 * width]
        rows = pl.ds(pl.multiple_of(q * quarter, quarter), quarter)
        normed_ref[s, rows, :] = (normal * (gain * (1.0 + scale)) + shift).astype(BF16)

    def project(q, s, index):
        rows = pl.ds(pl.multiple_of(q * quarter, quarter), quarter)
        got = mm(normed_ref[s, rows, :], wqkv_ref[...], NT)
        cosine = cos_ref[rows, :]
        sine = sin_ref[rows, :]
        lanes = lax.broadcasted_iota(jnp.int32, (quarter, 128), 1)
        for t in range(0, 2 * part, 128):
            tile = got[:, t : t + 128]
            tile = tile * cosine + turned(tile) * sine
            tile = jnp.where(lanes + t < part, tile * (1.0 / math.sqrt(HEAD)), tile)
            qkv_ref[s, rows, t : t + 128] = tile.astype(BF16)
        qkv_ref[s, rows, 2 * part :] = got[:, 2 * part :].astype(BF16)
        for src, dst, k in ((qkv_ref, qkv_out, 0), (normed_ref, normed_out, 1)):
            pltpu.make_async_copy(src.at[s, rows], dst.at[s, rows], local.at[k, index]).start()

    tall_ref[p.d] = tok_ref[...]
    for s in range(slots):
        normed_of(p.d, s)
    gather_forward(p, *qry[2:])
    for k in range(slots):
        token_copy(0, 2 * k).wait_recv()
        token_copy(0, 2 * k + 1).wait_recv()
        normed_of(p.sib_d, k)
    pass_on(2)
    gather_finish(*qry)
    sel = lax.broadcasted_iota(jnp.int32, (3 * part, qbuf.shape[0] * qbuf.shape[1]), 0)
    placing = (sel == place_ref[...]).astype(BF16)
    wqkv_ref[...] = mm(placing, qbuf[...].reshape(-1, width), NN).astype(BF16)
    for s in range(slots):
        project(p.d, s, s)
        project(p.sib_d, s, slots + s)
    gather_forward(p, *out[2:])
    pass_on(3)
    for s in range(slots):
        normed_of(p.far_d, s)
        project(p.far_d, s, 2 * slots + s)
        token_copy(2, 2 * s).wait_recv()
        token_copy(2, 2 * s + 1).wait_recv()
        normed_of(p.diag_d, s)
        project(p.diag_d, s, 3 * slots + s)
    gather_finish(*out)
    keep = pltpu.make_async_copy(obuf, wout_out, local.at[2, 0])
    keep.start()

    for i in range(1, n):
        peer = p.ring_f(i)
        push(cond_ref, cond_all_ref.at[p.f], cs.at[i], cr.at[i], (peer, p.d)).wait_send()
        push(mod_send.at[peer], mod_recv.at[p.f], ms.at[i], mr.at[i], (peer, p.d)).wait_send()
    for item in (vec, qry, out):
        gather_drain(*item)
    for k in range(2 * slots):
        for kind in range(3):
            token_copy(kind, k).wait_send()
    for s in range(slots):
        for j, q in enumerate((p.d, p.sib_d, p.far_d, p.diag_d)):
            rows = pl.ds(pl.multiple_of(q * quarter, quarter), quarter)
            for src, dst, k in ((qkv_ref, qkv_out, 0), (normed_ref, normed_out, 1)):
                pltpu.make_async_copy(src.at[s, rows], dst.at[s, rows], local.at[k, j * slots + s]).wait()
    keep.wait()


def front(n, m, per, length, tokens, cond, w_ada, b_ada, vec, qkv_rows, out_rows, place, cosine, sine):
    slots, quarter, width = tokens.shape
    part = width // m
    lines = n // 2
    dma = pltpu.SemaphoreType.DMA
    shape = jax.ShapeDtypeStruct
    return pl.pallas_call(
        functools.partial(front_kernel, n, m, per),
        out_shape=(
            shape((slots, length, 3 * part), BF16),
            shape((slots, length, width), BF16),
            shape((8, 6 * width), F32),
            shape((8, max(width, n * per[0])), F32),
            shape((3 * part, width), BF16),
            shape((n,) + out_rows.shape, BF16),
            shape((n,) + cond.shape, BF16),
        ),
        in_specs=[VM] * 10,
        out_specs=(ANY, ANY, VM, VM, VM, ANY, VM),
        scratch_shapes=[
            pltpu.VMEM((n,) + cond.shape, BF16),
            pltpu.VMEM((slots, length, 3 * part), BF16),
            pltpu.VMEM((slots, length, width), BF16),
            pltpu.VMEM((m, slots, quarter, width), BF16),
            pltpu.VMEM((n, 8, w_ada.shape[1]), F32),
            pltpu.VMEM((n, 8, w_ada.shape[1]), F32),
            pltpu.VMEM((n,) + vec.shape, BF16),
            pltpu.VMEM((n,) + qkv_rows.shape, BF16),
            pltpu.VMEM((n,) + out_rows.shape, BF16),
            dma((n,)),
            dma((n,)),
            dma((n,)),
            dma((n,)),
            dma((3, 4, lines)),
            dma((3, 2 * slots)),
            dma((3, 2 * slots)),
            dma((3, m * slots)),
        ],
        compiler_params=pltpu.CompilerParams(
            collective_id=1, has_side_effects=True, vmem_limit_bytes=48 << 20
        ),
        name="front",
    )(tokens, cond, w_ada, b_ada, vec, qkv_rows, out_rows, place, cosine, sine)


def column_plan(shards_n, ranks, columns):
    per = columns // shards_n
    rank_of = (np.arange(columns) // HEAD) % ranks
    lists = [
        [[c for c in range(per) if rank_of[f * per + c] == r] for r in range(ranks)]
        for f in range(shards_n)
    ]
    most = max(len(l) for row in lists for l in row)
    most = -(-most // 16) * 16
    take = np.full((shards_n, ranks, most), -1, np.int32)
    place = np.full((ranks, shards_n * most), -1, np.int32)
    home = np.full((shards_n, ranks * most), -1, np.int32)
    for r in range(ranks):
        order = {c: i for i, c in enumerate(np.flatnonzero(rank_of == r))}
        for f in range(shards_n):
            for i, c in enumerate(lists[f][r]):
                take[f, r, i] = c
                place[r, f * most + i] = order[f * per + c]
                home[f, r * most + i] = c
    return most, take, place, home


def pick(indices, size):
    return (indices[:, None] == jnp.arange(size, dtype=jnp.int32)[None, :]).astype(BF16)


def shards(
    tokens,
    condition,
    segments,
    w_ada,
    b_ada,
    gain_attn,
    w_qkv,
    w_out,
    gain_mlp,
    w_up,
    b_up,
    w_down,
    b_down,
    cotangent,
):
    slots, quarter, width = tokens.shape
    length = segments.shape[1]
    n = lax.axis_size("fsdp")
    m = lax.axis_size("dp")
    f = lax.axis_index("fsdp")
    d = lax.axis_index("dp")
    heads = width // HEAD
    part = width // m
    hidden_part = w_up.shape[1] * n // m
    tile = 256
    cos_np, sin_np = rope_table(length)
    cosine, sine = jnp.asarray(cos_np), jnp.asarray(sin_np)

    ups = b_up.shape[0]
    small = gain_attn.shape[0]
    most, take, place, home = column_plan(n, m, w_qkv.shape[1] * n)
    picked = pick(jnp.asarray(take)[f, d], w_qkv.shape[1])
    qkv_rows = mm(picked, w_qkv, NT).astype(BF16)
    up_rows = lax.dynamic_slice_in_dim(w_up, d * (ups // m), ups // m, 1).T
    down_rows = lax.dynamic_index_in_dim(
        w_down.reshape(n, m, ups // m, small), d, 1, False
    ).reshape(-1, small).T
    out_rows = w_out.reshape(heads // m, m, HEAD, small).transpose(1, 0, 2, 3).reshape(-1, small).T
    place_row = jnp.asarray(place)[d]
    placing = pick(place_row, 3 * part)

    pad_rows = lambda v, size: jnp.pad(v, ((0, size - v.shape[0]), (0, 0)))
    wide = max(width, n * (ups // m))
    vec = jnp.stack(
        [
            jnp.pad(v, (0, width - v.shape[0]))
            for v in (
                lax.dynamic_slice_in_dim(b_up, d * (ups // m), ups // m, 0),
                gain_attn,
                gain_mlp,
                b_down,
            )
        ]
    )
    qkv, normed, mod_rows, vec_rows, w_qkv_t, out_blocks, cond_blocks = front(
        n,
        m,
        (ups // m, small, small, small),
        length,
        tokens,
        pad_rows(condition, 16),
        w_ada,
        b_ada[None],
        pad_rows(vec, 16),
        qkv_rows,
        pad_rows(out_rows, round16(small)),
        place_row[None],
        jnp.concatenate([cosine, cosine], axis=1),
        jnp.concatenate([sine, sine], axis=1),
    )
    cond_all = cond_blocks[:, :slots].reshape(n * slots, -1)
    modulation = mod_rows[:slots]
    shift_attn, scale_attn, gate_attn, shift_mlp, scale_mlp, gate_mlp = [
        g[:, None, :] for g in jnp.split(modulation, 6, axis=-1)
    ]
    b_up_rank = vec_rows[0, : hidden_part]
    gain_attn_all, gain_mlp_all, b_down_all = [vec_rows[i, :width] for i in (1, 2, 3)]
    w_out_t = out_blocks[:, :small].reshape(width, width)
    w_up_t = lax.all_gather(up_rows, "fsdp", axis=0, tiled=True)
    w_down_t = lax.all_gather(down_rows, "fsdp", axis=0, tiled=True)

    attended, logs = attend(segments, qkv, tile)

    own = lax.all_to_all(attended, "dp", 1, 2, tiled=True)
    own_tokens = tokens.astype(F32)
    hr = heads // m
    flat = lambda v: v.reshape(-1, v.shape[-1])
    back = lambda v: v.reshape(slots, -1, v.shape[-1])
    branch_attn = back(mm(flat(own), w_out_t, NT))
    middle = own_tokens + gate_attn * branch_attn
    normal_mlp, inverse_mlp = norm_parts(middle)
    normed_mlp = (normal_mlp * (gain_mlp_all * (1.0 + scale_mlp)) + shift_mlp).astype(BF16)
    normed_mlp_all = flat(lax.all_gather(normed_mlp, "dp", axis=1, tiled=True))
    cot_all = lax.all_gather(cotangent, "dp", axis=1, tiled=True)
    gbm = flat((cot_all.astype(F32) * gate_mlp).astype(BF16))
    hidden = mm(normed_mlp_all, w_up_t, NT) + b_up_rank
    activated, gelu_pull = jax.vjp(lambda h: jax.nn.gelu(h, approximate=True), hidden)
    activated = activated.astype(BF16)
    branch_part = back(mm(activated, w_down_t, NT).astype(BF16))
    branch_mlp = lax.psum_scatter(branch_part, "dp", scatter_dimension=1, tiled=True).astype(F32) + b_down_all
    outputs = (middle + gate_mlp * branch_mlp).astype(BF16)
    grad_act = mm(gbm, w_down_t, NN)
    grad_hidden = gelu_pull(grad_act)[0].astype(BF16)
    grad_normed_part = back(mm(grad_hidden, w_up_t, NN).astype(BF16))
    grad_normed_mlp = lax.psum_scatter(
        grad_normed_part, "dp", scatter_dimension=1, tiled=True
    ).astype(F32)
    cot = cotangent.astype(F32)
    own_gbm = (cot * gate_mlp).astype(BF16).astype(F32)
    grad_middle = cot + norm_back(
        grad_normed_mlp, normal_mlp, inverse_mlp, gain_mlp_all * (1.0 + scale_mlp)
    )
    grad_branch_attn = (grad_middle * gate_attn).astype(BF16)
    grad_att_own = back(mm(flat(grad_branch_attn), w_out_t, NN).astype(BF16))
    grad_attended = lax.all_to_all(grad_att_own, "dp", 2, 1, tiled=True)

    dw_down_t = mm(gbm, activated, TN).astype(BF16)
    dw_up_t = mm(grad_hidden, normed_mlp_all, TN).astype(BF16)
    dw_out_t = mm(flat(grad_branch_attn), flat(own), TN).astype(BF16)
    db_up = jnp.sum(grad_hidden.astype(F32), axis=0)

    gqkv = attend_back(segments, qkv, grad_attended, attended, logs, cosine, sine, tile)
    gqkv_flat = flat(gqkv)
    dw_qkv_t = mm(gqkv_flat, flat(normed), TN).astype(BF16)
    grad_normed = lax.psum_scatter(
        back(mm(gqkv_flat, w_qkv_t, NN).astype(BF16)), "dp", scatter_dimension=1, tiled=True
    ).astype(F32)
    normal_attn, inverse_attn = norm_parts(own_tokens)
    d_tokens = (
        grad_middle
        + norm_back(grad_normed, normal_attn, inverse_attn, gain_attn_all * (1.0 + scale_attn))
    ).astype(BF16)

    sum_attn = jnp.sum(grad_normed * normal_attn, axis=1)
    sum_mlp = jnp.sum(grad_normed_mlp * normal_mlp, axis=1)
    sums = jnp.concatenate(
        [
            jnp.sum(grad_normed, axis=1),
            sum_attn,
            jnp.sum(grad_middle * branch_attn, axis=1),
            jnp.sum(grad_normed_mlp, axis=1),
            sum_mlp,
            jnp.sum(cot * branch_mlp, axis=1),
            jnp.sum(own_gbm, axis=1),
        ],
        axis=-1,
    )
    sums = lax.psum(sums, "dp")
    sh_a, sc_a, ga_a, sh_m, sc_m, ga_m, gb = jnp.split(sums, 7, axis=-1)
    d_gain_attn = jnp.sum(sc_a * (1.0 + scale_attn[:, 0]), axis=0)
    d_gain_mlp = jnp.sum(sc_m * (1.0 + scale_mlp[:, 0]), axis=0)
    d_b_down = jnp.sum(gb, axis=0)
    gmod = jnp.concatenate(
        [sh_a, sc_a * gain_attn_all, ga_a, sh_m, sc_m * gain_mlp_all, ga_m], axis=-1
    ).astype(BF16)
    gmod_cols = lax.all_to_all(gmod, "fsdp", 1, 0, tiled=True)
    d_w_ada = mm(cond_all, gmod_cols, TN)
    d_b_ada = jnp.sum(gmod_cols.astype(F32), axis=0)
    d_condition = lax.psum_scatter(
        mm(gmod_cols, w_ada, NT), "fsdp", scatter_dimension=0, tiled=True
    ).astype(BF16)
    vec_sums = lax.psum_scatter(
        jnp.stack([d_gain_attn, d_gain_mlp, d_b_down]), "fsdp", scatter_dimension=1, tiled=True
    )

    def scatter(v):
        return lax.psum_scatter(v, "fsdp", scatter_dimension=0, tiled=True)

    def spread(v):
        return lax.all_gather(v, "dp", axis=0)

    up_all = spread(scatter(dw_up_t))
    d_w_up = up_all.reshape(-1, width).astype(F32).T
    down_all = spread(scatter(dw_down_t))
    d_w_down = (
        down_all.reshape(m, small, n, ups // m).transpose(2, 0, 3, 1).reshape(-1, small).astype(F32)
    )
    out_all = lax.psum(scatter(dw_out_t).astype(F32), "dp")
    d_w_out = (
        out_all.reshape(small, m, heads // m, HEAD).transpose(2, 1, 3, 0).reshape(-1, small)
    )
    d_b_up = spread(scatter(db_up)).reshape(-1)
    qkv_all = spread(scatter(mm(placing, dw_qkv_t, NN).astype(BF16)))
    homing = pick(jnp.asarray(home)[f], w_qkv.shape[1])
    d_w_qkv = mm(qkv_all.reshape(-1, width), homing, TN)
    return (
        outputs,
        d_tokens,
        d_condition,
        d_w_ada,
        d_b_ada,
        vec_sums[0],
        d_w_qkv,
        d_w_out,
        vec_sums[1],
        d_w_up,
        d_b_up,
        d_w_down,
        vec_sums[2],
    )


def solution(mesh):
    return jax.shard_map(
        shards,
        mesh=mesh,
        in_specs=(
            P("fsdp", "dp", None),
            P("fsdp", None),
            P("fsdp", None),
            P(None, "fsdp"),
            P("fsdp"),
            P("fsdp"),
            P(None, "fsdp"),
            P(None, "fsdp"),
            P("fsdp"),
            P(None, "fsdp"),
            P("fsdp"),
            P(None, "fsdp"),
            P("fsdp"),
            P("fsdp", "dp", None),
        ),
        out_specs=(
            P("fsdp", "dp", None),
            P("fsdp", "dp", None),
            P("fsdp", None),
            P(None, "fsdp"),
            P("fsdp"),
            P("fsdp"),
            P(None, "fsdp"),
            P(None, "fsdp"),
            P("fsdp"),
            P(None, "fsdp"),
            P("fsdp"),
            P(None, "fsdp"),
            P("fsdp"),
        ),
        check_vma=False,
    )
```

```python
import functools
import math

import jax
import jax.numpy as jnp
import numpy as np
from jax import lax
from jax.experimental import pallas as pl
from jax.experimental.pallas import tpu as pltpu
from jax.sharding import PartitionSpec as P

HEAD = 64
EPS = 1e-05
ROPE_BASE = 10000.0
MASKED = -1e30
F32 = jnp.float32
BF16 = jnp.bfloat16

NN = (((1,), (0,)), ((), ()))
NT = (((1,), (1,)), ((), ()))
TN = (((0,), (0,)), ((), ()))


def mm(a, b, dims):
    return lax.dot_general(a, b, dims, preferred_element_type=F32)


def rope_table(length):
    inverse = ROPE_BASE ** (-2.0 * np.arange(HEAD // 2) / HEAD)
    angles = np.arange(length)[:, None] * inverse[None, :]
    cosine = np.concatenate([np.cos(angles)] * 2, axis=1)
    sine = np.concatenate([-np.sin(angles), np.sin(angles)], axis=1)
    return cosine.astype(np.float32), sine.astype(np.float32)


def swap_halves(v):
    half = HEAD // 2
    return jnp.concatenate([v[..., half:], v[..., :half]], axis=-1)


def key_window(segments_row, own_row, tile):
    first = jnp.min(own_row)
    last = jnp.max(own_row)
    low = jnp.sum((segments_row < first).astype(jnp.int32))
    high = jnp.sum((segments_row <= last).astype(jnp.int32)) - 1
    start = low // tile
    return start, high // tile - start + 1


def as_column(row):
    size = row.shape[1]
    return jnp.transpose(jnp.broadcast_to(row, (128, size)))[:, :1]


def attend_kernel(tile, seg_ref, qkv_ref, out_ref, log_ref):
    length = seg_ref.shape[2]
    part = qkv_ref.shape[2] // 3
    heads = part // HEAD
    rows = pl.ds(pl.multiple_of(pl.program_id(1) * tile, tile), tile)
    own_row = seg_ref[0, :, rows]
    start, width = key_window(seg_ref[0], own_row, tile)
    own_col = as_column(own_row)
    keys = pl.multiple_of(start * tile, tile)
    for w in range(1, length // tile + 1):

        @pl.when(width == w)
        def _(w=w):
            cols = pl.ds(keys, w * tile)
            same = own_col == seg_ref[0, :, cols]
            for h in range(heads):
                at = h * HEAD
                q = qkv_ref[0, rows, at : at + HEAD]
                k = qkv_ref[0, cols, part + at : part + at + HEAD]
                v = qkv_ref[0, cols, 2 * part + at : 2 * part + at + HEAD]
                scores = jnp.where(same, mm(q, k, NT), MASKED)
                largest = jnp.max(scores, axis=1, keepdims=True)
                weights = jnp.exp(scores - largest)
                total = jnp.sum(weights, axis=1, keepdims=True)
                result = mm(weights.astype(BF16), v, NN) / total
                half = tile // 2
                result = result.astype(BF16)
                out_ref[0, 0, :, at : at + HEAD] = result[:half]
                out_ref[0, 0, :, part + at : part + at + HEAD] = result[half:]
                log_ref[0, :, h : h + 1] = largest + jnp.log(total)


def attend(segments, qkv, tile):
    slots, length, wide = qkv.shape
    part = wide // 3
    return pl.pallas_call(
        functools.partial(attend_kernel, tile),
        grid=(slots, length // tile),
        out_shape=(
            jax.ShapeDtypeStruct((slots, length // tile, tile // 2, 2 * part), BF16),
            jax.ShapeDtypeStruct((slots, length, 128), F32),
        ),
        in_specs=[
            pl.BlockSpec((1, 1, length), lambda s, b: (s, 0, 0)),
            pl.BlockSpec((1, length, wide), lambda s, b: (s, 0, 0)),
        ],
        out_specs=(
            pl.BlockSpec((1, 1, tile // 2, 2 * part), lambda s, b: (s, b, 0, 0)),
            pl.BlockSpec((1, tile, 128), lambda s, b: (s, b, 0)),
        ),
        compiler_params=pltpu.CompilerParams(vmem_limit_bytes=48 << 20),
        name="attend",
    )(segments[:, None, :], qkv)


def attend_back_kernel(
    tile, seg_ref, qkv_ref, grad_ref, out_ref, log_ref, cos_ref, sin_ref, back_ref, dk_ref, dv_ref
):
    length = seg_ref.shape[2]
    part = qkv_ref.shape[2] // 3
    heads = part // HEAD
    step = pl.program_id(1)
    rows = pl.ds(pl.multiple_of(step * tile, tile), tile)
    own_row = seg_ref[0, :, rows]
    start, width = key_window(seg_ref[0], own_row, tile)
    own_col = as_column(own_row)
    keys = pl.multiple_of(start * tile, tile)
    scale = 1.0 / math.sqrt(HEAD)

    @pl.when(step == 0)
    def _():
        dk_ref[...] = jnp.zeros_like(dk_ref)
        dv_ref[...] = jnp.zeros_like(dv_ref)

    for w in range(1, length // tile + 1):

        @pl.when(width == w)
        def _(w=w):
            cols = pl.ds(keys, w * tile)
            same = own_col == seg_ref[0, :, cols]
            cosine = cos_ref[rows, :]
            sine = sin_ref[rows, :]
            for h in range(heads):
                at = h * HEAD
                q = qkv_ref[0, rows, at : at + HEAD]
                k = qkv_ref[0, cols, part + at : part + at + HEAD]
                v = qkv_ref[0, cols, 2 * part + at : 2 * part + at + HEAD]
                g, o = [
                    jnp.concatenate(
                        [ref[0, 0, :, at : at + HEAD], ref[0, 0, :, part + at : part + at + HEAD]]
                    )
                    for ref in (grad_ref, out_ref)
                ]
                inner = jnp.sum(g.astype(F32) * o.astype(F32), axis=1, keepdims=True)
                scores = jnp.where(same, mm(q, k, NT), MASKED)
                weights = jnp.exp(scores - log_ref[0, :, h : h + 1])
                dots = mm(g, v, NT)
                dscores = (weights * (dots - inner)).astype(BF16)
                dq = mm(dscores, k, NN) * scale
                back_ref[0, rows, at : at + HEAD] = (dq * cosine - swap_halves(dq) * sine).astype(BF16)
                dk_ref[cols, at : at + HEAD] += mm(dscores, q, TN)
                dv_ref[cols, at : at + HEAD] += mm(weights.astype(BF16), g, TN)

    @pl.when(step == pl.num_programs(1) - 1)
    def _():
        cosine = cos_ref[...]
        sine = sin_ref[...]
        for h in range(heads):
            at = h * HEAD
            dk = dk_ref[:, at : at + HEAD]
            back_ref[0, :, part + at : part + at + HEAD] = (
                dk * cosine - swap_halves(dk) * sine
            ).astype(BF16)
        back_ref[0, :, 2 * part :] = dv_ref[...].astype(BF16)


def attend_back(segments, qkv, grad, out, log, cosine, sine, tile):
    slots, length, wide = qkv.shape
    part = wide // 3
    whole = lambda s, b: (s, 0, 0)
    step = lambda s, b: (s, b, 0)
    table = lambda s, b: (0, 0)
    return pl.pallas_call(
        functools.partial(attend_back_kernel, tile),
        grid=(slots, length // tile),
        out_shape=jax.ShapeDtypeStruct((slots, length, wide), BF16),
        in_specs=[
            pl.BlockSpec((1, 1, length), whole),
            pl.BlockSpec((1, length, wide), whole),
            pl.BlockSpec((1, 1, tile // 2, 2 * part), lambda s, b: (s, b, 0, 0)),
            pl.BlockSpec((1, 1, tile // 2, 2 * part), lambda s, b: (s, b, 0, 0)),
            pl.BlockSpec((1, tile, 128), step),
            pl.BlockSpec((length, HEAD), table),
            pl.BlockSpec((length, HEAD), table),
        ],
        out_specs=pl.BlockSpec((1, length, wide), whole),
        scratch_shapes=[pltpu.VMEM((length, part), F32)] * 2,
        compiler_params=pltpu.CompilerParams(vmem_limit_bytes=48 << 20),
        name="attend_back",
    )(segments[:, None, :], qkv, grad, out, log, cosine, sine)


def norm_parts(stream):
    average = jnp.mean(stream, axis=-1, keepdims=True)
    centered = stream - average
    variance = jnp.mean(centered * centered, axis=-1, keepdims=True)
    inverse = lax.rsqrt(variance + EPS)
    return centered * inverse, inverse


def norm_back(grad, normal, inverse, factor):
    e = grad * factor
    mean_e = jnp.mean(e, axis=-1, keepdims=True)
    mean_en = jnp.mean(e * normal, axis=-1, keepdims=True)
    return inverse * (e - mean_e - normal * mean_en)


MESH = pl.DeviceIdType.MESH
VM = pl.BlockSpec(memory_space=pltpu.VMEM)
ANY = pl.BlockSpec(memory_space=pl.ANY)


def round16(size):
    return -(-size // 16) * 16


def greet(peers):
    barrier = pltpu.get_barrier_semaphore()
    for peer in peers:
        pl.semaphore_signal(barrier, inc=1, device_id=peer, device_id_type=MESH)
    pl.semaphore_wait(barrier, len(peers))


def push(src, dst, send, recv, peer):
    return pltpu.make_async_remote_copy(
        src_ref=src,
        dst_ref=dst,
        send_sem=send,
        recv_sem=recv,
        device_id=peer,
        device_id_type=MESH,
    )


class Place:
    def __init__(self, n, m):
        self.n, self.m = n, m
        self.f = lax.axis_index("fsdp")
        self.d = lax.axis_index("dp")
        self.lines = n // 2
        self.a = self.f // 2
        self.b = self.f % 2
        self.x = self.d // 2
        self.c = self.d % 2
        self.sib_d = self.x * 2 + 1 - self.c
        self.far_d = (1 - self.x) * 2 + self.c
        self.diag_d = (1 - self.x) * 2 + 1 - self.c
        self.sib = (self.f, self.sib_d)
        self.far = (self.f, self.far_d)
        self.diag = (self.f, self.diag_d)
        self.side_f = self.a * 2 + 1 - self.b
        self.side = (self.side_f, self.d)

    def line_f(self, step):
        return (self.a + step + self.lines) % self.lines * 2 + self.b

    def ring_f(self, step):
        return (self.f + step + self.n) % self.n


def gather_start(p, src, buf, zs, zr, ys, yr):
    copies = []
    for i in range(1, p.lines):
        copies.append(push(src, buf.at[p.f], zs.at[i], zr.at[i], (p.line_f(i), p.d)))
    copies.append(push(src, buf.at[p.f], ys.at[0], yr.at[0], p.side))
    for copy in copies:
        copy.start()


def gather_forward(p, buf, zs, zr, ys, yr):
    for i in range(1, p.lines):
        block = buf.at[p.line_f(-i)]
        push(block, block, zs.at[i], zr.at[i], (p.line_f(i), p.d)).wait_recv()
        push(block, block, ys.at[i], yr.at[i], p.side).start()


def gather_finish(p, src, buf, zs, zr, ys, yr):
    for i in range(p.lines):
        theirs = buf.at[(p.a - i + p.lines) % p.lines * 2 + 1 - p.b]
        push(theirs, theirs, ys.at[i], yr.at[i], p.side).wait_recv()


def gather_drain(p, src, buf, zs, zr, ys, yr):
    for i in range(1, p.lines):
        push(src, buf.at[p.f], zs.at[i], zr.at[i], (p.line_f(i), p.d)).wait_send()
    for i in range(p.lines):
        push(src, buf.at[p.f], ys.at[i], yr.at[i], p.side).wait_send()


def norm_rows(stream):
    average = jnp.mean(stream, axis=-1, keepdims=True)
    centered = stream - average
    variance = jnp.mean(centered * centered, axis=-1, keepdims=True)
    inverse = lax.rsqrt(variance + EPS)
    return centered * inverse, inverse


def turned(v):
    lanes = lax.broadcasted_iota(jnp.int32, v.shape, 1)
    half = HEAD // 2
    return jnp.where(lanes % HEAD < half, pltpu.roll(v, 128 - half, 1), pltpu.roll(v, half, 1))


def front_kernel(
    n,
    m,
    per,
    tok_ref,
    cond_ref,
    wada_ref,
    bada_ref,
    vec_ref,
    qrow_ref,
    orow_ref,
    place_ref,
    cos_ref,
    sin_ref,
    qkv_out,
    normed_out,
    mod_ref,
    vecs_ref,
    wqkv_ref,
    wout_out,
    cond_out,
    cond_all_ref,
    qkv_ref,
    normed_ref,
    tall_ref,
    mod_send,
    mod_recv,
    vbuf,
    qbuf,
    obuf,
    cs,
    cr,
    ms,
    mr,
    gz,
    ts,
    tr,
    local,
):
    p = Place(n, m)
    slots, quarter, width = tok_ref.shape
    half = quarter // 2
    part = width // m
    greet([p.sib, p.far] + [(p.ring_f(i), p.d) for i in range(1, n)])

    cond_all_ref[p.f] = cond_ref[...]
    for i in range(1, n):
        push(cond_ref, cond_all_ref.at[p.f], cs.at[i], cr.at[i], (p.ring_f(i), p.d)).start()
    vec = (p, vec_ref, vbuf) + tuple(gz.at[0, k] for k in range(4))
    qry = (p, qrow_ref, qbuf) + tuple(gz.at[1, k] for k in range(4))
    out = (p, orow_ref, obuf) + tuple(gz.at[2, k] for k in range(4))
    gather_start(*vec)

    def token_copy(kind, k):
        s, rows = k // 2, pl.ds(k % 2 * half, half)
        if kind == 2:
            block = tall_ref.at[p.far_d, s, rows]
            return push(block, block, ts.at[kind, k], tr.at[kind, k], p.sib)
        return push(
            tok_ref.at[s, rows],
            tall_ref.at[p.d, s, rows],
            ts.at[kind, k],
            tr.at[kind, k],
            p.sib if kind == 0 else p.far,
        )

    for k in range(2 * slots):
        token_copy(1, k).start()
    gather_start(*qry)
    for k in range(2 * slots):
        token_copy(0, k).start()
    gather_start(*out)
    vbuf[p.f] = vec_ref[...]
    qbuf[p.f] = qrow_ref[...]
    obuf[p.f] = orow_ref[...]

    def pass_on(k):
        token_copy(1, k).wait_recv()
        token_copy(2, k).start()

    for i in range(1, n):
        push(cond_ref, cond_all_ref.at[p.f], cs.at[i], cr.at[i], (p.ring_f(i), p.d)).wait_recv()
    cond_out[...] = cond_all_ref[...]
    conds = cond_all_ref[...].reshape(n * 16, cond_ref.shape[1])
    mod_cols = mm(conds, wada_ref[...], NN) + bada_ref[...].astype(F32)
    mod_send[...] = mod_cols.reshape(n, 16, mod_cols.shape[1])[:, :8]
    mod_recv[p.f] = mod_send[p.f]
    for i in range(1, n):
        peer = p.ring_f(i)
        push(mod_send.at[peer], mod_recv.at[p.f], ms.at[i], mr.at[i], (peer, p.d)).start()
    gather_forward(*vec[:1], *vec[2:])
    pass_on(0)
    for i in range(1, n):
        peer = p.ring_f(i)
        push(mod_send.at[peer], mod_recv.at[p.f], ms.at[i], mr.at[i], (peer, p.d)).wait_recv()
    cols = mod_cols.shape[1]
    for g in range(n):
        mod_ref[:, g * cols : (g + 1) * cols] = mod_recv[g]
    gather_finish(*vec)
    for g in range(n):
        row = vbuf[g].astype(F32)
        for k in range(4):
            vecs_ref[k : k + 1, g * per[k] : (g + 1) * per[k]] = row[k : k + 1, : per[k]]
    vecs_ref[4:8, :] = jnp.zeros((4, vecs_ref.shape[1]), F32)
    pass_on(1)

    gain = vecs_ref[1:2, :width]

    def normed_of(q, s):
        stream = tall_ref[q, s].astype(F32)
        normal, _ = norm_rows(stream)
        shift = mod_ref[s : s + 1, :width]
        scale = mod_ref[s : s + 1, width : 2 * width]
        rows = pl.ds(pl.multiple_of(q * quarter, quarter), quarter)
        normed_ref[s, rows, :] = (normal * (gain * (1.0 + scale)) + shift).astype(BF16)

    def project(q, s, index):
        rows = pl.ds(pl.multiple_of(q * quarter, quarter), quarter)
        got = mm(normed_ref[s, rows, :], wqkv_ref[...], NT)
        cosine = cos_ref[rows, :]
        sine = sin_ref[rows, :]
        lanes = lax.broadcasted_iota(jnp.int32, (quarter, 128), 1)
        for t in range(0, 2 * part, 128):
            tile = got[:, t : t + 128]
            tile = tile * cosine + turned(tile) * sine
            tile = jnp.where(lanes + t < part, tile * (1.0 / math.sqrt(HEAD)), tile)
            qkv_ref[s, rows, t : t + 128] = tile.astype(BF16)
        qkv_ref[s, rows, 2 * part :] = got[:, 2 * part :].astype(BF16)
        for src, dst, k in ((qkv_ref, qkv_out, 0), (normed_ref, normed_out, 1)):
            pltpu.make_async_copy(src.at[s, rows], dst.at[s, rows], local.at[k, index]).start()

    tall_ref[p.d] = tok_ref[...]
    for s in range(slots):
        normed_of(p.d, s)
    gather_forward(p, *qry[2:])
    for k in range(slots):
        token_copy(0, 2 * k).wait_recv()
        token_copy(0, 2 * k + 1).wait_recv()
        normed_of(p.sib_d, k)
    pass_on(2)
    gather_finish(*qry)
    sel = lax.broadcasted_iota(jnp.int32, (3 * part, qbuf.shape[0] * qbuf.shape[1]), 0)
    placing = (sel == place_ref[...]).astype(BF16)
    wqkv_ref[...] = mm(placing, qbuf[...].reshape(-1, width), NN).astype(BF16)
    for s in range(slots):
        project(p.d, s, s)
        project(p.sib_d, s, slots + s)
    gather_forward(p, *out[2:])
    pass_on(3)
    for s in range(slots):
        normed_of(p.far_d, s)
        project(p.far_d, s, 2 * slots + s)
        token_copy(2, 2 * s).wait_recv()
        token_copy(2, 2 * s + 1).wait_recv()
        normed_of(p.diag_d, s)
        project(p.diag_d, s, 3 * slots + s)
    gather_finish(*out)
    keep = pltpu.make_async_copy(obuf, wout_out, local.at[2, 0])
    keep.start()

    for i in range(1, n):
        peer = p.ring_f(i)
        push(cond_ref, cond_all_ref.at[p.f], cs.at[i], cr.at[i], (peer, p.d)).wait_send()
        push(mod_send.at[peer], mod_recv.at[p.f], ms.at[i], mr.at[i], (peer, p.d)).wait_send()
    for item in (vec, qry, out):
        gather_drain(*item)
    for k in range(2 * slots):
        for kind in range(3):
            token_copy(kind, k).wait_send()
    for s in range(slots):
        for j, q in enumerate((p.d, p.sib_d, p.far_d, p.diag_d)):
            rows = pl.ds(pl.multiple_of(q * quarter, quarter), quarter)
            for src, dst, k in ((qkv_ref, qkv_out, 0), (normed_ref, normed_out, 1)):
                pltpu.make_async_copy(src.at[s, rows], dst.at[s, rows], local.at[k, j * slots + s]).wait()
    keep.wait()


def front(n, m, per, length, tokens, cond, w_ada, b_ada, vec, qkv_rows, out_rows, place, cosine, sine):
    slots, quarter, width = tokens.shape
    part = width // m
    lines = n // 2
    dma = pltpu.SemaphoreType.DMA
    shape = jax.ShapeDtypeStruct
    return pl.pallas_call(
        functools.partial(front_kernel, n, m, per),
        out_shape=(
            shape((slots, length, 3 * part), BF16),
            shape((slots, length, width), BF16),
            shape((8, 6 * width), F32),
            shape((8, max(width, n * per[0])), F32),
            shape((3 * part, width), BF16),
            shape((n,) + out_rows.shape, BF16),
            shape((n,) + cond.shape, BF16),
        ),
        in_specs=[VM] * 10,
        out_specs=(ANY, ANY, VM, VM, VM, ANY, VM),
        scratch_shapes=[
            pltpu.VMEM((n,) + cond.shape, BF16),
            pltpu.VMEM((slots, length, 3 * part), BF16),
            pltpu.VMEM((slots, length, width), BF16),
            pltpu.VMEM((m, slots, quarter, width), BF16),
            pltpu.VMEM((n, 8, w_ada.shape[1]), F32),
            pltpu.VMEM((n, 8, w_ada.shape[1]), F32),
            pltpu.VMEM((n,) + vec.shape, BF16),
            pltpu.VMEM((n,) + qkv_rows.shape, BF16),
            pltpu.VMEM((n,) + out_rows.shape, BF16),
            dma((n,)),
            dma((n,)),
            dma((n,)),
            dma((n,)),
            dma((3, 4, lines)),
            dma((3, 2 * slots)),
            dma((3, 2 * slots)),
            dma((3, m * slots)),
        ],
        compiler_params=pltpu.CompilerParams(
            collective_id=1, has_side_effects=True, vmem_limit_bytes=48 << 20
        ),
        name="front",
    )(tokens, cond, w_ada, b_ada, vec, qkv_rows, out_rows, place, cosine, sine)


def gelu_parts(h):
    root = math.sqrt(2.0 / math.pi)
    square = h * h
    t = jnp.tanh(root * h * (1.0 + 0.044715 * square))
    half = 0.5 * (1.0 + t)
    slope = half + 0.5 * h * (1.0 - t * t) * (root * (1.0 + 3.0 * 0.044715 * square))
    return h * half, slope


def compact(blocks, per):
    count, rows, lanes = blocks.shape
    flat = blocks.reshape(count * rows, lanes)
    if rows == per:
        return flat
    want = lax.broadcasted_iota(jnp.int32, (count * per, count * rows), 0)
    have = lax.broadcasted_iota(jnp.int32, (count * per, count * rows), 1)
    chosen = (have == want // per * rows + want % per).astype(BF16)
    return mm(chosen, flat, NN).astype(BF16)


def middle_kernel(
    n,
    m,
    small,
    tok_ref,
    cot_ref,
    cotfar_ref,
    att_ref,
    mod_ref,
    vec_ref,
    wout_ref,
    urow_ref,
    drow_ref,
    gm_ref,
    base_ref,
    xsend_ref,
    gatt_ref,
    dwd_ref,
    dwu_ref,
    dwo_ref,
    dbup_ref,
    sums_ref,
    arecv,
    own_ref,
    br_ref,
    mid_ref,
    nrm_ref,
    inv_ref,
    nm_ref,
    ct_ref,
    act_ref,
    gp_ref,
    ubuf,
    dbuf,
    wdown_ref,
    psend,
    precv,
    xs_ref,
    xr_ref,
    gn_ref,
    bo_ref,
    gba_ref,
    gsend,
    grecv,
    a_s,
    a_r,
    n_s,
    n_r,
    c_s,
    c_r,
    gz,
    p_s,
    p_r,
    g_s,
    g_r,
):
    p = Place(n, m)
    slots, quarter, width = tok_ref.shape
    half = quarter // 2
    part = width // m
    peers = (p.sib, p.far, p.diag)
    ranks = (p.sib_d, p.far_d, p.diag_d)
    greet(list(peers) + [(p.line_f(i), p.d) for i in range(1, p.lines)] + [p.side])

    def att_copy(kind, s):
        return push(
            att_ref.at[s, ranks[kind]], arecv.at[s, p.d], a_s.at[kind, s], a_r.at[kind, s], peers[kind]
        )

    for s in range(slots):
        for kind in (2, 1, 0):
            att_copy(kind, s).start()
    up = (p, urow_ref, ubuf) + tuple(gz.at[0, k] for k in range(4))
    down = (p, drow_ref, dbuf) + tuple(gz.at[1, k] for k in range(4))
    gather_start(*up)
    gather_start(*down)

    def cot_copy(kind, s):
        src = cot_ref if kind == 0 else cotfar_ref
        at = p.d if kind == 0 else p.far_d
        return push(src.at[s], ct_ref.at[at, s], c_s.at[kind, s], c_r.at[kind, s], p.sib)

    for s in range(slots):
        for kind in range(2):
            cot_copy(kind, s).start()
    ubuf[p.f] = urow_ref[...]
    dbuf[p.f] = drow_ref[...]
    ct_ref[p.d] = cot_ref[...]
    ct_ref[p.far_d] = cotfar_ref[...]

    def group(s, k):
        return mod_ref[s : s + 1, k * width : (k + 1) * width]

    gain = vec_ref[2:3, :width]
    b_down = vec_ref[3:4, :width]
    b_up = vec_ref[0:1, : act_ref.shape[3]]

    def nm_copy(kind, k):
        s, rows = k // 2, pl.ds(k % 2 * half, half)
        at = p.far_d if kind == 2 else p.d
        block = nm_ref.at[at, s, rows]
        return push(block, block, n_s.at[kind, k], n_r.at[kind, k], p.far if kind == 1 else p.sib)

    for s in range(slots):
        arecv[s, p.d] = att_ref[s, p.d]
        for kind in range(3):
            att_copy(kind, s).wait_recv()
        for r in range(m):
            for h in range(2):
                own_ref[s, h * half : (h + 1) * half, r * part : (r + 1) * part] = arecv[
                    s, r, :, h * part : (h + 1) * part
                ]
        branch = mm(own_ref[s], wout_ref[...], NT)
        br_ref[s] = branch
        middle = tok_ref[s].astype(F32) + group(s, 2) * branch
        mid_ref[s] = middle
        normal, inverse = norm_rows(middle)
        nrm_ref[s] = normal
        inv_ref[s] = inverse
        nm_ref[p.d, s] = (normal * (gain * (1.0 + group(s, 4))) + group(s, 3)).astype(BF16)
        for k in (2 * s, 2 * s + 1):
            nm_copy(1, k).start()
        for k in (2 * s, 2 * s + 1):
            nm_copy(0, k).start()

    def pass_on(s):
        for k in (2 * s, 2 * s + 1):
            nm_copy(1, k).wait_recv()
            nm_copy(2, k).start()

    def arrived(kind, s):
        for k in (2 * s, 2 * s + 1):
            nm_copy(kind, k).wait_recv()

    w_up = lambda: ubuf[...].reshape(-1, width)

    def expand(q, s):
        hidden = mm(nm_ref[q, s], w_up(), NT) + b_up
        value, slope = gelu_parts(hidden)
        act_ref[q, s] = value.astype(BF16)
        gp_ref[q, s] = slope.astype(BF16)

    dbup_ref[...] = jnp.zeros_like(dbup_ref)

    def pull(q, s):
        g = (ct_ref[q, s].astype(F32) * group(s, 5)).astype(BF16)
        ct_ref[q, s] = g
        grad = (mm(g, wdown_ref[...], NN) * gp_ref[q, s].astype(F32)).astype(BF16)
        gp_ref[q, s] = grad
        dbup_ref[0:1, :] += jnp.sum(grad.astype(F32), axis=0, keepdims=True)
        return mm(grad, w_up(), NN), mm(act_ref[q, s], wdown_ref[...], NT)

    gather_forward(p, *up[2:])
    gather_finish(*up)
    for s in range(slots):
        expand(p.d, s)
    for s in range(slots):
        arrived(0, s)
        expand(p.sib_d, s)
    pass_on(0)
    expand(p.far_d, 0)
    arrived(2, 0)
    expand(p.diag_d, 0)
    gather_forward(p, *down[2:])
    for s in range(1, slots):
        pass_on(s)
        expand(p.far_d, s)
        arrived(2, s)
        expand(p.diag_d, s)
    gather_finish(*down)
    wdown_ref[...] = compact(dbuf[...], small)

    def part_copy(kind, s):
        if kind == 4:
            return push(xs_ref.at[s], xr_ref.at[s], p_s.at[4, s], p_r.at[4, s], p.far)
        return push(psend.at[kind, s], precv.at[kind, s], p_s.at[kind, s], p_r.at[kind, s], p.sib)

    for s in range(slots):
        for kind in range(2):
            cot_copy(kind, s).wait_recv()
        grad, branch = pull(p.diag_d, s)
        psend[0, s] = grad.astype(BF16)
        part_copy(0, s).start()
        psend[2, s] = branch.astype(BF16)
        part_copy(2, s).start()
        grad, branch = pull(p.far_d, s)
        part_copy(0, s).wait_recv()
        xs_ref[s] = (grad + precv[0, s].astype(F32)).astype(BF16)
        part_copy(4, s).start()
        part_copy(2, s).wait_recv()
        xsend_ref[s] = (branch + precv[2, s].astype(F32)).astype(BF16)
    for s in range(slots):
        grad, branch = pull(p.sib_d, s)
        psend[1, s] = grad.astype(BF16)
        part_copy(1, s).start()
        psend[3, s] = branch.astype(BF16)
        part_copy(3, s).start()
        grad, branch = pull(p.d, s)
        gn_ref[s] = grad
        bo_ref[s] = branch

    def weight_grad(left_ref, right_ref, out_ref):
        rows = m * slots * quarter
        left = left_ref.reshape(rows, left_ref.shape[3])
        right = right_ref.reshape(rows, right_ref.shape[3])
        step = 256

        @pl.loop(0, left.shape[1] // step)
        def _(i):
            at = pl.ds(pl.multiple_of(i * step, step), step)
            out_ref[at, :] = mm(left[:, at], right[...], TN).astype(BF16)

    weight_grad(ct_ref, act_ref, dwd_ref)

    def grad_copy(kind, s):
        return push(
            gsend.at[s, ranks[kind]], grecv.at[s, p.d], g_s.at[kind, s], g_r.at[kind, s], peers[kind]
        )

    for s in range(slots):
        part_copy(1, s).wait_recv()
        part_copy(3, s).wait_recv()
        part_copy(4, s).wait_recv()
        cot = cot_ref[s].astype(F32)
        gn = gn_ref[s] + precv[1, s].astype(F32) + xr_ref[s].astype(F32)
        normal = nrm_ref[s]
        factor = gain * (1.0 + group(s, 4))
        grad_middle = cot + norm_back(gn, normal, inv_ref[s], factor)
        gm_ref[s] = grad_middle
        gba = (grad_middle * group(s, 2)).astype(BF16)
        gba_ref[s] = gba
        gatt = mm(gba, wout_ref[...], NN).astype(BF16)
        for r in range(m):
            for h in range(2):
                gsend[s, r, :, h * part : (h + 1) * part] = gatt[
                    h * half : (h + 1) * half, r * part : (r + 1) * part
                ]
        for kind in (2, 1, 0):
            grad_copy(kind, s).start()
        grecv[s, p.d] = gsend[s, p.d]
        branch = bo_ref[s] + precv[3, s].astype(F32) + b_down
        base_ref[s] = mid_ref[s] + group(s, 5) * branch
        total = lambda v: jnp.sum(v, axis=0, keepdims=True)
        sums_ref[8 * s : 8 * s + 1, :] = total(gn)
        sums_ref[8 * s + 1 : 8 * s + 2, :] = total(gn * normal)
        sums_ref[8 * s + 2 : 8 * s + 3, :] = total(cot * branch)
        sums_ref[8 * s + 3 : 8 * s + 4, :] = total(grad_middle * br_ref[s])
        sums_ref[8 * s + 4 : 8 * s + 5, :] = total((cot * group(s, 5)).astype(BF16).astype(F32))
        sums_ref[8 * s + 5 : 8 * s + 8, :] = jnp.zeros((3, width), F32)

    weight_grad(gp_ref, nm_ref, dwu_ref)
    flat = lambda ref: ref.reshape(slots * quarter, width)
    gba_flat, own_flat = flat(gba_ref), flat(own_ref)

    @pl.loop(0, width // 256)
    def _(i):
        at = pl.ds(pl.multiple_of(i * 256, 256), 256)
        dwo_ref[at, :] = mm(gba_flat[:, at], own_flat[...], TN).astype(BF16)

    for s in range(slots):
        for kind in range(3):
            grad_copy(kind, s).wait_recv()
    gatt_ref[...] = grecv[...]

    gather_drain(*up)
    gather_drain(*down)
    for s in range(slots):
        for kind in range(3):
            att_copy(kind, s).wait_send()
            grad_copy(kind, s).wait_send()
        for kind in range(2):
            cot_copy(kind, s).wait_send()
        for kind in range(5):
            part_copy(kind, s).wait_send()
        for k in (2 * s, 2 * s + 1):
            for kind in range(3):
                nm_copy(kind, k).wait_send()


def middle(n, m, small, tokens, cot, cot_far, att, mod, vec, w_out_t, up_rows, down_rows):
    slots, quarter, width = tokens.shape
    dma = pltpu.SemaphoreType.DMA
    shape = jax.ShapeDtypeStruct
    rows = (slots, quarter, width)
    lines = n // 2
    inner = n * up_rows.shape[0]
    return pl.pallas_call(
        functools.partial(middle_kernel, n, m, small),
        out_shape=(
            shape(rows, F32),
            shape(rows, F32),
            shape(rows, BF16),
            shape(att.shape, BF16),
            shape((width, inner), BF16),
            shape((inner, width), BF16),
            shape((width, width), BF16),
            shape((8, inner), F32),
            shape((8 * slots, width), F32),
        ),
        in_specs=[VM] * 9,
        out_specs=(VM,) * 9,
        scratch_shapes=[
            pltpu.VMEM(att.shape, BF16),
            pltpu.VMEM(rows, BF16),
            pltpu.VMEM(rows, F32),
            pltpu.VMEM(rows, F32),
            pltpu.VMEM(rows, F32),
            pltpu.VMEM((slots, quarter, 1), F32),
            pltpu.VMEM((m,) + rows, BF16),
            pltpu.VMEM((m,) + rows, BF16),
            pltpu.VMEM((m, slots, quarter, inner), BF16),
            pltpu.VMEM((m, slots, quarter, inner), BF16),
            pltpu.VMEM((n,) + up_rows.shape, BF16),
            pltpu.VMEM((n,) + down_rows.shape, BF16),
            pltpu.VMEM((width, inner), BF16),
            pltpu.VMEM((4,) + rows, BF16),
            pltpu.VMEM((4,) + rows, BF16),
            pltpu.VMEM(rows, BF16),
            pltpu.VMEM(rows, BF16),
            pltpu.VMEM(rows, F32),
            pltpu.VMEM(rows, F32),
            pltpu.VMEM(rows, BF16),
            pltpu.VMEM(att.shape, BF16),
            pltpu.VMEM(att.shape, BF16),
            dma((3, slots)),
            dma((3, slots)),
            dma((3, 2 * slots)),
            dma((3, 2 * slots)),
            dma((2, slots)),
            dma((2, slots)),
            dma((2, 4, lines)),
            dma((5, slots)),
            dma((5, slots)),
            dma((3, slots)),
            dma((3, slots)),
        ],
        compiler_params=pltpu.CompilerParams(
            collective_id=2, has_side_effects=True, vmem_limit_bytes=62 << 20
        ),
        name="middle",
    )(tokens, cot, cot_far, att, mod, vec, w_out_t, up_rows, down_rows)


def back_kernel(
    n,
    m,
    per,
    small,
    gq_ref,
    normed_ref,
    wqkv_ref,
    tok_ref,
    gm_ref,
    base_ref,
    other_ref,
    cot_ref,
    mod_ref,
    vec_ref,
    sums_ref,
    cond_ref,
    wada_ref,
    dwd_ref,
    dwu_ref,
    dwo_ref,
    dbup_ref,
    place_ref,
    home_ref,
    out_ref,
    dtok_ref,
    dcond_ref,
    dwada_ref,
    dbada_ref,
    dvec_ref,
    dwqkv_out,
    dwout_out,
    dwup_out,
    dwdown_out,
    psend,
    precv,
    xs_ref,
    xr_ref,
    gn_ref,
    dwq_ref,
    qblk,
    yrecv,
    zsend,
    zrecv,
    spr,
    qyrecv,
    qzsend,
    qzrecv,
    qspr,
    ssend,
    srecv,
    gsend,
    grecv,
    vsend,
    vrecv,
    dsend,
    drecv,
    p_s,
    p_r,
    y_s,
    y_r,
    z_s,
    z_r,
    d_s,
    d_r,
    s_s,
    s_r,
    g_s,
    g_r,
    v_s,
    v_r,
    c_s,
    c_r,
):
    p = Place(n, m)
    slots, quarter, width = tok_ref.shape
    lines = p.lines
    peers = (p.sib, p.far, p.diag)
    greet(list(peers) + [(p.ring_f(i), p.d) for i in range(1, n)])

    def parts(item):
        if item == 3:
            return qblk, qyrecv, qzsend, qzrecv, qspr
        src = (dwd_ref, dwu_ref, dwo_ref)[item]
        src = src.reshape(n, src.shape[0] // n, src.shape[1])
        return src, yrecv.at[item], zsend.at[item], zrecv.at[item], spr.at[item]

    def y_copy(item, i):
        src, yr, _, _, _ = parts(item)
        a = (p.a + i) % lines
        return push(src.at[a * 2 + 1 - p.b], yr.at[a], y_s.at[item, i], y_r.at[item, i], p.side)

    def z_copy(item, i):
        _, _, zs, zr, _ = parts(item)
        return push(
            zs.at[(p.a + i) % lines], zr.at[i], z_s.at[item, i], z_r.at[item, i], (p.line_f(i), p.d)
        )

    def spread_copy(item, kind):
        sp = parts(item)[4]
        at = p.far_d if kind == 2 else p.d
        return push(
            sp.at[at], sp.at[at], d_s.at[item, kind], d_r.at[item, kind], p.far if kind == 1 else p.sib
        )

    def start_side(item):
        for i in range(1, lines):
            y_copy(item, i).start()
        y_copy(item, 0).start()

    def line_sum(item):
        src, yr, zs, _, _ = parts(item)
        for i in list(range(1, lines)) + [0]:
            a = (p.a + i) % lines
            y_copy(item, i).wait_recv()
            zs[a] = (src[a * 2 + p.b].astype(F32) + yr[a].astype(F32)).astype(BF16)
            if i:
                z_copy(item, i).start()

    def own_sum(item):
        _, _, zs, zr, sp = parts(item)
        total = zs[p.a].astype(F32)
        for i in range(1, lines):
            z_copy(item, i).wait_recv()
            total = total + zr[i].astype(F32)
        sp[p.d] = total.astype(BF16)
        spread_copy(item, 1).start()
        spread_copy(item, 0).start()

    def spread_on(item):
        spread_copy(item, 1).wait_recv()
        spread_copy(item, 2).start()

    def spread_wait(item):
        spread_copy(item, 0).wait_recv()
        spread_copy(item, 2).wait_recv()

    for item in range(3):
        start_side(item)

    def group(s, k):
        return mod_ref[s : s + 1, k * width : (k + 1) * width]

    def part_copy(kind, s):
        if kind == 2:
            return push(xs_ref.at[s], xr_ref.at[s], p_s.at[2, s], p_r.at[2, s], p.far)
        return push(psend.at[kind, s], precv.at[kind, s], p_s.at[kind, s], p_r.at[kind, s], p.sib)

    def pull(q, s):
        rows = pl.ds(pl.multiple_of(q * quarter, quarter), quarter)
        return mm(gq_ref[s, rows, :], wqkv_ref[...], NN)

    for s in range(slots):
        psend[0, s] = pull(p.diag_d, s).astype(BF16)
        part_copy(0, s).start()
        grad = pull(p.far_d, s)
        part_copy(0, s).wait_recv()
        xs_ref[s] = (grad + precv[0, s].astype(F32)).astype(BF16)
        part_copy(2, s).start()
    for s in range(slots):
        psend[1, s] = pull(p.sib_d, s).astype(BF16)
        part_copy(1, s).start()
        gn_ref[s] = pull(p.d, s)

    rows_all = slots * normed_ref.shape[1]
    gq_all = gq_ref.reshape(rows_all, gq_ref.shape[2])
    normed_all = normed_ref.reshape(rows_all, width)
    for at in range(0, gq_ref.shape[2], 256):
        size = min(256, gq_ref.shape[2] - at)
        dwq_ref[at : at + size, :] = mm(gq_all[:, at : at + size], normed_all[...], TN).astype(BF16)
    count = qblk.shape[0] * qblk.shape[1]
    sel = lax.broadcasted_iota(jnp.int32, (dwq_ref.shape[0], count), 0)
    placing = (sel == place_ref[...]).astype(BF16)
    qblk[...] = mm(placing, dwq_ref[...], TN).astype(BF16).reshape(qblk.shape)
    start_side(3)
    line_sum(0)

    gate_extra = []
    for s in range(slots):
        other = other_ref[s].astype(F32)
        out_ref[s] = (base_ref[s] + group(s, 5) * other).astype(BF16)
        gate_extra.append(jnp.sum(cot_ref[s].astype(F32) * other, axis=0, keepdims=True))

    line_sum(1)
    gain_attn = vec_ref[1:2, :width]
    gain_mlp = vec_ref[2:3, :width]
    wide = dbup_ref.shape[1]
    ssend[...] = jnp.zeros_like(ssend)
    for s in range(slots):
        part_copy(1, s).wait_recv()
        part_copy(2, s).wait_recv()
        gn = gn_ref[s] + precv[1, s].astype(F32) + xr_ref[s].astype(F32)
        normal, inverse = norm_rows(tok_ref[s].astype(F32))
        dtok_ref[s] = (
            gm_ref[s] + norm_back(gn, normal, inverse, gain_attn * (1.0 + group(s, 1)))
        ).astype(BF16)
        row = 8 * s
        ssend[row : row + 1, :width] = jnp.sum(gn, axis=0, keepdims=True)
        ssend[row + 1 : row + 2, :width] = jnp.sum(gn * normal, axis=0, keepdims=True)
        ssend[row + 2 : row + 3, :width] = sums_ref[row + 3 : row + 4, :]
        ssend[row + 3 : row + 5, :width] = sums_ref[row : row + 2, :]
        ssend[row + 5 : row + 6, :width] = sums_ref[row + 2 : row + 3, :] + gate_extra[s]
        ssend[row + 6 : row + 7, :width] = sums_ref[row + 4 : row + 5, :]
    ssend[7:8, :wide] = dbup_ref[0:1, :]

    def sums_copy(kind):
        return push(ssend, srecv.at[p.d], s_s.at[kind], s_r.at[kind], peers[kind])

    for kind in range(3):
        sums_copy(kind).start()
    srecv[p.d] = ssend[...]
    line_sum(2)
    for kind in range(3):
        sums_copy(kind).wait_recv()
    total = srecv[0]
    for r in range(1, m):
        total = total + srecv[r]
    cols = wada_ref.shape[1]
    gmod = []
    d_gain_attn = jnp.zeros((1, width), F32)
    d_gain_mlp = jnp.zeros((1, width), F32)
    d_b_down = jnp.zeros((1, width), F32)
    for s in range(slots):
        at = lambda k, s=s: total[8 * s + k : 8 * s + k + 1, :width]
        gmod.append(
            jnp.concatenate(
                [at(0), at(1) * gain_attn, at(2), at(3), at(4) * gain_mlp, at(5)], axis=1
            )
        )
        d_gain_attn = d_gain_attn + at(1) * (1.0 + group(s, 1))
        d_gain_mlp = d_gain_mlp + at(4) * (1.0 + group(s, 4))
        d_b_down = d_b_down + at(6)
    gmod = jnp.concatenate(gmod + [jnp.zeros((16 - slots, 6 * width), F32)], axis=0).astype(BF16)
    vecs = [d_gain_attn, d_gain_mlp, d_b_down]
    vsend[...] = jnp.zeros_like(vsend)
    for g in range(n):
        gsend[g] = gmod[:, g * cols : (g + 1) * cols]
        for k, v in enumerate(vecs):
            vsend[g, k : k + 1, :small] = v[:, g * small : (g + 1) * small]
        for r in range(m):
            vsend[g, 3 + r : 4 + r, :per] = srecv[r, 7:8, g * per : (g + 1) * per]

    def g_copy(i):
        peer = p.ring_f(i)
        return push(gsend.at[peer], grecv.at[p.f], g_s.at[i], g_r.at[i], (peer, p.d))

    def v_copy(i):
        peer = p.ring_f(i)
        return push(vsend.at[peer], vrecv.at[p.f], v_s.at[i], v_r.at[i], (peer, p.d))

    for i in range(1, n):
        g_copy(i).start()
        v_copy(i).start()
    grecv[p.f] = gsend[p.f]
    vrecv[p.f] = vsend[p.f]
    line_sum(3)
    own_sum(0)
    for i in range(1, n):
        g_copy(i).wait_recv()
    got = grecv[...].reshape(n * 16, cols)
    conds = cond_ref[...].reshape(n * 16, cond_ref.shape[2])
    dsend[...] = mm(got, wada_ref[...], NT).reshape(n, 16, conds.shape[1])[:, :8]

    def c_copy(i):
        peer = p.ring_f(i)
        return push(dsend.at[peer], drecv.at[p.f], c_s.at[i], c_r.at[i], (peer, p.d))

    for i in range(1, n):
        c_copy(i).start()
    drecv[p.f] = dsend[p.f]
    dwada_ref[...] = mm(conds, got, TN)
    dbada_ref[...] = jnp.sum(got.astype(F32), axis=0, keepdims=True)
    own_sum(1)
    for i in range(1, n):
        v_copy(i).wait_recv()
    total = vrecv[0]
    for g in range(1, n):
        total = total + vrecv[g]
    dvec_ref[...] = total
    spread_on(0)
    own_sum(2)
    spread_on(1)
    for i in range(1, n):
        c_copy(i).wait_recv()
    total = drecv[0]
    for g in range(1, n):
        total = total + drecv[g]
    dcond_ref[...] = total[:slots].astype(BF16)
    spread_wait(0)
    inner = width // m
    for r in range(m):
        piece = spr[0, r].astype(F32).T
        for g in range(n):
            row = (g * m + r) * per
            dwdown_out[row : row + per, :] = piece[g * round16(per) : g * round16(per) + per, :small]
    own_sum(3)
    spread_on(2)
    spread_wait(1)
    dwup_out[...] = jnp.concatenate([spr[1, r][:per, :width] for r in range(m)]).astype(F32).T
    spread_wait(2)
    piece = spr[2, 0].astype(F32)
    for r in range(1, m):
        piece = piece + spr[2, r].astype(F32)
    piece = piece.T
    heads = inner // HEAD
    for r in range(m):
        for h in range(heads):
            dwout_out[(h * m + r) * HEAD : (h * m + r + 1) * HEAD, :] = piece[
                r * inner + h * HEAD : r * inner + (h + 1) * HEAD, :small
            ]
    spread_on(3)
    spread_wait(3)
    count = qspr.shape[0] * qspr.shape[1]
    sel = lax.broadcasted_iota(jnp.int32, (dwqkv_out.shape[1], count), 0)
    homing = (sel == home_ref[...]).astype(BF16)
    dwqkv_out[...] = mm(qspr[...].reshape(count, width), homing, (((0,), (1,)), ((), ())))

    for s in range(slots):
        for kind in range(3):
            part_copy(kind, s).wait_send()
    for item in range(4):
        for i in range(lines):
            y_copy(item, i).wait_send()
            if i:
                z_copy(item, i).wait_send()
        for kind in range(3):
            spread_copy(item, kind).wait_send()
    for kind in range(3):
        sums_copy(kind).wait_send()
    for i in range(1, n):
        g_copy(i).wait_send()
        v_copy(i).wait_send()
        c_copy(i).wait_send()


def back(n, m, per, small, most, shards_in, args):
    gq, normed, w_qkv_t, tokens = args[:4]
    slots, quarter, width = tokens.shape
    cond_blocks, w_ada, dw_down = args[11:14]
    dma = pltpu.SemaphoreType.DMA
    shape = jax.ShapeDtypeStruct
    rows = (slots, quarter, width)
    lines = n // 2
    wide = max(width, n * round16(per))
    block = round16(small)
    cols = w_ada.shape[1]
    cond = w_ada.shape[0]
    assert round16(per) == block
    lane = dw_down.shape[1]
    return pl.pallas_call(
        functools.partial(back_kernel, n, m, per, small),
        out_shape=(
            shape(rows, BF16),
            shape(rows, BF16),
            shape((slots, cond), BF16),
            shape((cond, cols), F32),
            shape((1, cols), F32),
            shape((8, max(per, small)), F32),
            shape((width, shards_in), F32),
            shape((width, small), F32),
            shape((width, m * per), F32),
            shape((n * m * per, small), F32),
        ),
        in_specs=[VM] * len(args),
        out_specs=(VM,) * 10,
        scratch_shapes=[
            pltpu.VMEM((2,) + rows, BF16),
            pltpu.VMEM((2,) + rows, BF16),
            pltpu.VMEM(rows, BF16),
            pltpu.VMEM(rows, BF16),
            pltpu.VMEM(rows, F32),
            pltpu.VMEM((gq.shape[2], width), BF16),
            pltpu.VMEM((n, most, width), BF16),
            pltpu.VMEM((3, lines, block, lane), BF16),
            pltpu.VMEM((3, lines, block, lane), BF16),
            pltpu.VMEM((3, lines, block, lane), BF16),
            pltpu.VMEM((3, m, block, lane), BF16),
            pltpu.VMEM((lines, most, width), BF16),
            pltpu.VMEM((lines, most, width), BF16),
            pltpu.VMEM((lines, most, width), BF16),
            pltpu.VMEM((m, most, width), BF16),
            pltpu.VMEM((8 * slots, wide), F32),
            pltpu.VMEM((m, 8 * slots, wide), F32),
            pltpu.VMEM((n, 16, cols), BF16),
            pltpu.VMEM((n, 16, cols), BF16),
            pltpu.VMEM((n, 8, max(per, small)), F32),
            pltpu.VMEM((n, 8, max(per, small)), F32),
            pltpu.VMEM((n, 8, cond), F32),
            pltpu.VMEM((n, 8, cond), F32),
            dma((3, slots)),
            dma((3, slots)),
            dma((4, lines)),
            dma((4, lines)),
            dma((4, lines)),
            dma((4, lines)),
            dma((4, 3)),
            dma((4, 3)),
            dma((3,)),
            dma((3,)),
            dma((n,)),
            dma((n,)),
            dma((n,)),
            dma((n,)),
            dma((n,)),
            dma((n,)),
        ],
        compiler_params=pltpu.CompilerParams(
            collective_id=3, has_side_effects=True, vmem_limit_bytes=62 << 20
        ),
        name="back",
    )(*args)


def column_plan(shards_n, ranks, columns):
    per = columns // shards_n
    rank_of = (np.arange(columns) // HEAD) % ranks
    lists = [
        [[c for c in range(per) if rank_of[f * per + c] == r] for r in range(ranks)]
        for f in range(shards_n)
    ]
    most = max(len(l) for row in lists for l in row)
    most = -(-most // 16) * 16
    take = np.full((shards_n, ranks, most), -1, np.int32)
    place = np.full((ranks, shards_n * most), -1, np.int32)
    home = np.full((shards_n, ranks * most), -1, np.int32)
    for r in range(ranks):
        order = {c: i for i, c in enumerate(np.flatnonzero(rank_of == r))}
        for f in range(shards_n):
            for i, c in enumerate(lists[f][r]):
                take[f, r, i] = c
                place[r, f * most + i] = order[f * per + c]
                home[f, r * most + i] = c
    return most, take, place, home


def pad_blocks(v, count, rows, lanes=0):
    v = jnp.pad(v, ((0, 0), (0, max(0, lanes - v.shape[1]))))
    have = v.shape[0] // count
    if have == rows:
        return v
    blocks = v.reshape(count, have, v.shape[1])
    return jnp.pad(blocks, ((0, 0), (0, rows - have), (0, 0))).reshape(-1, v.shape[1])


def pick(indices, size):
    return (indices[:, None] == jnp.arange(size, dtype=jnp.int32)[None, :]).astype(BF16)


def shards(
    tokens,
    condition,
    segments,
    w_ada,
    b_ada,
    gain_attn,
    w_qkv,
    w_out,
    gain_mlp,
    w_up,
    b_up,
    w_down,
    b_down,
    cotangent,
):
    slots, quarter, width = tokens.shape
    length = segments.shape[1]
    n = lax.axis_size("fsdp")
    m = lax.axis_size("dp")
    f = lax.axis_index("fsdp")
    d = lax.axis_index("dp")
    heads = width // HEAD
    part = width // m
    hidden_part = w_up.shape[1] * n // m
    tile = quarter
    cos_np, sin_np = rope_table(length)
    cosine, sine = jnp.asarray(cos_np), jnp.asarray(sin_np)

    ups = b_up.shape[0]
    small = gain_attn.shape[0]
    most, take, place, home = column_plan(n, m, w_qkv.shape[1] * n)
    picked = pick(jnp.asarray(take)[f, d], w_qkv.shape[1])
    qkv_rows = mm(picked, w_qkv, NT).astype(BF16)
    up_rows = lax.dynamic_slice_in_dim(w_up, d * (ups // m), ups // m, 1).T
    down_rows = lax.dynamic_index_in_dim(
        w_down.reshape(n, m, ups // m, small), d, 1, False
    ).reshape(-1, small).T
    out_rows = w_out.reshape(heads // m, m, HEAD, small).transpose(1, 0, 2, 3).reshape(-1, small).T
    place_row = jnp.asarray(place)[d]
    placing = pick(place_row, 3 * part)

    pad_rows = lambda v, size: jnp.pad(v, ((0, size - v.shape[0]), (0, 0)))
    wide = max(width, n * (ups // m))
    vec = jnp.stack(
        [
            jnp.pad(v, (0, width - v.shape[0]))
            for v in (
                lax.dynamic_slice_in_dim(b_up, d * (ups // m), ups // m, 0),
                gain_attn,
                gain_mlp,
                b_down,
            )
        ]
    )
    qkv, normed, mod_rows, vec_rows, w_qkv_t, out_blocks, cond_blocks = front(
        n,
        m,
        (round16(ups // m), small, small, small),
        length,
        tokens,
        pad_rows(condition, 16),
        w_ada,
        b_ada[None],
        pad_rows(vec, 16),
        qkv_rows,
        pad_rows(out_rows, round16(small)),
        place_row[None],
        jnp.concatenate([cosine, cosine], axis=1),
        jnp.concatenate([sine, sine], axis=1),
    )
    cond_all = cond_blocks[:, :slots].reshape(n * slots, -1)
    modulation = mod_rows[:slots]
    shift_attn, scale_attn, gate_attn, shift_mlp, scale_mlp, gate_mlp = [
        g[:, None, :] for g in jnp.split(modulation, 6, axis=-1)
    ]
    b_up_rank = vec_rows[0, : hidden_part]
    gain_attn_all, gain_mlp_all, b_down_all = [vec_rows[i, :width] for i in (1, 2, 3)]
    w_out_t = out_blocks[:, :small].reshape(width, width)
    attended, logs = attend(segments, qkv, tile)

    own = lax.all_to_all(attended, "dp", 1, 2, tiled=True)
    far = [(i, (i + m // 2) % m) for i in range(m)]
    cot_far = lax.ppermute(cotangent, "dp", far)
    up_per, up_pad = ups // m, round16(ups // m)
    down_pad = jnp.pad(
        down_rows.reshape(small, n, up_per), ((0, 0), (0, 0), (0, up_pad - up_per))
    ).reshape(small, -1)
    grad_middle, base, far_part, grad_attended, dw_down_t, dw_up_t, dw_out_t, db_up, sums_mlp = middle(
        n,
        m,
        small,
        tokens,
        cotangent,
        cot_far,
        attended,
        mod_rows,
        vec_rows,
        w_out_t,
        pad_rows(up_rows, up_pad),
        pad_rows(down_pad, round16(small)),
    )
    other_part = lax.ppermute(far_part, "dp", far)
    gqkv = attend_back(segments, qkv, grad_attended, attended, logs, cosine, sine, tile)
    outputs, d_tokens, d_condition, d_w_ada, d_b_ada, d_vec, d_w_qkv, d_w_out, d_w_up, d_w_down = back(
        n,
        m,
        up_per,
        small,
        most,
        w_qkv.shape[1],
        (
            gqkv,
            normed,
            w_qkv_t,
            tokens,
            grad_middle,
            base,
            other_part,
            cotangent,
            mod_rows,
            vec_rows,
            sums_mlp,
            cond_blocks,
            w_ada,
            pad_blocks(dw_down_t, n, round16(small)),
            pad_blocks(dw_up_t, n, round16(up_per), dw_down_t.shape[1]),
            pad_blocks(dw_out_t, n, round16(small), dw_down_t.shape[1]),
            db_up,
            place_row[None],
            jnp.asarray(home)[f][None],
        ),
    )
    return (
        outputs,
        d_tokens,
        d_condition,
        d_w_ada,
        d_b_ada.reshape(-1),
        d_vec[0, :small],
        d_w_qkv,
        d_w_out,
        d_vec[1, :small],
        d_w_up,
        d_vec[3 : 3 + m, :up_per].reshape(-1),
        d_w_down,
        d_vec[2, :small],
    )


def solution(mesh):
    return jax.shard_map(
        shards,
        mesh=mesh,
        in_specs=(
            P("fsdp", "dp", None),
            P("fsdp", None),
            P("fsdp", None),
            P(None, "fsdp"),
            P("fsdp"),
            P("fsdp"),
            P(None, "fsdp"),
            P(None, "fsdp"),
            P("fsdp"),
            P(None, "fsdp"),
            P("fsdp"),
            P(None, "fsdp"),
            P("fsdp"),
            P("fsdp", "dp", None),
        ),
        out_specs=(
            P("fsdp", "dp", None),
            P("fsdp", "dp", None),
            P("fsdp", None),
            P(None, "fsdp"),
            P("fsdp"),
            P("fsdp"),
            P(None, "fsdp"),
            P(None, "fsdp"),
            P("fsdp"),
            P(None, "fsdp"),
            P("fsdp"),
            P(None, "fsdp"),
            P("fsdp"),
        ),
        check_vma=False,
    )
```

```python
import functools
import math

import jax
import jax.numpy as jnp
import numpy as np
from jax import lax
from jax.experimental import pallas as pl
from jax.experimental.pallas import tpu as pltpu
from jax.sharding import PartitionSpec as P

HEAD = 64
EPS = 1e-05
ROPE_BASE = 10000.0
MASKED = -1e30
F32 = jnp.float32
BF16 = jnp.bfloat16

NN = (((1,), (0,)), ((), ()))
NT = (((1,), (1,)), ((), ()))
TN = (((0,), (0,)), ((), ()))


def mm(a, b, dims):
    return lax.dot_general(a, b, dims, preferred_element_type=F32)


def rope_table(length):
    inverse = ROPE_BASE ** (-2.0 * np.arange(HEAD // 2) / HEAD)
    angles = np.arange(length)[:, None] * inverse[None, :]
    cosine = np.concatenate([np.cos(angles)] * 2, axis=1)
    sine = np.concatenate([-np.sin(angles), np.sin(angles)], axis=1)
    return cosine.astype(np.float32), sine.astype(np.float32)


def swap_halves(v):
    half = HEAD // 2
    return jnp.concatenate([v[..., half:], v[..., :half]], axis=-1)


MESH = pl.DeviceIdType.MESH
VM = pl.BlockSpec(memory_space=pltpu.VMEM)
ANY = pl.BlockSpec(memory_space=pl.ANY)
LIMIT = 63 << 20


def round16(size):
    return -(-size // 16) * 16


def iota(shape, dim):
    return lax.broadcasted_iota(jnp.int32, shape, dim)


def greet(peers, meanwhile=None):
    barrier = pltpu.get_barrier_semaphore()
    for peer in peers:
        pl.semaphore_signal(barrier, inc=1, device_id=peer, device_id_type=MESH)
    if meanwhile is not None:
        meanwhile()
    pl.semaphore_wait(barrier, len(peers))


def push(src, dst, send, recv, peer):
    return pltpu.make_async_remote_copy(
        src_ref=src,
        dst_ref=dst,
        send_sem=send,
        recv_sem=recv,
        device_id=peer,
        device_id_type=MESH,
    )


class Place:
    def __init__(self, n, m):
        self.n, self.m = n, m
        self.f = lax.axis_index("fsdp")
        self.d = lax.axis_index("dp")
        self.lines = n // 2
        self.a = self.f // 2
        self.b = self.f % 2
        self.x = self.d // 2
        self.c = self.d % 2
        self.sib_d = self.x * 2 + 1 - self.c
        self.far_d = (1 - self.x) * 2 + self.c
        self.diag_d = (1 - self.x) * 2 + 1 - self.c
        self.sib = (self.f, self.sib_d)
        self.far = (self.f, self.far_d)
        self.diag = (self.f, self.diag_d)
        self.side = (self.a * 2 + 1 - self.b, self.d)
        last = self.lines - 1
        self.right = (jnp.minimum(self.a + 1, last) * 2 + self.b, self.d)
        self.left = (jnp.maximum(self.a - 1, 0) * 2 + self.b, self.d)
        self.has_right = self.a < last
        self.has_left = self.a > 0

    def ring_f(self, step):
        return (self.f + step + self.n) % self.n

    def ring(self):
        return [(self.ring_f(i), self.d) for i in range(1, self.n)]

    def line_peers(self):
        return [((self.a + i) % self.lines * 2 + self.b, self.d) for i in range(1, self.lines)] + [
            self.side
        ]


class Gather:
    def __init__(self, p, src, slot, sems):
        self.p, self.src, self.slot = p, src, slot
        self.zs, self.zr, self.ys, self.yr = [sems.at[k] for k in range(4)]

    def line_copy(self, way, t):
        p = self.p
        block = self.slot(jnp.clip(p.a + (t if way else -t), 0, p.lines - 1) * 2 + p.b)
        return push(
            self.src if t == 0 else block,
            block,
            self.zs.at[way, t],
            self.zr.at[way, t + 1],
            p.left if way else p.right,
        )

    def line_wait(self, way, t):
        p = self.p
        block = self.slot(jnp.clip(p.a + (t if way else -t), 0, p.lines - 1) * 2 + p.b)
        push(block, block, self.zs.at[way, t], self.zr.at[way, t], p.left if way else p.right).wait_recv()

    def side_copy(self, way, t, theirs=False):
        p = self.p
        b = 1 - p.b if theirs else p.b
        block = self.slot(jnp.clip(p.a + (t if way else -t), 0, p.lines - 1) * 2 + b)
        return push(
            self.src if t == 0 else block, block, self.ys.at[way, t], self.yr.at[way, t], p.side
        )

    def held(self, way, t):
        p = self.p
        return p.a + t < p.lines if way else p.a - t >= 0

    def onward(self, way):
        return self.p.has_left if way else self.p.has_right

    def start(self):
        for way in range(2):
            pl.when(self.onward(way))(lambda way=way: self.line_copy(way, 0).start())
        self.side_copy(0, 0).start()

    def step(self, t):
        for way in range(2):

            @pl.when(self.held(way, t))
            def _(way=way):
                self.line_wait(way, t)
                if t < self.p.lines - 1:
                    pl.when(self.onward(way))(lambda: self.line_copy(way, t).start())
                self.side_copy(way, t).start()

    def finish(self):
        self.side_copy(0, 0, True).wait_recv()
        for t in range(1, self.p.lines):
            for way in range(2):
                pl.when(self.held(way, t))(
                    lambda way=way, t=t: self.side_copy(way, t, True).wait_recv()
                )

    def drain(self):
        self.side_copy(0, 0).wait_send()
        for way in range(2):
            pl.when(self.onward(way))(lambda way=way: self.line_copy(way, 0).wait_send())
        for t in range(1, self.p.lines):
            for way in range(2):

                @pl.when(self.held(way, t))
                def _(way=way, t=t):
                    if t < self.p.lines - 1:
                        pl.when(self.onward(way))(lambda: self.line_copy(way, t).wait_send())
                    self.side_copy(way, t).wait_send()


class Both:
    def __init__(self, *gathers):
        self.gathers = gathers

    def start(self):
        for g in self.gathers:
            g.start()

    def step(self, t):
        for g in self.gathers:
            g.step(t)

    def finish(self):
        for g in self.gathers:
            g.finish()

    def drain(self):
        for g in self.gathers:
            g.drain()


def gather_halves(p, src, buf, sems):
    rows = src.shape[0]
    if rows % 32:
        return Gather(p, src, lambda f: buf.at[f], sems.at[0])
    cut = [pl.ds(h * rows // 2, rows // 2) for h in range(2)]
    return Both(
        *[Gather(p, src.at[cut[h]], lambda f, h=h: buf.at[f, cut[h]], sems.at[h]) for h in range(2)]
    )


class Reduce:
    def __init__(self, p, src, side, total, zrecv, sems, summed=False):
        self.p, self.src, self.side, self.total = p, src, side, total
        self.zrecv, self.summed = zrecv, summed
        self.ys, self.yr, self.zs, self.zr = [sems.at[k] for k in range(4)]

    def order(self):
        lines = self.p.lines
        return [j for k in range(lines // 2) for j in (lines - 1 - k, k)]

    def side_copy(self, j):
        p = self.p
        return push(self.src(2 * j + 1 - p.b), self.side.at[j], self.ys.at[0, j], self.yr.at[0, j], p.side)

    def line_copy(self, way, j):
        p = self.p
        at = jnp.where(j == p.a - 1, p.lines, j) if way else j
        return push(
            self.total.at[j],
            self.zrecv.at[at],
            self.zs.at[way, j],
            self.zr.at[way, j],
            p.left if way else p.right,
        )

    def line_wait(self, way, j):
        p = self.p
        at = jnp.where(j == p.a, p.lines, j) if way else j
        block = self.zrecv.at[at]
        push(block, block, self.zs.at[way, j], self.zr.at[way, j], p.left if way else p.right).wait_recv()
        return block[...].astype(F32)

    def start(self):
        for j in self.order():
            self.side_copy(j).start()

    def side_sum(self, j):
        p = self.p
        self.side_copy(j).wait_recv()
        mine = self.src(2 * j + p.b)[...].astype(F32)
        self.total[j] = (mine + self.side[j].astype(F32)).astype(BF16)

    def step(self, t):
        p = self.p
        if 2 * t < p.lines and not self.summed:
            for j in self.order()[2 * t : 2 * t + 2]:
                self.side_sum(j)
        for way in range(2):
            j = t - (p.lines - 1 - p.a) if way else p.lines - 1 - (t - p.a)
            ahead = (j >= 0) & (j < p.a) if way else (j < p.lines) & (j > p.a)
            behind = p.has_right if way else p.has_left

            @pl.when(ahead)
            def _(way=way, j=j, behind=behind):
                @pl.when(behind)
                def _():
                    arrived = self.line_wait(way, j)
                    self.total[j] = (self.total[j].astype(F32) + arrived).astype(BF16)

                self.line_copy(way, j).start()

    def own(self, out):
        p = self.p
        for way in range(2):

            @pl.when(p.has_right if way else p.has_left)
            def _(way=way):
                arrived = self.line_wait(way, p.a)
                self.total[p.a] = (self.total[p.a].astype(F32) + arrived).astype(BF16)

        out[...] = self.total[p.a]

    def drain(self):
        p = self.p
        for j in range(p.lines):
            if not self.summed:
                self.side_copy(j).wait_send()
            for way in range(2):
                ahead = p.a > j if way else p.a < j
                pl.when(ahead)(lambda way=way, j=j: self.line_copy(way, j).wait_send())


class Spread:
    def __init__(self, p, buf, send, recv):
        self.p, self.buf, self.send, self.recv = p, buf, send, recv

    def copy(self, kind):
        p = self.p
        block = self.buf.at[p.far_d if kind == 2 else p.d]
        return push(block, block, self.send.at[kind], self.recv.at[kind], p.far if kind == 1 else p.sib)

    def start(self):
        self.copy(1).start()
        self.copy(0).start()

    def forward(self):
        self.copy(1).wait_recv()
        self.copy(2).start()

    def finish(self):
        self.copy(0).wait_recv()
        self.copy(2).wait_recv()

    def drain(self):
        for kind in range(3):
            self.copy(kind).wait_send()


def norm_rows(stream):
    average = jnp.mean(stream, axis=-1, keepdims=True)
    centered = stream - average
    variance = jnp.mean(centered * centered, axis=-1, keepdims=True)
    inverse = lax.rsqrt(variance + EPS)
    return centered * inverse, inverse


def norm_back(grad, normal, inverse, factor):
    e = grad * factor
    mean_e = jnp.mean(e, axis=-1, keepdims=True)
    mean_en = jnp.mean(e * normal, axis=-1, keepdims=True)
    return inverse * (e - mean_e - normal * mean_en)


def turned(v):
    lanes = iota(v.shape, 1)
    half = HEAD // 2
    return jnp.where(lanes % HEAD < half, pltpu.roll(v, 128 - half, 1), pltpu.roll(v, half, 1))


def gelu_parts(h):
    root = math.sqrt(2.0 / math.pi)
    square = h * h
    t = jnp.tanh(root * h * (1.0 + 0.044715 * square))
    half = 0.5 * (1.0 + t)
    slope = half + 0.5 * h * (1.0 - t * t) * (root * (1.0 + 3.0 * 0.044715 * square))
    return h * half, slope


def compact(blocks, per):
    count, rows, lanes = blocks.shape
    flat = blocks.reshape(count * rows, lanes)
    if rows == per:
        return flat
    want = iota((count * per, count * rows), 0)
    have = iota((count * per, count * rows), 1)
    chosen = (have == want // per * rows + want % per).astype(BF16)
    return mm(chosen, flat, NN).astype(BF16)


def as_column(row):
    size = row.shape[1]
    return jnp.transpose(jnp.broadcast_to(row, (128, size)))[:, :1]


def front_kernel(
    n,
    m,
    per,
    tile,
    tok_ref,
    cot_ref,
    cond_ref,
    seg_ref,
    wada_ref,
    bada_ref,
    bup_ref,
    ga_ref,
    gm_ref,
    bdown_ref,
    wqkv_ref,
    wout_ref,
    wup_ref,
    take_ref,
    place_ref,
    cos_ref,
    sin_ref,
    qkv_out,
    normed_out,
    att_out,
    own_out,
    log_out,
    cotfar_out,
    wout_out,
    up_out,
    mod_ref,
    vecs_ref,
    wqkvt_ref,
    vec_out,
    qkv_ref,
    normed_ref,
    tall_ref,
    att_v,
    arecv,
    log_v,
    cotfar_v,
    mod_send,
    mod_recv,
    vsrc,
    vbuf,
    qsrc,
    qbuf,
    osrc,
    obuf,
    usrc,
    ubuf,
    vs,
    vr,
    ms,
    mr,
    gz,
    ts,
    tr,
    os_,
    or_,
    as_,
    ar,
    cs,
    cr,
    local,
):
    p = Place(n, m)
    slots, quarter, width = tok_ref.shape
    half = quarter // 2
    part = width // m
    heads = part // HEAD
    hidden_per, small = per
    pad = round16(hidden_per)
    halves = obuf.shape[1]
    length = m * quarter
    peers = (p.sib, p.far, p.diag)
    ranks = (p.sib_d, p.far_d, p.diag_d)
    own_tokens = pltpu.make_async_copy(tok_ref, tall_ref.at[p.d], local.at[2, 0])
    own_tokens.start()
    log_v[...] = jnp.zeros_like(log_v)

    def prepare():
        vsrc[...] = jnp.zeros_like(vsrc)
        for row, ref in enumerate((bup_ref, ga_ref, gm_ref, bdown_ref)):
            vsrc[row : row + 1, : ref.shape[1]] = ref[...]
        vsrc[4 : 4 + slots, : cond_ref.shape[1]] = cond_ref[...]
        columns = wqkv_ref.shape[0]
        most = qsrc.shape[0]
        taking = take_ref[pl.ds(p.f * m + p.d, 1), :]
        chosen = (iota((columns, most), 0) == taking).astype(BF16)
        qsrc[...] = mm(chosen, wqkv_ref[...], TN).astype(BF16)

    greet(list(peers) + p.ring(), prepare)

    def vec_copy(i):
        return push(vsrc, vbuf.at[p.f], vs.at[i], vr.at[i], (p.ring_f(i), p.d))

    for i in range(1, n):
        vec_copy(i).start()

    def token_copy(kind, k):
        s, rows = k // 2, pl.ds(k % 2 * half, half)
        if kind == 2:
            block = tall_ref.at[p.far_d, s, rows]
            return push(block, block, ts.at[kind, k], tr.at[kind, k], p.sib)
        return push(
            tok_ref.at[s, rows],
            tall_ref.at[p.d, s, rows],
            ts.at[kind, k],
            tr.at[kind, k],
            p.sib if kind == 0 else p.far,
        )

    qry = gather_halves(p, qsrc, qbuf, gz.at[0])
    qry.start()
    for k in range(2 * slots):
        token_copy(1, k).start()
    for k in range(2 * slots):
        token_copy(0, k).start()
    vbuf[p.f] = vsrc[...]
    qbuf[p.f] = qsrc[...]

    lane = iota((1, width), 1)
    rank, inner = lane // part, lane % part
    want = (inner // HEAD * m + rank) * HEAD + inner % HEAD
    chosen = (iota((width, width), 0) == want).astype(BF16)
    got = mm(wout_ref[...], chosen, NN).astype(BF16)
    if small < osrc.shape[0]:
        got = jnp.concatenate([got, jnp.zeros((osrc.shape[0] - small, width), BF16)])
    osrc[...] = got
    split = osrc.shape[0] // halves
    mine = p.c if halves == 2 else 0
    out = Gather(
        p,
        osrc.at[pl.ds(pl.multiple_of(mine * split, 16), split)],
        lambda f: obuf.at[f, mine],
        gz.at[1, 0],
    )
    for h in range(halves):
        obuf[p.f, h] = osrc[h * split : (h + 1) * split]

    ups = wup_ref.shape[1]
    at, lane = iota((pad, ups), 0), iota((pad, ups), 1)
    chosen = ((lane == at + p.d * hidden_per) & (at < hidden_per)).astype(BF16)
    usrc[...] = mm(chosen, wup_ref[...], NT).astype(BF16)
    ubuf[p.f] = usrc[...]
    up = gather_halves(p, usrc, ubuf, gz.at[2])

    def pass_on(k):
        token_copy(1, k).wait_recv()
        token_copy(2, k).start()

    for i in range(1, n):
        vec_copy(i).wait_recv()
    vecs = vbuf[...].reshape(n * 16, width)
    mod_cols = mm(vecs[:, : cond_ref.shape[1]], wada_ref[...], NT) + bada_ref[...].astype(F32)
    mod_send[...] = mod_cols.reshape(n, 16, mod_cols.shape[1])[:, :8]
    mod_recv[p.f] = mod_send[p.f]

    def mod_copy(i):
        peer = p.ring_f(i)
        return push(mod_send.at[peer], mod_recv.at[p.f], ms.at[i], mr.at[i], (peer, p.d))

    for i in range(1, n):
        mod_copy(i).start()
    vec_out[...] = vbuf[...]
    vecs_ref[...] = jnp.zeros_like(vecs_ref)
    mine_up = (iota((ups, pad), 0) == iota((ups, pad), 1) + p.d * hidden_per) & (
        iota((ups, pad), 1) < hidden_per
    )
    b_up = mm(vecs[:, :ups], mine_up.astype(BF16), NN)
    for g in range(n):
        vecs_ref[0:1, g * pad : (g + 1) * pad] = b_up[16 * g : 16 * g + 1]
        rest = vecs[16 * g : 16 * g + 8].astype(F32)
        for k in range(1, 4):
            vecs_ref[k : k + 1, g * small : (g + 1) * small] = rest[k : k + 1, :small]
    qry.step(1)
    pass_on(0)
    for i in range(1, n):
        mod_copy(i).wait_recv()
    cols = mod_cols.shape[1]
    for g in range(n):
        for s in range(slots):
            mod_ref[s, :, g * cols : (g + 1) * cols] = mod_recv[g, 4 + s : 5 + s]
    gain = vecs_ref[1:2, :width]

    for k in range(2, p.lines - 1):
        qry.step(k)
    out.start()
    pass_on(1)
    qry.step(p.lines - 1)
    pass_on(2)
    def cot_copy(s):
        return push(cot_ref.at[s], cotfar_v.at[s], cs.at[s], cr.at[s], p.far)

    for s in range(slots):
        cot_copy(s).start()

    qry.finish()
    up.start()
    count = n * qsrc.shape[0]
    placing = (iota((3 * part, count), 0) == place_ref[pl.ds(p.d, 1), :]).astype(BF16)
    wqkvt_ref[...] = mm(placing, qbuf[...].reshape(count, width), NN).astype(BF16)
    own_tokens.wait()

    def chunk(i):
        q = jnp.where(
            i < 2, p.d, jnp.where(i < 4, p.sib_d, jnp.where(i % 2 == 0, p.far_d, p.diag_d))
        )
        s = jnp.where(i < 4, i % 2, (i - 4) // 2)
        return q, s, pl.ds(pl.multiple_of(q * quarter, quarter), quarter)

    def keeps(i):
        _, s, rows = chunk(i)
        return [
            pltpu.make_async_copy(src.at[s, rows], dst.at[s, rows], local.at[k, i])
            for k, (src, dst) in enumerate(((qkv_ref, qkv_out), (normed_ref, normed_out)))
        ]

    @pl.loop(0, m * slots)
    def _(i):
        for k in range(2):

            @pl.when(i == 2 + k)
            def _(k=k):
                token_copy(0, 2 * k).wait_recv()
                token_copy(0, 2 * k + 1).wait_recv()

            @pl.when(i == 5 + 2 * k)
            def _(k=k):
                token_copy(2, 2 * k).wait_recv()
                token_copy(2, 2 * k + 1).wait_recv()

        pl.when(i == 2)(lambda: out.step(1))
        pl.when(i == 4)(lambda: pass_on(3))

        q, s, rows = chunk(i)
        normal, _ = norm_rows(tall_ref[q, s].astype(F32))
        shift = mod_ref[s, :, :width]
        scale = mod_ref[s, :, width : 2 * width]
        normed = (normal * (gain * (1.0 + scale)) + shift).astype(BF16)
        normed_ref[s, rows, :] = normed
        got = mm(normed, wqkvt_ref[...], NT)
        cosine = cos_ref[rows, :]
        sine = sin_ref[rows, :]
        lanes = iota((quarter, 128), 1)
        for t in range(0, 2 * part, 128):
            piece = got[:, t : t + 128]
            piece = piece * cosine + turned(piece) * sine
            piece = jnp.where(lanes + t < part, piece * (1.0 / math.sqrt(HEAD)), piece)
            qkv_ref[s, rows, t : t + 128] = piece.astype(BF16)
        qkv_ref[s, rows, 2 * part :] = got[:, 2 * part :].astype(BF16)
        for keep in keeps(i):
            keep.start()

    def att_copy(kind, s):
        return push(
            att_v.at[s, ranks[kind]], arecv.at[s, p.d], as_.at[kind, s], ar.at[kind, s], peers[kind]
        )

    for k in range(2, p.lines):
        out.step(k)
    up.step(1)
    tiles = length // tile

    @pl.loop(0, slots * tiles)
    def _(i):
        s = i // tiles
        rows = pl.ds(pl.multiple_of(i % tiles * tile, tile), tile)
        same = as_column(seg_ref[pl.ds(s, 1), :]) == seg_ref[pl.ds(s, 1), rows]
        ones = jnp.ones((length, HEAD), BF16)
        for h in range(heads):
            at = h * HEAD
            q = qkv_ref[s, rows, at : at + HEAD]
            k = qkv_ref[s, :, part + at : part + at + HEAD]
            v = qkv_ref[s, :, 2 * part + at : 2 * part + at + HEAD]
            scores = jnp.where(same, mm(k, q, NT), MASKED)
            largest = jnp.max(scores, axis=0, keepdims=True)
            weights = jnp.exp(scores - largest)
            log_v[s, h : h + 1, rows] = largest + jnp.log(jnp.sum(weights, axis=0, keepdims=True))
            result = mm(weights.astype(BF16), jnp.concatenate([v, ones], axis=1), TN)
            result = (result[:, :HEAD] / result[:, HEAD : HEAD + 1]).astype(BF16)
            for j in range(tile // half):
                att_v[s, i % tiles * (tile // quarter) + j // 2, :, j % 2 * part + at : j % 2 * part + at + HEAD] = (
                    result[j * half : (j + 1) * half]
                )
        for k in range(2, p.lines):
            pl.when(i == k - 2)(lambda k=k: up.step(k))
        for k in range(slots):

            @pl.when(i == (k + 1) * tiles - 1)
            def _(k=k):
                for kind in (2, 1, 0):
                    att_copy(kind, k).start()

    for k in range(slots * tiles + 2, p.lines):
        up.step(k)
    stores = [
        pltpu.make_async_copy(src, dst, local.at[2, 1 + k])
        for k, (src, dst) in enumerate(
            (
                (att_v, att_out),
                (log_v, log_out),
                (obuf, wout_out),
                (ubuf, up_out),
                (cotfar_v, cotfar_out),
                (arecv, own_out),
            )
        )
    ]
    for k in range(2):
        stores[k].start()
    for s in range(slots):
        arecv[s, p.d] = att_v[s, p.d]
    out.finish()
    if halves == 2:

        def swap(h):
            return push(obuf.at[:, h], obuf.at[:, h], os_.at[0], or_.at[0], p.sib)

        swap(p.c).start()
        swap(1 - p.c).wait_recv()
    stores[2].start()
    up.finish()
    stores[3].start()
    for s in range(slots):
        cot_copy(s).wait_recv()
    stores[4].start()
    for s in range(slots):
        for kind in range(3):
            att_copy(kind, s).wait_recv()
    stores[5].start()

    for i in range(1, n):
        vec_copy(i).wait_send()
        mod_copy(i).wait_send()
    for item in (qry, out, up):
        item.drain()
    if halves == 2:
        swap(p.c).wait_send()
    for k in range(2 * slots):
        for kind in range(3):
            token_copy(kind, k).wait_send()
    for s in range(slots):
        cot_copy(s).wait_send()
        for kind in range(3):
            att_copy(kind, s).wait_send()

    @pl.loop(0, m * slots)
    def _(i):
        for keep in keeps(i):
            keep.wait()

    for copy in stores:
        copy.wait()


def front(n, m, length, tile, most, args):
    tokens, cond = args[0], args[2]
    w_ada, b_up, w_up = args[4], args[6], args[12]
    slots, quarter, width = tokens.shape
    part = width // m
    lines = n // 2
    dma = pltpu.SemaphoreType.DMA
    shape = jax.ShapeDtypeStruct
    vmem = pltpu.VMEM
    hidden_per = b_up.shape[1] // m
    small = width // n
    block = round16(small)
    pad = round16(hidden_per)
    halves = 2 if block % 32 == 0 else 1
    rows = (slots, quarter, width)
    att = (slots, m, quarter // 2, 2 * part)
    return pl.pallas_call(
        functools.partial(front_kernel, n, m, (hidden_per, small), tile),
        out_shape=(
            shape((slots, length, 3 * part), BF16),
            shape((slots, length, width), BF16),
            shape(att, BF16),
            shape(att, BF16),
            shape((slots, 8, length), F32),
            shape(rows, BF16),
            shape((n, halves, block // halves, width), BF16),
            shape((n, pad, width), BF16),
            shape((slots, 1, 6 * width), F32),
            shape((8, max(width, n * pad)), F32),
            shape((3 * part, width), BF16),
            shape((n, 16, width), BF16),
        ),
        in_specs=[ANY] * 2 + [VM] * (len(args) - 2),
        out_specs=(ANY,) * 8 + (VM,) * 4,
        scratch_shapes=[
            vmem((slots, length, 3 * part), BF16),
            vmem((slots, length, width), BF16),
            vmem((m,) + rows, BF16),
            vmem(att, BF16),
            vmem(att, BF16),
            vmem((slots, 8, length), F32),
            vmem(rows, BF16),
            vmem((n, 8, w_ada.shape[0]), F32),
            vmem((n, 8, w_ada.shape[0]), F32),
            vmem((16, width), BF16),
            vmem((n, 16, width), BF16),
            vmem((most, width), BF16),
            vmem((n, most, width), BF16),
            vmem((block, width), BF16),
            vmem((n, halves, block // halves, width), BF16),
            vmem((pad, width), BF16),
            vmem((n, pad, width), BF16),
            dma((n,)),
            dma((n,)),
            dma((n,)),
            dma((n,)),
            dma((3, 2, 4, 2, lines)),
            dma((3, 2 * slots)),
            dma((3, 2 * slots)),
            dma((1,)),
            dma((1,)),
            dma((3, slots)),
            dma((3, slots)),
            dma((slots,)),
            dma((slots,)),
            dma((3, m * slots)),
        ],
        compiler_params=pltpu.CompilerParams(
            collective_id=1, has_side_effects=True, vmem_limit_bytes=LIMIT
        ),
        name="front",
    )(*args)


def middle_kernel(
    n,
    m,
    tok_ref,
    cot_ref,
    cotfar_ref,
    att_ref,
    wout_ref,
    up_ref,
    mod_ref,
    vec_ref,
    wdown_ref,
    gm_out,
    base_out,
    xsend_out,
    gatt_out,
    dwu_out,
    downtotal_out,
    outsum_out,
    dbup_ref,
    sums_ref,
    tok_v,
    cot_v,
    wout_v,
    arecv,
    own_ref,
    br_ref,
    mid_ref,
    nrm_ref,
    inv_ref,
    nm_ref,
    ct_ref,
    act_ref,
    gp_ref,
    drow,
    ubuf,
    dbuf,
    down_v,
    gsc,
    psend,
    precv,
    xs_ref,
    xr_ref,
    gn_ref,
    bo_ref,
    gba_ref,
    gm_ref,
    xsend_ref,
    gsend,
    grecv,
    dwd_ref,
    dwu_ref,
    dwo_ref,
    oswap,
    side_d,
    total_d,
    n_s,
    n_r,
    c_s,
    c_r,
    gz,
    p_s,
    p_r,
    g_s,
    g_r,
    rz,
    o_s,
    o_r,
    local,
):
    p = Place(n, m)
    slots, quarter, width = tok_ref.shape
    half = quarter // 2
    part = width // m
    small = wdown_ref.shape[0]
    block, inner = drow.shape
    pad = ubuf.shape[1]
    hidden_per = wdown_ref.shape[1] // (n * m)
    peers = (p.sib, p.far, p.diag)
    ranks = (p.sib_d, p.far_d, p.diag_d)

    loads = [
        pltpu.make_async_copy(src, dst, local.at[k])
        for k, (src, dst) in enumerate(
            (
                (att_ref, arecv),
                (wout_ref, wout_v),
                (tok_ref, tok_v),
                (up_ref, ubuf),
                (cot_ref, ct_ref.at[p.d]),
                (cotfar_ref, ct_ref.at[p.far_d]),
                (cot_ref, cot_v),
            )
        )
    ]
    for load in loads:
        load.start()

    def prepare():
        row, lane = iota((wdown_ref.shape[1], inner), 0), iota((1, inner), 1)
        want = jnp.where(
            lane % pad < hidden_per, (lane // pad * m + p.d) * hidden_per + lane % pad, -1
        )
        got = mm(wdown_ref[...], (row == want).astype(BF16), NN).astype(BF16)
        if small < block:
            got = jnp.concatenate([got, jnp.zeros((block - small, inner), BF16)])
        drow[...] = got

    greet(list(peers) + p.line_peers(), prepare)
    down = gather_halves(p, drow, dbuf, gz)
    down.start()

    def cot_copy(kind, s):
        src = cot_ref if kind == 0 else cotfar_ref
        at = p.d if kind == 0 else p.far_d
        return push(src.at[s], ct_ref.at[at, s], c_s.at[kind, s], c_r.at[kind, s], p.sib)

    dbuf[p.f] = drow[...]

    def group(s, k):
        return mod_ref[s, :, k * width : (k + 1) * width]

    gain = vec_ref[2:3, :width]
    b_down = vec_ref[3:4, :width]
    b_up = vec_ref[0:1, :inner]

    def nm_copy(kind, s, h):
        k = s * 2 + h
        at = p.far_d if kind == 2 else p.d
        block = nm_ref.at[at, s, pl.ds(h * half, half)]
        return push(block, block, n_s.at[kind, k], n_r.at[kind, k], p.far if kind == 1 else p.sib)

    for k in range(3):
        loads[k].wait()

    @pl.loop(0, slots)
    def _(s):
        for r in range(m):
            for h in range(2):
                own_ref[s, h * half : (h + 1) * half, r * part : (r + 1) * part] = arecv[
                    s, r, :, h * part : (h + 1) * part
                ]
        branch = mm(own_ref[s], wout_v[...], NT)
        br_ref[s] = branch
        middle = tok_v[s].astype(F32) + group(s, 2) * branch
        mid_ref[s] = middle
        normal, inverse = norm_rows(middle)
        nrm_ref[s] = normal
        inv_ref[s] = inverse
        nm_ref[p.d, s] = (normal * (gain * (1.0 + group(s, 4))) + group(s, 3)).astype(BF16)
        for kind in (1, 0):
            for h in range(2):
                nm_copy(kind, s, h).start()

    def pass_on(s):
        for h in range(2):
            nm_copy(1, s, h).wait_recv()
            nm_copy(2, s, h).start()

    def arrived(kind, s):
        for h in range(2):
            nm_copy(kind, s, h).wait_recv()

    w_up = lambda: ubuf[...].reshape(-1, width)

    def expand(q, s):
        hidden = mm(nm_ref[q, s], w_up(), NT) + b_up
        value, slope = gelu_parts(hidden)
        act_ref[q, s] = value.astype(BF16)
        gp_ref[q, s] = slope.astype(BF16)

    dbup_ref[...] = jnp.zeros_like(dbup_ref)

    def pull(q, s):
        g = (ct_ref[q, s].astype(F32) * group(s, 5)).astype(BF16)
        ct_ref[q, s] = g
        grad = (mm(g, down_v[...], NN) * gp_ref[q, s].astype(F32)).astype(BF16)
        gp_ref[q, s] = grad
        dbup_ref[0:1, :] += jnp.sum(grad.astype(F32), axis=0, keepdims=True)
        gsc[...] = mm(grad, w_up(), NN)

    def part_copy(kind, s):
        if kind == 4:
            return push(xs_ref.at[s], xr_ref.at[s], p_s.at[4, s], p_r.at[4, s], p.far)
        return push(psend.at[kind, s], precv.at[kind, s], p_s.at[kind, s], p_r.at[kind, s], p.sib)

    for k in range(3, 7):
        loads[k].wait()
    for s in range(slots):
        for kind in range(2):
            cot_copy(kind, s).start()

    @pl.loop(0, 2 * slots)
    def _(i):
        s = i % slots
        pl.when(i >= slots)(lambda: arrived(0, s))
        expand(jnp.where(i < slots, p.d, p.sib_d), s)

    down.step(1)
    for s in range(slots):
        for kind in range(2):
            cot_copy(kind, s).wait_recv()
    pass_on(0)
    for t in range(2, p.lines):
        down.step(t)
    down.finish()
    down_v[...] = compact(dbuf[...], small)

    @pl.loop(0, 2 * slots)
    def _(i):
        s = i // 2
        first = i % 2 == 0
        pl.when(first & (s > 0))(lambda: pass_on(s))
        pl.when(first)(lambda: arrived(2, s))
        q = jnp.where(first, p.diag_d, p.far_d)
        expand(q, s)
        pull(q, s)

        @pl.when(first)
        def _():
            psend[0, s] = gsc[...].astype(BF16)
            part_copy(0, s).start()

        @pl.when(jnp.logical_not(first))
        def _():
            part_copy(0, s).wait_recv()
            xs_ref[s] = (gsc[...] + precv[0, s].astype(F32)).astype(BF16)
            part_copy(4, s).start()


    @pl.loop(0, 2 * slots)
    def _(i):
        s = i // 2
        first = i % 2 == 0
        pull(jnp.where(first, p.sib_d, p.d), s)

        @pl.when(first)
        def _():
            psend[1, s] = gsc[...].astype(BF16)
            part_copy(1, s).start()

        @pl.when(jnp.logical_not(first))
        def _():
            gn_ref[s] = gsc[...]

    def weight_grad(left, right, out_ref):
        step = 256

        @pl.loop(0, left.shape[1] // step)
        def _(i):
            at = pl.ds(pl.multiple_of(i * step, step), step)
            out_ref[at, :] = mm(left[:, at], right[...], TN).astype(BF16)

    every = lambda ref: ref.reshape(m * slots * quarter, ref.shape[3])
    weight_grad(every(ct_ref), every(act_ref), dwd_ref.at[:width])
    if small < block:
        dwd_ref[...] = padded(dwd_ref[:width], n, block)
    dwd = dwd_ref.reshape(n, block, inner)
    red_down = Reduce(p, lambda f: dwd.at[f], side_d, total_d, None, rz)
    red_down.start()
    def grad_copy(kind, s):
        return push(
            gsend.at[s, ranks[kind]], grecv.at[s, p.d], g_s.at[kind, s], g_r.at[kind, s], peers[kind]
        )

    def leave(s):
        part_copy(1, s).wait_recv()
        part_copy(4, s).wait_recv()
        cot = cot_v[s].astype(F32)
        gn = gn_ref[s] + precv[1, s].astype(F32) + xr_ref[s].astype(F32)
        normal = nrm_ref[s]
        grad_middle = cot + norm_back(gn, normal, inv_ref[s], gain * (1.0 + group(s, 4)))
        gm_ref[s] = grad_middle
        gba = (grad_middle * group(s, 2)).astype(BF16)
        gba_ref[s] = gba
        gatt = mm(gba, wout_v[...], NN).astype(BF16)
        for r in range(m):
            for h in range(2):
                gsend[s, r, :, h * part : (h + 1) * part] = gatt[
                    h * half : (h + 1) * half, r * part : (r + 1) * part
                ]
        for kind in (2, 1, 0):
            grad_copy(kind, s).start()
        grecv[s, p.d] = gsend[s, p.d]
        total = lambda v: jnp.sum(v, axis=0, keepdims=True)
        sums_ref[s, 0:1, :] = total(gn)
        sums_ref[s, 1:2, :] = total(gn * normal)
        sums_ref[s, 3:4, :] = total(grad_middle * br_ref[s])
        sums_ref[s, 4:5, :] = total((cot * group(s, 5)).astype(BF16).astype(F32))
        sums_ref[s, 5:8, :] = jnp.zeros((3, width), F32)

    leave(0)
    weight_grad(every(gp_ref), every(nm_ref), dwu_ref)

    stores = []

    def store(src, dst):
        stores.append(pltpu.make_async_copy(src, dst, local.at[7 + len(stores)]))
        stores[-1].start()

    store(dwu_ref.reshape(n, pad, width), dwu_out)


    @pl.loop(0, 4 * slots)
    def _(i):
        s = i // 4
        j = i % 4
        q = jnp.where(
            j < 2, jnp.where(j == 0, p.diag_d, p.sib_d), jnp.where(j == 2, p.d, p.far_d)
        )
        gsc[...] = mm(act_ref[q, s], down_v[...], NT)

        @pl.when(j == 0)
        def _():
            psend[2, s] = gsc[...].astype(BF16)
            part_copy(2, s).start()

        @pl.when(j == 1)
        def _():
            psend[3, s] = gsc[...].astype(BF16)
            part_copy(3, s).start()

        @pl.when(j == 2)
        def _():
            bo_ref[s] = gsc[...]

        @pl.when(j == 3)
        def _():
            part_copy(2, s).wait_recv()
            xsend_ref[s] = (gsc[...] + precv[2, s].astype(F32)).astype(BF16)

    store(xsend_ref, xsend_out)
    for s in range(1, slots):
        leave(s)
    store(gm_ref, gm_out)
    flat = lambda ref: ref.reshape(slots * quarter, width)
    weight_grad(flat(gba_ref), flat(own_ref), dwo_ref.at[:width])
    if small < block:
        dwo_ref[...] = padded(dwo_ref[:width], n, block)
    rows = oswap.shape[1]
    dwo = dwo_ref.reshape(n, block // rows, rows, width)
    mine = p.c if rows < block else 0
    theirs = 1 - p.c if rows < block else 0
    swap = push(dwo.at[:, theirs], oswap, o_s.at[0], o_r.at[0], p.sib)
    swap.start()

    @pl.loop(0, slots)
    def _(s):
        part_copy(3, s).wait_recv()
        branch = bo_ref[s] + precv[3, s].astype(F32) + b_down
        mid_ref[s] = mid_ref[s] + group(s, 5) * branch
        sums_ref[s, 2:3, :] = jnp.sum(cot_v[s].astype(F32) * branch, axis=0, keepdims=True)

    store(mid_ref, base_out)
    for j in red_down.order():
        red_down.side_sum(j)
    store(total_d, downtotal_out)
    swap.wait_recv()
    oswap[...] = (dwo[:, mine].astype(F32) + oswap[...].astype(F32)).astype(BF16)
    store(oswap, outsum_out)
    for s in range(slots):
        for kind in range(3):
            grad_copy(kind, s).wait_recv()
    store(grecv, gatt_out)

    down.drain()
    for j in range(p.lines):
        red_down.side_copy(j).wait_send()
    swap.wait_send()
    for s in range(slots):
        for kind in range(3):
            grad_copy(kind, s).wait_send()
            for h in range(2):
                nm_copy(kind, s, h).wait_send()
        for kind in range(2):
            cot_copy(kind, s).wait_send()
        for kind in range(5):
            part_copy(kind, s).wait_send()
    for copy in stores:
        copy.wait()


def padded(rows, count, block):
    per = rows.shape[0] // count
    want = iota((count * block, rows.shape[0]), 0)
    have = iota((count * block, rows.shape[0]), 1)
    chosen = (have == want // block * per + want % block) & (want % block < per)
    return mm(chosen.astype(BF16), rows, NN).astype(BF16)


def middle(n, m, args):
    tokens, att, up_t, w_down = args[0], args[3], args[5], args[8]
    slots, quarter, width = tokens.shape
    dma = pltpu.SemaphoreType.DMA
    shape = jax.ShapeDtypeStruct
    rows = (slots, quarter, width)
    lines = n // 2
    pad = up_t.shape[1]
    block = round16(w_down.shape[0])
    inner = n * pad
    swapped = block // 2 if block % 32 == 0 else block
    vmem = pltpu.VMEM
    return pl.pallas_call(
        functools.partial(middle_kernel, n, m),
        out_shape=(
            shape(rows, F32),
            shape(rows, F32),
            shape(rows, BF16),
            shape(att.shape, BF16),
            shape((n, pad, width), BF16),
            shape((lines, block, inner), BF16),
            shape((n, swapped, width), BF16),
            shape((8, inner), F32),
            shape((slots, 8, width), F32),
        ),
        in_specs=[ANY] * 6 + [VM] * 3,
        out_specs=(ANY,) * 7 + (VM,) * 2,
        scratch_shapes=[
            vmem(rows, BF16),
            vmem(rows, BF16),
            vmem((width, width), BF16),
            vmem(att.shape, BF16),
            vmem(rows, BF16),
            vmem(rows, F32),
            vmem(rows, F32),
            vmem(rows, F32),
            vmem((slots, quarter, 1), F32),
            vmem((m,) + rows, BF16),
            vmem((m,) + rows, BF16),
            vmem((m, slots, quarter, inner), BF16),
            vmem((m, slots, quarter, inner), BF16),
            vmem((block, inner), BF16),
            vmem((n, pad, width), BF16),
            vmem((n, block, inner), BF16),
            vmem((width, inner), BF16),
            vmem((quarter, width), F32),
            vmem((4,) + rows, BF16),
            vmem((4,) + rows, BF16),
            vmem(rows, BF16),
            vmem(rows, BF16),
            vmem(rows, F32),
            vmem(rows, F32),
            vmem(rows, BF16),
            vmem(rows, F32),
            vmem(rows, BF16),
            vmem(att.shape, BF16),
            vmem(att.shape, BF16),
            vmem((n * block, inner), BF16),
            vmem((inner, width), BF16),
            vmem((n * block, width), BF16),
            vmem((n, swapped, width), BF16),
            vmem((lines, block, inner), BF16),
            vmem((lines, block, inner), BF16),
            dma((3, 2 * slots)),
            dma((3, 2 * slots)),
            dma((2, slots)),
            dma((2, slots)),
            dma((2, 4, 2, lines)),
            dma((5, slots)),
            dma((5, slots)),
            dma((3, slots)),
            dma((3, slots)),
            dma((4, 2, lines)),
            dma((1,)),
            dma((1,)),
            dma((16,)),
        ],
        compiler_params=pltpu.CompilerParams(
            collective_id=2, has_side_effects=True, vmem_limit_bytes=LIMIT
        ),
        name="middle",
    )(*args)


def back_kernel(
    n,
    m,
    per,
    tile,
    qkv_ref,
    grad_ref,
    att_ref,
    normed_ref,
    tok_ref,
    gm_ref,
    xsend_ref,
    cot_ref,
    dwu_ref,
    downtotal_ref,
    outsum_ref,
    log_ref,
    seg_ref,
    cos_ref,
    sin_ref,
    wqkvt_ref,
    mod_ref,
    vec_ref,
    sums_ref,
    vblk_ref,
    wada_ref,
    dbup_ref,
    place_ref,
    dtok_out,
    other_out,
    down_out,
    up_out,
    wo_out,
    q_out,
    dcond_ref,
    dwada_ref,
    dbada_ref,
    dvec_ref,
    qkv_v,
    grad_v,
    att_v,
    gq_v,
    dk_ref,
    dv_ref,
    normed_v,
    tok_v,
    gm_v,
    other_v,
    cot_v,
    dtok_v,
    gsc,
    psend,
    precv,
    xs_ref,
    xr_ref,
    gn_ref,
    dwq_ref,
    qblk,
    dwu_v,
    outsum_v,
    total_d,
    zrecv_d,
    side_u,
    total_u,
    zrecv_u,
    side_o,
    total_o,
    zrecv_o,
    side_q,
    total_q,
    zrecv_q,
    spr_d,
    spr_u,
    spr_q,
    opiece,
    ofar,
    ofin,
    ssend,
    srecv,
    gsend,
    grecv,
    vsend,
    vrecv,
    dsend,
    drecv,
    p_s,
    p_r,
    rz,
    d_s,
    d_r,
    s_s,
    s_r,
    g_s,
    g_r,
    v_s,
    v_r,
    c_s,
    c_r,
    x_s,
    x_r,
    local,
):
    p = Place(n, m)
    hidden_per, small = per
    slots, quarter, width = tok_ref.shape
    length = m * quarter
    half = quarter // 2
    part = width // m
    heads = part // HEAD
    lines = p.lines
    peers = (p.sib, p.far, p.diag)
    loads = [
        pltpu.make_async_copy(src, dst, local.at[k])
        for k, (src, dst) in enumerate(
            (
                (qkv_ref, qkv_v),
                (grad_ref, grad_v),
                (att_ref, att_v),
                (downtotal_ref, total_d),
                (dwu_ref, dwu_v),
                (outsum_ref, outsum_v),
                (normed_ref, normed_v),
                (tok_ref, tok_v),
                (gm_ref, gm_v),
                (cot_ref, cot_v),
            )
        )
    ]
    for load in loads:
        load.start()
    greet(list(peers) + p.ring())

    def other_copy(s):
        return push(xsend_ref.at[s], other_v.at[s], x_s.at[s], x_r.at[s], p.far)

    def part_copy(kind, s):
        if kind == 2:
            return push(xs_ref.at[s], xr_ref.at[s], p_s.at[2, s], p_r.at[2, s], p.far)
        return push(psend.at[kind, s], precv.at[kind, s], p_s.at[kind, s], p_r.at[kind, s], p.sib)

    for s in range(slots):
        other_copy(s).start()
    red_d = Reduce(p, None, None, total_d, zrecv_d, rz.at[0], summed=True)
    red_u = Reduce(p, lambda f: dwu_v.at[f], side_u, total_u, zrecv_u, rz.at[1])
    red_o = Reduce(p, lambda f: outsum_v.at[f], side_o, total_o, zrecv_o, rz.at[2])
    red_q = Reduce(p, lambda f: qblk.at[f], side_q, total_q, zrecv_q, rz.at[3])
    down = Spread(p, spr_d, d_s.at[0], d_r.at[0])
    up = Spread(p, spr_u, d_s.at[1], d_r.at[1])
    qry = Spread(p, spr_q, d_s.at[2], d_r.at[2])
    loads[4].wait()
    red_u.start()
    loads[3].wait()
    red_d.step(0)
    for k in (0, 1, 2):
        loads[k].wait()
    tiles = length // tile

    @pl.loop(0, slots)
    def _(s):
        dk_ref[...] = jnp.zeros_like(dk_ref)
        dv_ref[...] = jnp.zeros_like(dv_ref)
        column = as_column(seg_ref[pl.ds(s, 1), :])

        @pl.loop(0, tiles)
        def _(i):
            rows = pl.ds(pl.multiple_of(i * tile, tile), tile)
            same = column == seg_ref[pl.ds(s, 1), rows]
            cosine = cos_ref[rows, :HEAD]
            sine = sin_ref[rows, :HEAD]
            ones = jnp.ones((8, HEAD), BF16)
            for h in range(heads):
                at = h * HEAD
                q = qkv_v[s, rows, at : at + HEAD]
                k = qkv_v[s, :, part + at : part + at + HEAD]
                v = qkv_v[s, :, 2 * part + at : 2 * part + at + HEAD]
                g, o = [
                    jnp.concatenate(
                        [
                            ref[s, i * (tile // quarter) + j // 2, :, j % 2 * part + at : j % 2 * part + at + HEAD]
                            for j in range(tile // half)
                        ]
                    )
                    for ref in (grad_v, att_v)
                ]
                both = g.astype(F32) * o.astype(F32)
                high = both.astype(BF16)
                low = (both - high.astype(F32)).astype(BF16)
                inner = (mm(ones, high, NT) + mm(ones, low, NT))[:1]
                scores = jnp.where(same, mm(k, q, NT), MASKED)
                weights = jnp.exp(scores - log_ref[s, h : h + 1, rows])
                dots = mm(v, g, NT)
                dscores = (weights * (dots - inner)).astype(BF16)
                dq = mm(dscores, k, TN) * (1.0 / math.sqrt(HEAD))
                gq_v[s, rows, at : at + HEAD] = (dq * cosine - swap_halves(dq) * sine).astype(BF16)
                dk_ref[:, at : at + HEAD] += mm(dscores, q, NN)
                dv_ref[:, at : at + HEAD] += mm(weights.astype(BF16), g, NN)

            def reductions(first, red, steps):
                spread = -(-len(steps) // tiles)
                for k, t in enumerate(steps):
                    pl.when((s == first) & (i == k // spread))(lambda t=t: red.step(t))

            reductions(0, red_d, range(1, lines - 1))
            reductions(1, red_u, range(1, lines - 1))

        for h in range(heads):
            at = h * HEAD
            dk = dk_ref[:, at : at + HEAD]
            dk = dk * cos_ref[:, :HEAD] - swap_halves(dk) * sin_ref[:, :HEAD]
            gq_v[s, :, part + at : part + at + HEAD] = dk.astype(BF16)
        gq_v[s, :, 2 * part :] = dv_ref[...].astype(BF16)

        @pl.loop(0, 4)
        def _(j):
            q = jnp.where(
                j < 2, jnp.where(j == 0, p.diag_d, p.far_d), jnp.where(j == 2, p.sib_d, p.d)
            )
            rows = pl.ds(pl.multiple_of(q * quarter, quarter), quarter)
            gsc[...] = mm(gq_v[s, rows, :], wqkvt_ref[...], NN)

            @pl.when(j == 0)
            def _():
                psend[0, s] = gsc[...].astype(BF16)
                part_copy(0, s).start()

            @pl.when(j == 1)
            def _():
                part_copy(0, s).wait_recv()
                xs_ref[s] = (gsc[...] + precv[0, s].astype(F32)).astype(BF16)
                part_copy(2, s).start()

            @pl.when(j == 2)
            def _():
                psend[1, s] = gsc[...].astype(BF16)
                part_copy(1, s).start()

            @pl.when(j == 3)
            def _():
                gn_ref[s] = gsc[...]

        @pl.when(s == 0)
        def _():
            loads[5].wait()
            red_o.start()
            red_d.own(spr_d.at[p.d])
            red_u.step(0)

    loads[6].wait()
    every = slots * length
    gq_all = gq_v.reshape(every, gq_v.shape[2])
    normed_all = normed_v.reshape(every, width)
    whole = gq_v.shape[2] // 128 * 128

    @pl.loop(0, whole // 128)
    def _(i):
        at = pl.ds(pl.multiple_of(i * 128, 128), 128)
        dwq_ref[at, :] = mm(gq_all[:, at], normed_all[...], TN).astype(BF16)

    if whole < gq_v.shape[2]:
        dwq_ref[whole:, :] = mm(gq_all[:, whole:], normed_all[...], TN).astype(BF16)
    count = n * qblk.shape[1]
    placing = (iota((dwq_ref.shape[0], count), 0) == place_ref[pl.ds(p.d, 1), :]).astype(BF16)
    qblk[...] = mm(placing, dwq_ref[...], TN).astype(BF16).reshape(qblk.shape)
    red_q.start()
    down.start()
    red_u.own(spr_u.at[p.d])
    up.start()
    for k in range(lines - 1):
        red_o.step(k)
    red_o.own(opiece)
    halved = ofin.shape[0] == 2
    mine = p.c if halved else 0
    o_far = push(opiece, ofar, d_s.at[3, 0], d_r.at[3, 0], p.far)
    o_far.start()

    def group(s, k):
        return mod_ref[s, :, k * width : (k + 1) * width]

    gain_attn = vec_ref[1:2, :width]
    gain_mlp = vec_ref[2:3, :width]
    wide = dbup_ref.shape[1]
    total_rows = lambda v: jnp.sum(v, axis=0, keepdims=True)
    for k in range(7, 10):
        loads[k].wait()
    ssend[...] = jnp.zeros_like(ssend)

    @pl.loop(0, slots)
    def _(s):
        other_copy(s).wait_recv()
        part_copy(1, s).wait_recv()
        part_copy(2, s).wait_recv()
        gn = gn_ref[s] + precv[1, s].astype(F32) + xr_ref[s].astype(F32)
        normal, inverse = norm_rows(tok_v[s].astype(F32))
        dtok_v[s] = (
            gm_v[s] + norm_back(gn, normal, inverse, gain_attn * (1.0 + group(s, 1)))
        ).astype(BF16)
        extra = total_rows(cot_v[s].astype(F32) * other_v[s].astype(F32))
        ssend[s, 0:1, :width] = total_rows(gn)
        ssend[s, 1:2, :width] = total_rows(gn * normal)
        ssend[s, 2:3, :width] = sums_ref[s, 3:4, :]
        ssend[s, 3:5, :width] = sums_ref[s, 0:2, :]
        ssend[s, 5:6, :width] = sums_ref[s, 2:3, :] + extra
        ssend[s, 6:7, :width] = sums_ref[s, 4:5, :]

    ssend[0, 7:8, :wide] = dbup_ref[0:1, :]

    def sums_copy(kind):
        return push(ssend, srecv.at[p.d], s_s.at[kind], s_r.at[kind], peers[kind])

    for kind in range(3):
        sums_copy(kind).start()
    srecv[p.d] = ssend[...]
    stores = []

    def store(src, dst):
        stores.append(pltpu.make_async_copy(src, dst, local.at[10 + len(stores)]))
        stores[-1].start()

    store(dtok_v, dtok_out)
    store(other_v, other_out)
    red_q.step(0)
    for kind in range(3):
        sums_copy(kind).wait_recv()
    total = srecv[0]
    for r in range(1, m):
        total = total + srecv[r]
    cols = wada_ref.shape[0]
    gmod = []
    vecs = [jnp.zeros((1, width), F32)] * 3
    for s in range(slots):
        at = lambda k, s=s: total[s, k : k + 1, :width]
        gmod.append(
            jnp.concatenate(
                [at(0), at(1) * gain_attn, at(2), at(3), at(4) * gain_mlp, at(5)], axis=1
            )
        )
        vecs = [
            vecs[0] + at(1) * (1.0 + group(s, 1)),
            vecs[1] + at(4) * (1.0 + group(s, 4)),
            vecs[2] + at(6),
        ]
    blank = jnp.zeros((4, 6 * width), F32)
    tail = jnp.zeros((12 - slots, 6 * width), F32)
    gmod = jnp.concatenate([blank] + gmod + [tail], axis=0).astype(BF16)
    vsend[...] = jnp.zeros_like(vsend)
    pad = round16(hidden_per)
    for g in range(n):
        gsend[g] = gmod[:, g * cols : (g + 1) * cols]
        for k, v in enumerate(vecs):
            vsend[g, k : k + 1, :small] = v[:, g * small : (g + 1) * small]
        for r in range(m):
            vsend[g, 3 + r : 4 + r, :hidden_per] = srecv[r, 0, 7:8, g * pad : g * pad + hidden_per]

    def g_copy(i):
        peer = p.ring_f(i)
        return push(gsend.at[peer], grecv.at[p.f], g_s.at[i], g_r.at[i], (peer, p.d))

    def v_copy(i):
        peer = p.ring_f(i)
        return push(vsend.at[peer], vrecv.at[p.f], v_s.at[i], v_r.at[i], (peer, p.d))

    for i in range(1, n):
        g_copy(i).start()
        v_copy(i).start()
    grecv[p.f] = gsend[p.f]
    vrecv[p.f] = vsend[p.f]
    for k in range(1, lines - 1):
        red_q.step(k)
    down.forward()
    up.forward()
    for i in range(1, n):
        g_copy(i).wait_recv()
    got = grecv[...].reshape(n * 16, cols)
    conds = vblk_ref[...].reshape(n * 16, width)[:, : wada_ref.shape[1]]
    dsend[...] = mm(got, wada_ref[...], NN).reshape(n, 16, conds.shape[1])[:, :8]

    def c_copy(i):
        peer = p.ring_f(i)
        return push(dsend.at[peer], drecv.at[p.f], c_s.at[i], c_r.at[i], (peer, p.d))

    for i in range(1, n):
        c_copy(i).start()
    drecv[p.f] = dsend[p.f]
    red_q.own(spr_q.at[p.d])
    qry.start()
    o_far.wait_recv()
    ofin[mine] = (opiece[...].astype(F32) + ofar[...].astype(F32)).astype(BF16)
    if halved:
        o_sib = push(ofin.at[mine], ofin.at[mine], d_s.at[3, 1], d_r.at[3, 1], p.sib)
        o_sib.start()
    dwada_ref[...] = mm(got, conds, TN)
    dbada_ref[...] = jnp.sum(got.astype(F32), axis=0, keepdims=True)
    for i in range(1, n):
        v_copy(i).wait_recv()
    total = vrecv[0]
    for g in range(1, n):
        total = total + vrecv[g]
    dvec_ref[...] = total
    down.finish()
    store(spr_d, down_out)
    up.finish()
    store(spr_u, up_out)
    if halved:
        push(ofin.at[1 - mine], ofin.at[1 - mine], d_s.at[3, 1], d_r.at[3, 1], p.sib).wait_recv()
    store(ofin, wo_out)
    for i in range(1, n):
        c_copy(i).wait_recv()
    total = drecv[0]
    for g in range(1, n):
        total = total + drecv[g]
    dcond_ref[...] = total[4 : 4 + slots]
    qry.forward()
    qry.finish()
    store(spr_q, q_out)

    for s in range(slots):
        other_copy(s).wait_send()
        for kind in range(3):
            part_copy(kind, s).wait_send()
    for red in (red_d, red_u, red_o, red_q):
        red.drain()
    for spread in (down, up, qry):
        spread.drain()
    o_far.wait_send()
    if halved:
        o_sib.wait_send()
    for kind in range(3):
        sums_copy(kind).wait_send()
    for i in range(1, n):
        g_copy(i).wait_send()
        v_copy(i).wait_send()
        c_copy(i).wait_send()
    for copy in stores:
        copy.wait()


def back(n, m, per, tile, args):
    qkv, grad, att, normed, tokens = args[:5]
    dwu, downtotal, outsum = args[8:11]
    vblk, w_ada, dbup, place = args[19:23]
    slots, quarter, width = tokens.shape
    dma = pltpu.SemaphoreType.DMA
    shape = jax.ShapeDtypeStruct
    vmem = pltpu.VMEM
    rows = (slots, quarter, width)
    length = m * quarter
    part = width // m
    lines = n // 2
    wide = max(width, dbup.shape[1])
    _, block, inner = downtotal.shape
    pad = dwu.shape[1]
    orows = outsum.shape[1]
    halves = 2 if orows < block else 1
    most = place.shape[1] // n
    cols, cond = w_ada.shape
    lanes = max(per)

    def reduced(rows, wide):
        return [vmem((lines, rows, wide), BF16)] * 2 + [vmem((lines + 1, rows, wide), BF16)]

    return pl.pallas_call(
        functools.partial(back_kernel, n, m, per, tile),
        out_shape=(
            shape(rows, BF16),
            shape(rows, BF16),
            shape((m, block, inner), BF16),
            shape((m, pad, width), BF16),
            shape((halves, orows, width), BF16),
            shape((m, most, width), BF16),
            shape((slots, cond), F32),
            shape((cols, cond), F32),
            shape((1, cols), F32),
            shape((8, lanes), F32),
        ),
        in_specs=[ANY] * 11 + [VM] * (len(args) - 11),
        out_specs=(ANY,) * 6 + (VM,) * 4,
        scratch_shapes=[
            vmem(qkv.shape, BF16),
            vmem(grad.shape, BF16),
            vmem(att.shape, BF16),
            vmem(qkv.shape, BF16),
            vmem((length, part), F32),
            vmem((length, part), F32),
            vmem(normed.shape, BF16),
            vmem(rows, BF16),
            vmem(rows, F32),
            vmem(rows, BF16),
            vmem(rows, BF16),
            vmem(rows, BF16),
            vmem((quarter, width), F32),
            vmem((2,) + rows, BF16),
            vmem((2,) + rows, BF16),
            vmem(rows, BF16),
            vmem(rows, BF16),
            vmem(rows, F32),
            vmem((qkv.shape[2], width), BF16),
            vmem((n, most, width), BF16),
            vmem(dwu.shape, BF16),
            vmem(outsum.shape, BF16),
        ]
        + reduced(block, inner)[1:]
        + reduced(pad, width)
        + reduced(orows, width)
        + reduced(most, width)
        + [
            vmem((m, block, inner), BF16),
            vmem((m, pad, width), BF16),
            vmem((m, most, width), BF16),
            vmem((orows, width), BF16),
            vmem((orows, width), BF16),
            vmem((halves, orows, width), BF16),
            vmem((slots, 8, wide), F32),
            vmem((m, slots, 8, wide), F32),
            vmem((n, 16, cols), BF16),
            vmem((n, 16, cols), BF16),
            vmem((n, 8, lanes), F32),
            vmem((n, 8, lanes), F32),
            vmem((n, 8, cond), F32),
            vmem((n, 8, cond), F32),
            dma((3, slots)),
            dma((3, slots)),
            dma((4, 4, 2, lines)),
            dma((4, 3)),
            dma((4, 3)),
            dma((3,)),
            dma((3,)),
            dma((n,)),
            dma((n,)),
            dma((n,)),
            dma((n,)),
            dma((n,)),
            dma((n,)),
            dma((slots,)),
            dma((slots,)),
            dma((24,)),
        ],
        compiler_params=pltpu.CompilerParams(
            collective_id=3, has_side_effects=True, vmem_limit_bytes=LIMIT
        ),
        name="back",
    )(*args)


def finish_kernel(
    n,
    m,
    per,
    base_ref,
    other_ref,
    mod_ref,
    dtok_ref,
    dcond_ref,
    dwada_ref,
    dbada_ref,
    dvec_ref,
    down_ref,
    up_ref,
    wo_ref,
    q_ref,
    home_ref,
    out_ref,
    dtok_out,
    dcond_out,
    dwada_out,
    dbada_out,
    dga_out,
    dwqkv_out,
    dwout_out,
    dgm_out,
    dwup_out,
    dbup_out,
    dwdown_out,
    dbdown_out,
):
    hidden_per, small = per
    slots, _, width = base_ref.shape
    pad = round16(hidden_per)
    part = width // m
    for s in range(slots):
        gate = mod_ref[s, :, 5 * width :]
        out_ref[s] = (base_ref[s] + gate * other_ref[s].astype(F32)).astype(BF16)
    dtok_out[...] = dtok_ref[...]
    dcond_out[...] = dcond_ref[...].astype(BF16)
    dwada_out[...] = dwada_ref[...]
    dbada_out[...] = dbada_ref[...]
    for row, ref in ((0, dga_out), (1, dgm_out), (2, dbdown_out)):
        ref[...] = dvec_ref[row : row + 1, :small]
    for r in range(m):
        dbup_out[:, r * hidden_per : (r + 1) * hidden_per] = dvec_ref[3 + r : 4 + r, :hidden_per]
        piece = down_ref[r, :small].astype(F32)
        for g in range(n):
            at = (g * m + r) * hidden_per
            dwdown_out[:, at : at + hidden_per] = piece[:, g * pad : g * pad + hidden_per]
    dwup_out[...] = jnp.concatenate([up_ref[r][:hidden_per] for r in range(m)]).astype(F32).T
    piece = wo_ref[...].reshape(-1, width)[:small].astype(F32)
    heads = part // HEAD
    for r in range(m):
        for h in range(heads):
            at = r * part + h * HEAD
            dwout_out[:, (h * m + r) * HEAD : (h * m + r + 1) * HEAD] = piece[:, at : at + HEAD]
    count = q_ref.shape[0] * q_ref.shape[1]
    f = lax.axis_index("fsdp")
    homing = (iota((dwqkv_out.shape[0], count), 0) == home_ref[pl.ds(f, 1), :]).astype(BF16)
    dwqkv_out[...] = mm(homing, q_ref[...].reshape(count, width), NN)


def finish(n, m, per, columns, args):
    base, dcond, dwada, dbada = args[0], args[4], args[5], args[6]
    hidden_per, small = per
    rows = base.shape
    width = rows[2]
    shape = jax.ShapeDtypeStruct
    return pl.pallas_call(
        functools.partial(finish_kernel, n, m, per),
        out_shape=(
            shape(rows, BF16),
            shape(rows, BF16),
            shape(dcond.shape, BF16),
            shape(dwada.shape, F32),
            shape(dbada.shape, F32),
            shape((1, small), F32),
            shape((columns, width), F32),
            shape((small, width), F32),
            shape((1, small), F32),
            shape((width, m * hidden_per), F32),
            shape((1, m * hidden_per), F32),
            shape((small, n * m * hidden_per), F32),
            shape((1, small), F32),
        ),
        in_specs=[VM] * len(args),
        out_specs=(VM,) * 13,
        compiler_params=pltpu.CompilerParams(vmem_limit_bytes=LIMIT),
        name="finish",
    )(*args)


def column_plan(shards_n, ranks, columns):
    per = columns // shards_n
    rank_of = (np.arange(columns) // HEAD) % ranks
    lists = [
        [[c for c in range(per) if rank_of[f * per + c] == r] for r in range(ranks)]
        for f in range(shards_n)
    ]
    most = max(len(l) for row in lists for l in row)
    most = -(-most // 16) * 16
    take = np.full((shards_n, ranks, most), -1, np.int32)
    place = np.full((ranks, shards_n * most), -1, np.int32)
    home = np.full((shards_n, ranks * most), -1, np.int32)
    for r in range(ranks):
        order = {c: i for i, c in enumerate(np.flatnonzero(rank_of == r))}
        for f in range(shards_n):
            for i, c in enumerate(lists[f][r]):
                take[f, r, i] = c
                place[r, f * most + i] = order[f * per + c]
                home[f, r * most + i] = c
    return most, take, place, home


def shards(
    tokens,
    condition,
    segments,
    w_ada,
    b_ada,
    gain_attn,
    w_qkv,
    w_out,
    gain_mlp,
    w_up,
    b_up,
    w_down,
    b_down,
    cotangent,
):
    slots, quarter, width = tokens.shape
    length = segments.shape[1]
    n = lax.axis_size("fsdp")
    m = lax.axis_size("dp")
    tile = 2 * quarter
    hidden_per = b_up.shape[0] // m
    small = gain_attn.shape[0]
    per = (hidden_per, small)
    columns = w_qkv.shape[1]
    most, take, place, home = column_plan(n, m, columns * n)
    place = jnp.asarray(place)
    cosine, sine = [jnp.asarray(np.concatenate([v, v], axis=1)) for v in rope_table(length)]
    row = lambda v: v[None]

    (
        qkv,
        normed,
        attended,
        own_attended,
        logs,
        cot_far,
        out_blocks,
        up_blocks,
        mod,
        vec,
        w_qkv_t,
        vec_blocks,
    ) = front(
        n,
        m,
        length,
        tile,
        most,
        (
            tokens,
            cotangent,
            condition,
            segments,
            w_ada.T,
            row(b_ada),
            row(b_up),
            row(gain_attn),
            row(gain_mlp),
            row(b_down),
            w_qkv.T,
            w_out.T,
            w_up,
            jnp.asarray(take.reshape(n * m, most)),
            place,
            cosine,
            sine,
        ),
    )
    w_out_t = out_blocks.reshape(n, -1, width)[:, :small].reshape(width, width)
    grad_middle, base, far_part, grad_attended, dw_up, down_total, out_sum, db_up, sums = middle(
        n,
        m,
        (tokens, cotangent, cot_far, own_attended, w_out_t, up_blocks, mod, vec, w_down.T),
    )
    d_tokens, other_part, down_all, up_all, out_all, qkv_all, d_cond, d_w_ada, d_b_ada, d_vec = back(
        n,
        m,
        per,
        tile,
        (
            qkv,
            grad_attended,
            attended,
            normed,
            tokens,
            grad_middle,
            far_part,
            cotangent,
            dw_up,
            down_total,
            out_sum,
            logs,
            segments,
            cosine,
            sine,
            w_qkv_t,
            mod,
            vec,
            sums,
            vec_blocks,
            w_ada.T,
            db_up,
            place,
        ),
    )
    done = finish(
        n,
        m,
        per,
        columns,
        (
            base,
            other_part,
            mod,
            d_tokens,
            d_cond,
            d_w_ada,
            d_b_ada,
            d_vec,
            down_all,
            up_all,
            out_all,
            qkv_all,
            jnp.asarray(home),
        ),
    )
    flat, turned_back = (4, 5, 8, 10, 12), (3, 6, 7, 11)
    return tuple(
        v.reshape(-1) if i in flat else v.T if i in turned_back else v for i, v in enumerate(done)
    )


def solution(mesh):
    return jax.shard_map(
        shards,
        mesh=mesh,
        in_specs=(
            P("fsdp", "dp", None),
            P("fsdp", None),
            P("fsdp", None),
            P(None, "fsdp"),
            P("fsdp"),
            P("fsdp"),
            P(None, "fsdp"),
            P(None, "fsdp"),
            P("fsdp"),
            P(None, "fsdp"),
            P("fsdp"),
            P(None, "fsdp"),
            P("fsdp"),
            P("fsdp", "dp", None),
        ),
        out_specs=(
            P("fsdp", "dp", None),
            P("fsdp", "dp", None),
            P("fsdp", None),
            P(None, "fsdp"),
            P("fsdp"),
            P("fsdp"),
            P(None, "fsdp"),
            P(None, "fsdp"),
            P("fsdp"),
            P(None, "fsdp"),
            P("fsdp"),
            P(None, "fsdp"),
            P("fsdp"),
        ),
        check_vma=False,
    )
```

```python
import functools
import math

import jax
import jax.numpy as jnp
import numpy as np
from jax import lax
from jax.experimental import pallas as pl
from jax.experimental.pallas import tpu as pltpu
from jax.sharding import PartitionSpec as P

HEAD = 64
EPS = 1e-05
ROPE_BASE = 10000.0
MASKED = -1e30
F32 = jnp.float32
BF16 = jnp.bfloat16

NN = (((1,), (0,)), ((), ()))
NT = (((1,), (1,)), ((), ()))
TN = (((0,), (0,)), ((), ()))


def mm(a, b, dims):
    return lax.dot_general(a, b, dims, preferred_element_type=F32)


def rope_table(length):
    inverse = ROPE_BASE ** (-2.0 * np.arange(HEAD // 2) / HEAD)
    angles = np.arange(length)[:, None] * inverse[None, :]
    cosine = np.concatenate([np.cos(angles)] * 2, axis=1)
    sine = np.concatenate([-np.sin(angles), np.sin(angles)], axis=1)
    return cosine.astype(np.float32), sine.astype(np.float32)


def swap_halves(v):
    half = HEAD // 2
    return jnp.concatenate([v[..., half:], v[..., :half]], axis=-1)


MESH = pl.DeviceIdType.MESH
VM = pl.BlockSpec(memory_space=pltpu.VMEM)
ANY = pl.BlockSpec(memory_space=pl.ANY)
LIMIT = 63 << 20


def round16(size):
    return -(-size // 16) * 16


def iota(shape, dim):
    return lax.broadcasted_iota(jnp.int32, shape, dim)


def greet(peers, meanwhile=None):
    barrier = pltpu.get_barrier_semaphore()
    for peer in peers:
        pl.semaphore_signal(barrier, inc=1, device_id=peer, device_id_type=MESH)
    if meanwhile is not None:
        meanwhile()
    pl.semaphore_wait(barrier, len(peers))


def push(src, dst, send, recv, peer):
    return pltpu.make_async_remote_copy(
        src_ref=src,
        dst_ref=dst,
        send_sem=send,
        recv_sem=recv,
        device_id=peer,
        device_id_type=MESH,
    )


class Place:
    def __init__(self, n, m):
        self.n, self.m = n, m
        self.f = lax.axis_index("fsdp")
        self.d = lax.axis_index("dp")
        self.lines = n // 2
        self.a = self.f // 2
        self.b = self.f % 2
        self.x = self.d // 2
        self.c = self.d % 2
        self.sib_d = self.x * 2 + 1 - self.c
        self.far_d = (1 - self.x) * 2 + self.c
        self.diag_d = (1 - self.x) * 2 + 1 - self.c
        self.sib = (self.f, self.sib_d)
        self.far = (self.f, self.far_d)
        self.diag = (self.f, self.diag_d)
        self.side = (self.a * 2 + 1 - self.b, self.d)
        last = self.lines - 1
        self.right = (jnp.minimum(self.a + 1, last) * 2 + self.b, self.d)
        self.left = (jnp.maximum(self.a - 1, 0) * 2 + self.b, self.d)
        self.has_right = self.a < last
        self.has_left = self.a > 0

    def ring_f(self, step):
        return (self.f + step + self.n) % self.n

    def ring(self):
        return [(self.ring_f(i), self.d) for i in range(1, self.n)]

    def line_peers(self):
        return [((self.a + i) % self.lines * 2 + self.b, self.d) for i in range(1, self.lines)] + [
            self.side
        ]


class Gather:
    def __init__(self, p, src, slot, sems):
        self.p, self.src, self.slot, self.sems = p, src, slot, sems

    def place(self, way, t):
        return jnp.clip(self.p.a + (t if way else -t), 0, self.p.lines - 1)

    def line_copy(self, way, t):
        p, j = self.p, self.place(way, t)
        block = self.slot(j * 2 + p.b)
        leave = 4 * p.lines if way and t == 0 else p.lines + j
        return push(
            self.src if t == 0 else block,
            block,
            self.sems.at[leave],
            self.sems.at[j],
            p.left if way else p.right,
        )

    def side_copy(self, way, t, theirs=False):
        p, j = self.p, self.place(way, t)
        block = self.slot(j * 2 + (1 - p.b if theirs else p.b))
        return push(
            self.src if t == 0 else block,
            block,
            self.sems.at[2 * p.lines + j],
            self.sems.at[3 * p.lines + j],
            p.side,
        )

    def held(self, way, t):
        p = self.p
        return p.a + t < p.lines if way else p.a - t >= 0

    def onward(self, way):
        return self.p.has_left if way else self.p.has_right

    def start(self):
        for way in range(2):
            pl.when(self.onward(way))(lambda way=way: self.line_copy(way, 0).start())
        self.side_copy(0, 0).start()

    def step(self, t):
        for way in range(2):

            @pl.when(self.held(way, t))
            def _(way=way):
                self.line_copy(way, t).wait_recv()
                if t < self.p.lines - 1:
                    pl.when(self.onward(way))(lambda: self.line_copy(way, t).start())
                self.side_copy(way, t).start()

    def finish(self):
        self.side_copy(0, 0, True).wait_recv()
        for t in range(1, self.p.lines):
            for way in range(2):
                pl.when(self.held(way, t))(
                    lambda way=way, t=t: self.side_copy(way, t, True).wait_recv()
                )

    def drain(self):
        self.side_copy(0, 0).wait_send()
        for way in range(2):
            pl.when(self.onward(way))(lambda way=way: self.line_copy(way, 0).wait_send())
        for t in range(1, self.p.lines):
            for way in range(2):

                @pl.when(self.held(way, t))
                def _(way=way, t=t):
                    if t < self.p.lines - 1:
                        pl.when(self.onward(way))(lambda: self.line_copy(way, t).wait_send())
                    self.side_copy(way, t).wait_send()


class Both:
    def __init__(self, *gathers):
        self.gathers = gathers

    def start(self):
        for g in self.gathers:
            g.start()

    def step(self, t):
        for g in self.gathers:
            g.step(t)

    def finish(self):
        for g in self.gathers:
            g.finish()

    def drain(self):
        for g in self.gathers:
            g.drain()


def gather_halves(p, src, buf, sems, first):
    rows = src.shape[0]
    if rows % 32:
        return Gather(p, src, lambda f: buf.at[f], sems.at[first])
    cut = [pl.ds(h * rows // 2, rows // 2) for h in range(2)]
    return Both(
        *[
            Gather(p, src.at[cut[h]], lambda f, h=h: buf.at[f, cut[h]], sems.at[first + h])
            for h in range(2)
        ]
    )


class Reduce:
    def __init__(self, p, src, side, total, zrecv, sems, summed=False):
        self.p, self.src, self.side, self.total = p, src, side, total
        self.zrecv, self.sems, self.summed = zrecv, sems, summed

    def order(self):
        lines = self.p.lines
        return [j for k in range(lines // 2) for j in (lines - 1 - k, k)]

    def side_copy(self, j):
        p = self.p
        return push(
            self.src(2 * j + 1 - p.b), self.side.at[j], self.sems.at[j], self.sems.at[p.lines + j], p.side
        )

    def line_copy(self, way, j):
        p = self.p
        at = jnp.where(j == p.a - 1, p.lines, j) if way else j
        return push(
            self.total.at[j],
            self.zrecv.at[at],
            self.sems.at[2 * p.lines + j],
            self.sems.at[3 * p.lines + at],
            p.left if way else p.right,
        )

    def line_wait(self, way, j):
        p = self.p
        at = jnp.where(j == p.a, p.lines, j) if way else j
        block = self.zrecv.at[at]
        push(
            block,
            block,
            self.sems.at[2 * p.lines + j],
            self.sems.at[3 * p.lines + at],
            p.left if way else p.right,
        ).wait_recv()
        return block[...].astype(F32)

    def start(self):
        for j in self.order():
            self.side_copy(j).start()

    def side_sum(self, j):
        p = self.p
        self.side_copy(j).wait_recv()
        mine = self.src(2 * j + p.b)[...].astype(F32)
        self.total[j] = (mine + self.side[j].astype(F32)).astype(BF16)

    def step(self, t):
        p = self.p
        if 2 * t < p.lines and not self.summed:
            for j in self.order()[2 * t : 2 * t + 2]:
                self.side_sum(j)
        for way in range(2):
            j = t - (p.lines - 1 - p.a) if way else p.lines - 1 - (t - p.a)
            ahead = (j >= 0) & (j < p.a) if way else (j < p.lines) & (j > p.a)
            behind = p.has_right if way else p.has_left

            @pl.when(ahead)
            def _(way=way, j=j, behind=behind):
                @pl.when(behind)
                def _():
                    arrived = self.line_wait(way, j)
                    self.total[j] = (self.total[j].astype(F32) + arrived).astype(BF16)

                self.line_copy(way, j).start()

    def own(self, out):
        p = self.p
        for way in range(2):

            @pl.when(p.has_right if way else p.has_left)
            def _(way=way):
                arrived = self.line_wait(way, p.a)
                self.total[p.a] = (self.total[p.a].astype(F32) + arrived).astype(BF16)

        out[...] = self.total[p.a]

    def drain(self):
        p = self.p
        for j in range(p.lines):
            if not self.summed:
                self.side_copy(j).wait_send()
            for way in range(2):
                ahead = p.a > j if way else p.a < j
                pl.when(ahead)(lambda way=way, j=j: self.line_copy(way, j).wait_send())


class Exchange:
    def __init__(self, p, src, buf, send, recv):
        self.p, self.src, self.buf, self.send, self.recv = p, src, buf, send, recv

    def start(self):
        p = self.p
        for i in range(1, p.n):
            peer = p.ring_f(i)
            push(self.src(peer), self.buf.at[p.f], self.send, self.recv, (peer, p.d)).start()

    def every(self):
        some = self.buf.at[pl.ds(0, self.p.n - 1)]
        return push(some, some, self.send, self.recv, self.p.side)

    def finish(self):
        self.every().wait_recv()

    def drain(self):
        self.every().wait_send()


class Spread:
    def __init__(self, p, slot, send, recv):
        self.p, self.slot, self.send, self.recv = p, slot, send, recv

    def copy(self, kind):
        p = self.p
        block = self.slot(p.far_d if kind == 2 else p.d)
        return push(block, block, self.send.at[kind], self.recv.at[kind], p.far if kind == 1 else p.sib)

    def start(self):
        self.copy(1).start()
        self.copy(0).start()

    def forward(self):
        self.copy(1).wait_recv()
        self.copy(2).start()

    def finish(self):
        self.copy(0).wait_recv()
        self.copy(2).wait_recv()

    def drain(self):
        for kind in range(3):
            self.copy(kind).wait_send()


def norm_rows(stream):
    average = jnp.mean(stream, axis=-1, keepdims=True)
    centered = stream - average
    variance = jnp.mean(centered * centered, axis=-1, keepdims=True)
    inverse = lax.rsqrt(variance + EPS)
    return centered * inverse, inverse


def norm_back(grad, normal, inverse, factor):
    e = grad * factor
    mean_e = jnp.mean(e, axis=-1, keepdims=True)
    mean_en = jnp.mean(e * normal, axis=-1, keepdims=True)
    return inverse * (e - mean_e - normal * mean_en)


def turned(v):
    lanes = iota(v.shape, 1)
    half = HEAD // 2
    return jnp.where(lanes % HEAD < half, pltpu.roll(v, 128 - half, 1), pltpu.roll(v, half, 1))


def gelu_parts(h):
    root = math.sqrt(2.0 / math.pi)
    square = h * h
    t = jnp.tanh(root * h * (1.0 + 0.044715 * square))
    half = 0.5 * (1.0 + t)
    slope = half + 0.5 * h * (1.0 - t * t) * (root * (1.0 + 3.0 * 0.044715 * square))
    return h * half, slope


def compact(blocks, per):
    count, rows, lanes = blocks.shape
    flat = blocks.reshape(count * rows, lanes)
    if rows == per:
        return flat
    want = iota((count * per, count * rows), 0)
    have = iota((count * per, count * rows), 1)
    chosen = (have == want // per * rows + want % per).astype(BF16)
    return mm(chosen, flat, NN).astype(BF16)


def as_column(row):
    size = row.shape[1]
    return jnp.transpose(jnp.broadcast_to(row, (128, size)))[:, :1]


def front_kernel(
    n,
    m,
    per,
    tile,
    tok_ref,
    cot_ref,
    cond_ref,
    seg_ref,
    wada_ref,
    bada_ref,
    bup_ref,
    ga_ref,
    gm_ref,
    bdown_ref,
    wqkv_ref,
    wout_ref,
    wup_ref,
    take_ref,
    place_ref,
    cos_ref,
    sin_ref,
    qkv_out,
    normed_out,
    att_out,
    own_out,
    log_out,
    cotfar_out,
    wout_out,
    up_out,
    mod_ref,
    vecs_ref,
    wqkvt_ref,
    vec_out,
    qkv_ref,
    normed_ref,
    tall_ref,
    att_v,
    arecv,
    log_v,
    cotfar_v,
    mod_send,
    mod_recv,
    vsrc,
    vbuf,
    qsrc,
    qbuf,
    osrc,
    obuf,
    usrc,
    ubuf,
    ex,
    gz,
    ts,
    tr,
    os_,
    or_,
    as_,
    ar,
    cs,
    cr,
    local,
):
    p = Place(n, m)
    slots, quarter, width = tok_ref.shape
    half = quarter // 2
    part = width // m
    heads = part // HEAD
    hidden_per, small = per
    pad = round16(hidden_per)
    halves = obuf.shape[1]
    length = m * quarter
    peers = (p.sib, p.far, p.diag)
    ranks = (p.sib_d, p.far_d, p.diag_d)
    own_tokens = pltpu.make_async_copy(tok_ref, tall_ref.at[p.d], local.at[2])
    own_tokens.start()
    log_v[...] = jnp.zeros_like(log_v)

    def prepare():
        vsrc[...] = jnp.zeros_like(vsrc)
        for row, ref in enumerate((ga_ref, gm_ref, bdown_ref)):
            vsrc[row : row + 1, : ref.shape[0]] = ref[...].reshape(1, -1)
        vsrc[4 : 4 + slots, :] = cond_ref[...]
        b_up = bup_ref[...].reshape(1, -1)
        for k in range(0, b_up.shape[1], 128):
            some = b_up[:, k : k + 128]
            vsrc[8 + k // 128 : 9 + k // 128, : some.shape[1]] = some
        columns = wqkv_ref.shape[0]
        most = qsrc.shape[0]
        taking = take_ref[pl.ds(p.f * m + p.d, 1), :]
        chosen = (iota((columns, most), 0) == taking).astype(BF16)
        qsrc[...] = mm(chosen, wqkv_ref[...], TN).astype(BF16)

    greet(list(peers) + p.ring(), prepare)

    vec = Exchange(p, lambda f: vsrc, vbuf, ex.at[0], ex.at[1])
    vec.start()

    def token_copy(kind, k):
        s, rows = k // 2, pl.ds(k % 2 * half, half)
        if kind == 2:
            block = tall_ref.at[p.far_d, s, rows]
            return push(block, block, ts.at[kind, k], tr.at[kind, k], p.sib)
        return push(
            tok_ref.at[s, rows],
            tall_ref.at[p.d, s, rows],
            ts.at[kind, k],
            tr.at[kind, k],
            p.sib if kind == 0 else p.far,
        )

    qry = gather_halves(p, qsrc, qbuf, gz, 0)
    qry.start()
    for k in range(2 * slots):
        token_copy(1, k).start()
    for k in range(2 * slots):
        token_copy(0, k).start()
    vbuf[p.f] = vsrc[...]
    qbuf[p.f] = qsrc[...]

    lane = iota((1, width), 1)
    rank, inner = lane // part, lane % part
    want = (inner // HEAD * m + rank) * HEAD + inner % HEAD
    chosen = (iota((width, width), 0) == want).astype(BF16)
    got = mm(wout_ref[...], chosen, NN).astype(BF16)
    if small < osrc.shape[0]:
        got = jnp.concatenate([got, jnp.zeros((osrc.shape[0] - small, width), BF16)])
    osrc[...] = got
    split = osrc.shape[0] // halves
    mine = p.c if halves == 2 else 0
    out = Gather(
        p,
        osrc.at[pl.ds(pl.multiple_of(mine * split, 16), split)],
        lambda f: obuf.at[f, mine],
        gz.at[2],
    )
    for h in range(halves):
        obuf[p.f, h] = osrc[h * split : (h + 1) * split]

    ups = wup_ref.shape[1]
    at, lane = iota((pad, ups), 0), iota((pad, ups), 1)
    chosen = ((lane == at + p.d * hidden_per) & (at < hidden_per)).astype(BF16)
    usrc[...] = mm(chosen, wup_ref[...], NT).astype(BF16)
    ubuf[p.f] = usrc[...]
    up = Gather(p, usrc, lambda f: ubuf.at[f], gz.at[3])

    def pass_on(k):
        token_copy(1, k).wait_recv()
        token_copy(2, k).start()

    qry.step(1)
    vec.finish()
    vecs = vbuf[...].reshape(n * 16, 128)
    mod_cols = mm(vecs, wada_ref[...], NT) + bada_ref[...].reshape(1, -1).astype(F32)
    mod_send[...] = mod_cols.reshape(n, 16, mod_cols.shape[1])[:, 4 : 4 + slots]
    mod_recv[p.f] = mod_send[p.f]

    mods = Exchange(p, lambda f: mod_send.at[f], mod_recv, ex.at[2], ex.at[3])
    mods.start()
    vec_out[...] = vbuf[...]
    vecs_ref[...] = jnp.zeros_like(vecs_ref)
    ups = bup_ref.shape[0]
    b_up = jnp.zeros((n * 16, pad), F32)
    for k in range(0, ups, 128):
        lane = iota((128, pad), 1)
        chosen = (iota((128, pad), 0) + k == lane + p.d * hidden_per) & (lane < hidden_per)
        some = mm(vecs, chosen.astype(BF16), NN)
        b_up = b_up + jnp.where(iota((n * 16, pad), 0) % 16 == 8 + k // 128, some, 0.0)
    for g in range(n):
        vecs_ref[0:1, g * pad : (g + 1) * pad] = jnp.sum(
            b_up[16 * g : 16 * (g + 1)], axis=0, keepdims=True
        )
        rest = vecs[16 * g : 16 * g + 8].astype(F32)
        for k in range(3):
            vecs_ref[k + 1 : k + 2, g * small : (g + 1) * small] = rest[k : k + 1, :small]
    for k in range(2, p.lines - 1):
        qry.step(k)
    pass_on(0)
    qry.step(p.lines - 1)
    out.start()
    mods.finish()
    cols = mod_cols.shape[1]
    for g in range(n):
        for s in range(slots):
            mod_ref[s, :, g * cols : (g + 1) * cols] = mod_recv[g, s : s + 1]
    gain = vecs_ref[1:2, :width]

    pass_on(1)
    pass_on(2)
    def cot_copy(s):
        return push(cot_ref.at[s], cotfar_v.at[s], cs.at[s], cr.at[s], p.far)

    for s in range(slots):
        cot_copy(s).start()

    qry.finish()
    up.start()
    count = n * qsrc.shape[0]
    placing = (iota((3 * part, count), 0) == place_ref[pl.ds(p.d, 1), :]).astype(BF16)
    wqkvt_ref[...] = mm(placing, qbuf[...].reshape(count, width), NN).astype(BF16)
    own_tokens.wait()

    def chunk(i):
        q = jnp.where(
            i < 2, p.d, jnp.where(i < 4, p.sib_d, jnp.where(i % 2 == 0, p.far_d, p.diag_d))
        )
        s = jnp.where(i < 4, i % 2, (i - 4) // 2)
        return q, s, pl.ds(pl.multiple_of(q * quarter, quarter), quarter)

    def keeps(i):
        _, s, rows = chunk(i)
        return [
            pltpu.make_async_copy(src.at[s, rows], dst.at[s, rows], local.at[k])
            for k, (src, dst) in enumerate(((qkv_ref, qkv_out), (normed_ref, normed_out)))
        ]

    @pl.loop(0, m * slots)
    def _(i):
        for k in range(2):

            @pl.when(i == 2 + k)
            def _(k=k):
                token_copy(0, 2 * k).wait_recv()
                token_copy(0, 2 * k + 1).wait_recv()

            @pl.when(i == 5 + 2 * k)
            def _(k=k):
                token_copy(2, 2 * k).wait_recv()
                token_copy(2, 2 * k + 1).wait_recv()

        pl.when(i == 2)(lambda: out.step(1))
        pl.when(i == 4)(lambda: pass_on(3))

        q, s, rows = chunk(i)
        normal, _ = norm_rows(tall_ref[q, s].astype(F32))
        shift = mod_ref[s, :, :width]
        scale = mod_ref[s, :, width : 2 * width]
        normed = (normal * (gain * (1.0 + scale)) + shift).astype(BF16)
        normed_ref[s, rows, :] = normed
        got = mm(normed, wqkvt_ref[...], NT)
        cosine = cos_ref[rows, :]
        sine = sin_ref[rows, :]
        lanes = iota((quarter, 128), 1)
        for t in range(0, 2 * part, 128):
            piece = got[:, t : t + 128]
            piece = piece * cosine + turned(piece) * sine
            piece = jnp.where(lanes + t < part, piece * (1.0 / math.sqrt(HEAD)), piece)
            qkv_ref[s, rows, t : t + 128] = piece.astype(BF16)
        qkv_ref[s, rows, 2 * part :] = got[:, 2 * part :].astype(BF16)
        for keep in keeps(i):
            keep.start()

    def att_copy(kind, s):
        return push(
            att_v.at[s, ranks[kind]], arecv.at[s, p.d], as_.at[kind, s], ar.at[kind, s], peers[kind]
        )

    for k in range(2, p.lines):
        out.step(k)
    up.step(1)
    tiles = length // tile

    @pl.loop(0, slots * tiles)
    def _(i):
        s = i // tiles
        rows = pl.ds(pl.multiple_of(i % tiles * tile, tile), tile)
        same = as_column(seg_ref[pl.ds(s, 1), :]) == seg_ref[pl.ds(s, 1), rows]
        ones = jnp.ones((length, HEAD), BF16)
        for h in range(heads):
            at = h * HEAD
            q = qkv_ref[s, rows, at : at + HEAD]
            k = qkv_ref[s, :, part + at : part + at + HEAD]
            v = qkv_ref[s, :, 2 * part + at : 2 * part + at + HEAD]
            scores = jnp.where(same, mm(k, q, NT), MASKED)
            largest = jnp.max(scores, axis=0, keepdims=True)
            weights = jnp.exp(scores - largest)
            log_v[s, h : h + 1, rows] = largest + jnp.log(jnp.sum(weights, axis=0, keepdims=True))
            result = mm(weights.astype(BF16), jnp.concatenate([v, ones], axis=1), TN)
            result = (result[:, :HEAD] / result[:, HEAD : HEAD + 1]).astype(BF16)
            for j in range(tile // half):
                att_v[s, i % tiles * (tile // quarter) + j // 2, :, j % 2 * part + at : j % 2 * part + at + HEAD] = (
                    result[j * half : (j + 1) * half]
                )
        for k in range(2, p.lines):
            pl.when(i == k - 2)(lambda k=k: up.step(k))
        for k in range(slots):

            @pl.when(i == (k + 1) * tiles - 1)
            def _(k=k):
                for kind in (2, 1, 0):
                    att_copy(kind, k).start()

    for k in range(slots * tiles + 2, p.lines):
        up.step(k)
    stores = [
        pltpu.make_async_copy(src, dst, local.at[3 + k])
        for k, (src, dst) in enumerate(
            (
                (att_v, att_out),
                (log_v, log_out),
                (obuf, wout_out),
                (ubuf, up_out),
                (cotfar_v, cotfar_out),
                (arecv, own_out),
            )
        )
    ]
    for k in range(2):
        stores[k].start()
    for s in range(slots):
        arecv[s, p.d] = att_v[s, p.d]
    out.finish()
    if halves == 2:

        def swap(h):
            return push(obuf.at[:, h], obuf.at[:, h], os_.at[0], or_.at[0], p.sib)

        swap(p.c).start()
        swap(1 - p.c).wait_recv()
    stores[2].start()
    up.finish()
    stores[3].start()
    for s in range(slots):
        cot_copy(s).wait_recv()
    stores[4].start()
    for s in range(slots):
        for kind in range(3):
            att_copy(kind, s).wait_recv()
    stores[5].start()

    vec.drain()
    mods.drain()
    for item in (qry, out, up):
        item.drain()
    if halves == 2:
        swap(p.c).wait_send()
    for k in range(2 * slots):
        for kind in range(3):
            token_copy(kind, k).wait_send()
    for s in range(slots):
        cot_copy(s).wait_send()
        for kind in range(3):
            att_copy(kind, s).wait_send()

    for k, (src, dst) in enumerate(((qkv_ref, qkv_out), (normed_ref, normed_out))):
        pltpu.make_async_copy(src, dst, local.at[k]).wait()

    for copy in stores:
        copy.wait()


def front(n, m, length, tile, most, args):
    tokens, cond = args[0], args[2]
    w_ada, b_up, w_up = args[4], args[6], args[12]
    slots, quarter, width = tokens.shape
    part = width // m
    lines = n // 2
    dma = pltpu.SemaphoreType.DMA
    shape = jax.ShapeDtypeStruct
    vmem = pltpu.VMEM
    hidden_per = b_up.shape[0] // m
    small = width // n
    block = round16(small)
    pad = round16(hidden_per)
    halves = 2 if block % 32 == 0 else 1
    rows = (slots, quarter, width)
    att = (slots, m, quarter // 2, 2 * part)
    return pl.pallas_call(
        functools.partial(front_kernel, n, m, (hidden_per, small), tile),
        out_shape=(
            shape((slots, length, 3 * part), BF16),
            shape((slots, length, width), BF16),
            shape(att, BF16),
            shape(att, BF16),
            shape((slots, 8, length), F32),
            shape(rows, BF16),
            shape((n, halves, block // halves, width), BF16),
            shape((n, pad, width), BF16),
            shape((slots, 1, 6 * width), F32),
            shape((8, max(width, n * pad)), F32),
            shape((3 * part, width), BF16),
            shape((n, 16, 128), BF16),
        ),
        in_specs=[ANY] * 2 + [VM] * (len(args) - 2),
        out_specs=(ANY,) * 8 + (VM,) * 4,
        scratch_shapes=[
            vmem((slots, length, 3 * part), BF16),
            vmem((slots, length, width), BF16),
            vmem((m,) + rows, BF16),
            vmem(att, BF16),
            vmem(att, BF16),
            vmem((slots, 8, length), F32),
            vmem(rows, BF16),
            vmem((n, slots, w_ada.shape[0]), F32),
            vmem((n, slots, w_ada.shape[0]), F32),
            vmem((16, 128), BF16),
            vmem((n, 16, 128), BF16),
            vmem((most, width), BF16),
            vmem((n, most, width), BF16),
            vmem((block, width), BF16),
            vmem((n, halves, block // halves, width), BF16),
            vmem((pad, width), BF16),
            vmem((n, pad, width), BF16),
            dma((4,)),
            dma((4, 4 * lines + 1)),
            dma((3, 2 * slots)),
            dma((3, 2 * slots)),
            dma((1,)),
            dma((1,)),
            dma((3, slots)),
            dma((3, slots)),
            dma((slots,)),
            dma((slots,)),
            dma((9,)),
        ],
        compiler_params=pltpu.CompilerParams(
            collective_id=1, has_side_effects=True, vmem_limit_bytes=LIMIT
        ),
        name="front",
    )(*args)


def middle_kernel(
    n,
    m,
    tok_ref,
    cot_ref,
    cotfar_ref,
    att_ref,
    wout_ref,
    up_ref,
    mod_ref,
    vec_ref,
    wdown_ref,
    gm_out,
    base_out,
    xsend_out,
    gatt_out,
    dwu_out,
    downtotal_out,
    outsum_out,
    dbup_ref,
    sums_ref,
    tok_v,
    cot_v,
    wout_v,
    arecv,
    own_ref,
    br_ref,
    mid_ref,
    nrm_ref,
    inv_ref,
    nm_ref,
    ct_ref,
    act_ref,
    gp_ref,
    drow,
    ubuf,
    dbuf,
    down_v,
    gsc,
    psend,
    precv,
    xs_ref,
    xr_ref,
    gn_ref,
    bo_ref,
    gba_ref,
    gm_ref,
    xsend_ref,
    gsend,
    grecv,
    dwd_ref,
    dwu_ref,
    dwo_ref,
    oswap,
    side_d,
    total_d,
    n_s,
    n_r,
    c_s,
    c_r,
    gz,
    p_s,
    p_r,
    g_s,
    g_r,
    rz,
    o_s,
    o_r,
    local,
):
    p = Place(n, m)
    slots, quarter, width = tok_ref.shape
    half = quarter // 2
    part = width // m
    small = wdown_ref.shape[0]
    block, inner = drow.shape
    pad = ubuf.shape[1]
    hidden_per = wdown_ref.shape[1] // (n * m)
    peers = (p.sib, p.far, p.diag)
    ranks = (p.sib_d, p.far_d, p.diag_d)

    loads = [
        pltpu.make_async_copy(src, dst, local.at[k])
        for k, (src, dst) in enumerate(
            (
                (att_ref, arecv),
                (wout_ref, wout_v),
                (tok_ref, tok_v),
                (up_ref, ubuf),
                (cot_ref, ct_ref.at[p.d]),
                (cotfar_ref, ct_ref.at[p.far_d]),
                (cot_ref, cot_v),
            )
        )
    ]
    for load in loads:
        load.start()

    def prepare():
        row, lane = iota((wdown_ref.shape[1], inner), 0), iota((1, inner), 1)
        want = jnp.where(
            lane % pad < hidden_per, (lane // pad * m + p.d) * hidden_per + lane % pad, -1
        )
        got = mm(wdown_ref[...], (row == want).astype(BF16), NN).astype(BF16)
        if small < block:
            got = jnp.concatenate([got, jnp.zeros((block - small, inner), BF16)])
        drow[...] = got

    greet(list(peers) + p.line_peers(), prepare)
    down = gather_halves(p, drow, dbuf, gz, 0)
    down.start()

    def cot_copy(kind, s):
        src = cot_ref if kind == 0 else cotfar_ref
        at = p.d if kind == 0 else p.far_d
        return push(src.at[s], ct_ref.at[at, s], c_s.at[kind, s], c_r.at[kind, s], p.sib)

    dbuf[p.f] = drow[...]

    def group(s, k):
        return mod_ref[s, :, k * width : (k + 1) * width]

    gain = vec_ref[2:3, :width]
    b_down = vec_ref[3:4, :width]
    b_up = vec_ref[0:1, :inner]

    def nm_copy(kind, s, h):
        k = s * 2 + h
        at = p.far_d if kind == 2 else p.d
        block = nm_ref.at[at, s, pl.ds(h * half, half)]
        return push(block, block, n_s.at[kind, k], n_r.at[kind, k], p.far if kind == 1 else p.sib)

    for k in range(3):
        loads[k].wait()

    @pl.loop(0, slots)
    def _(s):
        for r in range(m):
            for h in range(2):
                own_ref[s, h * half : (h + 1) * half, r * part : (r + 1) * part] = arecv[
                    s, r, :, h * part : (h + 1) * part
                ]
        branch = mm(own_ref[s], wout_v[...], NT)
        br_ref[s] = branch
        middle = tok_v[s].astype(F32) + group(s, 2) * branch
        mid_ref[s] = middle
        normal, inverse = norm_rows(middle)
        nrm_ref[s] = normal
        inv_ref[s] = inverse
        nm_ref[p.d, s] = (normal * (gain * (1.0 + group(s, 4))) + group(s, 3)).astype(BF16)
        for kind in (1, 0):
            for h in range(2):
                nm_copy(kind, s, h).start()

    def pass_on(s):
        for h in range(2):
            nm_copy(1, s, h).wait_recv()
            nm_copy(2, s, h).start()

    def arrived(kind, s):
        for h in range(2):
            nm_copy(kind, s, h).wait_recv()

    w_up = lambda: ubuf[...].reshape(-1, width)

    def expand(q, s):
        hidden = mm(nm_ref[q, s], w_up(), NT) + b_up
        value, slope = gelu_parts(hidden)
        act_ref[q, s] = value.astype(BF16)
        gp_ref[q, s] = slope.astype(BF16)

    dbup_ref[...] = jnp.zeros_like(dbup_ref)

    def pull(q, s):
        g = (ct_ref[q, s].astype(F32) * group(s, 5)).astype(BF16)
        ct_ref[q, s] = g
        grad = (mm(g, down_v[...], NN) * gp_ref[q, s].astype(F32)).astype(BF16)
        gp_ref[q, s] = grad
        dbup_ref[0:1, :] += jnp.sum(grad.astype(F32), axis=0, keepdims=True)
        gsc[...] = mm(grad, w_up(), NN)

    def part_copy(kind, s):
        if kind == 4:
            return push(xs_ref.at[s], xr_ref.at[s], p_s.at[4, s], p_r.at[4, s], p.far)
        return push(psend.at[kind, s], precv.at[kind, s], p_s.at[kind, s], p_r.at[kind, s], p.sib)

    for k in range(3, 7):
        loads[k].wait()
    for s in range(slots):
        for kind in range(2):
            cot_copy(kind, s).start()

    @pl.loop(0, 2 * slots)
    def _(i):
        s = i % slots
        pl.when(i >= slots)(lambda: arrived(0, s))
        expand(jnp.where(i < slots, p.d, p.sib_d), s)

    down.step(1)
    for s in range(slots):
        for kind in range(2):
            cot_copy(kind, s).wait_recv()
    pass_on(0)
    for t in range(2, p.lines):
        down.step(t)
    down.finish()
    down_v[...] = compact(dbuf[...], small)

    @pl.loop(0, 2 * slots)
    def _(i):
        s = i // 2
        first = i % 2 == 0
        pl.when(first & (s > 0))(lambda: pass_on(s))
        pl.when(first)(lambda: arrived(2, s))
        q = jnp.where(first, p.diag_d, p.far_d)
        expand(q, s)
        pull(q, s)

        @pl.when(first)
        def _():
            psend[0, s] = gsc[...].astype(BF16)
            part_copy(0, s).start()

        @pl.when(jnp.logical_not(first))
        def _():
            part_copy(0, s).wait_recv()
            xs_ref[s] = (gsc[...] + precv[0, s].astype(F32)).astype(BF16)
            part_copy(4, s).start()


    @pl.loop(0, 2 * slots)
    def _(i):
        s = i // 2
        first = i % 2 == 0
        pull(jnp.where(first, p.sib_d, p.d), s)

        @pl.when(first)
        def _():
            psend[1, s] = gsc[...].astype(BF16)
            part_copy(1, s).start()

        @pl.when(jnp.logical_not(first))
        def _():
            gn_ref[s] = gsc[...]

    def weight_grad(left, right, out_ref):
        step = 256

        @pl.loop(0, left.shape[1] // step)
        def _(i):
            at = pl.ds(pl.multiple_of(i * step, step), step)
            out_ref[at, :] = mm(left[:, at], right[...], TN).astype(BF16)

    every = lambda ref: ref.reshape(m * slots * quarter, ref.shape[3])
    weight_grad(every(ct_ref), every(act_ref), dwd_ref.at[:width])
    if small < block:
        dwd_ref[...] = padded(dwd_ref[:width], n, block)
    dwd = dwd_ref.reshape(n, block, inner)
    red_down = Reduce(p, lambda f: dwd.at[f], side_d, total_d, None, rz)
    red_down.start()
    def grad_copy(kind, s):
        return push(
            gsend.at[s, ranks[kind]], grecv.at[s, p.d], g_s.at[kind, s], g_r.at[kind, s], peers[kind]
        )

    def leave(s):
        part_copy(1, s).wait_recv()
        part_copy(4, s).wait_recv()
        cot = cot_v[s].astype(F32)
        gn = gn_ref[s] + precv[1, s].astype(F32) + xr_ref[s].astype(F32)
        normal = nrm_ref[s]
        grad_middle = cot + norm_back(gn, normal, inv_ref[s], gain * (1.0 + group(s, 4)))
        gm_ref[s] = grad_middle
        gba = (grad_middle * group(s, 2)).astype(BF16)
        gba_ref[s] = gba
        gatt = mm(gba, wout_v[...], NN).astype(BF16)
        for r in range(m):
            for h in range(2):
                gsend[s, r, :, h * part : (h + 1) * part] = gatt[
                    h * half : (h + 1) * half, r * part : (r + 1) * part
                ]
        for kind in (2, 1, 0):
            grad_copy(kind, s).start()
        grecv[s, p.d] = gsend[s, p.d]
        total = lambda v: jnp.sum(v, axis=0, keepdims=True)
        sums_ref[s, 0:1, :] = total(gn)
        sums_ref[s, 1:2, :] = total(gn * normal)
        sums_ref[s, 3:4, :] = total(grad_middle * br_ref[s])
        sums_ref[s, 4:5, :] = total((cot * group(s, 5)).astype(BF16).astype(F32))
        sums_ref[s, 5:8, :] = jnp.zeros((3, width), F32)

    leave(0)
    weight_grad(every(gp_ref), every(nm_ref), dwu_ref)

    stores = []

    def store(src, dst):
        stores.append(pltpu.make_async_copy(src, dst, local.at[7 + len(stores)]))
        stores[-1].start()

    store(dwu_ref.reshape(n, pad, width), dwu_out)

    for s in range(1, slots):
        leave(s)

    @pl.loop(0, 4 * slots)
    def _(i):
        s = i // 4
        j = i % 4
        q = jnp.where(
            j < 2, jnp.where(j == 0, p.diag_d, p.sib_d), jnp.where(j == 2, p.d, p.far_d)
        )
        gsc[...] = mm(act_ref[q, s], down_v[...], NT)

        @pl.when(j == 0)
        def _():
            psend[2, s] = gsc[...].astype(BF16)
            part_copy(2, s).start()

        @pl.when(j == 1)
        def _():
            psend[3, s] = gsc[...].astype(BF16)
            part_copy(3, s).start()

        @pl.when(j == 2)
        def _():
            bo_ref[s] = gsc[...]

        @pl.when(j == 3)
        def _():
            part_copy(2, s).wait_recv()
            xsend_ref[s] = (gsc[...] + precv[2, s].astype(F32)).astype(BF16)

    store(xsend_ref, xsend_out)
    store(gm_ref, gm_out)
    flat = lambda ref: ref.reshape(slots * quarter, width)
    weight_grad(flat(gba_ref), flat(own_ref), dwo_ref.at[:width])
    if small < block:
        dwo_ref[...] = padded(dwo_ref[:width], n, block)
    rows = oswap.shape[1]
    dwo = dwo_ref.reshape(n, block // rows, rows, width)
    mine = p.c if rows < block else 0
    theirs = 1 - p.c if rows < block else 0
    swap = push(dwo.at[:, theirs], oswap, o_s.at[0], o_r.at[0], p.sib)
    swap.start()

    @pl.loop(0, slots)
    def _(s):
        part_copy(3, s).wait_recv()
        branch = bo_ref[s] + precv[3, s].astype(F32) + b_down
        mid_ref[s] = mid_ref[s] + group(s, 5) * branch
        sums_ref[s, 2:3, :] = jnp.sum(cot_v[s].astype(F32) * branch, axis=0, keepdims=True)

    store(mid_ref, base_out)
    for j in red_down.order():
        red_down.side_sum(j)
    store(total_d, downtotal_out)
    swap.wait_recv()
    oswap[...] = (dwo[:, mine].astype(F32) + oswap[...].astype(F32)).astype(BF16)
    store(oswap, outsum_out)
    for s in range(slots):
        for kind in range(3):
            grad_copy(kind, s).wait_recv()
    store(grecv, gatt_out)

    down.drain()
    for j in range(p.lines):
        red_down.side_copy(j).wait_send()
    swap.wait_send()
    for s in range(slots):
        for kind in range(3):
            grad_copy(kind, s).wait_send()
            for h in range(2):
                nm_copy(kind, s, h).wait_send()
        for kind in range(2):
            cot_copy(kind, s).wait_send()
        for kind in range(5):
            part_copy(kind, s).wait_send()
    for copy in stores:
        copy.wait()


def padded(rows, count, block):
    per = rows.shape[0] // count
    want = iota((count * block, rows.shape[0]), 0)
    have = iota((count * block, rows.shape[0]), 1)
    chosen = (have == want // block * per + want % block) & (want % block < per)
    return mm(chosen.astype(BF16), rows, NN).astype(BF16)


def middle(n, m, args):
    tokens, att, up_t, w_down = args[0], args[3], args[5], args[8]
    slots, quarter, width = tokens.shape
    dma = pltpu.SemaphoreType.DMA
    shape = jax.ShapeDtypeStruct
    rows = (slots, quarter, width)
    lines = n // 2
    pad = up_t.shape[1]
    block = round16(w_down.shape[0])
    inner = n * pad
    swapped = block // 2 if block % 32 == 0 else block
    vmem = pltpu.VMEM
    return pl.pallas_call(
        functools.partial(middle_kernel, n, m),
        out_shape=(
            shape(rows, F32),
            shape(rows, F32),
            shape(rows, BF16),
            shape(att.shape, BF16),
            shape((n, pad, width), BF16),
            shape((lines, block, inner), BF16),
            shape((n, swapped, width), BF16),
            shape((8, inner), F32),
            shape((slots, 8, width), F32),
        ),
        in_specs=[ANY] * 6 + [VM] * 3,
        out_specs=(ANY,) * 7 + (VM,) * 2,
        scratch_shapes=[
            vmem(rows, BF16),
            vmem(rows, BF16),
            vmem((width, width), BF16),
            vmem(att.shape, BF16),
            vmem(rows, BF16),
            vmem(rows, F32),
            vmem(rows, F32),
            vmem(rows, F32),
            vmem((slots, quarter, 1), F32),
            vmem((m,) + rows, BF16),
            vmem((m,) + rows, BF16),
            vmem((m, slots, quarter, inner), BF16),
            vmem((m, slots, quarter, inner), BF16),
            vmem((block, inner), BF16),
            vmem((n, pad, width), BF16),
            vmem((n, block, inner), BF16),
            vmem((width, inner), BF16),
            vmem((quarter, width), F32),
            vmem((4,) + rows, BF16),
            vmem((4,) + rows, BF16),
            vmem(rows, BF16),
            vmem(rows, BF16),
            vmem(rows, F32),
            vmem(rows, F32),
            vmem(rows, BF16),
            vmem(rows, F32),
            vmem(rows, BF16),
            vmem(att.shape, BF16),
            vmem(att.shape, BF16),
            vmem((n * block, inner), BF16),
            vmem((inner, width), BF16),
            vmem((n * block, width), BF16),
            vmem((n, swapped, width), BF16),
            vmem((lines, block, inner), BF16),
            vmem((lines, block, inner), BF16),
            dma((3, 2 * slots)),
            dma((3, 2 * slots)),
            dma((2, slots)),
            dma((2, slots)),
            dma((2, 4 * lines + 1)),
            dma((5, slots)),
            dma((5, slots)),
            dma((3, slots)),
            dma((3, slots)),
            dma((4 * lines + 1,)),
            dma((1,)),
            dma((1,)),
            dma((16,)),
        ],
        compiler_params=pltpu.CompilerParams(
            collective_id=2, has_side_effects=True, vmem_limit_bytes=LIMIT
        ),
        name="middle",
    )(*args)


def back_kernel(
    n,
    m,
    per,
    tile,
    qkv_ref,
    grad_ref,
    att_ref,
    normed_ref,
    tok_ref,
    gm_ref,
    xsend_ref,
    cot_ref,
    dwu_ref,
    downtotal_ref,
    outsum_ref,
    log_ref,
    seg_ref,
    cos_ref,
    sin_ref,
    wqkvt_ref,
    mod_ref,
    vec_ref,
    sums_ref,
    vblk_ref,
    wada_ref,
    dbup_ref,
    place_ref,
    dtok_out,
    other_out,
    down_out,
    up_out,
    wo_out,
    q_out,
    dcond_ref,
    dwada_ref,
    dbada_ref,
    dvec_ref,
    qkv_v,
    grad_v,
    att_v,
    gq_v,
    dk_ref,
    dv_ref,
    normed_v,
    tok_v,
    gm_v,
    other_v,
    cot_v,
    dtok_v,
    gsc,
    psend,
    precv,
    xs_ref,
    xr_ref,
    gn_ref,
    dwq_ref,
    qblk,
    dwu_v,
    outsum_v,
    total_d,
    zrecv_d,
    side_u,
    total_u,
    zrecv_u,
    side_o,
    total_o,
    zrecv_o,
    side_q,
    total_q,
    zrecv_q,
    qpair,
    zrecv_l,
    lown,
    lside,
    l_s,
    spr_d,
    spr_u,
    spr_q,
    opiece,
    ofar,
    ofin,
    ssend,
    srecv,
    gsend,
    grecv,
    vsend,
    vrecv,
    dsend,
    drecv,
    p_s,
    p_r,
    rz,
    d_s,
    d_r,
    s_s,
    s_r,
    ex,
    x_s,
    x_r,
    local,
):
    p = Place(n, m)
    hidden_per, small = per
    slots, quarter, width = tok_ref.shape
    length = m * quarter
    half = quarter // 2
    part = width // m
    heads = part // HEAD
    lines = p.lines
    peers = (p.sib, p.far, p.diag)
    loads = [
        pltpu.make_async_copy(src, dst, local.at[k])
        for k, (src, dst) in enumerate(
            (
                (qkv_ref, qkv_v),
                (grad_ref, grad_v),
                (att_ref, att_v),
                (downtotal_ref, total_d),
                (dwu_ref, dwu_v),
                (outsum_ref, outsum_v),
                (normed_ref, normed_v),
                (tok_ref, tok_v),
                (gm_ref, gm_v),
                (cot_ref, cot_v),
            )
        )
    ]
    for load in loads:
        load.start()
    greet(list(peers) + p.ring())

    def other_copy(s):
        return push(xsend_ref.at[s], other_v.at[s], x_s.at[s], x_r.at[s], p.far)

    def part_copy(kind, s):
        if kind == 2:
            return push(xs_ref.at[s], xr_ref.at[s], p_s.at[2, s], p_r.at[2, s], p.far)
        return push(psend.at[kind, s], precv.at[kind, s], p_s.at[kind, s], p_r.at[kind, s], p.sib)

    for s in range(slots):
        other_copy(s).start()
    red_d = Reduce(p, None, None, total_d, zrecv_d, rz.at[0], summed=True)
    red_u = Reduce(p, lambda f: dwu_v.at[f], side_u, total_u, zrecv_u, rz.at[1])
    red_o = Reduce(p, lambda f: outsum_v.at[f], side_o, total_o, zrecv_o, rz.at[2])
    red_q = Reduce(p, lambda f: qblk.at[f], side_q, total_q, zrecv_q, rz.at[3])
    cuts = place_ref.shape[1] // (n * qblk.shape[1])
    if cuts == 2:
        red_l = Reduce(p, None, None, qpair, zrecv_l, rz.at[4], summed=True)

        def pair_copy(theirs):
            rows = pl.ds(pl.multiple_of((p.b if theirs else 1 - p.b) * qrows, 16), qrows)
            return push(lown.at[rows], lside, l_s.at[0], l_s.at[1], p.side)

    down = Spread(p, lambda r: spr_d.at[r], d_s.at[0], d_r.at[0])
    up = Spread(p, lambda r: spr_u.at[r], d_s.at[1], d_r.at[1])
    qrows = qblk.shape[1]
    qry = [
        Spread(p, lambda r, h=h: spr_q.at[r, pl.ds(h * qrows, qrows)], d_s.at[2 + h], d_r.at[2 + h])
        for h in range(cuts)
    ]
    loads[4].wait()
    red_u.start()
    loads[3].wait()
    red_d.step(0)
    for k in (0, 1, 2):
        loads[k].wait()
    tiles = length // tile

    @pl.loop(0, slots)
    def _(s):
        dk_ref[...] = jnp.zeros_like(dk_ref)
        dv_ref[...] = jnp.zeros_like(dv_ref)
        column = as_column(seg_ref[pl.ds(s, 1), :])

        @pl.loop(0, tiles)
        def _(i):
            rows = pl.ds(pl.multiple_of(i * tile, tile), tile)
            same = column == seg_ref[pl.ds(s, 1), rows]
            cosine = cos_ref[rows, :HEAD]
            sine = sin_ref[rows, :HEAD]
            ones = jnp.ones((8, HEAD), BF16)
            for h in range(heads):
                at = h * HEAD
                q = qkv_v[s, rows, at : at + HEAD]
                k = qkv_v[s, :, part + at : part + at + HEAD]
                v = qkv_v[s, :, 2 * part + at : 2 * part + at + HEAD]
                g, o = [
                    jnp.concatenate(
                        [
                            ref[s, i * (tile // quarter) + j // 2, :, j % 2 * part + at : j % 2 * part + at + HEAD]
                            for j in range(tile // half)
                        ]
                    )
                    for ref in (grad_v, att_v)
                ]
                both = g.astype(F32) * o.astype(F32)
                high = both.astype(BF16)
                low = (both - high.astype(F32)).astype(BF16)
                inner = (mm(ones, high, NT) + mm(ones, low, NT))[:1]
                scores = jnp.where(same, mm(k, q, NT), MASKED)
                weights = jnp.exp(scores - log_ref[s, h : h + 1, rows])
                dots = mm(v, g, NT)
                dscores = (weights * (dots - inner)).astype(BF16)
                dq = mm(dscores, k, TN) * (1.0 / math.sqrt(HEAD))
                gq_v[s, rows, at : at + HEAD] = (dq * cosine - swap_halves(dq) * sine).astype(BF16)
                dk_ref[:, at : at + HEAD] += mm(dscores, q, NN)
                dv_ref[:, at : at + HEAD] += mm(weights.astype(BF16), g, NN)

            def reductions(first, red, steps):
                spread = -(-len(steps) // tiles)
                for k, t in enumerate(steps):
                    pl.when((s == first) & (i == k // spread))(lambda t=t: red.step(t))

            reductions(0, red_d, range(1, lines - 1))
            reductions(1, red_u, range(1, lines - 1))
            reductions(1, red_o, range(lines - 2))

        for at in range(0, part, 128):
            size = min(128, part - at)
            dk = dk_ref[:, at : at + size]
            other = turned(dk) if size == 128 else swap_halves(dk)
            dk = dk * cos_ref[:, :size] - other * sin_ref[:, :size]
            gq_v[s, :, part + at : part + at + size] = dk.astype(BF16)
        gq_v[s, :, 2 * part :] = dv_ref[...].astype(BF16)

        @pl.loop(0, 4)
        def _(j):
            q = jnp.where(
                j < 2, jnp.where(j == 0, p.diag_d, p.sib_d), jnp.where(j == 2, p.far_d, p.d)
            )
            rows = pl.ds(pl.multiple_of(q * quarter, quarter), quarter)
            gsc[...] = mm(gq_v[s, rows, :], wqkvt_ref[...], NN)

            @pl.when(j == 0)
            def _():
                psend[0, s] = gsc[...].astype(BF16)
                part_copy(0, s).start()

            @pl.when(j == 2)
            def _():
                part_copy(0, s).wait_recv()
                xs_ref[s] = (gsc[...] + precv[0, s].astype(F32)).astype(BF16)
                part_copy(2, s).start()

            @pl.when(j == 1)
            def _():
                psend[1, s] = gsc[...].astype(BF16)
                part_copy(1, s).start()

            @pl.when(j == 3)
            def _():
                gn_ref[s] = gsc[...]

        @pl.when(s == 0)
        def _():
            loads[5].wait()
            red_o.start()
            red_d.own(spr_d.at[p.d])
            red_u.step(0)

    red_o.step(lines - 2)
    loads[6].wait()
    every = slots * length
    gq_all = gq_v.reshape(every, gq_v.shape[2])
    normed_all = normed_v.reshape(every, width)
    for at in range(0, gq_v.shape[2], part):
        dwq_ref[at : at + part, :] = mm(gq_all[:, at : at + part], normed_all[...], TN).astype(BF16)
    count = n * cuts * qrows
    placing = (iota((dwq_ref.shape[0], count), 0) == place_ref[pl.ds(p.d, 1), :]).astype(BF16)
    blocks = mm(placing, dwq_ref[...], TN).astype(BF16).reshape(n, cuts, qrows, width)
    qblk[...] = blocks[:, 0]
    red_q.start()
    if cuts == 2:
        qpair[...] = blocks[:, 1].reshape(qpair.shape)
        red_l.step(0)
    down.start()
    red_u.own(spr_u.at[p.d])
    up.start()
    red_o.own(opiece)
    halved = ofin.shape[0] == 2
    mine = p.c if halved else 0
    o_far = push(opiece, ofar, d_s.at[4, 0], d_r.at[4, 0], p.far)
    o_far.start()

    def group(s, k):
        return mod_ref[s, :, k * width : (k + 1) * width]

    gain_attn = vec_ref[1:2, :width]
    gain_mlp = vec_ref[2:3, :width]
    wide = dbup_ref.shape[1]
    total_rows = lambda v: jnp.sum(v, axis=0, keepdims=True)
    for k in range(7, 10):
        loads[k].wait()
    ssend[...] = jnp.zeros_like(ssend)

    def leave(s):
        other_copy(s).wait_recv()
        part_copy(1, s).wait_recv()
        part_copy(2, s).wait_recv()
        gn = gn_ref[s] + precv[1, s].astype(F32) + xr_ref[s].astype(F32)
        normal, inverse = norm_rows(tok_v[s].astype(F32))
        dtok_v[s] = (
            gm_v[s] + norm_back(gn, normal, inverse, gain_attn * (1.0 + group(s, 1)))
        ).astype(BF16)
        extra = total_rows(cot_v[s].astype(F32) * other_v[s].astype(F32))
        ssend[s, 0:1, :width] = total_rows(gn)
        ssend[s, 1:2, :width] = total_rows(gn * normal)
        ssend[s, 2:3, :width] = sums_ref[s, 3:4, :]
        ssend[s, 3:5, :width] = sums_ref[s, 0:2, :]
        ssend[s, 5:6, :width] = sums_ref[s, 2:3, :] + extra
        ssend[s, 6:7, :width] = sums_ref[s, 4:5, :]

    ssend[0, 7:8, :wide] = dbup_ref[0:1, :]
    leave(0)
    if cuts == 2:
        for k in range(1, lines - 2):
            red_l.step(k)
    for s in range(1, slots):
        leave(s)

    def sums_copy(kind):
        return push(ssend, srecv.at[p.d], s_s.at[kind], s_r.at[kind], peers[kind])

    for kind in range(3):
        sums_copy(kind).start()
    srecv[p.d] = ssend[...]
    stores = []

    def store(src, dst):
        stores.append(pltpu.make_async_copy(src, dst, local.at[10 + len(stores)]))
        stores[-1].start()

    store(dtok_v, dtok_out)
    store(other_v, other_out)
    red_q.step(0)
    if cuts == 2:
        red_l.step(lines - 2)
    for k in range(1, lines - 2):
        red_q.step(k)
    for kind in range(3):
        sums_copy(kind).wait_recv()
    total = srecv[0]
    for r in range(1, m):
        total = total + srecv[r]
    cols = wada_ref.shape[0]
    gmod = []
    vecs = [jnp.zeros((1, width), F32)] * 3
    for s in range(slots):
        at = lambda k, s=s: total[s, k : k + 1, :width]
        gmod.append(
            jnp.concatenate(
                [at(0), at(1) * gain_attn, at(2), at(3), at(4) * gain_mlp, at(5)], axis=1
            )
        )
        vecs = [
            vecs[0] + at(1) * (1.0 + group(s, 1)),
            vecs[1] + at(4) * (1.0 + group(s, 4)),
            vecs[2] + at(6),
        ]
    gmod = jnp.concatenate(gmod, axis=0).astype(BF16).astype(F32)
    vsend[...] = jnp.zeros_like(vsend)
    pad = round16(hidden_per)
    for g in range(n):
        gsend[g] = gmod[:, g * cols : (g + 1) * cols]
        for k, v in enumerate(vecs):
            vsend[g, k : k + 1, :small] = v[:, g * small : (g + 1) * small]
        for r in range(m):
            vsend[g, 3 + r : 4 + r, :hidden_per] = srecv[r, 0, 7:8, g * pad : g * pad + hidden_per]

    gmods = Exchange(p, lambda f: gsend.at[f], grecv, ex.at[0], ex.at[1])
    gvecs = Exchange(p, lambda f: vsend.at[f], vrecv, ex.at[2], ex.at[3])
    gmods.start()
    gvecs.start()
    grecv[p.f] = gsend[p.f]
    vrecv[p.f] = vsend[p.f]
    if cuts == 2:
        red_l.own(lown)
        pair_copy(False).start()
    red_q.step(lines - 2)
    down.forward()
    up.forward()
    gmods.finish()
    got = jnp.concatenate([grecv[g] for g in range(n)], axis=0).astype(BF16)
    conds = jnp.concatenate([vblk_ref[g, 4 : 4 + slots] for g in range(n)], axis=0)
    dsend[...] = mm(got, wada_ref[...], NN).reshape(n, slots, conds.shape[1])

    gconds = Exchange(p, lambda f: dsend.at[f], drecv, ex.at[4], ex.at[5])
    gconds.start()
    drecv[p.f] = dsend[p.f]
    if cuts == 2:
        pair_copy(True).wait_recv()
        mine_rows = pl.ds(pl.multiple_of(p.b * qrows, 16), qrows)
        qry[1].slot(p.d)[...] = (lown[mine_rows].astype(F32) + lside[...].astype(F32)).astype(BF16)
        qry[1].start()
    red_q.own(qry[0].slot(p.d))
    qry[0].start()
    o_far.wait_recv()
    ofin[mine] = (opiece[...].astype(F32) + ofar[...].astype(F32)).astype(BF16)
    if halved:
        o_sib = push(ofin.at[mine], ofin.at[mine], d_s.at[4, 1], d_r.at[4, 1], p.sib)
        o_sib.start()
    dwada_ref[...] = mm(got, conds, TN)
    dbada_ref[...] = jnp.sum(got.astype(F32), axis=0, keepdims=True)
    gvecs.finish()
    total = vrecv[0]
    for g in range(1, n):
        total = total + vrecv[g]
    dvec_ref[...] = total
    down.finish()
    store(spr_d, down_out)
    up.finish()
    store(spr_u, up_out)
    if halved:
        push(ofin.at[1 - mine], ofin.at[1 - mine], d_s.at[4, 1], d_r.at[4, 1], p.sib).wait_recv()
    store(ofin, wo_out)
    gconds.finish()
    total = drecv[0]
    for g in range(1, n):
        total = total + drecv[g]
    dcond_ref[...] = total
    for spread in qry:
        spread.forward()
    for spread in qry:
        spread.finish()
    store(spr_q, q_out)

    for s in range(slots):
        other_copy(s).wait_send()
        for kind in range(3):
            part_copy(kind, s).wait_send()
    for red in (red_d, red_u, red_o, red_q):
        red.drain()
    if cuts == 2:
        red_l.drain()
        pair_copy(False).wait_send()
    for spread in (down, up, *qry):
        spread.drain()
    o_far.wait_send()
    if halved:
        o_sib.wait_send()
    for kind in range(3):
        sums_copy(kind).wait_send()
    for exchange in (gmods, gvecs, gconds):
        exchange.drain()
    for copy in stores:
        copy.wait()


def back(n, m, per, tile, args):
    qkv, grad, att, normed, tokens = args[:5]
    dwu, downtotal, outsum = args[8:11]
    vblk, w_ada, dbup, place = args[19:23]
    slots, quarter, width = tokens.shape
    dma = pltpu.SemaphoreType.DMA
    shape = jax.ShapeDtypeStruct
    vmem = pltpu.VMEM
    rows = (slots, quarter, width)
    length = m * quarter
    part = width // m
    lines = n // 2
    wide = max(width, dbup.shape[1])
    _, block, inner = downtotal.shape
    pad = dwu.shape[1]
    orows = outsum.shape[1]
    halves = 2 if orows < block else 1
    most = place.shape[1] // n
    qrows = most // 2 if most % 32 == 0 else most
    pair = most if qrows < most else 32
    pair_lines = lines if qrows < most else 1
    cols, cond = w_ada.shape
    lanes = max(per)

    def reduced(rows, wide):
        return [vmem((lines, rows, wide), BF16)] * 2 + [vmem((lines + 1, rows, wide), BF16)]

    return pl.pallas_call(
        functools.partial(back_kernel, n, m, per, tile),
        out_shape=(
            shape(rows, BF16),
            shape(rows, BF16),
            shape((m, block, inner), BF16),
            shape((m, pad, width), BF16),
            shape((halves, orows, width), BF16),
            shape((m, most, width), BF16),
            shape((slots, cond), F32),
            shape((cols, cond), F32),
            shape((1, cols), F32),
            shape((8, lanes), F32),
        ),
        in_specs=[ANY] * 11 + [VM] * (len(args) - 11),
        out_specs=(ANY,) * 6 + (VM,) * 4,
        scratch_shapes=[
            vmem(qkv.shape, BF16),
            vmem(grad.shape, BF16),
            vmem(att.shape, BF16),
            vmem(qkv.shape, BF16),
            vmem((length, part), F32),
            vmem((length, part), F32),
            vmem(normed.shape, BF16),
            vmem(rows, BF16),
            vmem(rows, F32),
            vmem(rows, BF16),
            vmem(rows, BF16),
            vmem(rows, BF16),
            vmem((quarter, width), F32),
            vmem((2,) + rows, BF16),
            vmem((2,) + rows, BF16),
            vmem(rows, BF16),
            vmem(rows, BF16),
            vmem(rows, F32),
            vmem((qkv.shape[2], width), BF16),
            vmem((n, qrows, width), BF16),
            vmem(dwu.shape, BF16),
            vmem(outsum.shape, BF16),
        ]
        + reduced(block, inner)[1:]
        + reduced(pad, width)
        + reduced(orows, width)
        + reduced(qrows, width)
        + [
            vmem((pair_lines, pair, width), BF16),
            vmem((pair_lines + 1, pair, width), BF16),
            vmem((pair, width), BF16),
            vmem((pair // 2, width), BF16),
            dma((2,)),
        ]
        + [
            vmem((m, block, inner), BF16),
            vmem((m, pad, width), BF16),
            vmem((m, most, width), BF16),
            vmem((orows, width), BF16),
            vmem((orows, width), BF16),
            vmem((halves, orows, width), BF16),
            vmem((slots, 8, wide), F32),
            vmem((m, slots, 8, wide), F32),
            vmem((n, slots, cols), F32),
            vmem((n, slots, cols), F32),
            vmem((n, 8, lanes), F32),
            vmem((n, 8, lanes), F32),
            vmem((n, slots, cond), F32),
            vmem((n, slots, cond), F32),
            dma((3, slots)),
            dma((3, slots)),
            dma((5, 4 * lines + 1)),
            dma((5, 3)),
            dma((5, 3)),
            dma((3,)),
            dma((3,)),
            dma((6,)),
            dma((slots,)),
            dma((slots,)),
            dma((24,)),
        ],
        compiler_params=pltpu.CompilerParams(
            collective_id=3, has_side_effects=True, vmem_limit_bytes=LIMIT
        ),
        name="back",
    )(*args)


def finish_kernel(
    n,
    m,
    per,
    base_ref,
    other_ref,
    mod_ref,
    dtok_ref,
    dcond_ref,
    dwada_ref,
    dbada_ref,
    dvec_ref,
    down_ref,
    up_ref,
    wo_ref,
    q_ref,
    home_ref,
    out_ref,
    dtok_out,
    dcond_out,
    dwada_out,
    dbada_out,
    dga_out,
    dwqkv_out,
    dwout_out,
    dgm_out,
    dwup_out,
    dbup_out,
    dwdown_out,
    dbdown_out,
):
    hidden_per, small = per
    slots, _, width = base_ref.shape
    pad = round16(hidden_per)
    part = width // m
    for s in range(slots):
        gate = mod_ref[s, :, 5 * width :]
        out_ref[s] = (base_ref[s] + gate * other_ref[s].astype(F32)).astype(BF16)
    dtok_out[...] = dtok_ref[...]
    dcond_out[...] = dcond_ref[...].astype(BF16)
    dwada_out[...] = dwada_ref[...]
    dbada_out[...] = dbada_ref[0, :]
    for row, ref in ((0, dga_out), (1, dgm_out), (2, dbdown_out)):
        ref[...] = dvec_ref[row, :small]
    dbup_out[...] = jnp.concatenate(
        [dvec_ref[3 + r : 4 + r, :hidden_per] for r in range(m)], axis=1
    ).reshape(-1)
    for r in range(m):
        piece = down_ref[r, :small].astype(F32)
        for g in range(n):
            at = (g * m + r) * hidden_per
            dwdown_out[:, at : at + hidden_per] = piece[:, g * pad : g * pad + hidden_per]
    dwup_out[...] = jnp.concatenate([up_ref[r][:hidden_per] for r in range(m)]).astype(F32).T
    piece = wo_ref[...].reshape(-1, width)[:small].astype(F32)
    heads = part // HEAD
    for r in range(m):
        for h in range(heads):
            at = r * part + h * HEAD
            dwout_out[:, (h * m + r) * HEAD : (h * m + r + 1) * HEAD] = piece[:, at : at + HEAD]
    count = q_ref.shape[0] * q_ref.shape[1]
    f = lax.axis_index("fsdp")
    homing = (iota((dwqkv_out.shape[0], count), 0) == home_ref[pl.ds(f, 1), :]).astype(BF16)
    dwqkv_out[...] = mm(homing, q_ref[...].reshape(count, width), NN)


def finish(n, m, per, columns, args):
    base, dcond, dwada, dbada = args[0], args[4], args[5], args[6]
    hidden_per, small = per
    rows = base.shape
    width = rows[2]
    shape = jax.ShapeDtypeStruct
    return pl.pallas_call(
        functools.partial(finish_kernel, n, m, per),
        out_shape=(
            shape(rows, BF16),
            shape(rows, BF16),
            shape(dcond.shape, BF16),
            shape(dwada.shape, F32),
            shape(dbada.shape[1:], F32),
            shape((small,), F32),
            shape((columns, width), F32),
            shape((small, width), F32),
            shape((small,), F32),
            shape((width, m * hidden_per), F32),
            shape((m * hidden_per,), F32),
            shape((small, n * m * hidden_per), F32),
            shape((small,), F32),
        ),
        in_specs=[VM] * len(args),
        out_specs=(VM,) * 13,
        compiler_params=pltpu.CompilerParams(vmem_limit_bytes=LIMIT),
        name="finish",
    )(*args)


def column_plan(shards_n, ranks, columns):
    per = columns // shards_n
    rank_of = (np.arange(columns) // HEAD) % ranks
    lists = [
        [[c for c in range(per) if rank_of[f * per + c] == r] for r in range(ranks)]
        for f in range(shards_n)
    ]
    most = max(len(l) for row in lists for l in row)
    most = -(-most // 16) * 16
    take = np.full((shards_n, ranks, most), -1, np.int32)
    place = np.full((ranks, shards_n * most), -1, np.int32)
    home = np.full((shards_n, ranks * most), -1, np.int32)
    for r in range(ranks):
        order = {c: i for i, c in enumerate(np.flatnonzero(rank_of == r))}
        for f in range(shards_n):
            for i, c in enumerate(lists[f][r]):
                take[f, r, i] = c
                place[r, f * most + i] = order[f * per + c]
                home[f, r * most + i] = c
    return most, take, place, home


def shards(
    tokens,
    condition,
    segments,
    w_ada,
    b_ada,
    gain_attn,
    w_qkv,
    w_out,
    gain_mlp,
    w_up,
    b_up,
    w_down,
    b_down,
    cotangent,
):
    slots, quarter, width = tokens.shape
    length = segments.shape[1]
    n = lax.axis_size("fsdp")
    m = lax.axis_size("dp")
    tile = 2 * quarter
    hidden_per = b_up.shape[0] // m
    small = gain_attn.shape[0]
    per = (hidden_per, small)
    columns = w_qkv.shape[1]
    most, take, place, home = column_plan(n, m, columns * n)
    place = jnp.asarray(place)
    cosine, sine = [jnp.asarray(np.concatenate([v, v], axis=1)) for v in rope_table(length)]

    (
        qkv,
        normed,
        attended,
        own_attended,
        logs,
        cot_far,
        out_blocks,
        up_blocks,
        mod,
        vec,
        w_qkv_t,
        vec_blocks,
    ) = front(
        n,
        m,
        length,
        tile,
        most,
        (
            tokens,
            cotangent,
            condition,
            segments,
            w_ada.T,
            b_ada,
            b_up,
            gain_attn,
            gain_mlp,
            b_down,
            w_qkv.T,
            w_out.T,
            w_up,
            jnp.asarray(take.reshape(n * m, most)),
            place,
            cosine,
            sine,
        ),
    )
    w_out_t = out_blocks.reshape(n, -1, width)[:, :small].reshape(width, width)
    grad_middle, base, far_part, grad_attended, dw_up, down_total, out_sum, db_up, sums = middle(
        n,
        m,
        (tokens, cotangent, cot_far, own_attended, w_out_t, up_blocks, mod, vec, w_down.T),
    )
    d_tokens, other_part, down_all, up_all, out_all, qkv_all, d_cond, d_w_ada, d_b_ada, d_vec = back(
        n,
        m,
        per,
        tile,
        (
            qkv,
            grad_attended,
            attended,
            normed,
            tokens,
            grad_middle,
            far_part,
            cotangent,
            dw_up,
            down_total,
            out_sum,
            logs,
            segments,
            cosine,
            sine,
            w_qkv_t,
            mod,
            vec,
            sums,
            vec_blocks,
            w_ada.T,
            db_up,
            place,
        ),
    )
    done = finish(
        n,
        m,
        per,
        columns,
        (
            base,
            other_part,
            mod,
            d_tokens,
            d_cond,
            d_w_ada,
            d_b_ada,
            d_vec,
            down_all,
            up_all,
            out_all,
            qkv_all,
            jnp.asarray(home),
        ),
    )
    turned_back = (3, 6, 7, 11)
    return tuple(v.T if i in turned_back else v for i, v in enumerate(done))


def solution(mesh):
    return jax.shard_map(
        shards,
        mesh=mesh,
        in_specs=(
            P("fsdp", "dp", None),
            P("fsdp", None),
            P("fsdp", None),
            P(None, "fsdp"),
            P("fsdp"),
            P("fsdp"),
            P(None, "fsdp"),
            P(None, "fsdp"),
            P("fsdp"),
            P(None, "fsdp"),
            P("fsdp"),
            P(None, "fsdp"),
            P("fsdp"),
            P("fsdp", "dp", None),
        ),
        out_specs=(
            P("fsdp", "dp", None),
            P("fsdp", "dp", None),
            P("fsdp", None),
            P(None, "fsdp"),
            P("fsdp"),
            P("fsdp"),
            P(None, "fsdp"),
            P(None, "fsdp"),
            P("fsdp"),
            P(None, "fsdp"),
            P("fsdp"),
            P(None, "fsdp"),
            P("fsdp"),
        ),
        check_vma=False,
    )
```

```python
import functools
import math

import jax
import jax.numpy as jnp
import numpy as np
from jax import lax
from jax.experimental import pallas as pl
from jax.experimental.pallas import tpu as pltpu
from jax.sharding import PartitionSpec as P

HEAD = 64
EPS = 1e-05
ROPE_BASE = 10000.0
MASKED = -1e30
F32 = jnp.float32
BF16 = jnp.bfloat16

NN = (((1,), (0,)), ((), ()))
NT = (((1,), (1,)), ((), ()))
TN = (((0,), (0,)), ((), ()))


def mm(a, b, dims):
    return lax.dot_general(a, b, dims, preferred_element_type=F32)


def rope_table(length):
    inverse = ROPE_BASE ** (-2.0 * np.arange(HEAD // 2) / HEAD)
    angles = np.arange(length)[:, None] * inverse[None, :]
    cosine = np.concatenate([np.cos(angles)] * 2, axis=1)
    sine = np.concatenate([-np.sin(angles), np.sin(angles)], axis=1)
    return cosine.astype(np.float32), sine.astype(np.float32)


def swap_halves(v):
    half = HEAD // 2
    return jnp.concatenate([v[..., half:], v[..., :half]], axis=-1)


MESH = pl.DeviceIdType.MESH
VM = pl.BlockSpec(memory_space=pltpu.VMEM)
ANY = pl.BlockSpec(memory_space=pl.ANY)
LIMIT = (63 << 20) + (768 << 10)


def round16(size):
    return -(-size // 16) * 16


def iota(shape, dim):
    return lax.broadcasted_iota(jnp.int32, shape, dim)


def greet(peers, meanwhile=None):
    barrier = pltpu.get_barrier_semaphore()
    for peer in peers:
        pl.semaphore_signal(barrier, inc=1, device_id=peer, device_id_type=MESH)
    if meanwhile is not None:
        meanwhile()
    pl.semaphore_wait(barrier, len(peers))


def push(src, dst, send, recv, peer):
    return pltpu.make_async_remote_copy(
        src_ref=src,
        dst_ref=dst,
        send_sem=send,
        recv_sem=recv,
        device_id=peer,
        device_id_type=MESH,
    )


class Place:
    def __init__(self, n, m):
        self.n, self.m = n, m
        self.f = lax.axis_index("fsdp")
        self.d = lax.axis_index("dp")
        self.lines = n // 2
        self.a = self.f // 2
        self.b = self.f % 2
        self.x = self.d // 2
        self.c = self.d % 2
        self.sib_d = self.x * 2 + 1 - self.c
        self.far_d = (1 - self.x) * 2 + self.c
        self.diag_d = (1 - self.x) * 2 + 1 - self.c
        self.sib = (self.f, self.sib_d)
        self.far = (self.f, self.far_d)
        self.diag = (self.f, self.diag_d)
        self.side = (self.a * 2 + 1 - self.b, self.d)
        last = self.lines - 1
        self.right = (jnp.minimum(self.a + 1, last) * 2 + self.b, self.d)
        self.left = (jnp.maximum(self.a - 1, 0) * 2 + self.b, self.d)
        self.has_right = self.a < last
        self.has_left = self.a > 0

    def ring_f(self, step):
        return (self.f + step + self.n) % self.n

    def ring(self):
        return [(self.ring_f(i), self.d) for i in range(1, self.n)]

    def line_peers(self):
        return [((self.a + i) % self.lines * 2 + self.b, self.d) for i in range(1, self.lines)] + [
            self.side
        ]


class Gather:
    def __init__(self, p, src, slot, sems):
        self.p, self.src, self.slot, self.sems = p, src, slot, sems

    def place(self, way, t):
        return jnp.clip(self.p.a + (t if way else -t), 0, self.p.lines - 1)

    def line_copy(self, way, t):
        p, j = self.p, self.place(way, t)
        block = self.slot(j * 2 + p.b)
        leave = 4 * p.lines if way and t == 0 else p.lines + j
        return push(
            self.src if t == 0 else block,
            block,
            self.sems.at[leave],
            self.sems.at[j],
            p.left if way else p.right,
        )

    def side_copy(self, way, t, theirs=False):
        p, j = self.p, self.place(way, t)
        block = self.slot(j * 2 + (1 - p.b if theirs else p.b))
        return push(
            self.src if t == 0 else block,
            block,
            self.sems.at[2 * p.lines + j],
            self.sems.at[3 * p.lines + j],
            p.side,
        )

    def held(self, way, t):
        p = self.p
        return p.a + t < p.lines if way else p.a - t >= 0

    def onward(self, way):
        return self.p.has_left if way else self.p.has_right

    def start(self):
        for way in range(2):
            pl.when(self.onward(way))(lambda way=way: self.line_copy(way, 0).start())
        self.side_copy(0, 0).start()

    def step(self, t):
        for way in range(2):

            @pl.when(self.held(way, t))
            def _(way=way):
                self.line_copy(way, t).wait_recv()
                if t < self.p.lines - 1:
                    pl.when(self.onward(way))(lambda: self.line_copy(way, t).start())
                self.side_copy(way, t).start()

    def finish(self):
        self.side_copy(0, 0, True).wait_recv()
        for t in range(1, self.p.lines):
            for way in range(2):
                pl.when(self.held(way, t))(
                    lambda way=way, t=t: self.side_copy(way, t, True).wait_recv()
                )

    def drain(self):
        self.side_copy(0, 0).wait_send()
        for way in range(2):
            pl.when(self.onward(way))(lambda way=way: self.line_copy(way, 0).wait_send())
        for t in range(1, self.p.lines):
            for way in range(2):

                @pl.when(self.held(way, t))
                def _(way=way, t=t):
                    if t < self.p.lines - 1:
                        pl.when(self.onward(way))(lambda: self.line_copy(way, t).wait_send())
                    self.side_copy(way, t).wait_send()


class Both:
    def __init__(self, *gathers):
        self.gathers = gathers

    def start(self):
        for g in self.gathers:
            g.start()

    def step(self, t):
        for g in self.gathers:
            g.step(t)

    def finish(self):
        for g in self.gathers:
            g.finish()

    def drain(self):
        for g in self.gathers:
            g.drain()


def gather_halves(p, src, buf, sems, first):
    rows = src.shape[0]
    if rows % 32:
        return Gather(p, src, lambda f: buf.at[f], sems.at[first])
    cut = [pl.ds(h * rows // 2, rows // 2) for h in range(2)]
    return Both(
        *[
            Gather(p, src.at[cut[h]], lambda f, h=h: buf.at[f, cut[h]], sems.at[first + h])
            for h in range(2)
        ]
    )


class Reduce:
    def __init__(self, p, src, side, total, zrecv, sems, summed=False, only=None):
        self.p, self.src, self.side, self.total = p, src, side, total
        self.zrecv, self.sems, self.summed, self.only = zrecv, sems, summed, only

    def order(self):
        lines = self.p.lines
        if self.only is not None:
            return [self.only]
        return [j for k in range(lines // 2) for j in (lines - 1 - k, k)]

    def side_copy(self, j):
        p = self.p
        return push(
            self.src(2 * j + 1 - p.b), self.side.at[j], self.sems.at[j], self.sems.at[p.lines + j], p.side
        )

    def line_copy(self, way, j):
        p = self.p
        at = jnp.where(j == p.a - 1, p.lines, j) if way else j
        return push(
            self.total.at[j],
            self.zrecv.at[at],
            self.sems.at[2 * p.lines + j],
            self.sems.at[3 * p.lines + at],
            p.left if way else p.right,
        )

    def line_wait(self, way, j):
        p = self.p
        at = jnp.where(j == p.a, p.lines, j) if way else j
        block = self.zrecv.at[at]
        push(
            block,
            block,
            self.sems.at[2 * p.lines + j],
            self.sems.at[3 * p.lines + at],
            p.left if way else p.right,
        ).wait_recv()
        return block[...].astype(F32)

    def start(self):
        for j in self.order():
            self.side_copy(j).start()

    def side_sum(self, j):
        p = self.p
        self.side_copy(j).wait_recv()
        mine = self.src(2 * j + p.b)[...].astype(F32)
        self.total[j] = (mine + self.side[j].astype(F32)).astype(BF16)

    def step(self, t):
        p = self.p
        if 2 * t < p.lines and not self.summed:
            for j in self.order()[2 * t : 2 * t + 2]:
                self.side_sum(j)
        for way in range(2):
            j = t - (p.lines - 1 - p.a) if way else p.lines - 1 - (t - p.a)
            ahead = (j >= 0) & (j < p.a) if way else (j < p.lines) & (j > p.a)
            behind = p.has_right if way else p.has_left
            if self.only is not None:
                ahead &= j == self.only

            @pl.when(ahead)
            def _(way=way, j=j, behind=behind):
                @pl.when(behind)
                def _():
                    arrived = self.line_wait(way, j)
                    self.total[j] = (self.total[j].astype(F32) + arrived).astype(BF16)

                self.line_copy(way, j).start()

    def own(self, out):
        p = self.p
        held = True if self.only is None else p.a == self.only
        for way in range(2):

            @pl.when(held & (p.has_right if way else p.has_left))
            def _(way=way):
                arrived = self.line_wait(way, p.a)
                self.total[p.a] = (self.total[p.a].astype(F32) + arrived).astype(BF16)

        if self.only is None:
            out[...] = self.total[p.a]
        else:
            out[...] = jnp.zeros(out.shape, BF16)

            @pl.when(held)
            def _():
                out[...] = self.total[p.a]

    def drain(self):
        p = self.p
        for j in range(p.lines) if self.only is None else [self.only]:
            if not self.summed:
                self.side_copy(j).wait_send()
            for way in range(2):
                ahead = p.a > j if way else p.a < j
                pl.when(ahead)(lambda way=way, j=j: self.line_copy(way, j).wait_send())


class Exchange:
    def __init__(self, p, src, buf, send, recv):
        self.p, self.src, self.buf, self.send, self.recv = p, src, buf, send, recv

    def start(self):
        p = self.p
        for i in range(1, p.n):
            peer = p.ring_f(i)
            push(self.src(peer), self.buf.at[p.f], self.send, self.recv, (peer, p.d)).start()

    def every(self):
        some = self.buf.at[pl.ds(0, self.p.n - 1)]
        return push(some, some, self.send, self.recv, self.p.side)

    def finish(self):
        self.every().wait_recv()

    def drain(self):
        self.every().wait_send()


class Spread:
    def __init__(self, p, slot, send, recv):
        self.p, self.slot, self.send, self.recv = p, slot, send, recv

    def copy(self, kind):
        p = self.p
        block = self.slot(p.far_d if kind == 2 else p.d)
        return push(block, block, self.send.at[kind], self.recv.at[kind], p.far if kind == 1 else p.sib)

    def start(self):
        self.copy(1).start()
        self.copy(0).start()

    def forward(self):
        self.copy(1).wait_recv()
        self.copy(2).start()

    def finish(self):
        self.copy(0).wait_recv()
        self.copy(2).wait_recv()

    def drain(self):
        for kind in range(3):
            self.copy(kind).wait_send()


def norm_rows(stream):
    average = jnp.mean(stream, axis=-1, keepdims=True)
    centered = stream - average
    variance = jnp.mean(centered * centered, axis=-1, keepdims=True)
    inverse = lax.rsqrt(variance + EPS)
    return centered * inverse, inverse


def norm_back(grad, normal, inverse, factor):
    e = grad * factor
    mean_e = jnp.mean(e, axis=-1, keepdims=True)
    mean_en = jnp.mean(e * normal, axis=-1, keepdims=True)
    return inverse * (e - mean_e - normal * mean_en)


def turned(v):
    lanes = iota(v.shape, 1)
    half = HEAD // 2
    return jnp.where(lanes % HEAD < half, pltpu.roll(v, 128 - half, 1), pltpu.roll(v, half, 1))


def gelu_parts(h):
    root = math.sqrt(2.0 / math.pi)
    square = h * h
    t = jnp.tanh(root * h * (1.0 + 0.044715 * square))
    half = 0.5 * (1.0 + t)
    slope = half + 0.5 * h * (1.0 - t * t) * (root * (1.0 + 3.0 * 0.044715 * square))
    return h * half, slope


def compact(blocks, per):
    count, rows, lanes = blocks.shape
    flat = blocks.reshape(count * rows, lanes)
    if rows == per:
        return flat
    want = iota((count * per, count * rows), 0)
    have = iota((count * per, count * rows), 1)
    chosen = (have == want // per * rows + want % per).astype(BF16)
    return mm(chosen, flat, NN).astype(BF16)


def as_column(row):
    size = row.shape[1]
    return jnp.transpose(jnp.broadcast_to(row, (128, size)))[:, :1]


def front_kernel(
    n,
    m,
    per,
    tile,
    tok_ref,
    cot_ref,
    cond_ref,
    seg_ref,
    wada_ref,
    bada_ref,
    bup_ref,
    ga_ref,
    gmlp_ref,
    bdown_ref,
    wqkv_ref,
    wout_ref,
    wup_ref,
    wdown_ref,
    take_ref,
    place_ref,
    cos_ref,
    sin_ref,
    qkv_out,
    normed_out,
    att_out,
    log_out,
    gm_out,
    base_out,
    xsend_out,
    gatt_out,
    dwu_out,
    downtotal_out,
    outsum_out,
    mod_ref,
    vecs_ref,
    wqkvt_ref,
    vec_out,
    dbup_ref,
    sums_ref,
    qkv_ref,
    att_v,
    arecv,
    log_v,
    mod_send,
    mod_recv,
    vsrc,
    vbuf,
    qsrc,
    qbuf,
    osrc,
    obuf,
    usrc,
    ubuf,
    dsrc,
    dbuf,
    cot_v,
    own_ref,
    br_ref,
    mid_ref,
    nrm_ref,
    inv_ref,
    nm_ref,
    ct_ref,
    act_ref,
    gp_ref,
    gsc,
    psend,
    precv,
    xs_ref,
    xr_ref,
    gn_ref,
    bo_ref,
    gba_ref,
    gm_ref,
    gsend,
    grecv,
    dwd_ref,
    dwu_ref,
    dwo_ref,
    oswap,
    side_d,
    total_d,
    ex,
    gz,
    ts,
    tr,
    os_,
    or_,
    as_,
    ar,
    cs,
    cr,
    n_s,
    n_r,
    p_s,
    p_r,
    g_s,
    g_r,
    rz,
    o_s,
    o_r,
    local,
):
    p = Place(n, m)
    slots, quarter, width = tok_ref.shape
    half = quarter // 2
    part = width // m
    heads = part // HEAD
    hidden_per, small = per
    pad = usrc.shape[0]
    inner = n * hidden_per
    halves = obuf.shape[1]
    length = m * quarter
    tall_ref = gp_ref
    normed_ref = act_ref.reshape(slots, length, width)
    filled = pad > hidden_per or qbuf.shape[0] * osrc.shape[0] > width
    spare = qbuf.reshape(n * qsrc.shape[0], width)
    dense = [spare.at[pl.ds(k * width, width)] for k in range(3 if filled else 0)]
    peers = (p.sib, p.far, p.diag)
    ranks = (p.sib_d, p.far_d, p.diag_d)
    own_tokens = pltpu.make_async_copy(tok_ref, tall_ref.at[p.d], local.at[2])
    own_tokens.start()
    own_cots = [
        pltpu.make_async_copy(cot_ref, dst, local.at[3 + k])
        for k, dst in enumerate((cot_v, ct_ref.at[p.d]))
    ]
    for copy in own_cots:
        copy.start()
    log_v[...] = jnp.zeros_like(log_v)

    def prepare():
        vsrc[...] = jnp.zeros_like(vsrc)
        for row, ref in enumerate((ga_ref, gmlp_ref, bdown_ref)):
            vsrc[row : row + 1, : ref.shape[0]] = ref[...].reshape(1, -1)
        vsrc[4 : 4 + slots, :] = cond_ref[...]
        b_up = bup_ref[...].reshape(1, -1)
        for k in range(0, b_up.shape[1], 128):
            some = b_up[:, k : k + 128]
            vsrc[8 + k // 128 : 9 + k // 128, : some.shape[1]] = some
        columns = wqkv_ref.shape[0]
        most = qsrc.shape[0]
        taking = take_ref[pl.ds(p.f * m + p.d, 1), :]
        chosen = (iota((columns, most), 0) == taking).astype(BF16)
        qsrc[...] = mm(chosen, wqkv_ref[...], TN).astype(BF16)

    greet(list(peers) + p.ring(), prepare)

    vec = Exchange(p, lambda f: vsrc, vbuf, ex.at[0], ex.at[1])
    vec.start()

    def token_copy(kind, k):
        s, rows = k // 2, pl.ds(k % 2 * half, half)
        if kind == 2:
            block = tall_ref.at[p.far_d, s, rows]
            return push(block, block, ts.at[kind, k], tr.at[kind, k], p.sib)
        return push(
            tok_ref.at[s, rows],
            tall_ref.at[p.d, s, rows],
            ts.at[kind, k],
            tr.at[kind, k],
            p.sib if kind == 0 else p.far,
        )

    qry = gather_halves(p, qsrc, qbuf, gz, 0)
    qry.start()
    for k in range(2 * slots):
        token_copy(1, k).start()
    for k in range(2 * slots):
        token_copy(0, k).start()
    vbuf[p.f] = vsrc[...]
    qbuf[p.f] = qsrc[...]

    lane = iota((1, width), 1)
    rank, rest = lane // part, lane % part
    want = (rest // HEAD * m + rank) * HEAD + rest % HEAD
    chosen = (iota((width, width), 0) == want).astype(BF16)
    got = mm(wout_ref[...], chosen, NN).astype(BF16)
    if small < osrc.shape[0]:
        got = jnp.concatenate([got, jnp.zeros((osrc.shape[0] - small, width), BF16)])
    osrc[...] = got
    split = osrc.shape[0] // halves
    mine = p.c if halves == 2 else 0
    out = Gather(
        p,
        osrc.at[pl.ds(pl.multiple_of(mine * split, 16), split)],
        lambda f: obuf.at[f, mine],
        gz.at[2],
    )
    for h in range(halves):
        obuf[p.f, h] = osrc[h * split : (h + 1) * split]

    ups = wup_ref.shape[1]
    at, lane = iota((pad, ups), 0), iota((pad, ups), 1)
    chosen = ((lane == at + p.d * hidden_per) & (at < hidden_per)).astype(BF16)
    usrc[...] = mm(chosen, wup_ref[...], NT).astype(BF16)
    ubuf[p.f] = usrc[...]
    up = Gather(p, usrc, lambda f: ubuf.at[f], gz.at[3])
    block = dsrc.shape[0]
    lane = iota((1, inner), 1)
    want = (lane // hidden_per * m + p.d) * hidden_per + lane % hidden_per
    got = jnp.zeros((small, inner), F32)
    for at in range(0, wdown_ref.shape[1], width):
        chosen = (iota((width, inner), 0) + at == want).astype(BF16)
        got = got + mm(wdown_ref[:, at : at + width], chosen, NN)
    got = got.astype(BF16)
    if small < block:
        got = jnp.concatenate([got, jnp.zeros((block - small, inner), BF16)])
    dsrc[...] = got
    dbuf[p.f] = got
    down = Gather(p, dsrc, lambda f: dbuf.at[f], gz.at[4])

    def pass_on(k):
        token_copy(1, k).wait_recv()
        token_copy(2, k).start()

    qry.step(1)
    vec.finish()
    vecs = vbuf[...].reshape(n * 16, 128)
    mod_cols = mm(vecs, wada_ref[...], NT) + bada_ref[...].reshape(1, -1).astype(F32)
    mod_send[...] = mod_cols.reshape(n, 16, mod_cols.shape[1])[:, 4 : 4 + slots]
    mod_recv[p.f] = mod_send[p.f]

    mods = Exchange(p, lambda f: mod_send.at[f], mod_recv, ex.at[2], ex.at[3])
    mods.start()
    vec_out[...] = vbuf[...]
    vecs_ref[...] = jnp.zeros_like(vecs_ref)
    ups = bup_ref.shape[0]
    b_up = jnp.zeros((n * 16, pad), F32)
    for k in range(0, ups, 128):
        lane = iota((128, pad), 1)
        chosen = (iota((128, pad), 0) + k == lane + p.d * hidden_per) & (lane < hidden_per)
        some = mm(vecs, chosen.astype(BF16), NN)
        b_up = b_up + jnp.where(iota((n * 16, pad), 0) % 16 == 8 + k // 128, some, 0.0)
    for g in range(n):
        vecs_ref[0:1, g * hidden_per : (g + 1) * hidden_per] = jnp.sum(
            b_up[16 * g : 16 * (g + 1)], axis=0, keepdims=True
        )[:, :hidden_per]
        rest = vecs[16 * g : 16 * g + 8].astype(F32)
        for k in range(3):
            vecs_ref[k + 1 : k + 2, g * small : (g + 1) * small] = rest[k : k + 1, :small]
    for k in range(2, p.lines - 1):
        qry.step(k)
    pass_on(0)
    qry.step(p.lines - 1)
    out.start()
    mods.finish()
    cols = mod_cols.shape[1]
    for g in range(n):
        for s in range(slots):
            mod_ref[s, :, g * cols : (g + 1) * cols] = mod_recv[g, s : s + 1]
    gain = vecs_ref[1:2, :width]

    pass_on(1)
    pass_on(2)
    def cot_copy(kind, s):
        if kind == 2:
            block = ct_ref.at[p.far_d, s]
            return push(block, block, cs.at[kind, s], cr.at[kind, s], p.sib)
        return push(
            cot_ref.at[s],
            ct_ref.at[p.d, s],
            cs.at[kind, s],
            cr.at[kind, s],
            p.sib if kind else p.far,
        )

    for s in range(slots):
        cot_copy(0, s).start()

    qry.finish()
    up.start()
    count = n * qsrc.shape[0]
    flat_rows = qbuf[...].reshape(count, width)
    got = jnp.zeros((3 * part, width), F32)
    for at in range(0, count, width):
        some = place_ref[pl.ds(p.d, 1), at : at + width]
        placing = (iota((3 * part, some.shape[1]), 0) == some).astype(BF16)
        got = got + mm(placing, flat_rows[at : at + width], NN)
    wqkvt_ref[...] = got.astype(BF16)
    own_tokens.wait()

    def chunk(i):
        q = jnp.where(
            i < 2, p.d, jnp.where(i < 4, p.sib_d, jnp.where(i % 2 == 0, p.far_d, p.diag_d))
        )
        s = jnp.where(i < 4, i % 2, (i - 4) // 2)
        return q, s, pl.ds(pl.multiple_of(q * quarter, quarter), quarter)

    def keeps(i):
        _, s, rows = chunk(i)
        return [
            pltpu.make_async_copy(src.at[s, rows], dst.at[s, rows], local.at[k])
            for k, (src, dst) in enumerate(((qkv_ref, qkv_out), (normed_ref, normed_out)))
        ]

    @pl.loop(0, m * slots)
    def _(i):
        for k in range(2):

            @pl.when(i == 2 + k)
            def _(k=k):
                token_copy(0, 2 * k).wait_recv()
                token_copy(0, 2 * k + 1).wait_recv()

            @pl.when(i == 5 + 2 * k)
            def _(k=k):
                token_copy(2, 2 * k).wait_recv()
                token_copy(2, 2 * k + 1).wait_recv()

        pl.when(i == 2)(lambda: out.step(1))
        pl.when(i == 4)(lambda: pass_on(3))

        q, s, rows = chunk(i)
        normal, _ = norm_rows(tall_ref[q, s].astype(F32))
        shift = mod_ref[s, :, :width]
        scale = mod_ref[s, :, width : 2 * width]
        normed = (normal * (gain * (1.0 + scale)) + shift).astype(BF16)
        normed_ref[s, rows, :] = normed
        got = mm(normed, wqkvt_ref[...], NT)
        cosine = cos_ref[rows, :]
        sine = sin_ref[rows, :]
        lanes = iota((quarter, 128), 1)
        for t in range(0, 2 * part, 128):
            piece = got[:, t : t + 128]
            piece = piece * cosine + turned(piece) * sine
            piece = jnp.where(lanes + t < part, piece * (1.0 / math.sqrt(HEAD)), piece)
            qkv_ref[s, rows, t : t + 128] = piece.astype(BF16)
        qkv_ref[s, rows, 2 * part :] = got[:, 2 * part :].astype(BF16)
        for keep in keeps(i):
            keep.start()

    def att_copy(kind, s):
        return push(
            att_v.at[s, ranks[kind]], arecv.at[s, p.d], as_.at[kind, s], ar.at[kind, s], peers[kind]
        )

    def swap(h):
        return push(obuf.at[:, h], obuf.at[:, h], os_.at[0], or_.at[0], p.sib)

    def weight_ready():
        out.finish()
        if halves == 2:
            swap(p.c).start()
            swap(1 - p.c).wait_recv()
        if filled:
            qry.drain()
        if small < osrc.shape[0]:
            dense[0][...] = compact(obuf[:, 0], small)

    def group(s, k):
        return mod_ref[s, :, k * width : (k + 1) * width]

    gain_mlp = vecs_ref[2:3, :width]
    b_down = vecs_ref[3:4, :width]
    if small < osrc.shape[0]:
        w_out = lambda: dense[0][...]
    else:
        w_out = lambda: obuf[...].reshape(width, width)
    if pad > hidden_per:
        w_up = lambda: dense[1][...]
    else:
        w_up = lambda: ubuf[...].reshape(inner, width)
    if small < block:
        w_down = lambda: dense[2][...]
    else:
        w_down = lambda: dbuf[...].reshape(width, inner)

    def nm_copy(kind, s, h):
        k = s * 2 + h
        rows = nm_ref.at[p.far_d if kind == 2 else p.d, s, pl.ds(h * half, half)]
        return push(rows, rows, n_s.at[kind, k], n_r.at[kind, k], p.far if kind == 1 else p.sib)

    def enter(s):
        for kind in range(3):
            att_copy(kind, s).wait_recv()
        arecv[s, p.d] = att_v[s, p.d]
        for r in range(m):
            for h in range(2):
                own_ref[s, h * half : (h + 1) * half, r * part : (r + 1) * part] = arecv[
                    s, r, :, h * part : (h + 1) * part
                ]
        branch = mm(own_ref[s], w_out(), NT)
        br_ref[s] = branch
        middle = tall_ref[p.d, s].astype(F32) + group(s, 2) * branch
        mid_ref[s] = middle
        normal, inverse = norm_rows(middle)
        nrm_ref[s] = normal
        inv_ref[s] = inverse
        nm_ref[p.d, s] = (normal * (gain_mlp * (1.0 + group(s, 4))) + group(s, 3)).astype(BF16)
        for kind in (1, 0):
            for h in range(2):
                nm_copy(kind, s, h).start()

    def pass_rows(s):
        for h in range(2):
            nm_copy(1, s, h).wait_recv()
            nm_copy(2, s, h).start()

    def arrived(kind, s):
        for h in range(2):
            nm_copy(kind, s, h).wait_recv()

    for k in range(2, p.lines):
        out.step(k)
    up.step(1)
    tiles = length // tile

    @pl.loop(0, slots * tiles)
    def _(i):
        s = i // tiles
        rows = pl.ds(pl.multiple_of(i % tiles * tile, tile), tile)
        same = as_column(seg_ref[pl.ds(s, 1), :]) == seg_ref[pl.ds(s, 1), rows]
        ones = jnp.ones((length, HEAD), BF16)
        for h in range(heads):
            at = h * HEAD
            q = qkv_ref[s, rows, at : at + HEAD]
            k = qkv_ref[s, :, part + at : part + at + HEAD]
            v = qkv_ref[s, :, 2 * part + at : 2 * part + at + HEAD]
            scores = jnp.where(same, mm(k, q, NT), MASKED)
            largest = jnp.max(scores, axis=0, keepdims=True)
            weights = jnp.exp(scores - largest)
            log_v[s, h : h + 1, rows] = largest + jnp.log(jnp.sum(weights, axis=0, keepdims=True))
            result = mm(weights.astype(BF16), jnp.concatenate([v, ones], axis=1), TN)
            result = (result[:, :HEAD] / result[:, HEAD : HEAD + 1]).astype(BF16)
            for j in range(tile // half):
                att_v[s, i % tiles * (tile // quarter) + j // 2, :, j % 2 * part + at : j % 2 * part + at + HEAD] = (
                    result[j * half : (j + 1) * half]
                )
        for k in range(2, p.lines):
            pl.when(i == k - 2)(lambda k=k: up.step(k))

        @pl.when(i == tiles - 1)
        def _():
            for kind in (2, 1, 0):
                att_copy(kind, 0).start()
            weight_ready()
            down.start()

        @pl.when(i == tiles)
        def _():
            enter(0)
            down.step(1)

        @pl.when(i == slots * tiles - 1)
        def _():
            for s in range(1, slots):
                for kind in (2, 1, 0):
                    att_copy(kind, s).start()

    for k in range(slots * tiles + 2, p.lines):
        up.step(k)
    stores = []

    def store(src, dst):
        stores.append(pltpu.make_async_copy(src, dst, local.at[5 + len(stores)]))
        stores[-1].start()

    store(att_v, att_out)
    store(log_v, log_out)
    for k, (src, dst) in enumerate(((qkv_ref, qkv_out), (normed_ref, normed_out))):
        pltpu.make_async_copy(src, dst, local.at[k]).wait()
    for k in range(2 * slots):
        token_copy(2, k).wait_send()
    for copy in own_cots:
        copy.wait()
    for k in range(2, p.lines):
        down.step(k)
    pass_rows(0)
    for s in range(slots):
        cot_copy(0, s).wait_recv()
        cot_copy(2, s).start()
        cot_copy(1, s).start()
    for s in range(1, slots):
        enter(s)
    up.finish()
    if pad > hidden_per:
        dense[1][...] = compact(ubuf[...], hidden_per)
    down.finish()
    if small < block:
        dense[2][...] = compact(dbuf[...], small)
    for s in range(slots):
        cot_copy(1, s).wait_recv()
        cot_copy(2, s).wait_recv()
        cot_copy(2, s).wait_send()

    def expand(q, s):
        hidden = mm(nm_ref[q, s], w_up(), NT) + vecs_ref[0:1, :inner]
        value, slope = gelu_parts(hidden)
        act_ref[q, s] = value.astype(BF16)
        gp_ref[q, s] = slope.astype(BF16)

    dbup_ref[...] = jnp.zeros_like(dbup_ref)

    def pull(q, s):
        g = (ct_ref[q, s].astype(F32) * group(s, 5)).astype(BF16)
        ct_ref[q, s] = g
        grad = (mm(g, w_down(), NN) * gp_ref[q, s].astype(F32)).astype(BF16)
        gp_ref[q, s] = grad
        dbup_ref[0:1, :] += jnp.sum(grad.astype(F32), axis=0, keepdims=True)
        gsc[...] = mm(grad, w_up(), NN)

    def part_copy(kind, s):
        if kind == 4:
            return push(xs_ref.at[s], xr_ref.at[s], p_s.at[4, s], p_r.at[4, s], p.far)
        return push(psend.at[kind, s], precv.at[kind, s], p_s.at[kind, s], p_r.at[kind, s], p.sib)

    def far_rows(s):
        @pl.loop(0, 2)
        def _(i):
            first = i == 0
            pl.when(first)(lambda: arrived(2, s))
            q = jnp.where(first, p.diag_d, p.far_d)
            expand(q, s)
            pull(q, s)

            @pl.when(first)
            def _():
                psend[0, s] = gsc[...].astype(BF16)
                part_copy(0, s).start()

            @pl.when(jnp.logical_not(first))
            def _():
                part_copy(0, s).wait_recv()
                xs_ref[s] = (gsc[...] + precv[0, s].astype(F32)).astype(BF16)
                part_copy(4, s).start()

    far_rows(0)

    @pl.loop(0, 2 * slots)
    def _(i):
        s = i % slots
        pl.when(i >= slots)(lambda: arrived(0, s))
        expand(jnp.where(i < slots, p.d, p.sib_d), s)

    for s in range(1, slots):
        pass_rows(s)
        far_rows(s)

    @pl.loop(0, 2 * slots)
    def _(i):
        s = i // 2
        first = i % 2 == 0
        pull(jnp.where(first, p.sib_d, p.d), s)

        @pl.when(first)
        def _():
            psend[1, s] = gsc[...].astype(BF16)
            part_copy(1, s).start()

        @pl.when(jnp.logical_not(first))
        def _():
            gn_ref[s] = gsc[...]

    def weight_grad(left, right, out_ref, step=128):

        @pl.loop(0, left.shape[1] // step)
        def _(i):
            at = pl.ds(pl.multiple_of(i * step, step), step)
            out_ref[at, :] = mm(left[:, at], right[...], TN).astype(BF16)

    every = lambda ref: ref.reshape(m * slots * quarter, ref.shape[3])
    weight_grad(every(ct_ref), every(act_ref), dwd_ref.at[:width], 256)
    if small < block:
        dwd_ref[...] = padded(dwd_ref[:width], n, block)
    dwd = dwd_ref.reshape(n, block, inner)
    red_down = Reduce(p, lambda f: dwd.at[f], side_d, total_d, None, rz)
    red_down.start()
    def grad_copy(kind, s):
        return push(
            gsend.at[s, ranks[kind]], grecv.at[s, p.d], g_s.at[kind, s], g_r.at[kind, s], peers[kind]
        )

    def leave(s):
        part_copy(1, s).wait_recv()
        part_copy(4, s).wait_recv()
        cot = cot_v[s].astype(F32)
        gn = gn_ref[s] + precv[1, s].astype(F32) + xr_ref[s].astype(F32)
        normal = nrm_ref[s]
        grad_middle = cot + norm_back(gn, normal, inv_ref[s], gain_mlp * (1.0 + group(s, 4)))
        gm_ref[s] = grad_middle
        gba = (grad_middle * group(s, 2)).astype(BF16)
        gba_ref[s] = gba
        gatt = mm(gba, w_out(), NN).astype(BF16)
        for r in range(m):
            for h in range(2):
                gsend[s, r, :, h * part : (h + 1) * part] = gatt[
                    h * half : (h + 1) * half, r * part : (r + 1) * part
                ]
        for kind in (2, 1, 0):
            grad_copy(kind, s).start()
        grecv[s, p.d] = gsend[s, p.d]
        total = lambda v: jnp.sum(v, axis=0, keepdims=True)
        sums_ref[s, 0:1, :] = total(gn)
        sums_ref[s, 1:2, :] = total(gn * normal)
        sums_ref[s, 3:4, :] = total(grad_middle * br_ref[s])
        sums_ref[s, 4:5, :] = total((cot * group(s, 5)).astype(BF16).astype(F32))
        sums_ref[s, 5:8, :] = jnp.zeros((3, width), F32)

    leave(0)
    weight_grad(every(gp_ref), every(nm_ref), dwu_ref.at[:inner])
    if pad > hidden_per:
        dwu_ref[...] = padded(dwu_ref[:inner], n, pad)

    store(dwu_ref.reshape(n, pad, width), dwu_out)

    for s in range(1, slots):
        leave(s)

    @pl.loop(0, 4 * slots)
    def _(i):
        s = i // 4
        j = i % 4
        q = jnp.where(
            j < 2, jnp.where(j == 0, p.diag_d, p.sib_d), jnp.where(j == 2, p.d, p.far_d)
        )
        gsc[...] = mm(act_ref[q, s], w_down(), NT)

        @pl.when(j == 0)
        def _():
            psend[2, s] = gsc[...].astype(BF16)
            part_copy(2, s).start()

        @pl.when(j == 1)
        def _():
            psend[3, s] = gsc[...].astype(BF16)
            part_copy(3, s).start()

        @pl.when(j == 2)
        def _():
            bo_ref[s] = gsc[...]

        @pl.when(j == 3)
        def _():
            part_copy(2, s).wait_recv()
            part_copy(4, s).wait_send()
            xs_ref[s] = (gsc[...] + precv[2, s].astype(F32)).astype(BF16)

    store(xs_ref, xsend_out)
    store(gm_ref, gm_out)
    flat = lambda ref: ref.reshape(slots * quarter, width)
    weight_grad(flat(gba_ref), flat(own_ref), dwo_ref.at[:width])
    if small < block:
        dwo_ref[...] = padded(dwo_ref[:width], n, block)
    rows = oswap.shape[1]
    dwo = dwo_ref.reshape(n, block // rows, rows, width)
    mine = p.c if rows < block else 0
    theirs = 1 - p.c if rows < block else 0
    dwo_swap = push(dwo.at[:, theirs], oswap, o_s.at[0], o_r.at[0], p.sib)
    dwo_swap.start()

    @pl.loop(0, slots)
    def _(s):
        part_copy(3, s).wait_recv()
        branch = bo_ref[s] + precv[3, s].astype(F32) + b_down
        mid_ref[s] = mid_ref[s] + group(s, 5) * branch
        sums_ref[s, 2:3, :] = jnp.sum(cot_v[s].astype(F32) * branch, axis=0, keepdims=True)

    store(mid_ref, base_out)
    for j in red_down.order():
        red_down.side_sum(j)
    store(total_d, downtotal_out)
    dwo_swap.wait_recv()
    oswap[...] = (dwo[:, mine].astype(F32) + oswap[...].astype(F32)).astype(BF16)
    store(oswap, outsum_out)
    for s in range(slots):
        for kind in range(3):
            grad_copy(kind, s).wait_recv()
    store(grecv, gatt_out)

    vec.drain()
    mods.drain()
    for item in (out, up, down) if filled else (qry, out, up, down):
        item.drain()
    if halves == 2:
        swap(p.c).wait_send()
    for k in range(2 * slots):
        for kind in range(2):
            token_copy(kind, k).wait_send()
    for j in range(p.lines):
        red_down.side_copy(j).wait_send()
    dwo_swap.wait_send()
    for s in range(slots):
        for kind in range(2):
            cot_copy(kind, s).wait_send()
        for kind in range(3):
            att_copy(kind, s).wait_send()
            grad_copy(kind, s).wait_send()
            for h in range(2):
                nm_copy(kind, s, h).wait_send()
        for kind in range(4):
            part_copy(kind, s).wait_send()
    for copy in stores:
        copy.wait()


def padded(rows, count, block):
    per = rows.shape[0] // count
    want = iota((count * block, rows.shape[0]), 0)
    have = iota((count * block, rows.shape[0]), 1)
    chosen = (have == want // block * per + want % block) & (want % block < per)
    return mm(chosen.astype(BF16), rows, NN).astype(BF16)


def front(n, m, length, tile, most, args):
    tokens, cond = args[0], args[2]
    w_ada, b_up = args[4], args[6]
    slots, quarter, width = tokens.shape
    part = width // m
    lines = n // 2
    dma = pltpu.SemaphoreType.DMA
    shape = jax.ShapeDtypeStruct
    vmem = pltpu.VMEM
    hidden_per = b_up.shape[0] // m
    small = width // n
    block = round16(small)
    pad = round16(hidden_per)
    inner = n * hidden_per
    halves = 2 if block % 32 == 0 else 1
    swapped = block // halves
    rows = (slots, quarter, width)
    att = (slots, m, quarter // 2, 2 * part)
    assert inner == width
    return pl.pallas_call(
        functools.partial(front_kernel, n, m, (hidden_per, small), tile),
        out_shape=(
            shape((slots, length, 3 * part), BF16),
            shape((slots, length, width), BF16),
            shape(att, BF16),
            shape((slots, 8, length), F32),
            shape(rows, F32),
            shape(rows, F32),
            shape(rows, BF16),
            shape(att, BF16),
            shape((n, pad, width), BF16),
            shape((lines, block, inner), BF16),
            shape((n, swapped, width), BF16),
            shape((slots, 1, 6 * width), F32),
            shape((8, width), F32),
            shape((3 * part, width), BF16),
            shape((n, 16, 128), BF16),
            shape((8, inner), F32),
            shape((slots, 8, width), F32),
        ),
        in_specs=[ANY] * 2 + [VM] * (len(args) - 2),
        out_specs=(ANY,) * 11 + (VM,) * 6,
        scratch_shapes=[
            vmem((slots, length, 3 * part), BF16),
            vmem(att, BF16),
            vmem(att, BF16),
            vmem((slots, 8, length), F32),
            vmem((n, slots, w_ada.shape[0]), F32),
            vmem((n, slots, w_ada.shape[0]), F32),
            vmem((16, 128), BF16),
            vmem((n, 16, 128), BF16),
            vmem((most, width), BF16),
            vmem((n, most, width), BF16),
            vmem((block, width), BF16),
            vmem((n, halves, swapped, width), BF16),
            vmem((pad, width), BF16),
            vmem((n, pad, width), BF16),
            vmem((block, inner), BF16),
            vmem((n, block, inner), BF16),
            vmem(rows, BF16),
            vmem(rows, BF16),
            vmem(rows, F32),
            vmem(rows, F32),
            vmem(rows, F32),
            vmem((slots, quarter, 1), F32),
            vmem((m,) + rows, BF16),
            vmem((m,) + rows, BF16),
            vmem((m,) + rows, BF16),
            vmem((m,) + rows, BF16),
            vmem((quarter, width), F32),
            vmem((4,) + rows, BF16),
            vmem((4,) + rows, BF16),
            vmem(rows, BF16),
            vmem(rows, BF16),
            vmem(rows, F32),
            vmem(rows, F32),
            vmem(rows, BF16),
            vmem(rows, F32),
            vmem(att, BF16),
            vmem(att, BF16),
            vmem((n * block, inner), BF16),
            vmem((n * pad, width), BF16),
            vmem((n * block, width), BF16),
            vmem((n, swapped, width), BF16),
            vmem((lines, block, inner), BF16),
            vmem((lines, block, inner), BF16),
            dma((4,)),
            dma((5, 4 * lines + 1)),
            dma((3, 2 * slots)),
            dma((3, 2 * slots)),
            dma((1,)),
            dma((1,)),
            dma((3, slots)),
            dma((3, slots)),
            dma((3, slots)),
            dma((3, slots)),
            dma((3, 2 * slots)),
            dma((3, 2 * slots)),
            dma((5, slots)),
            dma((5, slots)),
            dma((3, slots)),
            dma((3, slots)),
            dma((4 * lines + 1,)),
            dma((1,)),
            dma((1,)),
            dma((16,)),
        ],
        compiler_params=pltpu.CompilerParams(
            collective_id=1, has_side_effects=True, vmem_limit_bytes=LIMIT
        ),
        name="front",
    )(*args)


def back_kernel(
    n,
    m,
    per,
    tile,
    q_few,
    qkv_ref,
    grad_ref,
    att_ref,
    normed_ref,
    tok_ref,
    gm_ref,
    xsend_ref,
    cot_ref,
    dwu_ref,
    downtotal_ref,
    outsum_ref,
    log_ref,
    seg_ref,
    cos_ref,
    sin_ref,
    wqkvt_ref,
    mod_ref,
    vec_ref,
    sums_ref,
    vblk_ref,
    wada_ref,
    dbup_ref,
    place_ref,
    dtok_out,
    other_out,
    down_out,
    up_out,
    wo_out,
    q_out,
    dcond_ref,
    dwada_ref,
    dbada_ref,
    dvec_ref,
    qkv_v,
    grad_v,
    att_v,
    gq_v,
    dk_ref,
    dv_ref,
    normed_v,
    tok_v,
    gm_v,
    other_v,
    cot_v,
    dtok_v,
    gsc,
    psend,
    precv,
    xs_ref,
    xr_ref,
    gn_ref,
    dwq_ref,
    dwu_v,
    outsum_v,
    total_d,
    zrecv_d,
    side_u,
    total_u,
    zrecv_u,
    side_o,
    total_o,
    zrecv_o,
    q_parts,
    q_sides,
    q_totals,
    q_zrecvs,
    spr_d,
    spr_u,
    spr_q,
    opiece,
    ofar,
    ofin,
    ssend,
    srecv,
    gsend,
    grecv,
    vsend,
    vrecv,
    dsend,
    drecv,
    p_s,
    p_r,
    rz,
    d_s,
    d_r,
    s_s,
    s_r,
    ex,
    x_s,
    x_r,
    local,
):
    p = Place(n, m)
    hidden_per, small = per
    slots, quarter, width = tok_ref.shape
    length = m * quarter
    half = quarter // 2
    part = width // m
    heads = part // HEAD
    lines = p.lines
    peers = (p.sib, p.far, p.diag)
    loads = [
        pltpu.make_async_copy(src, dst, local.at[k])
        for k, (src, dst) in enumerate(
            (
                (qkv_ref, qkv_v),
                (grad_ref, grad_v),
                (att_ref, att_v),
                (downtotal_ref, total_d),
                (dwu_ref, dwu_v),
                (outsum_ref, outsum_v),
                (normed_ref, normed_v),
                (tok_ref, tok_v),
                (gm_ref, gm_v),
                (cot_ref, cot_v),
            )
        )
    ]
    for load in loads:
        load.start()
    greet(list(peers) + p.ring())

    def other_copy(s):
        return push(xsend_ref.at[s], other_v.at[s], x_s.at[s], x_r.at[s], p.far)

    def part_copy(kind, s):
        if kind == 2:
            return push(xs_ref.at[s], xr_ref.at[s], p_s.at[2, s], p_r.at[2, s], p.far)
        return push(psend.at[kind, s], precv.at[kind, s], p_s.at[kind, s], p_r.at[kind, s], p.sib)

    for s in range(slots):
        other_copy(s).start()
    red_d = Reduce(p, None, None, total_d, zrecv_d, rz.at[0], summed=True)
    red_u = Reduce(p, lambda f: dwu_v.at[f], side_u, total_u, zrecv_u, rz.at[1])
    red_o = Reduce(p, lambda f: outsum_v.at[f], side_o, total_o, zrecv_o, rz.at[2])
    cuts = [ref.shape[1] for ref in q_parts]
    red_q = [
        Reduce(
            p,
            (lambda f, k=k: q_parts[k].at[f % 2]) if few else (lambda f, k=k: q_parts[k].at[f]),
            q_sides[k],
            q_totals[k],
            q_zrecvs[k],
            rz.at[3 + k],
            only=p.d if few else None,
        )
        for k, few in enumerate(q_few)
    ]
    down = Spread(p, lambda r: spr_d.at[r], d_s.at[0], d_r.at[0])
    up = Spread(p, lambda r: spr_u.at[r], d_s.at[1], d_r.at[1])
    firsts = [sum(cuts[:k]) for k in range(len(cuts))]
    qry = [
        Spread(
            p,
            lambda r, k=k: spr_q.at[r, pl.ds(firsts[k], cuts[k])],
            d_s.at[2 + k],
            d_r.at[2 + k],
        )
        for k in range(len(cuts))
    ]
    loads[4].wait()
    red_u.start()
    loads[3].wait()
    red_d.step(0)
    for k in (0, 1, 2):
        loads[k].wait()
    tiles = length // tile

    @pl.loop(0, slots)
    def _(s):
        dk_ref[...] = jnp.zeros_like(dk_ref)
        dv_ref[...] = jnp.zeros_like(dv_ref)
        column = as_column(seg_ref[pl.ds(s, 1), :])

        @pl.loop(0, tiles)
        def _(i):
            rows = pl.ds(pl.multiple_of(i * tile, tile), tile)
            same = column == seg_ref[pl.ds(s, 1), rows]
            cosine = cos_ref[rows, :HEAD]
            sine = sin_ref[rows, :HEAD]
            ones = jnp.ones((8, HEAD), BF16)
            for h in range(heads):
                at = h * HEAD
                q = qkv_v[s, rows, at : at + HEAD]
                k = qkv_v[s, :, part + at : part + at + HEAD]
                v = qkv_v[s, :, 2 * part + at : 2 * part + at + HEAD]
                g, o = [
                    jnp.concatenate(
                        [
                            ref[s, i * (tile // quarter) + j // 2, :, j % 2 * part + at : j % 2 * part + at + HEAD]
                            for j in range(tile // half)
                        ]
                    )
                    for ref in (grad_v, att_v)
                ]
                both = g.astype(F32) * o.astype(F32)
                high = both.astype(BF16)
                low = (both - high.astype(F32)).astype(BF16)
                inner = (mm(ones, high, NT) + mm(ones, low, NT))[:1]
                scores = jnp.where(same, mm(k, q, NT), MASKED)
                weights = jnp.exp(scores - log_ref[s, h : h + 1, rows])
                dots = mm(v, g, NT)
                dscores = (weights * (dots - inner)).astype(BF16)
                dq = mm(dscores, k, TN) * (1.0 / math.sqrt(HEAD))
                gq_v[s, rows, at : at + HEAD] = (dq * cosine - swap_halves(dq) * sine).astype(BF16)
                dk_ref[:, at : at + HEAD] += mm(dscores, q, NN)
                dv_ref[:, at : at + HEAD] += mm(weights.astype(BF16), g, NN)

            def reductions(first, red, steps):
                spread = -(-len(steps) // tiles)
                for k, t in enumerate(steps):
                    pl.when((s == first) & (i == k // spread))(lambda t=t: red.step(t))

            reductions(0, red_d, range(1, lines - 1))
            reductions(1, red_u, range(1, lines - 1))
            reductions(1, red_o, range(lines - 2))
            pl.when((s == 1) & (i == 0))(down.start)

        for at in range(0, part, 128):
            size = min(128, part - at)
            dk = dk_ref[:, at : at + size]
            other = turned(dk) if size == 128 else swap_halves(dk)
            dk = dk * cos_ref[:, :size] - other * sin_ref[:, :size]
            gq_v[s, :, part + at : part + at + size] = dk.astype(BF16)
        gq_v[s, :, 2 * part :] = dv_ref[...].astype(BF16)

        theirs = pl.ds(pl.multiple_of((1 - p.c) * quarter, quarter), quarter)
        ours = pl.ds(pl.multiple_of(p.c * quarter, quarter), quarter)

        def pull(j, chip):
            rows = pl.ds(pl.multiple_of(chip * 2 * quarter, 2 * quarter), 2 * quarter)
            gsc[...] = mm(gq_v[s, rows, :], wqkvt_ref[...], NN)
            psend[j, s] = gsc[theirs].astype(BF16)
            part_copy(j, s).start()

        pull(0, 1 - p.x)
        gn_ref[s] = gsc[ours]
        pull(1, p.x)
        part_copy(0, s).wait_recv()
        xs_ref[s] = (gn_ref[s] + precv[0, s].astype(F32)).astype(BF16)
        part_copy(2, s).start()
        gn_ref[s] = gsc[ours]

        @pl.when(s == 0)
        def _():
            loads[5].wait()
            red_o.start()
            red_d.own(spr_d.at[p.d])
            red_u.step(0)

    red_o.step(lines - 2)
    loads[6].wait()
    every = slots * length
    gq_all = gq_v.reshape(every, gq_v.shape[2])
    normed_all = normed_v.reshape(every, width)
    for at in range(0, gq_v.shape[2], part):
        dwq_ref[at : at + part, :] = mm(gq_all[:, at : at + part], normed_all[...], TN).astype(BF16)
    count = place_ref.shape[1]
    placing = (iota((dwq_ref.shape[0], count), 0) == place_ref[pl.ds(p.d, 1), :]).astype(BF16)
    blocks = mm(placing, dwq_ref[...], TN).astype(BF16)
    at = 0
    for ref in q_parts:
        size = ref.shape[0] * ref.shape[1]
        ref[...] = blocks[at : at + size].reshape(ref.shape)
        at += size
    for red in (*red_q[2:], red_q[0]):
        red.start()
    red_u.own(spr_u.at[p.d])
    red_o.own(opiece)
    halved = ofin.shape[0] == 2
    mine = p.c if halved else 0
    o_far = push(opiece, ofar, d_s.at[5, 0], d_r.at[5, 0], p.far)
    for red in red_q[1:2]:
        red.start()

    def group(s, k):
        return mod_ref[s, :, k * width : (k + 1) * width]

    gain_attn = vec_ref[1:2, :width]
    gain_mlp = vec_ref[2:3, :width]
    wide = dbup_ref.shape[1]
    total_rows = lambda v: jnp.sum(v, axis=0, keepdims=True)
    for k in range(7, 10):
        loads[k].wait()
    ssend[...] = jnp.zeros_like(ssend)

    def leave(s):
        other_copy(s).wait_recv()
        part_copy(1, s).wait_recv()
        part_copy(2, s).wait_recv()
        gn = gn_ref[s] + precv[1, s].astype(F32) + xr_ref[s].astype(F32)
        normal, inverse = norm_rows(tok_v[s].astype(F32))
        dtok_v[s] = (
            gm_v[s] + norm_back(gn, normal, inverse, gain_attn * (1.0 + group(s, 1)))
        ).astype(BF16)
        extra = total_rows(cot_v[s].astype(F32) * other_v[s].astype(F32))
        ssend[s, 0:1, :width] = total_rows(gn)
        ssend[s, 1:2, :width] = total_rows(gn * normal)
        ssend[s, 2:3, :width] = sums_ref[s, 3:4, :]
        ssend[s, 3:5, :width] = sums_ref[s, 0:2, :]
        ssend[s, 5:6, :width] = sums_ref[s, 2:3, :] + extra
        ssend[s, 6:7, :width] = sums_ref[s, 4:5, :]

    ssend[0, 7:8, :wide] = dbup_ref[0:1, :]
    leave(0)
    hops = [(k, t) for t in range(lines - 1) for k in reversed(range(len(cuts)))]
    hops = hops[: -len(cuts)], hops[-len(cuts) :]
    red_q[-1].step(0)
    for s in range(1, slots):
        leave(s)

    def sums_copy(kind):
        return push(ssend, srecv.at[p.d], s_s.at[kind], s_r.at[kind], peers[kind])

    for kind in (2, 1, 0):
        sums_copy(kind).start()
    o_far.start()
    up.start()
    srecv[p.d] = ssend[...]
    stores = []

    def store(src, dst):
        stores.append(pltpu.make_async_copy(src, dst, local.at[10 + len(stores)]))
        stores[-1].start()

    store(dtok_v, dtok_out)
    store(other_v, other_out)
    for k, t in hops[0][1:]:
        red_q[k].step(t)
    for kind in range(3):
        sums_copy(kind).wait_recv()
    total = srecv[0]
    for r in range(1, m):
        total = total + srecv[r]
    cols = wada_ref.shape[0]
    gmod = []
    vecs = [jnp.zeros((1, width), F32)] * 3
    for s in range(slots):
        at = lambda k, s=s: total[s, k : k + 1, :width]
        gmod.append(
            jnp.concatenate(
                [at(0), at(1) * gain_attn, at(2), at(3), at(4) * gain_mlp, at(5)], axis=1
            )
        )
        vecs = [
            vecs[0] + at(1) * (1.0 + group(s, 1)),
            vecs[1] + at(4) * (1.0 + group(s, 4)),
            vecs[2] + at(6),
        ]
    gmod = jnp.concatenate(gmod, axis=0).astype(BF16).astype(F32)
    vsend[...] = jnp.zeros_like(vsend)
    pad = hidden_per
    for g in range(n):
        gsend[g] = gmod[:, g * cols : (g + 1) * cols]
        for k, v in enumerate(vecs):
            vsend[g, k : k + 1, :small] = v[:, g * small : (g + 1) * small]
        for r in range(m):
            vsend[g, 3 + r : 4 + r, :hidden_per] = srecv[r, 0, 7:8, g * pad : g * pad + hidden_per]

    gmods = Exchange(p, lambda f: gsend.at[f], grecv, ex.at[0], ex.at[1])
    gvecs = Exchange(p, lambda f: vsend.at[f], vrecv, ex.at[2], ex.at[3])
    gmods.start()
    gvecs.start()
    grecv[p.f] = gsend[p.f]
    vrecv[p.f] = vsend[p.f]
    down.forward()
    for k, t in hops[1]:
        red_q[k].step(t)
    up.forward()
    for k in reversed(range(len(cuts))):
        red_q[k].own(qry[k].slot(p.d))
        qry[k].start()
    gmods.finish()
    got = jnp.concatenate([grecv[g] for g in range(n)], axis=0).astype(BF16)
    conds = jnp.concatenate([vblk_ref[g, 4 : 4 + slots] for g in range(n)], axis=0)
    dsend[...] = mm(got, wada_ref[...], NN).reshape(n, slots, conds.shape[1])

    gconds = Exchange(p, lambda f: dsend.at[f], drecv, ex.at[4], ex.at[5])
    gconds.start()
    drecv[p.f] = dsend[p.f]
    o_far.wait_recv()
    ofin[mine] = (opiece[...].astype(F32) + ofar[...].astype(F32)).astype(BF16)
    if halved:
        o_sib = push(ofin.at[mine], ofin.at[mine], d_s.at[5, 1], d_r.at[5, 1], p.sib)
        o_sib.start()
    dwada_ref[...] = mm(got, conds, TN)
    dbada_ref[...] = jnp.sum(got.astype(F32), axis=0, keepdims=True)
    gvecs.finish()
    total = vrecv[0]
    for g in range(1, n):
        total = total + vrecv[g]
    dvec_ref[...] = total
    down.finish()
    store(spr_d, down_out)
    up.finish()
    store(spr_u, up_out)
    if halved:
        push(ofin.at[1 - mine], ofin.at[1 - mine], d_s.at[5, 1], d_r.at[5, 1], p.sib).wait_recv()
    store(ofin, wo_out)
    gconds.finish()
    total = drecv[0]
    for g in range(1, n):
        total = total + drecv[g]
    dcond_ref[...] = total
    for spread in qry:
        spread.forward()
    for spread in qry:
        spread.finish()
    store(spr_q, q_out)

    for s in range(slots):
        other_copy(s).wait_send()
        for kind in range(3):
            part_copy(kind, s).wait_send()
    for red in (red_d, red_u, red_o, *red_q):
        red.drain()
    for spread in (down, up, *qry):
        spread.drain()
    o_far.wait_send()
    if halved:
        o_sib.wait_send()
    for kind in range(3):
        sums_copy(kind).wait_send()
    for exchange in (gmods, gvecs, gconds):
        exchange.drain()
    for copy in stores:
        copy.wait()


def back(n, m, per, tile, parts, args):
    qkv, grad, att, normed, tokens = args[:5]
    dwu, downtotal, outsum = args[8:11]
    vblk, w_ada, dbup, place = args[19:23]
    slots, quarter, width = tokens.shape
    dma = pltpu.SemaphoreType.DMA
    shape = jax.ShapeDtypeStruct
    vmem = pltpu.VMEM
    rows = (slots, quarter, width)
    length = m * quarter
    part = width // m
    lines = n // 2
    wide = max(width, dbup.shape[1])
    _, block, inner = downtotal.shape
    pad = dwu.shape[1]
    orows = outsum.shape[1]
    halves = 2 if orows < block else 1
    most = sum(rows_k for rows_k, _ in parts)
    cols, cond = w_ada.shape
    lanes = max(per)

    def reduced(rows, wide):
        return [vmem((lines, rows, wide), BF16)] * 2 + [vmem((lines + 1, rows, wide), BF16)]

    return pl.pallas_call(
        functools.partial(back_kernel, n, m, per, tile, [few for _, few in parts]),
        out_shape=(
            shape(rows, BF16),
            shape(rows, BF16),
            shape((m, block, inner), BF16),
            shape((m, pad, width), BF16),
            shape((halves, orows, width), BF16),
            shape((m, most, width), BF16),
            shape((slots, cond), F32),
            shape((cols, cond), F32),
            shape((1, cols), F32),
            shape((8, lanes), F32),
        ),
        in_specs=[ANY] * 11 + [VM] * (len(args) - 11),
        out_specs=(ANY,) * 6 + (VM,) * 4,
        scratch_shapes=[
            vmem(qkv.shape, BF16),
            vmem(grad.shape, BF16),
            vmem(att.shape, BF16),
            vmem(qkv.shape, BF16),
            vmem((length, part), F32),
            vmem((length, part), F32),
            vmem(normed.shape, BF16),
            vmem(rows, BF16),
            vmem(rows, F32),
            vmem(rows, BF16),
            vmem(rows, BF16),
            vmem(rows, BF16),
            vmem((2 * quarter, width), F32),
            vmem((2,) + rows, BF16),
            vmem((2,) + rows, BF16),
            vmem(rows, BF16),
            vmem(rows, BF16),
            vmem(rows, F32),
            vmem((qkv.shape[2], width), BF16),
            vmem(dwu.shape, BF16),
            vmem(outsum.shape, BF16),
        ]
        + reduced(block, inner)[1:]
        + reduced(pad, width)
        + reduced(orows, width)
        + [
            [vmem((2 if few else n, rows_k, width), BF16) for rows_k, few in parts],
            [vmem((lines, rows_k, width), BF16) for rows_k, _ in parts],
            [vmem((lines, rows_k, width), BF16) for rows_k, _ in parts],
            [vmem((lines + 1, rows_k, width), BF16) for rows_k, _ in parts],
        ]
        + [
            vmem((m, block, inner), BF16),
            vmem((m, pad, width), BF16),
            vmem((m, most, width), BF16),
            vmem((orows, width), BF16),
            vmem((orows, width), BF16),
            vmem((halves, orows, width), BF16),
            vmem((slots, 8, wide), F32),
            vmem((m, slots, 8, wide), F32),
            vmem((n, slots, cols), F32),
            vmem((n, slots, cols), F32),
            vmem((n, 8, lanes), F32),
            vmem((n, 8, lanes), F32),
            vmem((n, slots, cond), F32),
            vmem((n, slots, cond), F32),
            dma((3, slots)),
            dma((3, slots)),
            dma((6, 4 * lines + 1)),
            dma((6, 3)),
            dma((6, 3)),
            dma((3,)),
            dma((3,)),
            dma((6,)),
            dma((slots,)),
            dma((slots,)),
            dma((24,)),
        ],
        compiler_params=pltpu.CompilerParams(
            collective_id=3, has_side_effects=True, vmem_limit_bytes=LIMIT
        ),
        name="back",
    )(*args)


def finish_kernel(
    n,
    m,
    per,
    base_ref,
    other_ref,
    dtok_ref,
    dwada_ref,
    down_ref,
    up_ref,
    wo_ref,
    q_ref,
    mod_ref,
    dcond_ref,
    dbada_ref,
    dvec_ref,
    home_ref,
    out_ref,
    dtok_out,
    dwada_out,
    dwqkv_ref,
    dwout_ref,
    dwup_ref,
    dwdown_ref,
    dcond_out,
    dbada_out,
    dga_out,
    dgm_out,
    dbup_out,
    dbdown_out,
    up_v,
    down_v,
    q_v,
    wo_v,
    base_v,
    other_v,
    dtok_v,
    dwada_v,
    dwup_v,
    dwdown_v,
    dwqkv_v,
    dwout_v,
    out_v,
    local,
):
    hidden_per, small = per
    slots, _, width = base_ref.shape
    pad = hidden_per
    part = width // m
    sources = (up_ref, down_ref, q_ref, wo_ref, base_ref, other_ref, dtok_ref, dwada_ref)
    places = (up_v, down_v, q_v, wo_v, base_v, other_v, dtok_v, dwada_v)
    loads = [
        pltpu.make_async_copy(src, dst, local.at[k])
        for k, (src, dst) in enumerate(zip(sources, places))
    ]
    for load in loads:
        load.start()
    stores = []

    def store(src, dst):
        stores.append(pltpu.make_async_copy(src, dst, local.at[8 + len(stores)]))
        stores[-1].start()

    loads[0].wait()
    dwup_v[...] = jnp.concatenate([up_v[r][:hidden_per] for r in range(m)]).astype(F32).T
    store(dwup_v, dwup_ref)
    loads[1].wait()
    for r in range(m):
        piece = down_v[r, :small].astype(F32)
        for g in range(n):
            at = (g * m + r) * hidden_per
            dwdown_v[:, at : at + hidden_per] = piece[:, g * pad : g * pad + hidden_per]
    store(dwdown_v, dwdown_ref)
    loads[2].wait()
    count = q_v.shape[0] * q_v.shape[1]
    f = lax.axis_index("fsdp")
    homing = (iota((dwqkv_ref.shape[0], count), 0) == home_ref[pl.ds(f, 1), :]).astype(BF16)
    dwqkv_v[...] = mm(homing, q_v[...].reshape(count, width), NN)
    store(dwqkv_v, dwqkv_ref)
    for k in (4, 5):
        loads[k].wait()
    for s in range(slots):
        gate = mod_ref[s, :, 5 * width :]
        out_v[s] = (base_v[s] + gate * other_v[s].astype(F32)).astype(BF16)
    store(out_v, out_ref)
    for k, src, dst in ((6, dtok_v, dtok_out), (7, dwada_v, dwada_out)):
        loads[k].wait()
        store(src, dst)
    loads[3].wait()
    piece = wo_v[...].reshape(-1, width)[:small].astype(F32)
    heads = part // HEAD
    for r in range(m):
        for h in range(heads):
            at = r * part + h * HEAD
            dwout_v[:, (h * m + r) * HEAD : (h * m + r + 1) * HEAD] = piece[:, at : at + HEAD]
    store(dwout_v, dwout_ref)
    dcond_out[...] = dcond_ref[...].astype(BF16)
    dbada_out[...] = dbada_ref[0, :]
    for row, ref in ((0, dga_out), (1, dgm_out), (2, dbdown_out)):
        ref[...] = dvec_ref[row, :small]
    dbup_out[...] = jnp.concatenate(
        [dvec_ref[3 + r : 4 + r, :hidden_per] for r in range(m)], axis=1
    ).reshape(-1)
    for copy in stores:
        copy.wait()


def finish(n, m, per, columns, args):
    base, other, dtok, dwada, down, up, wo, q, _, dcond, dbada = args[:11]
    hidden_per, small = per
    rows = base.shape
    width = rows[2]
    shape = jax.ShapeDtypeStruct
    vmem = pltpu.VMEM
    sizes = (
        (width, m * hidden_per),
        (small, n * m * hidden_per),
        (columns, width),
        (small, width),
    )
    return pl.pallas_call(
        functools.partial(finish_kernel, n, m, per),
        out_shape=(
            shape(rows, BF16),
            shape(rows, BF16),
            shape(dwada.shape, F32),
            shape(sizes[2], F32),
            shape(sizes[3], F32),
            shape(sizes[0], F32),
            shape(sizes[1], F32),
            shape(dcond.shape, BF16),
            shape(dbada.shape[1:], F32),
            shape((small,), F32),
            shape((small,), F32),
            shape((m * hidden_per,), F32),
            shape((small,), F32),
        ),
        in_specs=[ANY] * 8 + [VM] * 5,
        out_specs=(ANY,) * 7 + (VM,) * 6,
        scratch_shapes=[
            vmem(up.shape, BF16),
            vmem(down.shape, BF16),
            vmem(q.shape, BF16),
            vmem(wo.shape, BF16),
            vmem(rows, F32),
            vmem(rows, BF16),
            vmem(rows, BF16),
            vmem(dwada.shape, F32),
        ]
        + [vmem(size, F32) for size in sizes]
        + [vmem(rows, BF16), pltpu.SemaphoreType.DMA((15,))],
        compiler_params=pltpu.CompilerParams(vmem_limit_bytes=LIMIT),
        name="finish",
    )(*args)


def column_plan(shards_n, ranks, columns):
    per = columns // shards_n
    rank_of = (np.arange(columns) // HEAD) % ranks
    lists = [
        [[c for c in range(per) if rank_of[f * per + c] == r] for r in range(ranks)]
        for f in range(shards_n)
    ]
    most = max(len(l) for row in lists for l in row)
    most = -(-most // 16) * 16
    take = np.full((shards_n, ranks, most), -1, np.int32)
    place = np.full((ranks, shards_n * most), -1, np.int32)
    home = np.full((shards_n, ranks * most), -1, np.int32)
    for r in range(ranks):
        order = {c: i for i, c in enumerate(np.flatnonzero(rank_of == r))}
        for f in range(shards_n):
            for i, c in enumerate(lists[f][r]):
                take[f, r, i] = c
                place[r, f * most + i] = order[f * per + c]
                home[f, r * most + i] = c
    return most, take, place, home


def row_parts(shards_n, ranks, columns):
    per = columns // shards_n
    rank_of = (np.arange(columns) // HEAD) % ranks
    lists = [
        [[c for c in range(per) if rank_of[f * per + c] == r] for r in range(ranks)]
        for f in range(shards_n)
    ]
    most = max(len(l) for row in lists for l in row)
    least = min(len(l) for row in lists for l in row)
    uneven = all(
        len(lists[f][r]) == (most if f // 2 == r else least)
        for f in range(shards_n)
        for r in range(ranks)
    )
    if uneven and least % 32 == 0 and (most - least) % 16 == 0 and most > least and shards_n == 2 * ranks:
        parts = [(least // 2, False), (least // 2, False), (most - least, True)]
    else:
        parts = [(round16(most), False)]
    place = []
    for r in range(ranks):
        order = {c: i for i, c in enumerate(np.flatnonzero(rank_of == r))}
        row, first = [], 0
        for rows, few in parts:
            for f in (2 * r, 2 * r + 1) if few else range(shards_n):
                own = lists[f][r][first : first + rows]
                row += [order[f * per + c] for c in own] + [-1] * (rows - len(own))
            first += rows
        place.append(row)
    home = []
    for f in range(shards_n):
        row = []
        for r in range(ranks):
            first = 0
            for rows, few in parts:
                own = lists[f][r][first : first + rows]
                row += own + [-1] * (rows - len(own))
                first += rows
        home.append(row)
    return parts, np.asarray(place, np.int32), np.asarray(home, np.int32)


def shards(
    tokens,
    condition,
    segments,
    w_ada,
    b_ada,
    gain_attn,
    w_qkv,
    w_out,
    gain_mlp,
    w_up,
    b_up,
    w_down,
    b_down,
    cotangent,
):
    slots, quarter, width = tokens.shape
    length = segments.shape[1]
    n = lax.axis_size("fsdp")
    m = lax.axis_size("dp")
    hidden_per = b_up.shape[0] // m
    small = gain_attn.shape[0]
    per = (hidden_per, small)
    columns = w_qkv.shape[1]
    most, take, place, _ = column_plan(n, m, columns * n)
    place = jnp.asarray(place)
    tile = 2 * quarter if n * most <= 2 * width else quarter
    parts, place_back, home = row_parts(n, m, columns * n)
    place_back = jnp.asarray(place_back)
    cosine, sine = [jnp.asarray(np.concatenate([v, v], axis=1)) for v in rope_table(length)]

    (
        qkv,
        normed,
        attended,
        logs,
        grad_middle,
        base,
        far_part,
        grad_attended,
        dw_up,
        down_total,
        out_sum,
        mod,
        vec,
        w_qkv_t,
        vec_blocks,
        db_up,
        sums,
    ) = front(
        n,
        m,
        length,
        tile,
        most,
        (
            tokens,
            cotangent,
            condition,
            segments,
            w_ada.T,
            b_ada,
            b_up,
            gain_attn,
            gain_mlp,
            b_down,
            w_qkv.T,
            w_out.T,
            w_up,
            w_down.T,
            jnp.asarray(take.reshape(n * m, most)),
            place,
            cosine,
            sine,
        ),
    )
    d_tokens, other_part, down_all, up_all, out_all, qkv_all, d_cond, d_w_ada, d_b_ada, d_vec = back(
        n,
        m,
        per,
        tile,
        parts,
        (
            qkv,
            grad_attended,
            attended,
            normed,
            tokens,
            grad_middle,
            far_part,
            cotangent,
            dw_up,
            down_total,
            out_sum,
            logs,
            segments,
            cosine,
            sine,
            w_qkv_t,
            mod,
            vec,
            sums,
            vec_blocks,
            w_ada.T,
            db_up,
            place_back,
        ),
    )
    (
        outputs,
        d_tokens,
        d_w_ada,
        d_w_qkv,
        d_w_out,
        d_w_up,
        d_w_down,
        d_cond,
        d_b_ada,
        d_gain_attn,
        d_gain_mlp,
        d_b_up,
        d_b_down,
    ) = finish(
        n,
        m,
        per,
        columns,
        (
            base,
            other_part,
            d_tokens,
            d_w_ada,
            down_all,
            up_all,
            out_all,
            qkv_all,
            mod,
            d_cond,
            d_b_ada,
            d_vec,
            jnp.asarray(home),
        ),
    )
    return (
        outputs,
        d_tokens,
        d_cond,
        d_w_ada.T,
        d_b_ada,
        d_gain_attn,
        d_w_qkv.T,
        d_w_out.T,
        d_gain_mlp,
        d_w_up,
        d_b_up,
        d_w_down.T,
        d_b_down,
    )


def solution(mesh):
    return jax.shard_map(
        shards,
        mesh=mesh,
        in_specs=(
            P("fsdp", "dp", None),
            P("fsdp", None),
            P("fsdp", None),
            P(None, "fsdp"),
            P("fsdp"),
            P("fsdp"),
            P(None, "fsdp"),
            P(None, "fsdp"),
            P("fsdp"),
            P(None, "fsdp"),
            P("fsdp"),
            P(None, "fsdp"),
            P("fsdp"),
            P("fsdp", "dp", None),
        ),
        out_specs=(
            P("fsdp", "dp", None),
            P("fsdp", "dp", None),
            P("fsdp", None),
            P(None, "fsdp"),
            P("fsdp"),
            P("fsdp"),
            P(None, "fsdp"),
            P(None, "fsdp"),
            P("fsdp"),
            P(None, "fsdp"),
            P("fsdp"),
            P(None, "fsdp"),
            P("fsdp"),
        ),
        check_vma=False,
    )
```

```python
import functools
import math

import jax
import jax.numpy as jnp
import numpy as np
from jax import lax
from jax.experimental import pallas as pl
from jax.experimental.pallas import tpu as pltpu
from jax.sharding import PartitionSpec as P

HEAD = 64
EPS = 1e-05
ROPE_BASE = 10000.0
MASKED = -1e30
F32 = jnp.float32
BF16 = jnp.bfloat16

NN = (((1,), (0,)), ((), ()))
NT = (((1,), (1,)), ((), ()))
TN = (((0,), (0,)), ((), ()))


def mm(a, b, dims):
    return lax.dot_general(a, b, dims, preferred_element_type=F32)


def rope_table(length):
    inverse = ROPE_BASE ** (-2.0 * np.arange(HEAD // 2) / HEAD)
    angles = np.arange(length)[:, None] * inverse[None, :]
    cosine = np.concatenate([np.cos(angles)] * 2, axis=1)
    sine = np.concatenate([-np.sin(angles), np.sin(angles)], axis=1)
    return cosine.astype(np.float32), sine.astype(np.float32)


def swap_halves(v):
    half = HEAD // 2
    return jnp.concatenate([v[..., half:], v[..., :half]], axis=-1)


MESH = pl.DeviceIdType.MESH
VM = pl.BlockSpec(memory_space=pltpu.VMEM)
ANY = pl.BlockSpec(memory_space=pl.ANY)
LIMIT = (63 << 20) + (768 << 10)


def round16(size):
    return -(-size // 16) * 16


def iota(shape, dim):
    return lax.broadcasted_iota(jnp.int32, shape, dim)


def greet(peers, meanwhile=None):
    barrier = pltpu.get_barrier_semaphore()
    for peer in peers:
        pl.semaphore_signal(barrier, inc=1, device_id=peer, device_id_type=MESH)
    if meanwhile is not None:
        meanwhile()
    pl.semaphore_wait(barrier, len(peers))


def push(src, dst, send, recv, peer):
    return pltpu.make_async_remote_copy(
        src_ref=src,
        dst_ref=dst,
        send_sem=send,
        recv_sem=recv,
        device_id=peer,
        device_id_type=MESH,
    )


class Place:
    def __init__(self, n, m):
        self.n, self.m = n, m
        self.f = lax.axis_index("fsdp")
        self.d = lax.axis_index("dp")
        self.lines = n // 2
        self.a = self.f // 2
        self.b = self.f % 2
        self.x = self.d // 2
        self.c = self.d % 2
        self.sib_d = self.x * 2 + 1 - self.c
        self.far_d = (1 - self.x) * 2 + self.c
        self.diag_d = (1 - self.x) * 2 + 1 - self.c
        self.sib = (self.f, self.sib_d)
        self.far = (self.f, self.far_d)
        self.diag = (self.f, self.diag_d)
        self.side = (self.a * 2 + 1 - self.b, self.d)
        last = self.lines - 1
        self.right = (jnp.minimum(self.a + 1, last) * 2 + self.b, self.d)
        self.left = (jnp.maximum(self.a - 1, 0) * 2 + self.b, self.d)
        self.has_right = self.a < last
        self.has_left = self.a > 0

    def ring_f(self, step):
        return (self.f + step + self.n) % self.n

    def ring(self):
        return [(self.ring_f(i), self.d) for i in range(1, self.n)]

    def line_peers(self):
        return [((self.a + i) % self.lines * 2 + self.b, self.d) for i in range(1, self.lines)] + [
            self.side
        ]


class Gather:
    def __init__(self, p, src, slot, sems):
        self.p, self.src, self.slot, self.sems = p, src, slot, sems

    def place(self, way, t):
        return jnp.clip(self.p.a + (t if way else -t), 0, self.p.lines - 1)

    def line_copy(self, way, t):
        p, j = self.p, self.place(way, t)
        block = self.slot(j * 2 + p.b)
        leave = 4 * p.lines if way and t == 0 else p.lines + j
        return push(
            self.src if t == 0 else block,
            block,
            self.sems.at[leave],
            self.sems.at[j],
            p.left if way else p.right,
        )

    def side_copy(self, way, t, theirs=False):
        p, j = self.p, self.place(way, t)
        block = self.slot(j * 2 + (1 - p.b if theirs else p.b))
        return push(
            self.src if t == 0 else block,
            block,
            self.sems.at[2 * p.lines + j],
            self.sems.at[3 * p.lines + j],
            p.side,
        )

    def held(self, way, t):
        p = self.p
        return p.a + t < p.lines if way else p.a - t >= 0

    def onward(self, way):
        return self.p.has_left if way else self.p.has_right

    def start(self):
        for way in range(2):
            pl.when(self.onward(way))(lambda way=way: self.line_copy(way, 0).start())
        self.side_copy(0, 0).start()

    def step(self, t):
        for way in range(2):

            @pl.when(self.held(way, t))
            def _(way=way):
                self.line_copy(way, t).wait_recv()
                if t < self.p.lines - 1:
                    pl.when(self.onward(way))(lambda: self.line_copy(way, t).start())
                self.side_copy(way, t).start()

    def finish(self):
        self.side_copy(0, 0, True).wait_recv()
        for t in range(1, self.p.lines):
            for way in range(2):
                pl.when(self.held(way, t))(
                    lambda way=way, t=t: self.side_copy(way, t, True).wait_recv()
                )

    def drain(self):
        self.side_copy(0, 0).wait_send()
        for way in range(2):
            pl.when(self.onward(way))(lambda way=way: self.line_copy(way, 0).wait_send())
        for t in range(1, self.p.lines):
            for way in range(2):

                @pl.when(self.held(way, t))
                def _(way=way, t=t):
                    if t < self.p.lines - 1:
                        pl.when(self.onward(way))(lambda: self.line_copy(way, t).wait_send())
                    self.side_copy(way, t).wait_send()


class Both:
    def __init__(self, *gathers):
        self.gathers = gathers

    def start(self):
        for g in self.gathers:
            g.start()

    def step(self, t):
        for g in self.gathers:
            g.step(t)

    def finish(self):
        for g in self.gathers:
            g.finish()

    def drain(self):
        for g in self.gathers:
            g.drain()


def gather_halves(p, src, buf, sems, first):
    rows = src.shape[0]
    if rows % 32:
        return Gather(p, src, lambda f: buf.at[f], sems.at[first])
    cut = [pl.ds(h * rows // 2, rows // 2) for h in range(2)]
    return Both(
        *[
            Gather(p, src.at[cut[h]], lambda f, h=h: buf.at[f, cut[h]], sems.at[first + h])
            for h in range(2)
        ]
    )


class Reduce:
    def __init__(self, p, src, side, total, zrecv, sems, summed=False, only=None):
        self.p, self.src, self.side, self.total = p, src, side, total
        self.zrecv, self.sems, self.summed, self.only = zrecv, sems, summed, only

    def order(self):
        lines = self.p.lines
        if self.only is not None:
            return [self.only]
        return [j for k in range(lines // 2) for j in (lines - 1 - k, k)]

    def side_copy(self, j):
        p = self.p
        return push(
            self.src(2 * j + 1 - p.b), self.side.at[j], self.sems.at[j], self.sems.at[p.lines + j], p.side
        )

    def line_copy(self, way, j):
        p = self.p
        at = jnp.where(j == p.a - 1, p.lines, j) if way else j
        return push(
            self.total.at[j],
            self.zrecv.at[at],
            self.sems.at[2 * p.lines + j],
            self.sems.at[3 * p.lines + at],
            p.left if way else p.right,
        )

    def line_wait(self, way, j):
        p = self.p
        at = jnp.where(j == p.a, p.lines, j) if way else j
        block = self.zrecv.at[at]
        push(
            block,
            block,
            self.sems.at[2 * p.lines + j],
            self.sems.at[3 * p.lines + at],
            p.left if way else p.right,
        ).wait_recv()
        return block[...].astype(F32)

    def start(self):
        for j in self.order():
            self.side_copy(j).start()

    def side_sum(self, j):
        p = self.p
        self.side_copy(j).wait_recv()
        mine = self.src(2 * j + p.b)[...].astype(F32)
        self.total[j] = (mine + self.side[j].astype(F32)).astype(BF16)

    def step(self, t):
        p = self.p
        if 2 * t < p.lines and not self.summed:
            for j in self.order()[2 * t : 2 * t + 2]:
                self.side_sum(j)
        for way in range(2):
            j = t - (p.lines - 1 - p.a) if way else p.lines - 1 - (t - p.a)
            ahead = (j >= 0) & (j < p.a) if way else (j < p.lines) & (j > p.a)
            behind = p.has_right if way else p.has_left
            if self.only is not None:
                ahead &= j == self.only

            @pl.when(ahead)
            def _(way=way, j=j, behind=behind):
                @pl.when(behind)
                def _():
                    arrived = self.line_wait(way, j)
                    self.total[j] = (self.total[j].astype(F32) + arrived).astype(BF16)

                self.line_copy(way, j).start()

    def own(self, out):
        p = self.p
        held = True if self.only is None else p.a == self.only
        for way in range(2):

            @pl.when(held & (p.has_right if way else p.has_left))
            def _(way=way):
                arrived = self.line_wait(way, p.a)
                self.total[p.a] = (self.total[p.a].astype(F32) + arrived).astype(BF16)

        if self.only is None:
            out[...] = self.total[p.a]
        else:
            out[...] = jnp.zeros(out.shape, BF16)

            @pl.when(held)
            def _():
                out[...] = self.total[p.a]

    def drain(self):
        p = self.p
        for j in range(p.lines) if self.only is None else [self.only]:
            if not self.summed:
                self.side_copy(j).wait_send()
            for way in range(2):
                ahead = p.a > j if way else p.a < j
                pl.when(ahead)(lambda way=way, j=j: self.line_copy(way, j).wait_send())


class Exchange:
    def __init__(self, p, src, buf, send, recv):
        self.p, self.src, self.buf, self.send, self.recv = p, src, buf, send, recv

    def start(self):
        p = self.p
        for i in range(1, p.n):
            peer = p.ring_f(i)
            push(self.src(peer), self.buf.at[p.f], self.send, self.recv, (peer, p.d)).start()

    def every(self):
        some = self.buf.at[pl.ds(0, self.p.n - 1)]
        return push(some, some, self.send, self.recv, self.p.side)

    def finish(self):
        self.every().wait_recv()

    def drain(self):
        self.every().wait_send()


class Spread:
    def __init__(self, p, slot, send, recv):
        self.p, self.slot, self.send, self.recv = p, slot, send, recv

    def copy(self, kind):
        p = self.p
        block = self.slot(p.far_d if kind == 2 else p.d)
        return push(block, block, self.send.at[kind], self.recv.at[kind], p.far if kind == 1 else p.sib)

    def start(self):
        self.copy(1).start()
        self.copy(0).start()

    def forward(self):
        self.copy(1).wait_recv()
        self.copy(2).start()

    def finish(self):
        self.copy(0).wait_recv()
        self.copy(2).wait_recv()

    def drain(self):
        for kind in range(3):
            self.copy(kind).wait_send()


def norm_rows(stream):
    average = jnp.mean(stream, axis=-1, keepdims=True)
    centered = stream - average
    variance = jnp.mean(centered * centered, axis=-1, keepdims=True)
    inverse = lax.rsqrt(variance + EPS)
    return centered * inverse, inverse


def norm_back(grad, normal, inverse, factor):
    e = grad * factor
    mean_e = jnp.mean(e, axis=-1, keepdims=True)
    mean_en = jnp.mean(e * normal, axis=-1, keepdims=True)
    return inverse * (e - mean_e - normal * mean_en)


def turned(v):
    lanes = iota(v.shape, 1)
    half = HEAD // 2
    return jnp.where(lanes % HEAD < half, pltpu.roll(v, 128 - half, 1), pltpu.roll(v, half, 1))


def gelu_parts(h):
    root = math.sqrt(2.0 / math.pi)
    square = h * h
    t = jnp.tanh(root * h * (1.0 + 0.044715 * square))
    half = 0.5 * (1.0 + t)
    slope = half + 0.5 * h * (1.0 - t * t) * (root * (1.0 + 3.0 * 0.044715 * square))
    return h * half, slope


def compact(blocks, per):
    count, rows, lanes = blocks.shape
    flat = blocks.reshape(count * rows, lanes)
    if rows == per:
        return flat
    want = iota((count * per, count * rows), 0)
    have = iota((count * per, count * rows), 1)
    chosen = (have == want // per * rows + want % per).astype(BF16)
    return mm(chosen, flat, NN).astype(BF16)


def as_column(row):
    size = row.shape[1]
    return jnp.transpose(jnp.broadcast_to(row, (128, size)))[:, :1]


def front_kernel(
    n,
    m,
    per,
    tile,
    tok_ref,
    cot_ref,
    cond_ref,
    seg_ref,
    wada_ref,
    bada_ref,
    bup_ref,
    ga_ref,
    gmlp_ref,
    bdown_ref,
    wqkv_ref,
    wout_ref,
    wup_ref,
    wdown_ref,
    take_ref,
    place_ref,
    cos_ref,
    sin_ref,
    qkv_out,
    normed_out,
    att_out,
    log_out,
    gm_out,
    base_out,
    xsend_out,
    gatt_out,
    dwu_out,
    downtotal_out,
    outsum_out,
    mod_ref,
    vecs_ref,
    wqkvt_ref,
    vec_out,
    dbup_ref,
    sums_ref,
    qkv_ref,
    att_v,
    arecv,
    log_v,
    mod_send,
    mod_recv,
    vsrc,
    vbuf,
    qsrc,
    qbuf,
    osrc,
    obuf,
    usrc,
    ubuf,
    dsrc,
    dbuf,
    cot_v,
    own_ref,
    br_ref,
    mid_ref,
    nrm_ref,
    inv_ref,
    nm_ref,
    ct_ref,
    act_ref,
    gp_ref,
    gsc,
    psend,
    precv,
    xs_ref,
    xr_ref,
    gn_ref,
    bo_ref,
    gba_ref,
    gm_ref,
    gsend,
    grecv,
    dwd_ref,
    dwu_ref,
    dwo_ref,
    oswap,
    side_d,
    total_d,
    ex,
    gz,
    ts,
    tr,
    os_,
    or_,
    as_,
    ar,
    cs,
    cr,
    n_s,
    n_r,
    p_s,
    p_r,
    g_s,
    g_r,
    rz,
    o_s,
    o_r,
    local,
):
    p = Place(n, m)
    slots, quarter, width = tok_ref.shape
    half = quarter // 2
    part = width // m
    heads = part // HEAD
    hidden_per, small = per
    pad = usrc.shape[0]
    inner = n * hidden_per
    halves = obuf.shape[1]
    length = m * quarter
    tall_ref = gp_ref
    normed_ref = act_ref.reshape(slots, length, width)
    filled = pad > hidden_per or qbuf.shape[0] * osrc.shape[0] > width
    spare = qbuf.reshape(n * qsrc.shape[0], width)
    dense = [spare.at[pl.ds(k * width, width)] for k in range(3 if filled else 0)]
    peers = (p.sib, p.far, p.diag)
    ranks = (p.sib_d, p.far_d, p.diag_d)
    own_tokens = pltpu.make_async_copy(tok_ref, tall_ref.at[p.d], local.at[2])
    own_tokens.start()
    own_cots = [
        pltpu.make_async_copy(cot_ref, dst, local.at[3 + k])
        for k, dst in enumerate((cot_v, ct_ref.at[p.d]))
    ]
    for copy in own_cots:
        copy.start()
    log_v[...] = jnp.zeros_like(log_v)

    def prepare():
        vsrc[...] = jnp.zeros_like(vsrc)
        for row, ref in enumerate((ga_ref, gmlp_ref, bdown_ref)):
            vsrc[row : row + 1, : ref.shape[0]] = ref[...].reshape(1, -1)
        vsrc[4 : 4 + slots, :] = cond_ref[...]
        b_up = bup_ref[...].reshape(1, -1)
        for k in range(0, b_up.shape[1], 128):
            some = b_up[:, k : k + 128]
            vsrc[8 + k // 128 : 9 + k // 128, : some.shape[1]] = some
        columns = wqkv_ref.shape[0]
        most = qsrc.shape[0]
        taking = take_ref[pl.ds(p.f * m + p.d, 1), :]
        chosen = (iota((columns, most), 0) == taking).astype(BF16)
        qsrc[...] = mm(chosen, wqkv_ref[...], TN).astype(BF16)

    greet(list(peers) + p.ring(), prepare)

    vec = Exchange(p, lambda f: vsrc, vbuf, ex.at[0], ex.at[1])
    vec.start()

    def token_copy(kind, k):
        s, rows = k // 2, pl.ds(k % 2 * half, half)
        if kind == 2:
            block = tall_ref.at[p.far_d, s, rows]
            return push(block, block, ts.at[kind, k], tr.at[kind, k], p.sib)
        return push(
            tok_ref.at[s, rows],
            tall_ref.at[p.d, s, rows],
            ts.at[kind, k],
            tr.at[kind, k],
            p.sib if kind == 0 else p.far,
        )

    qry = gather_halves(p, qsrc, qbuf, gz, 0)
    qry.start()
    for k in range(2 * slots):
        token_copy(1, k).start()
    for k in range(2 * slots):
        token_copy(0, k).start()
    vbuf[p.f] = vsrc[...]
    qbuf[p.f] = qsrc[...]

    lane = iota((1, width), 1)
    rank, rest = lane // part, lane % part
    want = (rest // HEAD * m + rank) * HEAD + rest % HEAD
    chosen = (iota((width, width), 0) == want).astype(BF16)
    got = mm(wout_ref[...], chosen, NN).astype(BF16)
    if small < osrc.shape[0]:
        got = jnp.concatenate([got, jnp.zeros((osrc.shape[0] - small, width), BF16)])
    osrc[...] = got
    split = osrc.shape[0] // halves
    mine = p.c if halves == 2 else 0
    out = Gather(
        p,
        osrc.at[pl.ds(pl.multiple_of(mine * split, 16), split)],
        lambda f: obuf.at[f, mine],
        gz.at[2],
    )
    for h in range(halves):
        obuf[p.f, h] = osrc[h * split : (h + 1) * split]

    ups = wup_ref.shape[1]
    at, lane = iota((pad, ups), 0), iota((pad, ups), 1)
    chosen = ((lane == at + p.d * hidden_per) & (at < hidden_per)).astype(BF16)
    usrc[...] = mm(chosen, wup_ref[...], NT).astype(BF16)
    ubuf[p.f] = usrc[...]
    up = Gather(p, usrc, lambda f: ubuf.at[f], gz.at[3])
    block = dsrc.shape[0]
    lane = iota((1, inner), 1)
    want = (lane // hidden_per * m + p.d) * hidden_per + lane % hidden_per
    got = jnp.zeros((small, inner), F32)
    for at in range(0, wdown_ref.shape[1], width):
        chosen = (iota((width, inner), 0) + at == want).astype(BF16)
        got = got + mm(wdown_ref[:, at : at + width], chosen, NN)
    got = got.astype(BF16)
    if small < block:
        got = jnp.concatenate([got, jnp.zeros((block - small, inner), BF16)])
    dsrc[...] = got
    dbuf[p.f] = got
    down = Gather(p, dsrc, lambda f: dbuf.at[f], gz.at[4])

    def pass_on(k):
        token_copy(1, k).wait_recv()
        token_copy(2, k).start()

    qry.step(1)
    vec.finish()
    vecs = vbuf[...].reshape(n * 16, 128)
    mod_cols = mm(vecs, wada_ref[...], NT) + bada_ref[...].reshape(1, -1).astype(F32)
    mod_send[...] = mod_cols.reshape(n, 16, mod_cols.shape[1])[:, 4 : 4 + slots]
    mod_recv[p.f] = mod_send[p.f]

    mods = Exchange(p, lambda f: mod_send.at[f], mod_recv, ex.at[2], ex.at[3])
    mods.start()
    vec_out[...] = vbuf[...]
    vecs_ref[...] = jnp.zeros_like(vecs_ref)
    ups = bup_ref.shape[0]
    b_up = jnp.zeros((n * 16, pad), F32)
    for k in range(0, ups, 128):
        lane = iota((128, pad), 1)
        chosen = (iota((128, pad), 0) + k == lane + p.d * hidden_per) & (lane < hidden_per)
        some = mm(vecs, chosen.astype(BF16), NN)
        b_up = b_up + jnp.where(iota((n * 16, pad), 0) % 16 == 8 + k // 128, some, 0.0)
    for g in range(n):
        vecs_ref[0:1, g * hidden_per : (g + 1) * hidden_per] = jnp.sum(
            b_up[16 * g : 16 * (g + 1)], axis=0, keepdims=True
        )[:, :hidden_per]
        rest = vecs[16 * g : 16 * g + 8].astype(F32)
        for k in range(3):
            vecs_ref[k + 1 : k + 2, g * small : (g + 1) * small] = rest[k : k + 1, :small]
    for k in range(2, p.lines - 1):
        qry.step(k)
    pass_on(0)
    qry.step(p.lines - 1)
    out.start()
    mods.finish()
    cols = mod_cols.shape[1]
    for g in range(n):
        for s in range(slots):
            mod_ref[s, :, g * cols : (g + 1) * cols] = mod_recv[g, s : s + 1]
    gain = vecs_ref[1:2, :width]

    pass_on(1)
    pass_on(2)
    def cot_copy(kind, s):
        if kind == 2:
            block = ct_ref.at[p.far_d, s]
            return push(block, block, cs.at[kind, s], cr.at[kind, s], p.sib)
        return push(
            cot_ref.at[s],
            ct_ref.at[p.d, s],
            cs.at[kind, s],
            cr.at[kind, s],
            p.sib if kind else p.far,
        )

    for s in range(slots):
        cot_copy(0, s).start()

    qry.finish()
    up.start()
    count = n * qsrc.shape[0]
    flat_rows = qbuf[...].reshape(count, width)
    got = jnp.zeros((3 * part, width), F32)
    for at in range(0, count, width):
        some = place_ref[pl.ds(p.d, 1), at : at + width]
        placing = (iota((3 * part, some.shape[1]), 0) == some).astype(BF16)
        got = got + mm(placing, flat_rows[at : at + width], NN)
    wqkvt_ref[...] = got.astype(BF16)
    own_tokens.wait()

    def chunk(i):
        q = jnp.where(
            i < 2, p.d, jnp.where(i < 4, p.sib_d, jnp.where(i % 2 == 0, p.far_d, p.diag_d))
        )
        s = jnp.where(i < 4, i % 2, (i - 4) // 2)
        return q, s, pl.ds(pl.multiple_of(q * quarter, quarter), quarter)

    def keeps(i):
        _, s, rows = chunk(i)
        return [
            pltpu.make_async_copy(src.at[s, rows], dst.at[s, rows], local.at[k])
            for k, (src, dst) in enumerate(((qkv_ref, qkv_out), (normed_ref, normed_out)))
        ]

    @pl.loop(0, m * slots)
    def _(i):
        for k in range(2):

            @pl.when(i == 2 + k)
            def _(k=k):
                token_copy(0, 2 * k).wait_recv()
                token_copy(0, 2 * k + 1).wait_recv()

            @pl.when(i == 5 + 2 * k)
            def _(k=k):
                token_copy(2, 2 * k).wait_recv()
                token_copy(2, 2 * k + 1).wait_recv()

        pl.when(i == 2)(lambda: out.step(1))
        pl.when(i == 4)(lambda: pass_on(3))

        q, s, rows = chunk(i)
        normal, _ = norm_rows(tall_ref[q, s].astype(F32))
        shift = mod_ref[s, :, :width]
        scale = mod_ref[s, :, width : 2 * width]
        normed = (normal * (gain * (1.0 + scale)) + shift).astype(BF16)
        normed_ref[s, rows, :] = normed
        got = mm(normed, wqkvt_ref[...], NT)
        cosine = cos_ref[rows, :]
        sine = sin_ref[rows, :]
        lanes = iota((quarter, 128), 1)
        for t in range(0, 2 * part, 128):
            piece = got[:, t : t + 128]
            piece = piece * cosine + turned(piece) * sine
            piece = jnp.where(lanes + t < part, piece * (1.0 / math.sqrt(HEAD)), piece)
            qkv_ref[s, rows, t : t + 128] = piece.astype(BF16)
        qkv_ref[s, rows, 2 * part :] = got[:, 2 * part :].astype(BF16)
        for keep in keeps(i):
            keep.start()

    def att_copy(kind, s):
        return push(
            att_v.at[s, ranks[kind]], arecv.at[s, p.d], as_.at[kind, s], ar.at[kind, s], peers[kind]
        )

    def swap(h):
        return push(obuf.at[:, h], obuf.at[:, h], os_.at[0], or_.at[0], p.sib)

    def weight_ready():
        out.finish()
        if halves == 2:
            swap(p.c).start()
            swap(1 - p.c).wait_recv()
        if filled:
            qry.drain()
        if small < osrc.shape[0]:
            dense[0][...] = compact(obuf[:, 0], small)

    def group(s, k):
        return mod_ref[s, :, k * width : (k + 1) * width]

    gain_mlp = vecs_ref[2:3, :width]
    b_down = vecs_ref[3:4, :width]
    if small < osrc.shape[0]:
        w_out = lambda: dense[0][...]
    else:
        w_out = lambda: obuf[...].reshape(width, width)
    if pad > hidden_per:
        w_up = lambda: dense[1][...]
    else:
        w_up = lambda: ubuf[...].reshape(inner, width)
    if small < block:
        w_down = lambda: dense[2][...]
    else:
        w_down = lambda: dbuf[...].reshape(width, inner)

    def nm_copy(kind, s, h):
        k = s * 2 + h
        rows = nm_ref.at[p.far_d if kind == 2 else p.d, s, pl.ds(h * half, half)]
        return push(rows, rows, n_s.at[kind, k], n_r.at[kind, k], p.far if kind == 1 else p.sib)

    def enter(s):
        for kind in range(3):
            att_copy(kind, s).wait_recv()
        arecv[s, p.d] = att_v[s, p.d]
        for r in range(m):
            for h in range(2):
                own_ref[s, h * half : (h + 1) * half, r * part : (r + 1) * part] = arecv[
                    s, r, :, h * part : (h + 1) * part
                ]
        branch = mm(own_ref[s], w_out(), NT)
        br_ref[s] = branch
        middle = tall_ref[p.d, s].astype(F32) + group(s, 2) * branch
        mid_ref[s] = middle
        normal, inverse = norm_rows(middle)
        nrm_ref[s] = normal
        inv_ref[s] = inverse
        nm_ref[p.d, s] = (normal * (gain_mlp * (1.0 + group(s, 4))) + group(s, 3)).astype(BF16)
        for kind in (1, 0):
            for h in range(2):
                nm_copy(kind, s, h).start()

    def pass_rows(s):
        for h in range(2):
            nm_copy(1, s, h).wait_recv()
            nm_copy(2, s, h).start()

    def arrived(kind, s):
        for h in range(2):
            nm_copy(kind, s, h).wait_recv()

    for k in range(2, p.lines):
        out.step(k)
    up.step(1)
    tiles = length // tile

    @pl.loop(0, slots * tiles)
    def _(i):
        s = i // tiles
        rows = pl.ds(pl.multiple_of(i % tiles * tile, tile), tile)
        same = as_column(seg_ref[pl.ds(s, 1), :]) == seg_ref[pl.ds(s, 1), rows]
        ones = jnp.ones((length, HEAD), BF16)
        for h in range(heads):
            at = h * HEAD
            q = qkv_ref[s, rows, at : at + HEAD]
            k = qkv_ref[s, :, part + at : part + at + HEAD]
            v = qkv_ref[s, :, 2 * part + at : 2 * part + at + HEAD]
            scores = jnp.where(same, mm(k, q, NT), MASKED)
            largest = jnp.max(scores, axis=0, keepdims=True)
            weights = jnp.exp(scores - largest)
            log_v[s, h : h + 1, rows] = largest + jnp.log(jnp.sum(weights, axis=0, keepdims=True))
            result = mm(weights.astype(BF16), jnp.concatenate([v, ones], axis=1), TN)
            result = (result[:, :HEAD] / result[:, HEAD : HEAD + 1]).astype(BF16)
            for j in range(tile // half):
                att_v[s, i % tiles * (tile // quarter) + j // 2, :, j % 2 * part + at : j % 2 * part + at + HEAD] = (
                    result[j * half : (j + 1) * half]
                )
        for k in range(2, p.lines):
            pl.when(i == k - 2)(lambda k=k: up.step(k))

        @pl.when(i == tiles - 1)
        def _():
            for kind in (2, 1, 0):
                att_copy(kind, 0).start()
            weight_ready()
            down.start()

        @pl.when(i == tiles)
        def _():
            enter(0)
            down.step(1)

        @pl.when(i == slots * tiles - 1)
        def _():
            for s in range(1, slots):
                for kind in (2, 1, 0):
                    att_copy(kind, s).start()

    def expand(q, s):
        hidden = mm(nm_ref[q, s], w_up(), NT) + vecs_ref[0:1, :inner]
        value, slope = gelu_parts(hidden)
        act_ref[q, s] = value.astype(BF16)
        gp_ref[q, s] = slope.astype(BF16)

    for k in range(slots * tiles + 2, p.lines):
        up.step(k)
    stores = []

    def store(src, dst):
        stores.append(pltpu.make_async_copy(src, dst, local.at[5 + len(stores)]))
        stores[-1].start()

    store(att_v, att_out)
    store(log_v, log_out)
    for k, (src, dst) in enumerate(((qkv_ref, qkv_out), (normed_ref, normed_out))):
        pltpu.make_async_copy(src, dst, local.at[k]).wait()
    for k in range(2 * slots):
        token_copy(2, k).wait_send()
    for copy in own_cots:
        copy.wait()
    for k in range(2, p.lines):
        down.step(k)
    pass_rows(0)
    for s in range(slots):
        cot_copy(0, s).wait_recv()
        cot_copy(2, s).start()
        cot_copy(1, s).start()
    up.finish()
    if pad > hidden_per:
        dense[1][...] = compact(ubuf[...], hidden_per)

    def near_rows(s):
        @pl.loop(0, 2)
        def _(i):
            pl.when(i > 0)(lambda: arrived(0, s))
            expand(jnp.where(i == 0, p.d, p.sib_d), s)

    near_rows(0)
    for s in range(1, slots):
        enter(s)
    down.finish()
    if small < block:
        dense[2][...] = compact(dbuf[...], small)
    for s in range(slots):
        cot_copy(1, s).wait_recv()
        cot_copy(2, s).wait_recv()
        cot_copy(2, s).wait_send()

    dbup_ref[...] = jnp.zeros_like(dbup_ref)

    def pull(q, s):
        g = (ct_ref[q, s].astype(F32) * group(s, 5)).astype(BF16)
        ct_ref[q, s] = g
        grad = (mm(g, w_down(), NN) * gp_ref[q, s].astype(F32)).astype(BF16)
        gp_ref[q, s] = grad
        dbup_ref[0:1, :] += jnp.sum(grad.astype(F32), axis=0, keepdims=True)
        gsc[...] = mm(grad, w_up(), NN)

    def part_copy(kind, s):
        if kind == 4:
            return push(xs_ref.at[s], xr_ref.at[s], p_s.at[4, s], p_r.at[4, s], p.far)
        return push(psend.at[kind, s], precv.at[kind, s], p_s.at[kind, s], p_r.at[kind, s], p.sib)

    def far_rows(s):
        @pl.loop(0, 2)
        def _(i):
            first = i == 0
            pl.when(first)(lambda: arrived(2, s))
            q = jnp.where(first, p.diag_d, p.far_d)
            expand(q, s)
            pull(q, s)

            @pl.when(first)
            def _():
                psend[0, s] = gsc[...].astype(BF16)
                part_copy(0, s).start()

            @pl.when(jnp.logical_not(first))
            def _():
                part_copy(0, s).wait_recv()
                xs_ref[s] = (gsc[...] + precv[0, s].astype(F32)).astype(BF16)
                part_copy(4, s).start()

    far_rows(0)
    for s in range(1, slots):
        near_rows(s)
    for s in range(1, slots):
        pass_rows(s)
        far_rows(s)

    @pl.loop(0, 2 * slots)
    def _(i):
        s = i // 2
        first = i % 2 == 0
        pull(jnp.where(first, p.sib_d, p.d), s)

        @pl.when(first)
        def _():
            psend[1, s] = gsc[...].astype(BF16)
            part_copy(1, s).start()

        @pl.when(jnp.logical_not(first))
        def _():
            gn_ref[s] = gsc[...]

    def weight_grad(left, right, out_ref, step=128):

        @pl.loop(0, left.shape[1] // step)
        def _(i):
            at = pl.ds(pl.multiple_of(i * step, step), step)
            out_ref[at, :] = mm(left[:, at], right[...], TN).astype(BF16)

    every = lambda ref: ref.reshape(m * slots * quarter, ref.shape[3])
    weight_grad(every(ct_ref), every(act_ref), dwd_ref.at[:width])
    if small < block:
        dwd_ref[...] = padded(dwd_ref[:width], n, block)
    dwd = dwd_ref.reshape(n, block, inner)
    red_down = Reduce(p, lambda f: dwd.at[f], side_d, total_d, None, rz)
    red_down.start()
    def grad_copy(kind, s):
        return push(
            gsend.at[s, ranks[kind]], grecv.at[s, p.d], g_s.at[kind, s], g_r.at[kind, s], peers[kind]
        )

    def leave(s):
        part_copy(1, s).wait_recv()
        part_copy(4, s).wait_recv()
        cot = cot_v[s].astype(F32)
        gn = gn_ref[s] + precv[1, s].astype(F32) + xr_ref[s].astype(F32)
        normal = nrm_ref[s]
        grad_middle = cot + norm_back(gn, normal, inv_ref[s], gain_mlp * (1.0 + group(s, 4)))
        gm_ref[s] = grad_middle
        gba = (grad_middle * group(s, 2)).astype(BF16)
        gba_ref[s] = gba
        gatt = mm(gba, w_out(), NN).astype(BF16)
        for r in range(m):
            for h in range(2):
                gsend[s, r, :, h * part : (h + 1) * part] = gatt[
                    h * half : (h + 1) * half, r * part : (r + 1) * part
                ]
        for kind in (2, 1, 0):
            grad_copy(kind, s).start()
        grecv[s, p.d] = gsend[s, p.d]
        total = lambda v: jnp.sum(v, axis=0, keepdims=True)
        sums_ref[s, 0:1, :] = total(gn)
        sums_ref[s, 1:2, :] = total(gn * normal)
        sums_ref[s, 3:4, :] = total(grad_middle * br_ref[s])
        sums_ref[s, 4:5, :] = total((cot * group(s, 5)).astype(BF16).astype(F32))
        sums_ref[s, 5:8, :] = jnp.zeros((3, width), F32)

    leave(0)
    weight_grad(every(gp_ref), every(nm_ref), dwu_ref.at[:inner])
    if pad > hidden_per:
        dwu_ref[...] = padded(dwu_ref[:inner], n, pad)

    store(dwu_ref.reshape(n, pad, width), dwu_out)

    for s in range(1, slots):
        leave(s)

    @pl.loop(0, 4 * slots)
    def _(i):
        s = i // 4
        j = i % 4
        q = jnp.where(
            j < 2, jnp.where(j == 0, p.diag_d, p.sib_d), jnp.where(j == 2, p.d, p.far_d)
        )
        gsc[...] = mm(act_ref[q, s], w_down(), NT)

        @pl.when(j == 0)
        def _():
            psend[2, s] = gsc[...].astype(BF16)
            part_copy(2, s).start()

        @pl.when(j == 1)
        def _():
            psend[3, s] = gsc[...].astype(BF16)
            part_copy(3, s).start()

        @pl.when(j == 2)
        def _():
            bo_ref[s] = gsc[...]

        @pl.when(j == 3)
        def _():
            part_copy(2, s).wait_recv()
            part_copy(4, s).wait_send()
            xs_ref[s] = (gsc[...] + precv[2, s].astype(F32)).astype(BF16)

    store(xs_ref, xsend_out)
    store(gm_ref, gm_out)
    flat = lambda ref: ref.reshape(slots * quarter, width)
    weight_grad(flat(gba_ref), flat(own_ref), dwo_ref.at[:width])
    if small < block:
        dwo_ref[...] = padded(dwo_ref[:width], n, block)
    rows = oswap.shape[1]
    dwo = dwo_ref.reshape(n, block // rows, rows, width)
    mine = p.c if rows < block else 0
    theirs = 1 - p.c if rows < block else 0
    dwo_swap = push(dwo.at[:, theirs], oswap, o_s.at[0], o_r.at[0], p.sib)
    dwo_swap.start()

    @pl.loop(0, slots)
    def _(s):
        part_copy(3, s).wait_recv()
        branch = bo_ref[s] + precv[3, s].astype(F32) + b_down
        mid_ref[s] = mid_ref[s] + group(s, 5) * branch
        sums_ref[s, 2:3, :] = jnp.sum(cot_v[s].astype(F32) * branch, axis=0, keepdims=True)

    store(mid_ref, base_out)
    for j in red_down.order():
        red_down.side_sum(j)
    store(total_d, downtotal_out)
    dwo_swap.wait_recv()
    oswap[...] = (dwo[:, mine].astype(F32) + oswap[...].astype(F32)).astype(BF16)
    store(oswap, outsum_out)
    for s in range(slots):
        for kind in range(3):
            grad_copy(kind, s).wait_recv()
    store(grecv, gatt_out)

    vec.drain()
    mods.drain()
    for item in (out, up, down) if filled else (qry, out, up, down):
        item.drain()
    if halves == 2:
        swap(p.c).wait_send()
    for k in range(2 * slots):
        for kind in range(2):
            token_copy(kind, k).wait_send()
    for j in range(p.lines):
        red_down.side_copy(j).wait_send()
    dwo_swap.wait_send()
    for s in range(slots):
        for kind in range(2):
            cot_copy(kind, s).wait_send()
        for kind in range(3):
            att_copy(kind, s).wait_send()
            grad_copy(kind, s).wait_send()
            for h in range(2):
                nm_copy(kind, s, h).wait_send()
        for kind in range(4):
            part_copy(kind, s).wait_send()
    for copy in stores:
        copy.wait()


def padded(rows, count, block):
    per = rows.shape[0] // count
    want = iota((count * block, rows.shape[0]), 0)
    have = iota((count * block, rows.shape[0]), 1)
    chosen = (have == want // block * per + want % block) & (want % block < per)
    return mm(chosen.astype(BF16), rows, NN).astype(BF16)


def front(n, m, length, tile, most, args):
    tokens, cond = args[0], args[2]
    w_ada, b_up = args[4], args[6]
    slots, quarter, width = tokens.shape
    part = width // m
    lines = n // 2
    dma = pltpu.SemaphoreType.DMA
    shape = jax.ShapeDtypeStruct
    vmem = pltpu.VMEM
    hidden_per = b_up.shape[0] // m
    small = width // n
    block = round16(small)
    pad = round16(hidden_per)
    inner = n * hidden_per
    halves = 2 if block % 32 == 0 else 1
    swapped = block // halves
    rows = (slots, quarter, width)
    att = (slots, m, quarter // 2, 2 * part)
    assert inner == width
    return pl.pallas_call(
        functools.partial(front_kernel, n, m, (hidden_per, small), tile),
        out_shape=(
            shape((slots, length, 3 * part), BF16),
            shape((slots, length, width), BF16),
            shape(att, BF16),
            shape((slots, 8, length), F32),
            shape(rows, F32),
            shape(rows, F32),
            shape(rows, BF16),
            shape(att, BF16),
            shape((n, pad, width), BF16),
            shape((lines, block, inner), BF16),
            shape((n, swapped, width), BF16),
            shape((slots, 1, 6 * width), F32),
            shape((8, width), F32),
            shape((3 * part, width), BF16),
            shape((n, 16, 128), BF16),
            shape((8, inner), F32),
            shape((slots, 8, width), F32),
        ),
        in_specs=[ANY] * 2 + [VM] * (len(args) - 2),
        out_specs=(ANY,) * 11 + (VM,) * 6,
        scratch_shapes=[
            vmem((slots, length, 3 * part), BF16),
            vmem(att, BF16),
            vmem(att, BF16),
            vmem((slots, 8, length), F32),
            vmem((n, slots, w_ada.shape[0]), F32),
            vmem((n, slots, w_ada.shape[0]), F32),
            vmem((16, 128), BF16),
            vmem((n, 16, 128), BF16),
            vmem((most, width), BF16),
            vmem((n, most, width), BF16),
            vmem((block, width), BF16),
            vmem((n, halves, swapped, width), BF16),
            vmem((pad, width), BF16),
            vmem((n, pad, width), BF16),
            vmem((block, inner), BF16),
            vmem((n, block, inner), BF16),
            vmem(rows, BF16),
            vmem(rows, BF16),
            vmem(rows, F32),
            vmem(rows, F32),
            vmem(rows, F32),
            vmem((slots, quarter, 1), F32),
            vmem((m,) + rows, BF16),
            vmem((m,) + rows, BF16),
            vmem((m,) + rows, BF16),
            vmem((m,) + rows, BF16),
            vmem((quarter, width), F32),
            vmem((4,) + rows, BF16),
            vmem((4,) + rows, BF16),
            vmem(rows, BF16),
            vmem(rows, BF16),
            vmem(rows, F32),
            vmem(rows, F32),
            vmem(rows, BF16),
            vmem(rows, F32),
            vmem(att, BF16),
            vmem(att, BF16),
            vmem((n * block, inner), BF16),
            vmem((n * pad, width), BF16),
            vmem((n * block, width), BF16),
            vmem((n, swapped, width), BF16),
            vmem((lines, block, inner), BF16),
            vmem((lines, block, inner), BF16),
            dma((4,)),
            dma((5, 4 * lines + 1)),
            dma((3, 2 * slots)),
            dma((3, 2 * slots)),
            dma((1,)),
            dma((1,)),
            dma((3, slots)),
            dma((3, slots)),
            dma((3, slots)),
            dma((3, slots)),
            dma((3, 2 * slots)),
            dma((3, 2 * slots)),
            dma((5, slots)),
            dma((5, slots)),
            dma((3, slots)),
            dma((3, slots)),
            dma((4 * lines + 1,)),
            dma((1,)),
            dma((1,)),
            dma((16,)),
        ],
        compiler_params=pltpu.CompilerParams(
            collective_id=1, has_side_effects=True, vmem_limit_bytes=LIMIT
        ),
        name="front",
    )(*args)


def back_kernel(
    n,
    m,
    per,
    tile,
    q_few,
    qkv_ref,
    grad_ref,
    att_ref,
    normed_ref,
    tok_ref,
    gm_ref,
    xsend_ref,
    cot_ref,
    base_ref,
    dwu_ref,
    downtotal_ref,
    outsum_ref,
    log_ref,
    seg_ref,
    cos_ref,
    sin_ref,
    wqkvt_ref,
    mod_ref,
    vec_ref,
    sums_ref,
    vblk_ref,
    wada_ref,
    dbup_ref,
    place_ref,
    dtok_out,
    out_out,
    down_out,
    up_out,
    wo_out,
    q_out,
    dcond_ref,
    dwada_ref,
    dbada_ref,
    dvec_ref,
    qkv_v,
    grad_v,
    att_v,
    gq_v,
    dk_ref,
    dv_ref,
    normed_v,
    tok_v,
    gm_v,
    other_v,
    cot_v,
    dtok_v,
    gsc,
    psend,
    precv,
    xs_ref,
    xr_ref,
    gn_ref,
    dwq_ref,
    dwu_v,
    outsum_v,
    total_d,
    zrecv_d,
    side_u,
    total_u,
    zrecv_u,
    side_o,
    total_o,
    zrecv_o,
    q_parts,
    q_sides,
    q_totals,
    q_zrecvs,
    spr_d,
    spr_u,
    spr_q,
    opiece,
    ofar,
    ofin,
    ssend,
    srecv,
    gsend,
    grecv,
    vsend,
    vrecv,
    dsend,
    drecv,
    p_s,
    p_r,
    rz,
    d_s,
    d_r,
    s_s,
    s_r,
    ex,
    x_s,
    x_r,
    local,
):
    p = Place(n, m)
    hidden_per, small = per
    slots, quarter, width = tok_ref.shape
    length = m * quarter
    half = quarter // 2
    part = width // m
    heads = part // HEAD
    lines = p.lines
    peers = (p.sib, p.far, p.diag)
    loads = [
        pltpu.make_async_copy(src, dst, local.at[k])
        for k, (src, dst) in enumerate(
            (
                (qkv_ref, qkv_v),
                (grad_ref, grad_v),
                (att_ref, att_v),
                (downtotal_ref, total_d),
                (dwu_ref, dwu_v),
                (outsum_ref, outsum_v),
                (normed_ref, normed_v),
                (tok_ref, tok_v),
                (gm_ref, gm_v),
                (cot_ref, cot_v),
            )
        )
    ]
    for load in loads:
        load.start()
    greet(list(peers) + p.ring())

    def other_copy(s):
        return push(xsend_ref.at[s], other_v.at[s], x_s.at[s], x_r.at[s], p.far)

    def part_copy(kind, s):
        if kind == 2:
            return push(xs_ref.at[s], xr_ref.at[s], p_s.at[2, s], p_r.at[2, s], p.far)
        return push(psend.at[kind, s], precv.at[kind, s], p_s.at[kind, s], p_r.at[kind, s], p.sib)

    for s in range(slots):
        other_copy(s).start()
    red_d = Reduce(p, None, None, total_d, zrecv_d, rz.at[0], summed=True)
    red_u = Reduce(p, lambda f: dwu_v.at[f], side_u, total_u, zrecv_u, rz.at[1])
    red_o = Reduce(p, lambda f: outsum_v.at[f], side_o, total_o, zrecv_o, rz.at[2])
    cuts = [ref.shape[1] for ref in q_parts]
    red_q = [
        Reduce(
            p,
            (lambda f, k=k: q_parts[k].at[f % 2]) if few else (lambda f, k=k: q_parts[k].at[f]),
            q_sides[k],
            q_totals[k],
            q_zrecvs[k],
            rz.at[3 + k],
            only=p.d if few else None,
        )
        for k, few in enumerate(q_few)
    ]
    down = Spread(p, lambda r: spr_d.at[r], d_s.at[0], d_r.at[0])
    up = Spread(p, lambda r: spr_u.at[r], d_s.at[1], d_r.at[1])
    firsts = [sum(cuts[:k]) for k in range(len(cuts))]
    qry = [
        Spread(
            p,
            lambda r, k=k: spr_q.at[r, pl.ds(firsts[k], cuts[k])],
            d_s.at[2 + k],
            d_r.at[2 + k],
        )
        for k in range(len(cuts))
    ]
    loads[4].wait()
    red_u.start()
    loads[3].wait()
    red_d.step(0)
    for k in (0, 1, 2):
        loads[k].wait()
    tiles = length // tile

    @pl.loop(0, slots)
    def _(s):
        dk_ref[...] = jnp.zeros_like(dk_ref)
        dv_ref[...] = jnp.zeros_like(dv_ref)
        column = as_column(seg_ref[pl.ds(s, 1), :])

        @pl.loop(0, tiles)
        def _(i):
            rows = pl.ds(pl.multiple_of(i * tile, tile), tile)
            same = column == seg_ref[pl.ds(s, 1), rows]
            cosine = cos_ref[rows, :HEAD]
            sine = sin_ref[rows, :HEAD]
            ones = jnp.ones((8, HEAD), BF16)
            for h in range(heads):
                at = h * HEAD
                q = qkv_v[s, rows, at : at + HEAD]
                k = qkv_v[s, :, part + at : part + at + HEAD]
                v = qkv_v[s, :, 2 * part + at : 2 * part + at + HEAD]
                g, o = [
                    jnp.concatenate(
                        [
                            ref[s, i * (tile // quarter) + j // 2, :, j % 2 * part + at : j % 2 * part + at + HEAD]
                            for j in range(tile // half)
                        ]
                    )
                    for ref in (grad_v, att_v)
                ]
                both = g.astype(F32) * o.astype(F32)
                high = both.astype(BF16)
                low = (both - high.astype(F32)).astype(BF16)
                inner = (mm(ones, high, NT) + mm(ones, low, NT))[:1]
                scores = jnp.where(same, mm(k, q, NT), MASKED)
                weights = jnp.exp(scores - log_ref[s, h : h + 1, rows])
                dots = mm(v, g, NT)
                dscores = (weights * (dots - inner)).astype(BF16)
                dq = mm(dscores, k, TN) * (1.0 / math.sqrt(HEAD))
                gq_v[s, rows, at : at + HEAD] = (dq * cosine - swap_halves(dq) * sine).astype(BF16)
                dk_ref[:, at : at + HEAD] += mm(dscores, q, NN)
                dv_ref[:, at : at + HEAD] += mm(weights.astype(BF16), g, NN)

            def reductions(first, red, steps):
                spread = -(-len(steps) // tiles)
                for k, t in enumerate(steps):
                    pl.when((s == first) & (i == k // spread))(lambda t=t: red.step(t))

            reductions(0, red_d, range(1, lines - 1))
            reductions(1, red_u, range(1, lines - 1))
            reductions(1, red_o, range(lines - 2))
            pl.when((s == 1) & (i == 0))(down.start)

        for at in range(0, part, 128):
            size = min(128, part - at)
            dk = dk_ref[:, at : at + size]
            other = turned(dk) if size == 128 else swap_halves(dk)
            dk = dk * cos_ref[:, :size] - other * sin_ref[:, :size]
            gq_v[s, :, part + at : part + at + size] = dk.astype(BF16)
        gq_v[s, :, 2 * part :] = dv_ref[...].astype(BF16)

        theirs = pl.ds(pl.multiple_of((1 - p.c) * quarter, quarter), quarter)
        ours = pl.ds(pl.multiple_of(p.c * quarter, quarter), quarter)

        def pull(j, chip):
            rows = pl.ds(pl.multiple_of(chip * 2 * quarter, 2 * quarter), 2 * quarter)
            gsc[...] = mm(gq_v[s, rows, :], wqkvt_ref[...], NN)
            psend[j, s] = gsc[theirs].astype(BF16)
            part_copy(j, s).start()

        pull(0, 1 - p.x)
        gn_ref[s] = gsc[ours]
        pull(1, p.x)
        part_copy(0, s).wait_recv()
        xs_ref[s] = (gn_ref[s] + precv[0, s].astype(F32)).astype(BF16)
        part_copy(2, s).start()
        gn_ref[s] = gsc[ours]

        @pl.when(s == 0)
        def _():
            loads[5].wait()
            red_o.start()
            red_d.own(spr_d.at[p.d])
            red_u.step(0)

    red_o.step(lines - 2)
    loads[6].wait()
    every = slots * length
    gq_all = gq_v.reshape(every, gq_v.shape[2])
    normed_all = normed_v.reshape(every, width)
    for at in range(0, gq_v.shape[2], part):
        dwq_ref[at : at + part, :] = mm(gq_all[:, at : at + part], normed_all[...], TN).astype(BF16)
    count = place_ref.shape[1]
    placing = (iota((dwq_ref.shape[0], count), 0) == place_ref[pl.ds(p.d, 1), :]).astype(BF16)
    blocks = mm(placing, dwq_ref[...], TN).astype(BF16)
    at = 0
    for ref in q_parts:
        size = ref.shape[0] * ref.shape[1]
        ref[...] = blocks[at : at + size].reshape(ref.shape)
        at += size
    for red in (*red_q[2:], red_q[0]):
        red.start()
    red_u.own(spr_u.at[p.d])
    red_o.own(opiece)
    halved = ofin.shape[0] == 2
    mine = p.c if halved else 0
    o_far = push(opiece, ofar, d_s.at[5, 0], d_r.at[5, 0], p.far)
    for red in red_q[1:2]:
        red.start()

    def group(s, k):
        return mod_ref[s, :, k * width : (k + 1) * width]

    gain_attn = vec_ref[1:2, :width]
    gain_mlp = vec_ref[2:3, :width]
    wide = dbup_ref.shape[1]
    total_rows = lambda v: jnp.sum(v, axis=0, keepdims=True)
    for k in range(7, 10):
        loads[k].wait()
    ssend[...] = jnp.zeros_like(ssend)

    def leave(s):
        other_copy(s).wait_recv()
        part_copy(1, s).wait_recv()
        part_copy(2, s).wait_recv()
        gn = gn_ref[s] + precv[1, s].astype(F32) + xr_ref[s].astype(F32)
        normal, inverse = norm_rows(tok_v[s].astype(F32))
        dtok_v[s] = (
            gm_v[s] + norm_back(gn, normal, inverse, gain_attn * (1.0 + group(s, 1)))
        ).astype(BF16)
        extra = total_rows(cot_v[s].astype(F32) * other_v[s].astype(F32))
        ssend[s, 0:1, :width] = total_rows(gn)
        ssend[s, 1:2, :width] = total_rows(gn * normal)
        ssend[s, 2:3, :width] = sums_ref[s, 3:4, :]
        ssend[s, 3:5, :width] = sums_ref[s, 0:2, :]
        ssend[s, 5:6, :width] = sums_ref[s, 2:3, :] + extra
        ssend[s, 6:7, :width] = sums_ref[s, 4:5, :]

    ssend[0, 7:8, :wide] = dbup_ref[0:1, :]
    leave(0)
    hops = [(k, t) for t in range(lines - 1) for k in reversed(range(len(cuts)))]
    hops = hops[: -len(cuts)], hops[-len(cuts) :]
    red_q[-1].step(0)
    for s in range(1, slots):
        leave(s)

    def sums_copy(kind):
        return push(ssend, srecv.at[p.d], s_s.at[kind], s_r.at[kind], peers[kind])

    for kind in (2, 1, 0):
        sums_copy(kind).start()
    o_far.start()
    up.start()
    srecv[p.d] = ssend[...]
    stores = []

    def store(src, dst):
        stores.append(pltpu.make_async_copy(src, dst, local.at[10 + len(stores)]))
        stores[-1].start()

    store(dtok_v, dtok_out)
    base_load = pltpu.make_async_copy(base_ref, gn_ref, local.at[23])
    base_load.start()
    for k, t in hops[0][1:]:
        red_q[k].step(t)
    for kind in range(3):
        sums_copy(kind).wait_recv()
    total = srecv[0]
    for r in range(1, m):
        total = total + srecv[r]
    cols = wada_ref.shape[0]
    gmod = []
    vecs = [jnp.zeros((1, width), F32)] * 3
    for s in range(slots):
        at = lambda k, s=s: total[s, k : k + 1, :width]
        gmod.append(
            jnp.concatenate(
                [at(0), at(1) * gain_attn, at(2), at(3), at(4) * gain_mlp, at(5)], axis=1
            )
        )
        vecs = [
            vecs[0] + at(1) * (1.0 + group(s, 1)),
            vecs[1] + at(4) * (1.0 + group(s, 4)),
            vecs[2] + at(6),
        ]
    gmod = jnp.concatenate(gmod, axis=0).astype(BF16).astype(F32)
    vsend[...] = jnp.zeros_like(vsend)
    pad = hidden_per
    for g in range(n):
        gsend[g] = gmod[:, g * cols : (g + 1) * cols]
        for k, v in enumerate(vecs):
            vsend[g, k : k + 1, :small] = v[:, g * small : (g + 1) * small]
        for r in range(m):
            vsend[g, 3 + r : 4 + r, :hidden_per] = srecv[r, 0, 7:8, g * pad : g * pad + hidden_per]

    gmods = Exchange(p, lambda f: gsend.at[f], grecv, ex.at[0], ex.at[1])
    gvecs = Exchange(p, lambda f: vsend.at[f], vrecv, ex.at[2], ex.at[3])
    gmods.start()
    gvecs.start()
    grecv[p.f] = gsend[p.f]
    vrecv[p.f] = vsend[p.f]
    base_load.wait()
    for s in range(slots):
        other_v[s] = (gn_ref[s] + group(s, 5) * other_v[s].astype(F32)).astype(BF16)
    store(other_v, out_out)
    down.forward()
    for k, t in hops[1]:
        red_q[k].step(t)
    up.forward()
    for k in reversed(range(len(cuts))):
        red_q[k].own(qry[k].slot(p.d))
        qry[k].start()
    gmods.finish()
    got = jnp.concatenate([grecv[g] for g in range(n)], axis=0).astype(BF16)
    conds = jnp.concatenate([vblk_ref[g, 4 : 4 + slots] for g in range(n)], axis=0)
    dsend[...] = mm(got, wada_ref[...], NN).reshape(n, slots, conds.shape[1])

    gconds = Exchange(p, lambda f: dsend.at[f], drecv, ex.at[4], ex.at[5])
    gconds.start()
    drecv[p.f] = dsend[p.f]
    o_far.wait_recv()
    ofin[mine] = (opiece[...].astype(F32) + ofar[...].astype(F32)).astype(BF16)
    if halved:
        o_sib = push(ofin.at[mine], ofin.at[mine], d_s.at[5, 1], d_r.at[5, 1], p.sib)
        o_sib.start()
    dwada_ref[...] = mm(got, conds, TN)
    dbada_ref[...] = jnp.sum(got.astype(F32), axis=0, keepdims=True)
    gvecs.finish()
    total = vrecv[0]
    for g in range(1, n):
        total = total + vrecv[g]
    dvec_ref[...] = total
    down.finish()
    store(spr_d, down_out)
    up.finish()
    store(spr_u, up_out)
    if halved:
        push(ofin.at[1 - mine], ofin.at[1 - mine], d_s.at[5, 1], d_r.at[5, 1], p.sib).wait_recv()
    store(ofin, wo_out)
    gconds.finish()
    total = drecv[0]
    for g in range(1, n):
        total = total + drecv[g]
    dcond_ref[...] = total
    for spread in qry:
        spread.forward()
    for spread in qry:
        spread.finish()
    store(spr_q, q_out)

    for s in range(slots):
        other_copy(s).wait_send()
        for kind in range(3):
            part_copy(kind, s).wait_send()
    for red in (red_d, red_u, red_o, *red_q):
        red.drain()
    for spread in (down, up, *qry):
        spread.drain()
    o_far.wait_send()
    if halved:
        o_sib.wait_send()
    for kind in range(3):
        sums_copy(kind).wait_send()
    for exchange in (gmods, gvecs, gconds):
        exchange.drain()
    for copy in stores:
        copy.wait()


def back(n, m, per, tile, parts, args):
    qkv, grad, att, normed, tokens = args[:5]
    dwu, downtotal, outsum = args[9:12]
    vblk, w_ada, dbup, place = args[20:24]
    slots, quarter, width = tokens.shape
    dma = pltpu.SemaphoreType.DMA
    shape = jax.ShapeDtypeStruct
    vmem = pltpu.VMEM
    rows = (slots, quarter, width)
    length = m * quarter
    part = width // m
    lines = n // 2
    wide = max(width, dbup.shape[1])
    _, block, inner = downtotal.shape
    pad = dwu.shape[1]
    orows = outsum.shape[1]
    halves = 2 if orows < block else 1
    most = sum(rows_k for rows_k, _ in parts)
    cols, cond = w_ada.shape
    lanes = max(per)

    def reduced(rows, wide):
        return [vmem((lines, rows, wide), BF16)] * 2 + [vmem((lines + 1, rows, wide), BF16)]

    return pl.pallas_call(
        functools.partial(back_kernel, n, m, per, tile, [few for _, few in parts]),
        out_shape=(
            shape(rows, BF16),
            shape(rows, BF16),
            shape((m, block, inner), BF16),
            shape((m, pad, width), BF16),
            shape((halves, orows, width), BF16),
            shape((m, most, width), BF16),
            shape((slots, cond), F32),
            shape((cols, cond), F32),
            shape((1, cols), F32),
            shape((8, lanes), F32),
        ),
        in_specs=[ANY] * 12 + [VM] * (len(args) - 12),
        out_specs=(ANY,) * 6 + (VM,) * 4,
        scratch_shapes=[
            vmem(qkv.shape, BF16),
            vmem(grad.shape, BF16),
            vmem(att.shape, BF16),
            vmem(qkv.shape, BF16),
            vmem((length, part), F32),
            vmem((length, part), F32),
            vmem(normed.shape, BF16),
            vmem(rows, BF16),
            vmem(rows, F32),
            vmem(rows, BF16),
            vmem(rows, BF16),
            vmem(rows, BF16),
            vmem((2 * quarter, width), F32),
            vmem((2,) + rows, BF16),
            vmem((2,) + rows, BF16),
            vmem(rows, BF16),
            vmem(rows, BF16),
            vmem(rows, F32),
            vmem((qkv.shape[2], width), BF16),
            vmem(dwu.shape, BF16),
            vmem(outsum.shape, BF16),
        ]
        + reduced(block, inner)[1:]
        + reduced(pad, width)
        + reduced(orows, width)
        + [
            [vmem((2 if few else n, rows_k, width), BF16) for rows_k, few in parts],
            [vmem((lines, rows_k, width), BF16) for rows_k, _ in parts],
            [vmem((lines, rows_k, width), BF16) for rows_k, _ in parts],
            [vmem((lines + 1, rows_k, width), BF16) for rows_k, _ in parts],
        ]
        + [
            vmem((m, block, inner), BF16),
            vmem((m, pad, width), BF16),
            vmem((m, most, width), BF16),
            vmem((orows, width), BF16),
            vmem((orows, width), BF16),
            vmem((halves, orows, width), BF16),
            vmem((slots, 8, wide), F32),
            vmem((m, slots, 8, wide), F32),
            vmem((n, slots, cols), F32),
            vmem((n, slots, cols), F32),
            vmem((n, 8, lanes), F32),
            vmem((n, 8, lanes), F32),
            vmem((n, slots, cond), F32),
            vmem((n, slots, cond), F32),
            dma((3, slots)),
            dma((3, slots)),
            dma((6, 4 * lines + 1)),
            dma((6, 3)),
            dma((6, 3)),
            dma((3,)),
            dma((3,)),
            dma((6,)),
            dma((slots,)),
            dma((slots,)),
            dma((24,)),
        ],
        compiler_params=pltpu.CompilerParams(
            collective_id=3, has_side_effects=True, vmem_limit_bytes=LIMIT
        ),
        name="back",
    )(*args)


def finish_kernel(
    n,
    m,
    per,
    outs_ref,
    dtok_ref,
    dwada_ref,
    down_ref,
    up_ref,
    wo_ref,
    q_ref,
    dcond_ref,
    dbada_ref,
    dvec_ref,
    home_ref,
    out_ref,
    dtok_out,
    dwada_out,
    dwqkv_ref,
    dwout_ref,
    dwup_ref,
    dwdown_ref,
    dcond_out,
    dbada_out,
    dga_out,
    dgm_out,
    dbup_out,
    dbdown_out,
    up_v,
    down_v,
    q_v,
    wo_v,
    dtok_v,
    dwada_v,
    dwup_v,
    dwdown_v,
    dwqkv_v,
    dwout_v,
    out_v,
    local,
):
    hidden_per, small = per
    width = outs_ref.shape[2]
    pad = hidden_per
    part = width // m
    sources = (up_ref, down_ref, q_ref, wo_ref, outs_ref, dtok_ref, dwada_ref)
    places = (up_v, down_v, q_v, wo_v, out_v, dtok_v, dwada_v)
    loads = [
        pltpu.make_async_copy(src, dst, local.at[k])
        for k, (src, dst) in enumerate(zip(sources, places))
    ]
    for load in loads:
        load.start()
    stores = []

    def store(src, dst):
        stores.append(pltpu.make_async_copy(src, dst, local.at[7 + len(stores)]))
        stores[-1].start()

    loads[0].wait()
    dwup_v[...] = jnp.concatenate([up_v[r][:hidden_per] for r in range(m)]).astype(F32).T
    store(dwup_v, dwup_ref)
    loads[1].wait()
    for r in range(m):
        piece = down_v[r, :small].astype(F32)
        for g in range(n):
            at = (g * m + r) * hidden_per
            dwdown_v[:, at : at + hidden_per] = piece[:, g * pad : g * pad + hidden_per]
    store(dwdown_v, dwdown_ref)
    loads[2].wait()
    count = q_v.shape[0] * q_v.shape[1]
    f = lax.axis_index("fsdp")
    homing = (iota((dwqkv_ref.shape[0], count), 0) == home_ref[pl.ds(f, 1), :]).astype(BF16)
    dwqkv_v[...] = mm(homing, q_v[...].reshape(count, width), NN)
    store(dwqkv_v, dwqkv_ref)
    for k, src, dst in ((4, out_v, out_ref), (5, dtok_v, dtok_out), (6, dwada_v, dwada_out)):
        loads[k].wait()
        store(src, dst)
    loads[3].wait()
    piece = wo_v[...].reshape(-1, width)[:small].astype(F32)
    heads = part // HEAD
    for r in range(m):
        for h in range(heads):
            at = r * part + h * HEAD
            dwout_v[:, (h * m + r) * HEAD : (h * m + r + 1) * HEAD] = piece[:, at : at + HEAD]
    store(dwout_v, dwout_ref)
    dcond_out[...] = dcond_ref[...].astype(BF16)
    dbada_out[...] = dbada_ref[0, :]
    for row, ref in ((0, dga_out), (1, dgm_out), (2, dbdown_out)):
        ref[...] = dvec_ref[row, :small]
    dbup_out[...] = jnp.concatenate(
        [dvec_ref[3 + r : 4 + r, :hidden_per] for r in range(m)], axis=1
    ).reshape(-1)
    for copy in stores:
        copy.wait()


def finish(n, m, per, columns, args):
    outs, dtok, dwada, down, up, wo, q, dcond, dbada = args[:9]
    hidden_per, small = per
    rows = outs.shape
    width = rows[2]
    shape = jax.ShapeDtypeStruct
    vmem = pltpu.VMEM
    sizes = (
        (width, m * hidden_per),
        (small, n * m * hidden_per),
        (columns, width),
        (small, width),
    )
    return pl.pallas_call(
        functools.partial(finish_kernel, n, m, per),
        out_shape=(
            shape(rows, BF16),
            shape(rows, BF16),
            shape(dwada.shape, F32),
            shape(sizes[2], F32),
            shape(sizes[3], F32),
            shape(sizes[0], F32),
            shape(sizes[1], F32),
            shape(dcond.shape, BF16),
            shape(dbada.shape[1:], F32),
            shape((small,), F32),
            shape((small,), F32),
            shape((m * hidden_per,), F32),
            shape((small,), F32),
        ),
        in_specs=[ANY] * 7 + [VM] * 4,
        out_specs=(ANY,) * 7 + (VM,) * 6,
        scratch_shapes=[
            vmem(up.shape, BF16),
            vmem(down.shape, BF16),
            vmem(q.shape, BF16),
            vmem(wo.shape, BF16),
            vmem(rows, BF16),
            vmem(dwada.shape, F32),
        ]
        + [vmem(size, F32) for size in sizes]
        + [vmem(rows, BF16), pltpu.SemaphoreType.DMA((14,))],
        compiler_params=pltpu.CompilerParams(vmem_limit_bytes=LIMIT),
        name="finish",
    )(*args)


def column_plan(shards_n, ranks, columns):
    per = columns // shards_n
    rank_of = (np.arange(columns) // HEAD) % ranks
    lists = [
        [[c for c in range(per) if rank_of[f * per + c] == r] for r in range(ranks)]
        for f in range(shards_n)
    ]
    most = max(len(l) for row in lists for l in row)
    most = -(-most // 16) * 16
    take = np.full((shards_n, ranks, most), -1, np.int32)
    place = np.full((ranks, shards_n * most), -1, np.int32)
    home = np.full((shards_n, ranks * most), -1, np.int32)
    for r in range(ranks):
        order = {c: i for i, c in enumerate(np.flatnonzero(rank_of == r))}
        for f in range(shards_n):
            for i, c in enumerate(lists[f][r]):
                take[f, r, i] = c
                place[r, f * most + i] = order[f * per + c]
                home[f, r * most + i] = c
    return most, take, place, home


def row_parts(shards_n, ranks, columns):
    per = columns // shards_n
    rank_of = (np.arange(columns) // HEAD) % ranks
    lists = [
        [[c for c in range(per) if rank_of[f * per + c] == r] for r in range(ranks)]
        for f in range(shards_n)
    ]
    most = max(len(l) for row in lists for l in row)
    least = min(len(l) for row in lists for l in row)
    uneven = all(
        len(lists[f][r]) == (most if f // 2 == r else least)
        for f in range(shards_n)
        for r in range(ranks)
    )
    if uneven and least % 32 == 0 and (most - least) % 16 == 0 and most > least and shards_n == 2 * ranks:
        parts = [(least // 2, False), (least // 2, False), (most - least, True)]
    else:
        parts = [(round16(most), False)]
    place = []
    for r in range(ranks):
        order = {c: i for i, c in enumerate(np.flatnonzero(rank_of == r))}
        row, first = [], 0
        for rows, few in parts:
            for f in (2 * r, 2 * r + 1) if few else range(shards_n):
                own = lists[f][r][first : first + rows]
                row += [order[f * per + c] for c in own] + [-1] * (rows - len(own))
            first += rows
        place.append(row)
    home = []
    for f in range(shards_n):
        row = []
        for r in range(ranks):
            first = 0
            for rows, few in parts:
                own = lists[f][r][first : first + rows]
                row += own + [-1] * (rows - len(own))
                first += rows
        home.append(row)
    return parts, np.asarray(place, np.int32), np.asarray(home, np.int32)


def shards(
    tokens,
    condition,
    segments,
    w_ada,
    b_ada,
    gain_attn,
    w_qkv,
    w_out,
    gain_mlp,
    w_up,
    b_up,
    w_down,
    b_down,
    cotangent,
):
    slots, quarter, width = tokens.shape
    length = segments.shape[1]
    n = lax.axis_size("fsdp")
    m = lax.axis_size("dp")
    hidden_per = b_up.shape[0] // m
    small = gain_attn.shape[0]
    per = (hidden_per, small)
    columns = w_qkv.shape[1]
    most, take, place, _ = column_plan(n, m, columns * n)
    place = jnp.asarray(place)
    tile = 2 * quarter if n * most <= 2 * width else quarter
    parts, place_back, home = row_parts(n, m, columns * n)
    place_back = jnp.asarray(place_back)
    cosine, sine = [jnp.asarray(np.concatenate([v, v], axis=1)) for v in rope_table(length)]

    (
        qkv,
        normed,
        attended,
        logs,
        grad_middle,
        base,
        far_part,
        grad_attended,
        dw_up,
        down_total,
        out_sum,
        mod,
        vec,
        w_qkv_t,
        vec_blocks,
        db_up,
        sums,
    ) = front(
        n,
        m,
        length,
        tile,
        most,
        (
            tokens,
            cotangent,
            condition,
            segments,
            w_ada.T,
            b_ada,
            b_up,
            gain_attn,
            gain_mlp,
            b_down,
            w_qkv.T,
            w_out.T,
            w_up,
            w_down.T,
            jnp.asarray(take.reshape(n * m, most)),
            place,
            cosine,
            sine,
        ),
    )
    d_tokens, outputs, down_all, up_all, out_all, qkv_all, d_cond, d_w_ada, d_b_ada, d_vec = back(
        n,
        m,
        per,
        tile,
        parts,
        (
            qkv,
            grad_attended,
            attended,
            normed,
            tokens,
            grad_middle,
            far_part,
            cotangent,
            base,
            dw_up,
            down_total,
            out_sum,
            logs,
            segments,
            cosine,
            sine,
            w_qkv_t,
            mod,
            vec,
            sums,
            vec_blocks,
            w_ada.T,
            db_up,
            place_back,
        ),
    )
    (
        outputs,
        d_tokens,
        d_w_ada,
        d_w_qkv,
        d_w_out,
        d_w_up,
        d_w_down,
        d_cond,
        d_b_ada,
        d_gain_attn,
        d_gain_mlp,
        d_b_up,
        d_b_down,
    ) = finish(
        n,
        m,
        per,
        columns,
        (
            outputs,
            d_tokens,
            d_w_ada,
            down_all,
            up_all,
            out_all,
            qkv_all,
            d_cond,
            d_b_ada,
            d_vec,
            jnp.asarray(home),
        ),
    )
    return (
        outputs,
        d_tokens,
        d_cond,
        d_w_ada.T,
        d_b_ada,
        d_gain_attn,
        d_w_qkv.T,
        d_w_out.T,
        d_gain_mlp,
        d_w_up,
        d_b_up,
        d_w_down.T,
        d_b_down,
    )


def solution(mesh):
    return jax.shard_map(
        shards,
        mesh=mesh,
        in_specs=(
            P("fsdp", "dp", None),
            P("fsdp", None),
            P("fsdp", None),
            P(None, "fsdp"),
            P("fsdp"),
            P("fsdp"),
            P(None, "fsdp"),
            P(None, "fsdp"),
            P("fsdp"),
            P(None, "fsdp"),
            P("fsdp"),
            P(None, "fsdp"),
            P("fsdp"),
            P("fsdp", "dp", None),
        ),
        out_specs=(
            P("fsdp", "dp", None),
            P("fsdp", "dp", None),
            P("fsdp", None),
            P(None, "fsdp"),
            P("fsdp"),
            P("fsdp"),
            P(None, "fsdp"),
            P(None, "fsdp"),
            P("fsdp"),
            P(None, "fsdp"),
            P("fsdp"),
            P(None, "fsdp"),
            P("fsdp"),
        ),
        check_vma=False,
    )
```

```python
import functools
import math

import jax
import jax.numpy as jnp
import numpy as np
from jax import lax
from jax.experimental import pallas as pl
from jax.experimental.pallas import tpu as pltpu
from jax.sharding import PartitionSpec as P

HEAD = 64
EPS = 1e-05
ROPE_BASE = 10000.0
MASKED = -1e30
F32 = jnp.float32
BF16 = jnp.bfloat16

NN = (((1,), (0,)), ((), ()))
NT = (((1,), (1,)), ((), ()))
TN = (((0,), (0,)), ((), ()))


def mm(a, b, dims):
    return lax.dot_general(a, b, dims, preferred_element_type=F32)


def rope_table(length):
    inverse = ROPE_BASE ** (-2.0 * np.arange(HEAD // 2) / HEAD)
    angles = np.arange(length)[:, None] * inverse[None, :]
    cosine = np.concatenate([np.cos(angles)] * 2, axis=1)
    sine = np.concatenate([-np.sin(angles), np.sin(angles)], axis=1)
    return cosine.astype(np.float32), sine.astype(np.float32)


def swap_halves(v):
    half = HEAD // 2
    return jnp.concatenate([v[..., half:], v[..., :half]], axis=-1)


MESH = pl.DeviceIdType.MESH
VM = pl.BlockSpec(memory_space=pltpu.VMEM)
ANY = pl.BlockSpec(memory_space=pl.ANY)
LIMIT = (63 << 20) + (768 << 10)


def round16(size):
    return -(-size // 16) * 16


def iota(shape, dim):
    return lax.broadcasted_iota(jnp.int32, shape, dim)


def greet(peers, meanwhile=None):
    barrier = pltpu.get_barrier_semaphore()
    for peer in peers:
        pl.semaphore_signal(barrier, inc=1, device_id=peer, device_id_type=MESH)
    if meanwhile is not None:
        meanwhile()
    pl.semaphore_wait(barrier, len(peers))


def push(src, dst, send, recv, peer):
    return pltpu.make_async_remote_copy(
        src_ref=src,
        dst_ref=dst,
        send_sem=send,
        recv_sem=recv,
        device_id=peer,
        device_id_type=MESH,
    )


class Place:
    def __init__(self, n, m):
        self.n, self.m = n, m
        self.f = lax.axis_index("fsdp")
        self.d = lax.axis_index("dp")
        self.lines = n // 2
        self.a = self.f // 2
        self.b = self.f % 2
        self.x = self.d // 2
        self.c = self.d % 2
        self.sib_d = self.x * 2 + 1 - self.c
        self.far_d = (1 - self.x) * 2 + self.c
        self.diag_d = (1 - self.x) * 2 + 1 - self.c
        self.sib = (self.f, self.sib_d)
        self.far = (self.f, self.far_d)
        self.diag = (self.f, self.diag_d)
        self.side = (self.a * 2 + 1 - self.b, self.d)
        last = self.lines - 1
        self.right = (jnp.minimum(self.a + 1, last) * 2 + self.b, self.d)
        self.left = (jnp.maximum(self.a - 1, 0) * 2 + self.b, self.d)
        self.has_right = self.a < last
        self.has_left = self.a > 0

    def ring_f(self, step):
        return (self.f + step + self.n) % self.n

    def ring(self):
        return [(self.ring_f(i), self.d) for i in range(1, self.n)]

    def line_peers(self):
        return [((self.a + i) % self.lines * 2 + self.b, self.d) for i in range(1, self.lines)] + [
            self.side
        ]


class Gather:
    def __init__(self, p, src, slot, sems):
        self.p, self.src, self.slot, self.sems = p, src, slot, sems

    def place(self, way, t):
        return jnp.clip(self.p.a + (t if way else -t), 0, self.p.lines - 1)

    def line_copy(self, way, t):
        p, j = self.p, self.place(way, t)
        block = self.slot(j * 2 + p.b)
        leave = 4 * p.lines if way and t == 0 else p.lines + j
        return push(
            self.src if t == 0 else block,
            block,
            self.sems.at[leave],
            self.sems.at[j],
            p.left if way else p.right,
        )

    def side_copy(self, way, t, theirs=False):
        p, j = self.p, self.place(way, t)
        block = self.slot(j * 2 + (1 - p.b if theirs else p.b))
        return push(
            self.src if t == 0 else block,
            block,
            self.sems.at[2 * p.lines + j],
            self.sems.at[3 * p.lines + j],
            p.side,
        )

    def held(self, way, t):
        p = self.p
        return p.a + t < p.lines if way else p.a - t >= 0

    def onward(self, way):
        return self.p.has_left if way else self.p.has_right

    def start(self):
        for way in range(2):
            pl.when(self.onward(way))(lambda way=way: self.line_copy(way, 0).start())
        self.side_copy(0, 0).start()

    def step(self, t):
        for way in range(2):

            @pl.when(self.held(way, t))
            def _(way=way):
                self.line_copy(way, t).wait_recv()
                if t < self.p.lines - 1:
                    pl.when(self.onward(way))(lambda: self.line_copy(way, t).start())
                self.side_copy(way, t).start()

    def finish(self):
        self.side_copy(0, 0, True).wait_recv()
        for t in range(1, self.p.lines):
            for way in range(2):
                pl.when(self.held(way, t))(
                    lambda way=way, t=t: self.side_copy(way, t, True).wait_recv()
                )

    def drain(self):
        self.side_copy(0, 0).wait_send()
        for way in range(2):
            pl.when(self.onward(way))(lambda way=way: self.line_copy(way, 0).wait_send())
        for t in range(1, self.p.lines):
            for way in range(2):

                @pl.when(self.held(way, t))
                def _(way=way, t=t):
                    if t < self.p.lines - 1:
                        pl.when(self.onward(way))(lambda: self.line_copy(way, t).wait_send())
                    self.side_copy(way, t).wait_send()


class Both:
    def __init__(self, *gathers):
        self.gathers = gathers

    def start(self):
        for g in self.gathers:
            g.start()

    def step(self, t):
        for g in self.gathers:
            g.step(t)

    def finish(self):
        for g in self.gathers:
            g.finish()

    def drain(self):
        for g in self.gathers:
            g.drain()


def gather_halves(p, src, buf, sems, first):
    rows = src.shape[0]
    if rows % 32:
        return Gather(p, src, lambda f: buf.at[f], sems.at[first])
    cut = [pl.ds(h * rows // 2, rows // 2) for h in range(2)]
    return Both(
        *[
            Gather(p, src.at[cut[h]], lambda f, h=h: buf.at[f, cut[h]], sems.at[first + h])
            for h in range(2)
        ]
    )


class Reduce:
    def __init__(self, p, src, side, total, zrecv, sems, summed=False, only=None):
        self.p, self.src, self.side, self.total = p, src, side, total
        self.zrecv, self.sems, self.summed, self.only = zrecv, sems, summed, only

    def order(self):
        lines = self.p.lines
        if self.only is not None:
            return [self.only]
        return [j for k in range(lines // 2) for j in (lines - 1 - k, k)]

    def side_copy(self, j):
        p = self.p
        return push(
            self.src(2 * j + 1 - p.b), self.side.at[j], self.sems.at[j], self.sems.at[p.lines + j], p.side
        )

    def line_copy(self, way, j):
        p = self.p
        at = jnp.where(j == p.a - 1, p.lines, j) if way else j
        return push(
            self.total.at[j],
            self.zrecv.at[at],
            self.sems.at[2 * p.lines + j],
            self.sems.at[3 * p.lines + at],
            p.left if way else p.right,
        )

    def line_wait(self, way, j):
        p = self.p
        at = jnp.where(j == p.a, p.lines, j) if way else j
        block = self.zrecv.at[at]
        push(
            block,
            block,
            self.sems.at[2 * p.lines + j],
            self.sems.at[3 * p.lines + at],
            p.left if way else p.right,
        ).wait_recv()
        return block[...].astype(F32)

    def start(self):
        for j in self.order():
            self.side_copy(j).start()

    def side_sum(self, j):
        p = self.p
        self.side_copy(j).wait_recv()
        mine = self.src(2 * j + p.b)[...].astype(F32)
        self.total[j] = (mine + self.side[j].astype(F32)).astype(BF16)

    def step(self, t):
        p = self.p
        if 2 * t < p.lines and not self.summed:
            for j in self.order()[2 * t : 2 * t + 2]:
                self.side_sum(j)
        for way in range(2):
            j = t - (p.lines - 1 - p.a) if way else p.lines - 1 - (t - p.a)
            ahead = (j >= 0) & (j < p.a) if way else (j < p.lines) & (j > p.a)
            behind = p.has_right if way else p.has_left
            if self.only is not None:
                ahead &= j == self.only

            @pl.when(ahead)
            def _(way=way, j=j, behind=behind):
                @pl.when(behind)
                def _():
                    arrived = self.line_wait(way, j)
                    self.total[j] = (self.total[j].astype(F32) + arrived).astype(BF16)

                self.line_copy(way, j).start()

    def own(self, out):
        p = self.p
        held = True if self.only is None else p.a == self.only
        for way in range(2):

            @pl.when(held & (p.has_right if way else p.has_left))
            def _(way=way):
                arrived = self.line_wait(way, p.a)
                self.total[p.a] = (self.total[p.a].astype(F32) + arrived).astype(BF16)

        if self.only is None:
            out[...] = self.total[p.a]
        else:
            out[...] = jnp.zeros(out.shape, BF16)

            @pl.when(held)
            def _():
                out[...] = self.total[p.a]

    def drain(self):
        p = self.p
        for j in range(p.lines) if self.only is None else [self.only]:
            if not self.summed:
                self.side_copy(j).wait_send()
            for way in range(2):
                ahead = p.a > j if way else p.a < j
                pl.when(ahead)(lambda way=way, j=j: self.line_copy(way, j).wait_send())


class Exchange:
    def __init__(self, p, src, buf, send, recv):
        self.p, self.src, self.buf, self.send, self.recv = p, src, buf, send, recv

    def start(self):
        p = self.p
        for i in range(1, p.n):
            peer = p.ring_f(i)
            push(self.src(peer), self.buf.at[p.f], self.send, self.recv, (peer, p.d)).start()

    def every(self):
        some = self.buf.at[pl.ds(0, self.p.n - 1)]
        return push(some, some, self.send, self.recv, self.p.side)

    def finish(self):
        self.every().wait_recv()

    def drain(self):
        self.every().wait_send()


class Spread:
    def __init__(self, p, slot, send, recv):
        self.p, self.slot, self.send, self.recv = p, slot, send, recv

    def copy(self, kind):
        p = self.p
        block = self.slot(p.far_d if kind == 2 else p.d)
        return push(block, block, self.send.at[kind], self.recv.at[kind], p.far if kind == 1 else p.sib)

    def start(self):
        self.copy(1).start()
        self.copy(0).start()

    def forward(self):
        self.copy(1).wait_recv()
        self.copy(2).start()

    def finish(self):
        self.copy(0).wait_recv()
        self.copy(2).wait_recv()

    def drain(self):
        for kind in range(3):
            self.copy(kind).wait_send()


def norm_rows(stream):
    average = jnp.mean(stream, axis=-1, keepdims=True)
    centered = stream - average
    variance = jnp.mean(centered * centered, axis=-1, keepdims=True)
    inverse = lax.rsqrt(variance + EPS)
    return centered * inverse, inverse


def norm_back(grad, normal, inverse, factor):
    e = grad * factor
    mean_e = jnp.mean(e, axis=-1, keepdims=True)
    mean_en = jnp.mean(e * normal, axis=-1, keepdims=True)
    return inverse * (e - mean_e - normal * mean_en)


def turned(v):
    lanes = iota(v.shape, 1)
    half = HEAD // 2
    return jnp.where(lanes % HEAD < half, pltpu.roll(v, 128 - half, 1), pltpu.roll(v, half, 1))


def gelu_parts(h):
    root = math.sqrt(2.0 / math.pi)
    square = h * h
    t = jnp.tanh(root * h * (1.0 + 0.044715 * square))
    half = 0.5 * (1.0 + t)
    slope = half + 0.5 * h * (1.0 - t * t) * (root * (1.0 + 3.0 * 0.044715 * square))
    return h * half, slope


def compact(blocks, per):
    count, rows, lanes = blocks.shape
    flat = blocks.reshape(count * rows, lanes)
    if rows == per:
        return flat
    want = iota((count * per, count * rows), 0)
    have = iota((count * per, count * rows), 1)
    chosen = (have == want // per * rows + want % per).astype(BF16)
    return mm(chosen, flat, NN).astype(BF16)


def as_column(row):
    size = row.shape[1]
    return jnp.transpose(jnp.broadcast_to(row, (128, size)))[:, :1]


def front_kernel(
    n,
    m,
    per,
    tile,
    tok_ref,
    cot_ref,
    cond_ref,
    seg_ref,
    wada_ref,
    bada_ref,
    bup_ref,
    ga_ref,
    gmlp_ref,
    bdown_ref,
    wqkv_ref,
    wout_ref,
    wup_ref,
    wdown_ref,
    take_ref,
    place_ref,
    cos_ref,
    sin_ref,
    qkv_out,
    normed_out,
    att_out,
    log_out,
    gm_out,
    base_out,
    xsend_out,
    gatt_out,
    dwu_out,
    downtotal_out,
    outsum_out,
    mod_ref,
    vecs_ref,
    wqkvt_ref,
    vec_out,
    dbup_ref,
    sums_ref,
    qkv_ref,
    att_v,
    arecv,
    log_v,
    mod_send,
    mod_recv,
    vsrc,
    vbuf,
    qsrc,
    qbuf,
    osrc,
    obuf,
    usrc,
    ubuf,
    dsrc,
    dbuf,
    cot_v,
    own_ref,
    br_ref,
    mid_ref,
    nrm_ref,
    inv_ref,
    nm_ref,
    ct_ref,
    act_ref,
    gp_ref,
    gsc,
    psend,
    precv,
    xs_ref,
    xr_ref,
    gn_ref,
    bo_ref,
    gba_ref,
    gm_ref,
    gsend,
    grecv,
    dwd_ref,
    dwu_ref,
    dwo_ref,
    oswap,
    side_d,
    total_d,
    ex,
    gz,
    ts,
    tr,
    os_,
    or_,
    as_,
    ar,
    cs,
    cr,
    n_s,
    n_r,
    p_s,
    p_r,
    g_s,
    g_r,
    rz,
    o_s,
    o_r,
    local,
):
    p = Place(n, m)
    slots, quarter, width = tok_ref.shape
    half = quarter // 2
    part = width // m
    heads = part // HEAD
    hidden_per, small = per
    pad = usrc.shape[0]
    inner = n * hidden_per
    halves = obuf.shape[1]
    length = m * quarter
    tall_ref = gp_ref
    normed_ref = act_ref.reshape(slots, length, width)
    filled = pad > hidden_per or qbuf.shape[0] * osrc.shape[0] > width
    spare = qbuf.reshape(n * qsrc.shape[0], width)
    dense = [spare.at[pl.ds(k * width, width)] for k in range(3 if filled else 0)]
    peers = (p.sib, p.far, p.diag)
    ranks = (p.sib_d, p.far_d, p.diag_d)
    own_tokens = pltpu.make_async_copy(tok_ref, tall_ref.at[p.d], local.at[2])
    own_tokens.start()
    own_cots = [
        pltpu.make_async_copy(cot_ref, dst, local.at[3 + k])
        for k, dst in enumerate((cot_v, ct_ref.at[p.d]))
    ]
    for copy in own_cots:
        copy.start()
    log_v[...] = jnp.zeros_like(log_v)

    def prepare():
        vsrc[...] = jnp.zeros_like(vsrc)
        for row, ref in enumerate((ga_ref, gmlp_ref, bdown_ref)):
            vsrc[row : row + 1, : ref.shape[0]] = ref[...].reshape(1, -1)
        vsrc[4 : 4 + slots, :] = cond_ref[...]
        b_up = bup_ref[...].reshape(1, -1)
        for k in range(0, b_up.shape[1], 128):
            some = b_up[:, k : k + 128]
            vsrc[8 + k // 128 : 9 + k // 128, : some.shape[1]] = some
        columns = wqkv_ref.shape[0]
        most = qsrc.shape[0]
        taking = take_ref[pl.ds(p.f * m + p.d, 1), :]
        chosen = (iota((columns, most), 0) == taking).astype(BF16)
        qsrc[...] = mm(chosen, wqkv_ref[...], TN).astype(BF16)

    greet(list(peers) + p.ring(), prepare)

    vec = Exchange(p, lambda f: vsrc, vbuf, ex.at[0], ex.at[1])
    vec.start()

    def token_copy(kind, k):
        s, rows = k // 2, pl.ds(k % 2 * half, half)
        if kind == 2:
            block = tall_ref.at[p.far_d, s, rows]
            return push(block, block, ts.at[kind, k], tr.at[kind, k], p.sib)
        return push(
            tok_ref.at[s, rows],
            tall_ref.at[p.d, s, rows],
            ts.at[kind, k],
            tr.at[kind, k],
            p.sib if kind == 0 else p.far,
        )

    qry = gather_halves(p, qsrc, qbuf, gz, 0)
    qry.start()
    for k in range(2 * slots):
        token_copy(1, k).start()
    for k in range(2 * slots):
        token_copy(0, k).start()
    vbuf[p.f] = vsrc[...]
    qbuf[p.f] = qsrc[...]

    lane = iota((1, width), 1)
    rank, rest = lane // part, lane % part
    want = (rest // HEAD * m + rank) * HEAD + rest % HEAD
    chosen = (iota((width, width), 0) == want).astype(BF16)
    got = mm(wout_ref[...], chosen, NN).astype(BF16)
    if small < osrc.shape[0]:
        got = jnp.concatenate([got, jnp.zeros((osrc.shape[0] - small, width), BF16)])
    osrc[...] = got
    split = osrc.shape[0] // halves
    mine = p.c if halves == 2 else 0
    out = Gather(
        p,
        osrc.at[pl.ds(pl.multiple_of(mine * split, 16), split)],
        lambda f: obuf.at[f, mine],
        gz.at[2],
    )
    for h in range(halves):
        obuf[p.f, h] = osrc[h * split : (h + 1) * split]

    ups = wup_ref.shape[1]
    at, lane = iota((pad, ups), 0), iota((pad, ups), 1)
    chosen = ((lane == at + p.d * hidden_per) & (at < hidden_per)).astype(BF16)
    usrc[...] = mm(chosen, wup_ref[...], NT).astype(BF16)
    ubuf[p.f] = usrc[...]
    up = Gather(p, usrc, lambda f: ubuf.at[f], gz.at[3])
    block = dsrc.shape[0]
    lane = iota((1, inner), 1)
    want = (lane // hidden_per * m + p.d) * hidden_per + lane % hidden_per
    got = jnp.zeros((small, inner), F32)
    for at in range(0, wdown_ref.shape[1], width):
        chosen = (iota((width, inner), 0) + at == want).astype(BF16)
        got = got + mm(wdown_ref[:, at : at + width], chosen, NN)
    got = got.astype(BF16)
    if small < block:
        got = jnp.concatenate([got, jnp.zeros((block - small, inner), BF16)])
    dsrc[...] = got
    dbuf[p.f] = got
    down = Gather(p, dsrc, lambda f: dbuf.at[f], gz.at[4])

    def pass_on(k):
        token_copy(1, k).wait_recv()
        token_copy(2, k).start()

    qry.step(1)
    vec.finish()
    vecs = vbuf[...].reshape(n * 16, 128)
    mod_cols = mm(vecs, wada_ref[...], NT) + bada_ref[...].reshape(1, -1).astype(F32)
    mod_send[...] = mod_cols.reshape(n, 16, mod_cols.shape[1])[:, 4 : 4 + slots]
    mod_recv[p.f] = mod_send[p.f]

    mods = Exchange(p, lambda f: mod_send.at[f], mod_recv, ex.at[2], ex.at[3])
    mods.start()
    vec_out[...] = vbuf[...]
    vecs_ref[...] = jnp.zeros_like(vecs_ref)
    ups = bup_ref.shape[0]
    b_up = jnp.zeros((n * 16, pad), F32)
    for k in range(0, ups, 128):
        lane = iota((128, pad), 1)
        chosen = (iota((128, pad), 0) + k == lane + p.d * hidden_per) & (lane < hidden_per)
        some = mm(vecs, chosen.astype(BF16), NN)
        b_up = b_up + jnp.where(iota((n * 16, pad), 0) % 16 == 8 + k // 128, some, 0.0)
    for g in range(n):
        vecs_ref[0:1, g * hidden_per : (g + 1) * hidden_per] = jnp.sum(
            b_up[16 * g : 16 * (g + 1)], axis=0, keepdims=True
        )[:, :hidden_per]
        rest = vecs[16 * g : 16 * g + 8].astype(F32)
        for k in range(3):
            vecs_ref[k + 1 : k + 2, g * small : (g + 1) * small] = rest[k : k + 1, :small]
    for k in range(2, p.lines - 1):
        qry.step(k)
    pass_on(0)
    qry.step(p.lines - 1)
    out.start()
    mods.finish()
    cols = mod_cols.shape[1]
    for g in range(n):
        for s in range(slots):
            mod_ref[s, :, g * cols : (g + 1) * cols] = mod_recv[g, s : s + 1]
    gain = vecs_ref[1:2, :width]

    pass_on(1)
    pass_on(2)
    def cot_copy(kind, s):
        if kind == 2:
            block = ct_ref.at[p.far_d, s]
            return push(block, block, cs.at[kind, s], cr.at[kind, s], p.sib)
        return push(
            cot_ref.at[s],
            ct_ref.at[p.d, s],
            cs.at[kind, s],
            cr.at[kind, s],
            p.sib if kind else p.far,
        )

    for s in range(slots):
        cot_copy(0, s).start()

    qry.finish()
    up.start()
    count = n * qsrc.shape[0]
    flat_rows = qbuf[...].reshape(count, width)
    got = jnp.zeros((3 * part, width), F32)
    for at in range(0, count, width):
        some = place_ref[pl.ds(p.d, 1), at : at + width]
        placing = (iota((3 * part, some.shape[1]), 0) == some).astype(BF16)
        got = got + mm(placing, flat_rows[at : at + width], NN)
    wqkvt_ref[...] = got.astype(BF16)
    own_tokens.wait()

    def chunk(i):
        q = jnp.where(
            i < 2, p.d, jnp.where(i < 4, p.sib_d, jnp.where(i % 2 == 0, p.far_d, p.diag_d))
        )
        s = jnp.where(i < 4, i % 2, (i - 4) // 2)
        return q, s, pl.ds(pl.multiple_of(q * quarter, quarter), quarter)

    def keeps(i):
        _, s, rows = chunk(i)
        return [
            pltpu.make_async_copy(src.at[s, rows], dst.at[s, rows], local.at[k])
            for k, (src, dst) in enumerate(((qkv_ref, qkv_out), (normed_ref, normed_out)))
        ]

    @pl.loop(0, m * slots)
    def _(i):
        for k in range(2):

            @pl.when(i == 2 + k)
            def _(k=k):
                token_copy(0, 2 * k).wait_recv()
                token_copy(0, 2 * k + 1).wait_recv()

            @pl.when(i == 5 + 2 * k)
            def _(k=k):
                token_copy(2, 2 * k).wait_recv()
                token_copy(2, 2 * k + 1).wait_recv()

        pl.when(i == 2)(lambda: out.step(1))
        pl.when(i == 4)(lambda: pass_on(3))

        q, s, rows = chunk(i)
        normal, _ = norm_rows(tall_ref[q, s].astype(F32))
        shift = mod_ref[s, :, :width]
        scale = mod_ref[s, :, width : 2 * width]
        normed = (normal * (gain * (1.0 + scale)) + shift).astype(BF16)
        normed_ref[s, rows, :] = normed
        got = mm(normed, wqkvt_ref[...], NT)
        cosine = cos_ref[rows, :]
        sine = sin_ref[rows, :]
        lanes = iota((quarter, 128), 1)
        for t in range(0, 2 * part, 128):
            piece = got[:, t : t + 128]
            piece = piece * cosine + turned(piece) * sine
            piece = jnp.where(lanes + t < part, piece * (1.0 / math.sqrt(HEAD)), piece)
            qkv_ref[s, rows, t : t + 128] = piece.astype(BF16)
        qkv_ref[s, rows, 2 * part :] = got[:, 2 * part :].astype(BF16)
        for keep in keeps(i):
            keep.start()

    def att_copy(kind, s):
        return push(
            att_v.at[s, ranks[kind]], arecv.at[s, p.d], as_.at[kind, s], ar.at[kind, s], peers[kind]
        )

    def swap(h):
        return push(obuf.at[:, h], obuf.at[:, h], os_.at[0], or_.at[0], p.sib)

    def weight_ready():
        out.finish()
        if halves == 2:
            swap(p.c).start()
            swap(1 - p.c).wait_recv()
        if filled:
            qry.drain()
        if small < osrc.shape[0]:
            dense[0][...] = compact(obuf[:, 0], small)

    def group(s, k):
        return mod_ref[s, :, k * width : (k + 1) * width]

    gain_mlp = vecs_ref[2:3, :width]
    b_down = vecs_ref[3:4, :width]
    if small < osrc.shape[0]:
        w_out = lambda: dense[0][...]
    else:
        w_out = lambda: obuf[...].reshape(width, width)
    if pad > hidden_per:
        w_up = lambda: dense[1][...]
    else:
        w_up = lambda: ubuf[...].reshape(inner, width)
    if small < block:
        w_down = lambda: dense[2][...]
    else:
        w_down = lambda: dbuf[...].reshape(width, inner)

    def nm_copy(kind, s, h):
        k = s * 2 + h
        rows = nm_ref.at[p.far_d if kind == 2 else p.d, s, pl.ds(h * half, half)]
        return push(rows, rows, n_s.at[kind, k], n_r.at[kind, k], p.far if kind == 1 else p.sib)

    def enter(s):
        for kind in range(3):
            att_copy(kind, s).wait_recv()
        arecv[s, p.d] = att_v[s, p.d]
        for r in range(m):
            for h in range(2):
                own_ref[s, h * half : (h + 1) * half, r * part : (r + 1) * part] = arecv[
                    s, r, :, h * part : (h + 1) * part
                ]
        branch = mm(own_ref[s], w_out(), NT)
        br_ref[s] = branch
        middle = tall_ref[p.d, s].astype(F32) + group(s, 2) * branch
        mid_ref[s] = middle
        normal, inverse = norm_rows(middle)
        nrm_ref[s] = normal
        inv_ref[s] = inverse
        nm_ref[p.d, s] = (normal * (gain_mlp * (1.0 + group(s, 4))) + group(s, 3)).astype(BF16)
        for kind in (1, 0):
            for h in range(2):
                nm_copy(kind, s, h).start()

    def pass_rows(s):
        for h in range(2):
            nm_copy(1, s, h).wait_recv()
            nm_copy(2, s, h).start()

    def arrived(kind, s):
        for h in range(2):
            nm_copy(kind, s, h).wait_recv()

    for k in range(2, p.lines):
        out.step(k)
    up.step(1)
    tiles = length // tile

    @pl.loop(0, slots * tiles)
    def _(i):
        s = i // tiles
        rows = pl.ds(pl.multiple_of(i % tiles * tile, tile), tile)
        same = as_column(seg_ref[pl.ds(s, 1), :]) == seg_ref[pl.ds(s, 1), rows]
        ones = jnp.ones((length, HEAD), BF16)
        for h in range(heads):
            at = h * HEAD
            q = qkv_ref[s, rows, at : at + HEAD]
            k = qkv_ref[s, :, part + at : part + at + HEAD]
            v = qkv_ref[s, :, 2 * part + at : 2 * part + at + HEAD]
            scores = jnp.where(same, mm(k, q, NT), MASKED)
            largest = jnp.max(scores, axis=0, keepdims=True)
            weights = jnp.exp(scores - largest)
            log_v[s, h : h + 1, rows] = largest + jnp.log(jnp.sum(weights, axis=0, keepdims=True))
            result = mm(weights.astype(BF16), jnp.concatenate([v, ones], axis=1), TN)
            result = (result[:, :HEAD] / result[:, HEAD : HEAD + 1]).astype(BF16)
            for j in range(tile // half):
                att_v[s, i % tiles * (tile // quarter) + j // 2, :, j % 2 * part + at : j % 2 * part + at + HEAD] = (
                    result[j * half : (j + 1) * half]
                )
        for k in range(2, p.lines):
            pl.when(i == k - 2)(lambda k=k: up.step(k))

        @pl.when(i == tiles - 1)
        def _():
            for kind in (2, 1, 0):
                att_copy(kind, 0).start()
            weight_ready()
            down.start()

        @pl.when(i == tiles)
        def _():
            enter(0)
            down.step(1)

        @pl.when(i == slots * tiles - 1)
        def _():
            for s in range(1, slots):
                for kind in (2, 1, 0):
                    att_copy(kind, s).start()

    def expand(q, s):
        hidden = mm(nm_ref[q, s], w_up(), NT) + vecs_ref[0:1, :inner]
        value, slope = gelu_parts(hidden)
        act_ref[q, s] = value.astype(BF16)
        gp_ref[q, s] = slope.astype(BF16)

    for k in range(slots * tiles + 2, p.lines):
        up.step(k)
    stores = []

    def store(src, dst):
        stores.append(pltpu.make_async_copy(src, dst, local.at[5 + len(stores)]))
        stores[-1].start()

    store(att_v, att_out)
    store(log_v, log_out)
    for k, (src, dst) in enumerate(((qkv_ref, qkv_out), (normed_ref, normed_out))):
        pltpu.make_async_copy(src, dst, local.at[k]).wait()
    for k in range(2 * slots):
        token_copy(2, k).wait_send()
    for copy in own_cots:
        copy.wait()
    for k in range(2, p.lines):
        down.step(k)
    pass_rows(0)
    for s in range(slots):
        cot_copy(0, s).wait_recv()
        cot_copy(2, s).start()
        cot_copy(1, s).start()
    up.finish()
    if pad > hidden_per:
        dense[1][...] = compact(ubuf[...], hidden_per)

    def near_rows(s):
        @pl.loop(0, 2)
        def _(i):
            pl.when(i > 0)(lambda: arrived(0, s))
            expand(jnp.where(i == 0, p.d, p.sib_d), s)

    near_rows(0)
    for s in range(1, slots):
        enter(s)
    down.finish()
    if small < block:
        dense[2][...] = compact(dbuf[...], small)
    for s in range(slots):
        cot_copy(1, s).wait_recv()
        cot_copy(2, s).wait_recv()
        cot_copy(2, s).wait_send()

    dbup_ref[...] = jnp.zeros_like(dbup_ref)

    def pull(q, s):
        g = (ct_ref[q, s].astype(F32) * group(s, 5)).astype(BF16)
        ct_ref[q, s] = g
        grad = (mm(g, w_down(), NN) * gp_ref[q, s].astype(F32)).astype(BF16)
        gp_ref[q, s] = grad
        dbup_ref[0:1, :] += jnp.sum(grad.astype(F32), axis=0, keepdims=True)
        gsc[...] = mm(grad, w_up(), NN)

    def part_copy(kind, s):
        if kind == 4:
            return push(xs_ref.at[s], xr_ref.at[s], p_s.at[4, s], p_r.at[4, s], p.far)
        return push(psend.at[kind, s], precv.at[kind, s], p_s.at[kind, s], p_r.at[kind, s], p.sib)

    def far_rows(s):
        @pl.loop(0, 2)
        def _(i):
            first = i == 0
            pl.when(first)(lambda: arrived(2, s))
            q = jnp.where(first, p.diag_d, p.far_d)
            expand(q, s)
            pull(q, s)

            @pl.when(first)
            def _():
                psend[0, s] = gsc[...].astype(BF16)
                part_copy(0, s).start()

            @pl.when(jnp.logical_not(first))
            def _():
                part_copy(0, s).wait_recv()
                xs_ref[s] = (gsc[...] + precv[0, s].astype(F32)).astype(BF16)
                part_copy(4, s).start()

    far_rows(0)
    for s in range(1, slots):
        near_rows(s)
    for s in range(1, slots):
        pass_rows(s)
        far_rows(s)

    @pl.loop(0, 2 * slots)
    def _(i):
        s = i // 2
        first = i % 2 == 0
        pull(jnp.where(first, p.sib_d, p.d), s)

        @pl.when(first)
        def _():
            psend[1, s] = gsc[...].astype(BF16)
            part_copy(1, s).start()

        @pl.when(jnp.logical_not(first))
        def _():
            gn_ref[s] = gsc[...]

    def weight_grad(left, right, out_ref, step=128):

        @pl.loop(0, left.shape[1] // step)
        def _(i):
            at = pl.ds(pl.multiple_of(i * step, step), step)
            out_ref[at, :] = mm(left[:, at], right[...], TN).astype(BF16)

    every = lambda ref: ref.reshape(m * slots * quarter, ref.shape[3])
    weight_grad(every(ct_ref), every(act_ref), dwd_ref.at[:width])
    if small < block:
        dwd_ref[...] = padded(dwd_ref[:width], n, block)
    dwd = dwd_ref.reshape(n, block, inner)
    red_down = Reduce(p, lambda f: dwd.at[f], side_d, total_d, None, rz)
    red_down.start()
    def grad_copy(kind, s):
        return push(
            gsend.at[s, ranks[kind]], grecv.at[s, p.d], g_s.at[kind, s], g_r.at[kind, s], peers[kind]
        )

    def leave(s):
        part_copy(1, s).wait_recv()
        part_copy(4, s).wait_recv()
        cot = cot_v[s].astype(F32)
        gn = gn_ref[s] + precv[1, s].astype(F32) + xr_ref[s].astype(F32)
        normal = nrm_ref[s]
        grad_middle = cot + norm_back(gn, normal, inv_ref[s], gain_mlp * (1.0 + group(s, 4)))
        gm_ref[s] = grad_middle
        gba = (grad_middle * group(s, 2)).astype(BF16)
        gba_ref[s] = gba
        gatt = mm(gba, w_out(), NN).astype(BF16)
        for r in range(m):
            for h in range(2):
                gsend[s, r, :, h * part : (h + 1) * part] = gatt[
                    h * half : (h + 1) * half, r * part : (r + 1) * part
                ]
        for kind in (2, 1, 0):
            grad_copy(kind, s).start()
        grecv[s, p.d] = gsend[s, p.d]
        total = lambda v: jnp.sum(v, axis=0, keepdims=True)
        sums_ref[s, 0:1, :] = total(gn)
        sums_ref[s, 1:2, :] = total(gn * normal)
        sums_ref[s, 3:4, :] = total(grad_middle * br_ref[s])
        sums_ref[s, 4:5, :] = total((cot * group(s, 5)).astype(BF16).astype(F32))
        sums_ref[s, 5:8, :] = jnp.zeros((3, width), F32)

    leave(0)
    weight_grad(every(gp_ref), every(nm_ref), dwu_ref.at[:inner])
    if pad > hidden_per:
        dwu_ref[...] = padded(dwu_ref[:inner], n, pad)

    store(dwu_ref.reshape(n, pad, width), dwu_out)

    for s in range(1, slots):
        leave(s)

    @pl.loop(0, 4 * slots)
    def _(i):
        s = i // 4
        j = i % 4
        q = jnp.where(
            j < 2, jnp.where(j == 0, p.diag_d, p.sib_d), jnp.where(j == 2, p.d, p.far_d)
        )
        gsc[...] = mm(act_ref[q, s], w_down(), NT)

        @pl.when(j == 0)
        def _():
            psend[2, s] = gsc[...].astype(BF16)
            part_copy(2, s).start()

        @pl.when(j == 1)
        def _():
            psend[3, s] = gsc[...].astype(BF16)
            part_copy(3, s).start()

        @pl.when(j == 2)
        def _():
            bo_ref[s] = gsc[...]

        @pl.when(j == 3)
        def _():
            part_copy(2, s).wait_recv()
            part_copy(4, s).wait_send()
            xs_ref[s] = (gsc[...] + precv[2, s].astype(F32)).astype(BF16)

    store(xs_ref, xsend_out)
    store(gm_ref, gm_out)
    flat = lambda ref: ref.reshape(slots * quarter, width)
    weight_grad(flat(gba_ref), flat(own_ref), dwo_ref.at[:width])
    if small < block:
        dwo_ref[...] = padded(dwo_ref[:width], n, block)
    rows = oswap.shape[1]
    dwo = dwo_ref.reshape(n, block // rows, rows, width)
    mine = p.c if rows < block else 0
    theirs = 1 - p.c if rows < block else 0
    dwo_swap = push(dwo.at[:, theirs], oswap, o_s.at[0], o_r.at[0], p.sib)
    dwo_swap.start()

    @pl.loop(0, slots)
    def _(s):
        part_copy(3, s).wait_recv()
        branch = bo_ref[s] + precv[3, s].astype(F32) + b_down
        mid_ref[s] = mid_ref[s] + group(s, 5) * branch
        sums_ref[s, 2:3, :] = jnp.sum(cot_v[s].astype(F32) * branch, axis=0, keepdims=True)

    store(mid_ref, base_out)
    for j in red_down.order():
        red_down.side_sum(j)
    store(total_d, downtotal_out)
    dwo_swap.wait_recv()
    oswap[...] = (dwo[:, mine].astype(F32) + oswap[...].astype(F32)).astype(BF16)
    store(oswap, outsum_out)
    for s in range(slots):
        for kind in range(3):
            grad_copy(kind, s).wait_recv()
    store(grecv, gatt_out)

    vec.drain()
    mods.drain()
    for item in (out, up, down) if filled else (qry, out, up, down):
        item.drain()
    if halves == 2:
        swap(p.c).wait_send()
    for k in range(2 * slots):
        for kind in range(2):
            token_copy(kind, k).wait_send()
    for j in range(p.lines):
        red_down.side_copy(j).wait_send()
    dwo_swap.wait_send()
    for s in range(slots):
        for kind in range(2):
            cot_copy(kind, s).wait_send()
        for kind in range(3):
            att_copy(kind, s).wait_send()
            grad_copy(kind, s).wait_send()
            for h in range(2):
                nm_copy(kind, s, h).wait_send()
        for kind in range(4):
            part_copy(kind, s).wait_send()
    for copy in stores:
        copy.wait()


def padded(rows, count, block):
    per = rows.shape[0] // count
    want = iota((count * block, rows.shape[0]), 0)
    have = iota((count * block, rows.shape[0]), 1)
    chosen = (have == want // block * per + want % block) & (want % block < per)
    return mm(chosen.astype(BF16), rows, NN).astype(BF16)


def front(n, m, length, tile, most, args):
    tokens, cond = args[0], args[2]
    w_ada, b_up = args[4], args[6]
    slots, quarter, width = tokens.shape
    part = width // m
    lines = n // 2
    dma = pltpu.SemaphoreType.DMA
    shape = jax.ShapeDtypeStruct
    vmem = pltpu.VMEM
    hidden_per = b_up.shape[0] // m
    small = width // n
    block = round16(small)
    pad = round16(hidden_per)
    inner = n * hidden_per
    halves = 2 if block % 32 == 0 else 1
    swapped = block // halves
    rows = (slots, quarter, width)
    att = (slots, m, quarter // 2, 2 * part)
    assert inner == width
    return pl.pallas_call(
        functools.partial(front_kernel, n, m, (hidden_per, small), tile),
        out_shape=(
            shape((slots, length, 3 * part), BF16),
            shape((slots, length, width), BF16),
            shape(att, BF16),
            shape((slots, 8, length), F32),
            shape(rows, F32),
            shape(rows, F32),
            shape(rows, BF16),
            shape(att, BF16),
            shape((n, pad, width), BF16),
            shape((lines, block, inner), BF16),
            shape((n, swapped, width), BF16),
            shape((slots, 1, 6 * width), F32),
            shape((8, width), F32),
            shape((3 * part, width), BF16),
            shape((n, 16, 128), BF16),
            shape((8, inner), F32),
            shape((slots, 8, width), F32),
        ),
        in_specs=[ANY] * 2 + [VM] * (len(args) - 2),
        out_specs=(ANY,) * 11 + (VM,) * 6,
        scratch_shapes=[
            vmem((slots, length, 3 * part), BF16),
            vmem(att, BF16),
            vmem(att, BF16),
            vmem((slots, 8, length), F32),
            vmem((n, slots, w_ada.shape[0]), F32),
            vmem((n, slots, w_ada.shape[0]), F32),
            vmem((16, 128), BF16),
            vmem((n, 16, 128), BF16),
            vmem((most, width), BF16),
            vmem((n, most, width), BF16),
            vmem((block, width), BF16),
            vmem((n, halves, swapped, width), BF16),
            vmem((pad, width), BF16),
            vmem((n, pad, width), BF16),
            vmem((block, inner), BF16),
            vmem((n, block, inner), BF16),
            vmem(rows, BF16),
            vmem(rows, BF16),
            vmem(rows, F32),
            vmem(rows, F32),
            vmem(rows, F32),
            vmem((slots, quarter, 1), F32),
            vmem((m,) + rows, BF16),
            vmem((m,) + rows, BF16),
            vmem((m,) + rows, BF16),
            vmem((m,) + rows, BF16),
            vmem((quarter, width), F32),
            vmem((4,) + rows, BF16),
            vmem((4,) + rows, BF16),
            vmem(rows, BF16),
            vmem(rows, BF16),
            vmem(rows, F32),
            vmem(rows, F32),
            vmem(rows, BF16),
            vmem(rows, F32),
            vmem(att, BF16),
            vmem(att, BF16),
            vmem((n * block, inner), BF16),
            vmem((n * pad, width), BF16),
            vmem((n * block, width), BF16),
            vmem((n, swapped, width), BF16),
            vmem((lines, block, inner), BF16),
            vmem((lines, block, inner), BF16),
            dma((4,)),
            dma((5, 4 * lines + 1)),
            dma((3, 2 * slots)),
            dma((3, 2 * slots)),
            dma((1,)),
            dma((1,)),
            dma((3, slots)),
            dma((3, slots)),
            dma((3, slots)),
            dma((3, slots)),
            dma((3, 2 * slots)),
            dma((3, 2 * slots)),
            dma((5, slots)),
            dma((5, slots)),
            dma((3, slots)),
            dma((3, slots)),
            dma((4 * lines + 1,)),
            dma((1,)),
            dma((1,)),
            dma((16,)),
        ],
        compiler_params=pltpu.CompilerParams(
            collective_id=1, has_side_effects=True, vmem_limit_bytes=LIMIT
        ),
        name="front",
    )(*args)


def back_kernel(
    n,
    m,
    per,
    tile,
    q_few,
    qkv_ref,
    grad_ref,
    att_ref,
    normed_ref,
    tok_ref,
    gm_ref,
    xsend_ref,
    cot_ref,
    base_ref,
    dwu_ref,
    downtotal_ref,
    outsum_ref,
    log_ref,
    seg_ref,
    cos_ref,
    sin_ref,
    wqkvt_ref,
    mod_ref,
    vec_ref,
    sums_ref,
    vblk_ref,
    wada_ref,
    dbup_ref,
    place_ref,
    dtok_out,
    out_out,
    down_out,
    up_out,
    wo_out,
    q_out,
    dcond_ref,
    dwada_ref,
    dbada_ref,
    dvec_ref,
    qkv_v,
    grad_v,
    att_v,
    gq_v,
    dk_ref,
    dv_ref,
    normed_v,
    tok_v,
    gm_v,
    other_v,
    cot_v,
    dtok_v,
    gsc,
    psend,
    precv,
    xs_ref,
    xr_ref,
    gn_ref,
    dwq_ref,
    dwu_v,
    outsum_v,
    total_d,
    zrecv_d,
    side_u,
    total_u,
    zrecv_u,
    side_o,
    total_o,
    zrecv_o,
    q_parts,
    q_sides,
    q_totals,
    q_zrecvs,
    spr_d,
    spr_u,
    spr_q,
    opiece,
    ofar,
    ofin,
    ssend,
    srecv,
    gsend,
    grecv,
    vsend,
    vrecv,
    dsend,
    drecv,
    p_s,
    p_r,
    rz,
    d_s,
    d_r,
    s_s,
    s_r,
    ex,
    x_s,
    x_r,
    local,
):
    p = Place(n, m)
    hidden_per, small = per
    slots, quarter, width = tok_ref.shape
    length = m * quarter
    half = quarter // 2
    part = width // m
    heads = part // HEAD
    lines = p.lines
    peers = (p.sib, p.far, p.diag)
    loads = [
        pltpu.make_async_copy(src, dst, local.at[k])
        for k, (src, dst) in enumerate(
            (
                (qkv_ref, qkv_v),
                (grad_ref, grad_v),
                (att_ref, att_v),
                (downtotal_ref, total_d),
                (dwu_ref, dwu_v),
                (outsum_ref, outsum_v),
                (normed_ref, normed_v),
                (tok_ref, tok_v),
                (gm_ref, gm_v),
                (cot_ref, cot_v),
            )
        )
    ]
    for load in loads:
        load.start()
    greet(list(peers) + p.ring())

    def other_copy(s):
        return push(xsend_ref.at[s], other_v.at[s], x_s.at[s], x_r.at[s], p.far)

    def part_copy(kind, s):
        if kind == 2:
            return push(xs_ref.at[s], xr_ref.at[s], p_s.at[2, s], p_r.at[2, s], p.far)
        return push(psend.at[kind, s], precv.at[kind, s], p_s.at[kind, s], p_r.at[kind, s], p.sib)

    for s in range(slots):
        other_copy(s).start()
    red_d = Reduce(p, None, None, total_d, zrecv_d, rz.at[0], summed=True)
    red_u = Reduce(p, lambda f: dwu_v.at[f], side_u, total_u, zrecv_u, rz.at[1])
    red_o = Reduce(p, lambda f: outsum_v.at[f], side_o, total_o, zrecv_o, rz.at[2])
    cuts = [ref.shape[1] for ref in q_parts]
    red_q = [
        Reduce(
            p,
            (lambda f, k=k: q_parts[k].at[f % 2]) if few else (lambda f, k=k: q_parts[k].at[f]),
            q_sides[k],
            q_totals[k],
            q_zrecvs[k],
            rz.at[3 + k],
            only=p.d if few else None,
        )
        for k, few in enumerate(q_few)
    ]
    down = Spread(p, lambda r: spr_d.at[r], d_s.at[0], d_r.at[0])
    up = Spread(p, lambda r: spr_u.at[r], d_s.at[1], d_r.at[1])
    firsts = [sum(cuts[:k]) for k in range(len(cuts))]
    qry = [
        Spread(
            p,
            lambda r, k=k: spr_q.at[r, pl.ds(firsts[k], cuts[k])],
            d_s.at[2 + k],
            d_r.at[2 + k],
        )
        for k in range(len(cuts))
    ]
    loads[4].wait()
    red_u.start()
    loads[3].wait()
    red_d.step(0)
    for k in (0, 1, 2):
        loads[k].wait()
    tiles = length // tile

    @pl.loop(0, slots)
    def _(s):
        dk_ref[...] = jnp.zeros_like(dk_ref)
        dv_ref[...] = jnp.zeros_like(dv_ref)
        column = as_column(seg_ref[pl.ds(s, 1), :])

        @pl.loop(0, tiles)
        def _(i):
            rows = pl.ds(pl.multiple_of(i * tile, tile), tile)
            same = column == seg_ref[pl.ds(s, 1), rows]
            cosine = cos_ref[rows, :HEAD]
            sine = sin_ref[rows, :HEAD]
            ones = jnp.ones((8, HEAD), BF16)
            for h in range(heads):
                at = h * HEAD
                q = qkv_v[s, rows, at : at + HEAD]
                k = qkv_v[s, :, part + at : part + at + HEAD]
                v = qkv_v[s, :, 2 * part + at : 2 * part + at + HEAD]
                g, o = [
                    jnp.concatenate(
                        [
                            ref[s, i * (tile // quarter) + j // 2, :, j % 2 * part + at : j % 2 * part + at + HEAD]
                            for j in range(tile // half)
                        ]
                    )
                    for ref in (grad_v, att_v)
                ]
                both = g.astype(F32) * o.astype(F32)
                high = both.astype(BF16)
                low = (both - high.astype(F32)).astype(BF16)
                inner = (mm(ones, high, NT) + mm(ones, low, NT))[:1]
                scores = jnp.where(same, mm(k, q, NT), MASKED)
                weights = jnp.exp(scores - log_ref[s, h : h + 1, rows])
                dots = mm(v, g, NT)
                dscores = (weights * (dots - inner)).astype(BF16)
                dq = mm(dscores, k, TN) * (1.0 / math.sqrt(HEAD))
                gq_v[s, rows, at : at + HEAD] = (dq * cosine - swap_halves(dq) * sine).astype(BF16)
                dk_ref[:, at : at + HEAD] += mm(dscores, q, NN)
                dv_ref[:, at : at + HEAD] += mm(weights.astype(BF16), g, NN)

            def reductions(first, red, steps):
                spread = -(-len(steps) // tiles)
                for k, t in enumerate(steps):
                    pl.when((s == first) & (i == k // spread))(lambda t=t: red.step(t))

            reductions(0, red_d, range(1, lines - 1))
            reductions(1, red_u, range(1, lines - 1))
            reductions(1, red_o, range(lines - 2))
            pl.when((s == 1) & (i == 0))(down.start)

        for at in range(0, part, 128):
            size = min(128, part - at)
            dk = dk_ref[:, at : at + size]
            other = turned(dk) if size == 128 else swap_halves(dk)
            dk = dk * cos_ref[:, :size] - other * sin_ref[:, :size]
            gq_v[s, :, part + at : part + at + size] = dk.astype(BF16)
        gq_v[s, :, 2 * part :] = dv_ref[...].astype(BF16)

        theirs = pl.ds(pl.multiple_of((1 - p.c) * quarter, quarter), quarter)
        ours = pl.ds(pl.multiple_of(p.c * quarter, quarter), quarter)

        def pull(j, chip):
            rows = pl.ds(pl.multiple_of(chip * 2 * quarter, 2 * quarter), 2 * quarter)
            gsc[...] = mm(gq_v[s, rows, :], wqkvt_ref[...], NN)
            psend[j, s] = gsc[theirs].astype(BF16)
            part_copy(j, s).start()

        pull(0, 1 - p.x)
        gn_ref[s] = gsc[ours]
        pull(1, p.x)
        part_copy(0, s).wait_recv()
        xs_ref[s] = (gn_ref[s] + precv[0, s].astype(F32)).astype(BF16)
        part_copy(2, s).start()
        gn_ref[s] = gsc[ours]

        @pl.when(s == 0)
        def _():
            loads[5].wait()
            red_o.start()
            red_d.own(spr_d.at[p.d])
            red_u.step(0)

    red_o.step(lines - 2)
    loads[6].wait()
    every = slots * length
    gq_all = gq_v.reshape(every, gq_v.shape[2])
    normed_all = normed_v.reshape(every, width)
    for at in range(0, gq_v.shape[2], part):
        dwq_ref[at : at + part, :] = mm(gq_all[:, at : at + part], normed_all[...], TN).astype(BF16)
    count = place_ref.shape[1]
    placing = (iota((dwq_ref.shape[0], count), 0) == place_ref[pl.ds(p.d, 1), :]).astype(BF16)
    blocks = mm(placing, dwq_ref[...], TN).astype(BF16)
    at = 0
    for ref in q_parts:
        size = ref.shape[0] * ref.shape[1]
        ref[...] = blocks[at : at + size].reshape(ref.shape)
        at += size
    for red in (*red_q[2:], red_q[0]):
        red.start()
    red_u.own(spr_u.at[p.d])
    red_o.own(opiece)
    halved = ofin.shape[0] == 2
    mine = p.c if halved else 0
    o_far = push(opiece, ofar, d_s.at[5, 0], d_r.at[5, 0], p.far)
    for red in red_q[1:2]:
        red.start()

    def group(s, k):
        return mod_ref[s, :, k * width : (k + 1) * width]

    gain_attn = vec_ref[1:2, :width]
    gain_mlp = vec_ref[2:3, :width]
    wide = dbup_ref.shape[1]
    total_rows = lambda v: jnp.sum(v, axis=0, keepdims=True)
    for k in range(7, 10):
        loads[k].wait()
    ssend[...] = jnp.zeros_like(ssend)

    def leave(s):
        other_copy(s).wait_recv()
        part_copy(1, s).wait_recv()
        part_copy(2, s).wait_recv()
        gn = gn_ref[s] + precv[1, s].astype(F32) + xr_ref[s].astype(F32)
        normal, inverse = norm_rows(tok_v[s].astype(F32))
        dtok_v[s] = (
            gm_v[s] + norm_back(gn, normal, inverse, gain_attn * (1.0 + group(s, 1)))
        ).astype(BF16)
        extra = total_rows(cot_v[s].astype(F32) * other_v[s].astype(F32))
        ssend[s, 0:1, :width] = total_rows(gn)
        ssend[s, 1:2, :width] = total_rows(gn * normal)
        ssend[s, 2:3, :width] = sums_ref[s, 3:4, :]
        ssend[s, 3:5, :width] = sums_ref[s, 0:2, :]
        ssend[s, 5:6, :width] = sums_ref[s, 2:3, :] + extra
        ssend[s, 6:7, :width] = sums_ref[s, 4:5, :]

    ssend[0, 7:8, :wide] = dbup_ref[0:1, :]
    leave(0)
    hops = [(k, t) for t in range(lines - 1) for k in reversed(range(len(cuts)))]
    hops = hops[: -len(cuts)], hops[-len(cuts) :]
    red_q[-1].step(0)
    for s in range(1, slots):
        leave(s)

    def sums_copy(kind):
        return push(ssend, srecv.at[p.d], s_s.at[kind], s_r.at[kind], peers[kind])

    for kind in (2, 1, 0):
        sums_copy(kind).start()
    o_far.start()
    up.start()
    srecv[p.d] = ssend[...]
    stores = []

    def store(src, dst):
        stores.append(pltpu.make_async_copy(src, dst, local.at[10 + len(stores)]))
        stores[-1].start()

    store(dtok_v, dtok_out)
    base_load = pltpu.make_async_copy(base_ref, gn_ref, local.at[23])
    base_load.start()
    for k, t in hops[0][1:]:
        red_q[k].step(t)
    for kind in range(3):
        sums_copy(kind).wait_recv()
    total = srecv[0]
    for r in range(1, m):
        total = total + srecv[r]
    cols = wada_ref.shape[0]
    gmod = []
    vecs = [jnp.zeros((1, width), F32)] * 3
    for s in range(slots):
        at = lambda k, s=s: total[s, k : k + 1, :width]
        gmod.append(
            jnp.concatenate(
                [at(0), at(1) * gain_attn, at(2), at(3), at(4) * gain_mlp, at(5)], axis=1
            )
        )
        vecs = [
            vecs[0] + at(1) * (1.0 + group(s, 1)),
            vecs[1] + at(4) * (1.0 + group(s, 4)),
            vecs[2] + at(6),
        ]
    gmod = jnp.concatenate(gmod, axis=0).astype(BF16).astype(F32)
    vsend[...] = jnp.zeros_like(vsend)
    pad = hidden_per
    for g in range(n):
        gsend[g] = gmod[:, g * cols : (g + 1) * cols]
        for k, v in enumerate(vecs):
            vsend[g, k : k + 1, :small] = v[:, g * small : (g + 1) * small]
        for r in range(m):
            vsend[g, 3 + r : 4 + r, :hidden_per] = srecv[r, 0, 7:8, g * pad : g * pad + hidden_per]

    gmods = Exchange(p, lambda f: gsend.at[f], grecv, ex.at[0], ex.at[1])
    gvecs = Exchange(p, lambda f: vsend.at[f], vrecv, ex.at[2], ex.at[3])
    gmods.start()
    gvecs.start()
    grecv[p.f] = gsend[p.f]
    vrecv[p.f] = vsend[p.f]
    base_load.wait()
    for s in range(slots):
        other_v[s] = (gn_ref[s] + group(s, 5) * other_v[s].astype(F32)).astype(BF16)
    store(other_v, out_out)
    down.forward()
    for k, t in hops[1]:
        red_q[k].step(t)
    up.forward()
    o_far.wait_recv()
    ofin[mine] = (opiece[...].astype(F32) + ofar[...].astype(F32)).astype(BF16)
    if halved:
        o_sib = push(ofin.at[mine], ofin.at[mine], d_s.at[5, 1], d_r.at[5, 1], p.sib)
        o_sib.start()
    for k in reversed(range(len(cuts))):
        red_q[k].own(qry[k].slot(p.d))
        qry[k].start()
    gmods.finish()
    got = jnp.concatenate([grecv[g] for g in range(n)], axis=0).astype(BF16)
    conds = jnp.concatenate([vblk_ref[g, 4 : 4 + slots] for g in range(n)], axis=0)
    dsend[...] = mm(got, wada_ref[...], NN).reshape(n, slots, conds.shape[1])

    gconds = Exchange(p, lambda f: dsend.at[f], drecv, ex.at[4], ex.at[5])
    gconds.start()
    drecv[p.f] = dsend[p.f]
    dwada_ref[...] = mm(got, conds, TN)
    dbada_ref[...] = jnp.sum(got.astype(F32), axis=0, keepdims=True)
    gvecs.finish()
    total = vrecv[0]
    for g in range(1, n):
        total = total + vrecv[g]
    dvec_ref[...] = total
    down.finish()
    store(spr_d, down_out)
    up.finish()
    store(spr_u, up_out)
    if halved:
        push(ofin.at[1 - mine], ofin.at[1 - mine], d_s.at[5, 1], d_r.at[5, 1], p.sib).wait_recv()
    store(ofin, wo_out)
    gconds.finish()
    total = drecv[0]
    for g in range(1, n):
        total = total + drecv[g]
    dcond_ref[...] = total
    for spread in qry:
        spread.forward()
    for spread in qry:
        spread.finish()
    store(spr_q, q_out)

    for s in range(slots):
        other_copy(s).wait_send()
        for kind in range(3):
            part_copy(kind, s).wait_send()
    for red in (red_d, red_u, red_o, *red_q):
        red.drain()
    for spread in (down, up, *qry):
        spread.drain()
    o_far.wait_send()
    if halved:
        o_sib.wait_send()
    for kind in range(3):
        sums_copy(kind).wait_send()
    for exchange in (gmods, gvecs, gconds):
        exchange.drain()
    for copy in stores:
        copy.wait()


def back(n, m, per, tile, parts, args):
    qkv, grad, att, normed, tokens = args[:5]
    dwu, downtotal, outsum = args[9:12]
    vblk, w_ada, dbup, place = args[20:24]
    slots, quarter, width = tokens.shape
    dma = pltpu.SemaphoreType.DMA
    shape = jax.ShapeDtypeStruct
    vmem = pltpu.VMEM
    rows = (slots, quarter, width)
    length = m * quarter
    part = width // m
    lines = n // 2
    wide = max(width, dbup.shape[1])
    _, block, inner = downtotal.shape
    pad = dwu.shape[1]
    orows = outsum.shape[1]
    halves = 2 if orows < block else 1
    most = sum(rows_k for rows_k, _ in parts)
    cols, cond = w_ada.shape
    lanes = max(per)

    def reduced(rows, wide):
        return [vmem((lines, rows, wide), BF16)] * 2 + [vmem((lines + 1, rows, wide), BF16)]

    return pl.pallas_call(
        functools.partial(back_kernel, n, m, per, tile, [few for _, few in parts]),
        out_shape=(
            shape(rows, BF16),
            shape(rows, BF16),
            shape((m, block, inner), BF16),
            shape((m, pad, width), BF16),
            shape((halves, orows, width), BF16),
            shape((m, most, width), BF16),
            shape((slots, cond), F32),
            shape((cols, cond), F32),
            shape((1, cols), F32),
            shape((8, lanes), F32),
        ),
        in_specs=[ANY] * 12 + [VM] * (len(args) - 12),
        out_specs=(ANY,) * 6 + (VM,) * 4,
        scratch_shapes=[
            vmem(qkv.shape, BF16),
            vmem(grad.shape, BF16),
            vmem(att.shape, BF16),
            vmem(qkv.shape, BF16),
            vmem((length, part), F32),
            vmem((length, part), F32),
            vmem(normed.shape, BF16),
            vmem(rows, BF16),
            vmem(rows, F32),
            vmem(rows, BF16),
            vmem(rows, BF16),
            vmem(rows, BF16),
            vmem((2 * quarter, width), F32),
            vmem((2,) + rows, BF16),
            vmem((2,) + rows, BF16),
            vmem(rows, BF16),
            vmem(rows, BF16),
            vmem(rows, F32),
            vmem((qkv.shape[2], width), BF16),
            vmem(dwu.shape, BF16),
            vmem(outsum.shape, BF16),
        ]
        + reduced(block, inner)[1:]
        + reduced(pad, width)
        + reduced(orows, width)
        + [
            [vmem((2 if few else n, rows_k, width), BF16) for rows_k, few in parts],
            [vmem((lines, rows_k, width), BF16) for rows_k, _ in parts],
            [vmem((lines, rows_k, width), BF16) for rows_k, _ in parts],
            [vmem((lines + 1, rows_k, width), BF16) for rows_k, _ in parts],
        ]
        + [
            vmem((m, block, inner), BF16),
            vmem((m, pad, width), BF16),
            vmem((m, most, width), BF16),
            vmem((orows, width), BF16),
            vmem((orows, width), BF16),
            vmem((halves, orows, width), BF16),
            vmem((slots, 8, wide), F32),
            vmem((m, slots, 8, wide), F32),
            vmem((n, slots, cols), F32),
            vmem((n, slots, cols), F32),
            vmem((n, 8, lanes), F32),
            vmem((n, 8, lanes), F32),
            vmem((n, slots, cond), F32),
            vmem((n, slots, cond), F32),
            dma((3, slots)),
            dma((3, slots)),
            dma((6, 4 * lines + 1)),
            dma((6, 3)),
            dma((6, 3)),
            dma((3,)),
            dma((3,)),
            dma((6,)),
            dma((slots,)),
            dma((slots,)),
            dma((24,)),
        ],
        compiler_params=pltpu.CompilerParams(
            collective_id=3, has_side_effects=True, vmem_limit_bytes=LIMIT
        ),
        name="back",
    )(*args)


def finish_kernel(
    n,
    m,
    per,
    outs_ref,
    dtok_ref,
    dwada_ref,
    down_ref,
    up_ref,
    wo_ref,
    q_ref,
    dcond_ref,
    dbada_ref,
    dvec_ref,
    home_ref,
    out_ref,
    dtok_out,
    dwada_out,
    dwqkv_ref,
    dwout_ref,
    dwup_ref,
    dwdown_ref,
    dcond_out,
    dbada_out,
    dga_out,
    dgm_out,
    dbup_out,
    dbdown_out,
    up_v,
    down_v,
    q_v,
    wo_v,
    dtok_v,
    dwada_v,
    dwup_v,
    dwdown_v,
    dwqkv_v,
    dwout_v,
    out_v,
    local,
):
    hidden_per, small = per
    width = outs_ref.shape[2]
    pad = hidden_per
    part = width // m
    sources = (up_ref, down_ref, q_ref, wo_ref, outs_ref, dtok_ref, dwada_ref)
    places = (up_v, down_v, q_v, wo_v, out_v, dtok_v, dwada_v)
    loads = [
        pltpu.make_async_copy(src, dst, local.at[k])
        for k, (src, dst) in enumerate(zip(sources, places))
    ]
    for load in loads:
        load.start()
    stores = []

    def store(src, dst):
        stores.append(pltpu.make_async_copy(src, dst, local.at[7 + len(stores)]))
        stores[-1].start()

    loads[0].wait()
    dwup_v[...] = jnp.concatenate([up_v[r][:hidden_per] for r in range(m)]).astype(F32).T
    store(dwup_v, dwup_ref)
    loads[1].wait()
    for r in range(m):
        piece = down_v[r, :small].astype(F32)
        for g in range(n):
            at = (g * m + r) * hidden_per
            dwdown_v[:, at : at + hidden_per] = piece[:, g * pad : g * pad + hidden_per]
    store(dwdown_v, dwdown_ref)
    loads[2].wait()
    count = q_v.shape[0] * q_v.shape[1]
    f = lax.axis_index("fsdp")
    homing = (iota((dwqkv_ref.shape[0], count), 0) == home_ref[pl.ds(f, 1), :]).astype(BF16)
    dwqkv_v[...] = mm(homing, q_v[...].reshape(count, width), NN)
    store(dwqkv_v, dwqkv_ref)
    for k, src, dst in ((4, out_v, out_ref), (5, dtok_v, dtok_out), (6, dwada_v, dwada_out)):
        loads[k].wait()
        store(src, dst)
    loads[3].wait()
    piece = wo_v[...].reshape(-1, width)[:small].astype(F32)
    heads = part // HEAD
    for r in range(m):
        for h in range(heads):
            at = r * part + h * HEAD
            dwout_v[:, (h * m + r) * HEAD : (h * m + r + 1) * HEAD] = piece[:, at : at + HEAD]
    store(dwout_v, dwout_ref)
    dcond_out[...] = dcond_ref[...].astype(BF16)
    dbada_out[...] = dbada_ref[0, :]
    for row, ref in ((0, dga_out), (1, dgm_out), (2, dbdown_out)):
        ref[...] = dvec_ref[row, :small]
    dbup_out[...] = jnp.concatenate(
        [dvec_ref[3 + r : 4 + r, :hidden_per] for r in range(m)], axis=1
    ).reshape(-1)
    for copy in stores:
        copy.wait()


def finish(n, m, per, columns, args):
    outs, dtok, dwada, down, up, wo, q, dcond, dbada = args[:9]
    hidden_per, small = per
    rows = outs.shape
    width = rows[2]
    shape = jax.ShapeDtypeStruct
    vmem = pltpu.VMEM
    sizes = (
        (width, m * hidden_per),
        (small, n * m * hidden_per),
        (columns, width),
        (small, width),
    )
    return pl.pallas_call(
        functools.partial(finish_kernel, n, m, per),
        out_shape=(
            shape(rows, BF16),
            shape(rows, BF16),
            shape(dwada.shape, F32),
            shape(sizes[2], F32),
            shape(sizes[3], F32),
            shape(sizes[0], F32),
            shape(sizes[1], F32),
            shape(dcond.shape, BF16),
            shape(dbada.shape[1:], F32),
            shape((small,), F32),
            shape((small,), F32),
            shape((m * hidden_per,), F32),
            shape((small,), F32),
        ),
        in_specs=[ANY] * 7 + [VM] * 4,
        out_specs=(ANY,) * 7 + (VM,) * 6,
        scratch_shapes=[
            vmem(up.shape, BF16),
            vmem(down.shape, BF16),
            vmem(q.shape, BF16),
            vmem(wo.shape, BF16),
            vmem(rows, BF16),
            vmem(dwada.shape, F32),
        ]
        + [vmem(size, F32) for size in sizes]
        + [vmem(rows, BF16), pltpu.SemaphoreType.DMA((14,))],
        compiler_params=pltpu.CompilerParams(vmem_limit_bytes=LIMIT),
        name="finish",
    )(*args)


def column_plan(shards_n, ranks, columns):
    per = columns // shards_n
    rank_of = (np.arange(columns) // HEAD) % ranks
    lists = [
        [[c for c in range(per) if rank_of[f * per + c] == r] for r in range(ranks)]
        for f in range(shards_n)
    ]
    most = max(len(l) for row in lists for l in row)
    most = -(-most // 16) * 16
    take = np.full((shards_n, ranks, most), -1, np.int32)
    place = np.full((ranks, shards_n * most), -1, np.int32)
    home = np.full((shards_n, ranks * most), -1, np.int32)
    for r in range(ranks):
        order = {c: i for i, c in enumerate(np.flatnonzero(rank_of == r))}
        for f in range(shards_n):
            for i, c in enumerate(lists[f][r]):
                take[f, r, i] = c
                place[r, f * most + i] = order[f * per + c]
                home[f, r * most + i] = c
    return most, take, place, home


def row_parts(shards_n, ranks, columns):
    per = columns // shards_n
    rank_of = (np.arange(columns) // HEAD) % ranks
    lists = [
        [[c for c in range(per) if rank_of[f * per + c] == r] for r in range(ranks)]
        for f in range(shards_n)
    ]
    most = max(len(l) for row in lists for l in row)
    least = min(len(l) for row in lists for l in row)
    uneven = all(
        len(lists[f][r]) == (most if f // 2 == r else least)
        for f in range(shards_n)
        for r in range(ranks)
    )
    if uneven and least % 32 == 0 and (most - least) % 16 == 0 and most > least and shards_n == 2 * ranks:
        parts = [(least // 2, False), (least // 2, False), (most - least, True)]
    else:
        parts = [(round16(most), False)]
    place = []
    for r in range(ranks):
        order = {c: i for i, c in enumerate(np.flatnonzero(rank_of == r))}
        row, first = [], 0
        for rows, few in parts:
            for f in (2 * r, 2 * r + 1) if few else range(shards_n):
                own = lists[f][r][first : first + rows]
                row += [order[f * per + c] for c in own] + [-1] * (rows - len(own))
            first += rows
        place.append(row)
    home = []
    for f in range(shards_n):
        row = []
        for r in range(ranks):
            first = 0
            for rows, few in parts:
                own = lists[f][r][first : first + rows]
                row += own + [-1] * (rows - len(own))
                first += rows
        home.append(row)
    return parts, np.asarray(place, np.int32), np.asarray(home, np.int32)


def shards(
    tokens,
    condition,
    segments,
    w_ada,
    b_ada,
    gain_attn,
    w_qkv,
    w_out,
    gain_mlp,
    w_up,
    b_up,
    w_down,
    b_down,
    cotangent,
):
    slots, quarter, width = tokens.shape
    length = segments.shape[1]
    n = lax.axis_size("fsdp")
    m = lax.axis_size("dp")
    hidden_per = b_up.shape[0] // m
    small = gain_attn.shape[0]
    per = (hidden_per, small)
    columns = w_qkv.shape[1]
    most, take, place, _ = column_plan(n, m, columns * n)
    place = jnp.asarray(place)
    tile = 2 * quarter if n * most <= 2 * width else quarter
    parts, place_back, home = row_parts(n, m, columns * n)
    place_back = jnp.asarray(place_back)
    cosine, sine = [jnp.asarray(np.concatenate([v, v], axis=1)) for v in rope_table(length)]

    (
        qkv,
        normed,
        attended,
        logs,
        grad_middle,
        base,
        far_part,
        grad_attended,
        dw_up,
        down_total,
        out_sum,
        mod,
        vec,
        w_qkv_t,
        vec_blocks,
        db_up,
        sums,
    ) = front(
        n,
        m,
        length,
        tile,
        most,
        (
            tokens,
            cotangent,
            condition,
            segments,
            w_ada.T,
            b_ada,
            b_up,
            gain_attn,
            gain_mlp,
            b_down,
            w_qkv.T,
            w_out.T,
            w_up,
            w_down.T,
            jnp.asarray(take.reshape(n * m, most)),
            place,
            cosine,
            sine,
        ),
    )
    d_tokens, outputs, down_all, up_all, out_all, qkv_all, d_cond, d_w_ada, d_b_ada, d_vec = back(
        n,
        m,
        per,
        tile,
        parts,
        (
            qkv,
            grad_attended,
            attended,
            normed,
            tokens,
            grad_middle,
            far_part,
            cotangent,
            base,
            dw_up,
            down_total,
            out_sum,
            logs,
            segments,
            cosine,
            sine,
            w_qkv_t,
            mod,
            vec,
            sums,
            vec_blocks,
            w_ada.T,
            db_up,
            place_back,
        ),
    )
    (
        outputs,
        d_tokens,
        d_w_ada,
        d_w_qkv,
        d_w_out,
        d_w_up,
        d_w_down,
        d_cond,
        d_b_ada,
        d_gain_attn,
        d_gain_mlp,
        d_b_up,
        d_b_down,
    ) = finish(
        n,
        m,
        per,
        columns,
        (
            outputs,
            d_tokens,
            d_w_ada,
            down_all,
            up_all,
            out_all,
            qkv_all,
            d_cond,
            d_b_ada,
            d_vec,
            jnp.asarray(home),
        ),
    )
    return (
        outputs,
        d_tokens,
        d_cond,
        d_w_ada.T,
        d_b_ada,
        d_gain_attn,
        d_w_qkv.T,
        d_w_out.T,
        d_gain_mlp,
        d_w_up,
        d_b_up,
        d_w_down.T,
        d_b_down,
    )


def solution(mesh):
    return jax.shard_map(
        shards,
        mesh=mesh,
        in_specs=(
            P("fsdp", "dp", None),
            P("fsdp", None),
            P("fsdp", None),
            P(None, "fsdp"),
            P("fsdp"),
            P("fsdp"),
            P(None, "fsdp"),
            P(None, "fsdp"),
            P("fsdp"),
            P(None, "fsdp"),
            P("fsdp"),
            P(None, "fsdp"),
            P("fsdp"),
            P("fsdp", "dp", None),
        ),
        out_specs=(
            P("fsdp", "dp", None),
            P("fsdp", "dp", None),
            P("fsdp", None),
            P(None, "fsdp"),
            P("fsdp"),
            P("fsdp"),
            P(None, "fsdp"),
            P(None, "fsdp"),
            P("fsdp"),
            P(None, "fsdp"),
            P("fsdp"),
            P(None, "fsdp"),
            P("fsdp"),
        ),
        check_vma=False,
    )
```
